32 devices in a mesh: group: 2 (over x), row: 16 (over z, y, core).
Axes of the slice: x: 2, y: 2, z: 4, core: 2. Of those that a mesh axis runs over, the one named last changes fastest.
Arguments:
- features: bfloat16 [32, 65536], P(None, ('group', 'row')), parts along dimension 1
- right_side: float32 [8, 65536], P(None, ('group', 'row')), parts along dimension 1
- variance: float32 [65536], P(('group', 'row')), parts along dimension 0, may hold values from 0.5 to 2
- hilbert_order: int32 [32, 2048], P(('group', 'row')), parts along dimension 0, may hold values from 0 to 2047, each once within a row
- tile_list: int32 [32, 5, 2], P(('group', 'row')), parts along dimension 0, may hold values from -1 to 15, as said below
Outputs:
- solution: float32 [8, 65536], P(None, ('group', 'row')), parts along dimension 1
- residual: float32 [8, 65536], P(None, ('group', 'row')), parts along dimension 1
The draws below stay inside these ranges and needn't reach their ends.
There are 2 independent parts, one for each index of `group`. The reference program is written for one: setup_inputs(seed, part) draws one part's arguments, and reference() takes and returns one part's arrays. A program takes and returns all parts, laid end to end along the dimension named above; each array names one. Nothing has to cross between parts.
Inputs may be any that keep to these rules, and one draw needn't show every extreme that they name: `tile_list`: row s lists the blocks coupled to block s above it: valid entries (s, b) with b > s first, in rising b, then (-1, -1). The blocks fall into disjoint groups of at most 6 blocks; two blocks are coupled exactly when they share a group. Some block lists 5 entries. `hilbert_order`: each row is a permutation.
All inputs are finite; a program needn't handle non-finite values.
Results may differ from the reference program's by a relative error of at most 0.0072.
Values may be sent and summed in bfloat16 or wider, within the bound.
No kernel may reach another device: no remote copies, remote signals or barrier semaphores. Data moves between devices by JAX's collectives and lax.ppermute only.
A program may use at most 128 MiB of HBM per device.

```python
import math
import jax
import jax.numpy as jnp
from jax import lax

FEAT = 32
RHS = 8
TILE = 2048
LM = 6
ITERS = 2
MAXT = 5
BLOCKS = 16
POINTS = 32768


def block_groups(key):
    key = jax.random.fold_in(key, 5)
    key_perm, key_start, key_flag = jax.random.split(key, 3)
    position = jnp.arange(BLOCKS, dtype=jnp.int32)
    shuffled = jax.random.permutation(key_perm, BLOCKS).astype(jnp.int32)
    first_start = jax.random.randint(key_start, (), 0, BLOCKS - LM + 1)
    coin_flip = jax.random.randint(key_flag, (BLOCKS,), 0, 4)
    starts = (coin_flip == 0) | (jnp.mod(position - first_start, LM) == 0) | (position == 0)
    inside = (position > first_start) & (position < first_start + LM)
    starts = starts & jnp.logical_not(inside)
    group_pos = jnp.cumsum(starts.astype(jnp.int32))
    return jnp.zeros((BLOCKS,), jnp.int32).at[shuffled].set(group_pos)


def draw_features(key, part):
    group_of = block_groups(key)
    key = jax.random.fold_in(key, 11)
    key_cent, key_pick, key_scale, key_noise, key_size = jax.random.split(key, 5)
    per_group = max(TILE // 4, 1)
    centre_count = (BLOCKS + 1) * per_group
    block_index = jnp.arange(POINTS, dtype=jnp.int32) // TILE
    cluster = group_of[block_index] * per_group + jax.random.randint(key_pick, (POINTS,), 0, per_group)
    lower_end, upper_end = (0.316, 0.6)
    noise_low, noise_high = (0.03, 0.12)
    centre_base = jax.random.normal(key_cent, (FEAT, centre_count), jnp.float32)
    noise_base = jax.random.normal(key_noise, (FEAT, POINTS), jnp.float32)
    centre_scale = jnp.exp(jax.random.uniform(key_scale, (centre_count,), jnp.float32, math.log(lower_end), math.log(upper_end)))
    noise_scale = jnp.exp(jax.random.uniform(key_size, (POINTS,), jnp.float32, math.log(noise_low), math.log(noise_high)))
    centres = centre_base * centre_scale[None, :] / math.sqrt(FEAT)
    values = jnp.take(centres, cluster, axis=1) + noise_base * noise_scale[None, :] / math.sqrt(FEAT)
    return values.astype(jnp.bfloat16)


def draw_right_side(key, part):
    key = jax.random.fold_in(key, 17)
    key_spread, key_values = jax.random.split(key)
    along = jnp.arange(POINTS, dtype=jnp.float32) / POINTS
    rising = 1.0 + 2.0 * along
    spread_log = math.log(3.3)
    base_values = jax.random.normal(key_values, (RHS, POINTS), jnp.float32)
    spread = jnp.exp(jax.random.uniform(key_spread, (POINTS,), jnp.float32, 0.0, spread_log))
    return base_values * (rising * spread)[None, :]


def draw_tile_list(key, part):
    group_of = block_groups(key)
    position = jnp.arange(BLOCKS, dtype=jnp.int32)
    shared = (group_of[:, None] == group_of[None, :]) & (position[None, :] > position[:, None])
    ranking = jnp.where(shared, position[None, :], BLOCKS + position[None, :])
    picked = jnp.sort(ranking, axis=1)[:, :MAXT]
    valid = picked < BLOCKS
    partner = jnp.where(valid, picked, -1)
    owner_block = jnp.where(valid, position[:, None], -1)
    return jnp.stack([owner_block, partner], axis=-1).astype(jnp.int32)


def level_of(own_key, dims, cuts, smallest, largest):
    gain, own = 1.0, jax.random.fold_in(own_key, 6)
    for axis_at, blocks in cuts:
        heights = jnp.exp(jax.random.uniform(jax.random.fold_in(own, axis_at), (blocks,), jnp.float32, smallest / len(cuts), largest / len(cuts)))
        gain = gain * jnp.repeat(heights, dims[axis_at] // blocks).reshape([-1 if axis == axis_at else 1 for axis in range(len(dims))])
    return gain


def setup_inputs(seed: int = 0, part: int = 0) -> dict:
    keys = jax.random.split(jax.random.key(seed), 6)
    part_keys = jax.random.split(jax.random.fold_in(keys[5], part), 6)
    features = draw_features(jax.random.fold_in(jax.random.fold_in(keys[5], part), 71), part)
    right_side = draw_right_side(jax.random.fold_in(jax.random.fold_in(keys[5], part), 71), part)
    variance = jnp.clip(jnp.exp(math.log(2.0) - 1.3862944 * jax.random.uniform(part_keys[2], (POINTS,), jnp.float32) ** level_of(part_keys[2], (POINTS,), ((0, 16),), -0.2, 0.2)), 0.5, 2.0)
    hilbert_order = jax.vmap(lambda own: jax.random.permutation(own, TILE))(jax.random.split(part_keys[3], BLOCKS)).reshape((BLOCKS, TILE)).astype(jnp.int32)
    tile_list = draw_tile_list(jax.random.fold_in(jax.random.fold_in(keys[5], part), 71), part)
    return dict(features=features, right_side=right_side, variance=variance, hilbert_order=hilbert_order, tile_list=tile_list)


def wendland(left_feat, left_norm, right_feat, right_norm):
    gram = jnp.dot(left_feat.T, right_feat, preferred_element_type=jnp.float32)
    dist_sq = jnp.maximum(left_norm[:, None] + right_norm[None, :] - 2.0 * gram, 0.0)
    radius = jnp.sqrt(dist_sq)
    remain = jnp.maximum(1.0 - radius, 0.0)
    power_two = remain * remain
    power_four = power_two * power_two
    power_eight = power_four * power_four
    power_sixteen = power_eight * power_eight
    return (power_sixteen * power_two * remain * (19.0 * radius + 1.0)).astype(jnp.bfloat16)

def block_of(array_in, block_id):
    start_col = (block_id * TILE).astype(jnp.int32)
    return lax.dynamic_slice_in_dim(array_in, start_col, TILE, array_in.ndim - 1)

def add_block(accum, block_id, term):
    start_col = (block_id * TILE).astype(jnp.int32)
    old_part = lax.dynamic_slice_in_dim(accum, start_col, TILE, 1)
    return lax.dynamic_update_slice_in_dim(accum, old_part + term, start_col, 1)

def operate(direction, ordered, norm_all, var_ordered, tile_list):
    rounded = direction.astype(jnp.bfloat16)
    result = var_ordered[None, :] * direction

    def diag_step(block_idx, accum):
        block_id = jnp.asarray(block_idx).astype(jnp.int32)
        kernel = wendland(block_of(ordered, block_id), block_of(norm_all, block_id), block_of(ordered, block_id), block_of(norm_all, block_id))
        term = jnp.dot(block_of(rounded, block_id), kernel.T, preferred_element_type=jnp.float32)
        return add_block(accum, block_id, term)
    result = lax.fori_loop(0, BLOCKS, diag_step, result)
    flat_list = tile_list.reshape(-1, 2).astype(jnp.int32)

    def pair_step(entry_idx, accum):
        row_block = flat_list[entry_idx, 0]
        col_block = flat_list[entry_idx, 1]

        def pair_work(acc_in):
            kernel = wendland(block_of(ordered, row_block), block_of(norm_all, row_block), block_of(ordered, col_block), block_of(norm_all, col_block))
            row_term = jnp.dot(block_of(rounded, col_block), kernel.T, preferred_element_type=jnp.float32)
            col_term = jnp.dot(block_of(rounded, row_block), kernel, preferred_element_type=jnp.float32)
            acc_out = add_block(acc_in, row_block, row_term)
            return add_block(acc_out, col_block, col_term)
        return lax.cond(row_block >= 0, pair_work, lambda acc_in: acc_in, accum)
    return lax.fori_loop(0, flat_list.shape[0], pair_step, result)

def reference(features, right_side, variance, hilbert_order, tile_list):
    position = (jnp.arange(BLOCKS, dtype=jnp.int32)[:, None] * TILE + hilbert_order.astype(jnp.int32)).reshape(-1)
    ordered = features[:, position]
    rhs_ordered = right_side[:, position]
    var_ordered = variance[position]
    norm_all = lax.optimization_barrier(jnp.sum(jnp.square(ordered.astype(jnp.float32)), axis=0))
    sol_ord = jnp.zeros_like(rhs_ordered)
    res_ord = rhs_ordered
    direction = rhs_ordered
    norm_now = lax.optimization_barrier(jnp.sum(res_ord * res_ord, axis=1))
    for iteration in range(ITERS):
        image = operate(direction, ordered, norm_all, var_ordered, tile_list)
        step_size = norm_now / lax.optimization_barrier(jnp.sum(direction * image, axis=1))
        sol_ord = sol_ord + step_size[:, None] * direction
        res_ord = res_ord - step_size[:, None] * image
        if iteration + 1 < ITERS:
            norm_next = lax.optimization_barrier(jnp.sum(res_ord * res_ord, axis=1))
            direction = res_ord + (norm_next / norm_now)[:, None] * direction
            norm_now = norm_next
    return (sol_ord, res_ord)
```

```python
import jax
import jax.numpy as jnp
import numpy as np
from jax import lax
from jax.experimental import pallas as pl
from jax.experimental.pallas import tpu as pltpu
from jax.sharding import PartitionSpec as P

SHRINK = 0.95
SCALE = 20.0 * (20.0 / 19.0) ** 19
DIAGONAL = float(1.0 - SCALE * float(np.float32(1.0 / SCALE).astype(jnp.bfloat16)))
KDIM = 128
CHUNK = 256
ROWS = 512


def split_three(value):
    high = value.astype(jnp.bfloat16).astype(jnp.float32)
    rest = value - high
    middle = rest.astype(jnp.bfloat16).astype(jnp.float32)
    return high, middle, rest - middle


def norm_rows(norm, first):
    high, middle, low = split_three(norm)
    row = lax.broadcasted_iota(jnp.int32, (32, norm.shape[1]), 0)
    out = jnp.where(row < 6, 1.0, 0.0)
    out = jnp.where(row == first, high, out)
    out = jnp.where(row == first + 1, middle, out)
    return jnp.where(row == first + 2, low, out).astype(jnp.bfloat16)


def own_factor(feat):
    wide = feat.astype(jnp.float32)
    norm = jnp.sum(wide * wide, axis=0, keepdims=True) * (SHRINK * SHRINK)
    pieces = split_three(wide * (-2.0 * SHRINK * SHRINK))
    return jnp.concatenate(
        [piece.astype(jnp.bfloat16) for piece in pieces] + [norm_rows(norm, 0)], axis=0
    )


def other_factor(feat):
    wide = feat.astype(jnp.float32)
    norm = jnp.sum(wide * wide, axis=0, keepdims=True) * (SHRINK * SHRINK)
    whole = jnp.concatenate([feat, feat, feat, norm_rows(norm, 3)], axis=0)
    return jnp.transpose(whole)


def psi_tile(dist):
    dist = jnp.maximum(dist, 1e-30)
    radius = dist * lax.rsqrt(dist)
    u = jnp.maximum(SHRINK - radius, 0.0)
    two = u * u
    four = two * two
    eight = four * four
    sixteen = eight * eight
    return (sixteen * two * (u - two)).astype(jnp.bfloat16)


def tile_rows(left_ref, right_ref, vec_ref, begin, tile_ref, sum_ref):
    width = right_ref.shape[1]

    def step(index, carry):
        at = pl.multiple_of(index * CHUNK, CHUNK)
        left = left_ref[pl.ds(pl.multiple_of(begin + at, CHUNK), CHUNK), :]
        vec = vec_ref[:, pl.ds(pl.multiple_of(begin + at, CHUNK), CHUNK)]
        for col in range(0, width, CHUNK):
            parts = []
            for half in range(0, CHUNK, 128):
                dist = jnp.dot(
                    left[half : half + 128],
                    right_ref[:, col : col + CHUNK],
                    preferred_element_type=jnp.float32,
                )
                part = psi_tile(dist)
                tile_ref[pl.ds(at + half, 128), col : col + CHUNK] = part
                parts.append(part)
            sum_ref[:, col : col + CHUNK] += jnp.dot(
                vec, jnp.concatenate(parts, axis=0), preferred_element_type=jnp.float32
            )
        return carry

    lax.fori_loop(0, ROWS // CHUNK, step, 0)


def own_kernel(pay_ref, tile_ref, sum_ref, left_ref, right_ref, vec_ref):
    step = pl.program_id(0)

    @pl.when(step == 0)
    def _():
        pay = pay_ref[...]
        left_ref[...] = other_factor(pay[:32])
        right_ref[...] = own_factor(pay[:32])
        vec_ref[...] = pay[32:40]
        sum_ref[...] = jnp.zeros_like(sum_ref)

    tile_rows(left_ref, right_ref, vec_ref, step * ROWS, tile_ref, sum_ref)


def pair_kernel(
    slots_ref, own_ref, pay_ref, first_ref, tile_ref, sum_ref, left_ref, right_ref, vec_ref
):
    slot, step = pl.program_id(0), pl.program_id(1)

    @pl.when((slot == 0) & (step == 0))
    def _():
        right_ref[...] = own_factor(own_ref[...][:32])
        sum_ref[...] = first_ref[...]

    @pl.when(slot < slots_ref[0])
    def _():
        @pl.when(step == 0)
        def _():
            pay = pay_ref[0]
            left_ref[...] = other_factor(pay[:32])
            vec_ref[...] = pay[32:40]

        tile_rows(left_ref, right_ref, vec_ref, step * ROWS, tile_ref.at[0], sum_ref)


def again_kernel(slots_ref, tile_ref, vec_ref, first_ref, sum_ref):
    slot, step = pl.program_id(0), pl.program_id(1)

    @pl.when((slot == 0) & (step == 0))
    def _():
        sum_ref[...] = first_ref[...]

    @pl.when(slot < slots_ref[0])
    def _():
        at = pl.multiple_of(step * ROWS, ROWS)
        sum_ref[...] += jnp.dot(
            vec_ref[0, :, pl.ds(at, ROWS)], tile_ref[0], preferred_element_type=jnp.float32
        )


def own_again_kernel(tile_ref, vec_ref, sum_ref):
    step = pl.program_id(0)

    @pl.when(step == 0)
    def _():
        sum_ref[...] = jnp.zeros_like(sum_ref)

    at = pl.multiple_of(step * ROWS, ROWS)
    sum_ref[...] += jnp.dot(
        vec_ref[:, pl.ds(at, ROWS)], tile_ref[...], preferred_element_type=jnp.float32
    )


def order_kernel(rows_ref, perm_ref, out_ref):
    rows = rows_ref[...]
    count, width = rows.shape
    pieces = jnp.concatenate([piece for piece in split_three(rows)], axis=0).astype(jnp.bfloat16)
    perm = perm_ref[...]
    for col in range(0, width, CHUNK):
        total = jnp.zeros((3 * count, CHUNK), jnp.float32)
        for at in range(0, width, CHUNK):
            index = lax.broadcasted_iota(jnp.int32, (CHUNK, CHUNK), 0) + at
            pick = jnp.where(index == perm[:, col : col + CHUNK], 1.0, 0.0).astype(jnp.bfloat16)
            total += jnp.dot(pieces[:, at : at + CHUNK], pick, preferred_element_type=jnp.float32)
        out_ref[:, col : col + CHUNK] = (
            total[:count] + total[count : 2 * count] + total[2 * count :]
        )


def swap(value, mask, count):
    return lax.ppermute(value, "row", [(i, i ^ mask) for i in range(count)])


def halves(count):
    mask = count // 2
    while mask:
        yield mask
        mask //= 2


def tree_sum(value, count):
    for mask in halves(count):
        value = value + swap(value, mask, count)
    return value


def tree_gather(value, count):
    blocks, masks = value[None], [0]
    for mask in halves(count):
        blocks = jnp.concatenate([blocks, swap(blocks, mask, count)], axis=0)
        masks = masks + [other ^ mask for other in masks]
    return blocks, masks


def partners(tile_list, count):
    most = tile_list.shape[1]
    me = lax.axis_index("row")
    lists, masks = tree_gather(tile_list[0, :, 1], count)
    number = me ^ jnp.asarray(masks, jnp.int32)
    lower = jnp.any(lists == me, axis=1)
    upper = jnp.any(tile_list[0, :, 1][None, :] == number[:, None], axis=1)
    valid = lower | upper
    before = jnp.sum((valid[None, :] & (number[None, :] < number[:, None])).astype(jnp.int32), axis=1)
    total = jnp.sum(valid.astype(jnp.int32))
    place = jnp.minimum(jnp.arange(most), jnp.maximum(total - 1, 0))
    hit = valid[None, :] & (before[None, :] == place[:, None])
    picked = jnp.sum(jnp.where(hit, number[None, :], 0), axis=1)
    return jnp.concatenate([total[None], picked]).astype(jnp.int32)


def local(features, right_side, variance, hilbert_order, tile_list):
    width = features.shape[1]
    count = lax.axis_size("row")
    most = tile_list.shape[1]
    steps = width // ROWS
    f32 = jnp.float32
    shape = jax.ShapeDtypeStruct
    params = pltpu.CompilerParams(vmem_limit_bytes=40 * 1024 * 1024)

    payload = jnp.concatenate([features, right_side.astype(jnp.bfloat16)], axis=0)
    slots = partners(tile_list, count)
    every = lax.all_gather(payload, "row", axis=0)
    scratch = [
        pltpu.VMEM((width, KDIM), jnp.bfloat16),
        pltpu.VMEM((KDIM, width), jnp.bfloat16),
        pltpu.VMEM((8, width), jnp.bfloat16),
    ]
    own_tile, own_sum = pl.pallas_call(
        own_kernel,
        grid=(steps,),
        in_specs=[pl.BlockSpec(payload.shape, lambda i: (0, 0))],
        out_specs=[
            pl.BlockSpec((ROWS, width), lambda i: (i, 0)),
            pl.BlockSpec((8, width), lambda i: (0, 0)),
        ],
        out_shape=[shape((width, width), jnp.bfloat16), shape((8, width), f32)],
        scratch_shapes=scratch,
        compiler_params=params,
        cost_estimate=pl.CostEstimate(
            flops=30 * width * width, bytes_accessed=2 * width * width, transcendentals=width * width
        ),
        name="own_tile",
    )(payload)

    def tile_at(k, i, s):
        live = k < s[0]
        return (jnp.minimum(k, jnp.maximum(s[0] - 1, 0)), jnp.where(live, i, steps - 1), 0)

    pair_tiles, pair_sum = pl.pallas_call(
        pair_kernel,
        grid_spec=pltpu.PrefetchScalarGridSpec(
            num_scalar_prefetch=1,
            grid=(most, steps),
            in_specs=[
                pl.BlockSpec(payload.shape, lambda k, i, s: (0, 0)),
                pl.BlockSpec((1,) + payload.shape, lambda k, i, s: (s[1 + k], 0, 0)),
                pl.BlockSpec((8, width), lambda k, i, s: (0, 0)),
            ],
            out_specs=[
                pl.BlockSpec((1, ROWS, width), tile_at),
                pl.BlockSpec((8, width), lambda k, i, s: (0, 0)),
            ],
            scratch_shapes=scratch,
        ),
        out_shape=[shape((most, width, width), jnp.bfloat16), shape((8, width), f32)],
        compiler_params=params,
        name="pair_tiles",
    )(slots, payload, every, own_sum)

    first = (variance + DIAGONAL)[None, :] * right_side + SCALE * pair_sum
    rounded = first.astype(jnp.bfloat16)
    every_first = lax.all_gather(rounded, "row", axis=0)

    sums = jnp.stack([jnp.sum(right_side * right_side, axis=1), jnp.sum(right_side * first, axis=1)])
    sums = tree_sum(sums, count)
    step_one = sums[0] / sums[1]
    res_one = right_side - step_one[:, None] * first
    norm_one = tree_sum(jnp.sum(res_one * res_one, axis=1), count)
    ratio = norm_one / sums[0]

    own_again = pl.pallas_call(
        own_again_kernel,
        grid=(steps,),
        in_specs=[
            pl.BlockSpec((ROWS, width), lambda i: (i, 0)),
            pl.BlockSpec((8, width), lambda i: (0, 0)),
        ],
        out_specs=pl.BlockSpec((8, width), lambda i: (0, 0)),
        out_shape=shape((8, width), f32),
        compiler_params=params,
        name="own_again",
    )(own_tile, rounded)
    pair_again = pl.pallas_call(
        again_kernel,
        grid_spec=pltpu.PrefetchScalarGridSpec(
            num_scalar_prefetch=1,
            grid=(most, steps),
            in_specs=[
                pl.BlockSpec((1, ROWS, width), tile_at),
                pl.BlockSpec((1, 8, width), lambda k, i, s: (s[1 + k], 0, 0)),
                pl.BlockSpec((8, width), lambda k, i, s: (0, 0)),
            ],
            out_specs=pl.BlockSpec((8, width), lambda k, i, s: (0, 0)),
        ),
        out_shape=shape((8, width), f32),
        compiler_params=params,
        name="pair_again",
    )(slots, pair_tiles, every_first, own_again)
    second = (variance + DIAGONAL)[None, :] * first + SCALE * pair_again

    direction = res_one + ratio[:, None] * right_side
    image = (1.0 + ratio)[:, None] * first - step_one[:, None] * second
    curve = tree_sum(jnp.sum(direction * image, axis=1), count)
    step_two = norm_one / curve

    rows = jnp.concatenate([step_one[:, None] * right_side, direction, res_one, image], axis=0)
    ordered = pl.pallas_call(
        order_kernel,
        out_shape=shape(rows.shape, f32),
        compiler_params=params,
        name="curve_order",
    )(rows, hilbert_order)
    solved = ordered[:8] + step_two[:, None] * ordered[8:16]
    residual = ordered[16:24] - step_two[:, None] * ordered[24:32]
    return (solved, residual)


def solution(mesh):
    in_specs = (
        P(None, ("group", "row")),
        P(None, ("group", "row")),
        P(("group", "row")),
        P(("group", "row"), None),
        P(("group", "row"), None, None),
    )
    out_specs = (P(None, ("group", "row")), P(None, ("group", "row")))
    return jax.shard_map(local, mesh=mesh, in_specs=in_specs, out_specs=out_specs, check_vma=False)
```

```python
import jax
import jax.numpy as jnp
import numpy as np
from jax import lax
from jax.experimental import pallas as pl
from jax.experimental.pallas import tpu as pltpu
from jax.sharding import PartitionSpec as P

SHRINK = 0.95
SCALE = 20.0 * (20.0 / 19.0) ** 19
DIAGONAL = float(1.0 - SCALE * float(np.float32(1.0 / SCALE).astype(jnp.bfloat16)))
KDIM = 128
COLS = 512
ROWS = 512
TAIL = 128
BF16 = jnp.bfloat16
F32 = jnp.float32
CONTRACT_LANES = (((1,), (1,)), ((), ()))


def split_three(value):
    high = value.astype(BF16).astype(F32)
    rest = value - high
    middle = rest.astype(BF16).astype(F32)
    return high, middle, rest - middle


def norm_rows(norm, first):
    high, middle, low = split_three(norm)
    row = lax.broadcasted_iota(jnp.int32, (32, norm.shape[1]), 0)
    out = jnp.where(row < 6, 1.0, 0.0)
    out = jnp.where(row == first, high, out)
    out = jnp.where(row == first + 1, middle, out)
    return jnp.where(row == first + 2, low, out).astype(BF16)


def own_factor(feat):
    wide = feat.astype(F32)
    norm = jnp.sum(wide * wide, axis=0, keepdims=True) * (SHRINK * SHRINK)
    pieces = split_three(wide * (-2.0 * SHRINK * SHRINK))
    whole = jnp.concatenate([piece.astype(BF16) for piece in pieces] + [norm_rows(norm, 0)], axis=0)
    return jnp.transpose(whole)


def other_factor(feat):
    wide = feat.astype(F32)
    norm = jnp.sum(wide * wide, axis=0, keepdims=True) * (SHRINK * SHRINK)
    return jnp.concatenate([feat, feat, feat, norm_rows(norm, 3)], axis=0)


def psi_tile(dist):
    dist = jnp.maximum(dist, 1e-30)
    radius = dist * lax.rsqrt(dist)
    u = jnp.maximum(SHRINK - radius, 0.0)
    two = u * u
    four = two * two
    eight = four * four
    sixteen = eight * eight
    return (sixteen * two * (u - two)).astype(BF16)


def tile_columns(left_ref, right_ref, vec_ref, begin, tile_ref, sum_ref):
    at = pl.multiple_of(begin, COLS)
    right = right_ref[:, pl.ds(at, COLS)]
    vec = vec_ref[:, pl.ds(at, COLS)]

    def step(index, carry):
        rows = pl.multiple_of(index * ROWS, ROWS)
        dist = jnp.dot(left_ref[pl.ds(rows, ROWS), :], right, preferred_element_type=F32)
        parts = []
        for sub in range(0, ROWS, 64):
            part = psi_tile(dist[sub : sub + 64])
            tile_ref[pl.ds(rows + sub, 64), :] = part
            parts.append(part)
        sum_ref[pl.ds(rows, ROWS), :] += lax.dot_general(
            jnp.concatenate(parts, axis=0), vec, CONTRACT_LANES, preferred_element_type=F32
        )
        return carry

    lax.fori_loop(0, left_ref.shape[0] // ROWS, step, 0)


def own_kernel(pay_ref, tile_ref, sum_ref, left_ref, right_ref, vec_ref):
    step = pl.program_id(0)

    @pl.when(step == 0)
    def _():
        pay = pay_ref[...]
        left_ref[...] = own_factor(pay[:32])
        right_ref[...] = other_factor(pay[:32])
        vec_ref[...] = pay[32:40]
        sum_ref[...] = jnp.zeros_like(sum_ref)

    tile_columns(left_ref, right_ref, vec_ref, step * COLS, tile_ref, sum_ref)


def pair_kernel(
    slots_ref, own_ref, pay_ref, first_ref, rhs_ref, var_ref,
    tile_ref, image_ref, send_ref,
    left_ref, right_ref, vec_ref, sum_ref,
):
    slot, step = pl.program_id(0), pl.program_id(1)

    @pl.when((slot == 0) & (step == 0))
    def _():
        left_ref[...] = own_factor(own_ref[...][:32])
        sum_ref[...] = first_ref[...]

    @pl.when(slot < slots_ref[0])
    def _():
        @pl.when(step == 0)
        def _():
            pay = pay_ref[0]
            right_ref[...] = other_factor(pay[:32])
            vec_ref[...] = pay[32:40]

        tile_columns(left_ref, right_ref, vec_ref, step * COLS, tile_ref.at[0], sum_ref)

    @pl.when((slot == pl.num_programs(0) - 1) & (step == pl.num_programs(1) - 1))
    def _():
        rhs = rhs_ref[...]
        width = rhs.shape[1]
        image = (var_ref[...] + DIAGONAL) * rhs + SCALE * jnp.transpose(sum_ref[...])
        image_ref[...] = image
        send_ref[:, :width] = image.astype(BF16)
        pieces = split_three(jnp.sum(rhs * rhs, axis=1, keepdims=True))
        pieces += split_three(jnp.sum(rhs * image, axis=1, keepdims=True))
        lane = lax.broadcasted_iota(jnp.int32, (rhs.shape[0], TAIL), 1)
        tail = jnp.zeros((rhs.shape[0], TAIL), F32)
        for place, piece in enumerate(pieces):
            tail = jnp.where(lane == place, piece, tail)
        send_ref[:, width:] = tail.astype(BF16)


def own_again_kernel(tile_ref, vec_ref, sum_ref):
    width = tile_ref.shape[1]
    sum_ref[...] = lax.dot_general(
        tile_ref[...], vec_ref[:, :width], CONTRACT_LANES, preferred_element_type=F32
    )


def again_kernel(
    slots_ref, tile_ref, vec_ref, tails_ref, first_ref, rhs_ref, var_ref, image_ref,
    rows_ref, dots_ref, step_ref,
    sum_ref,
):
    slot, step = pl.program_id(0), pl.program_id(1)
    width = rhs_ref.shape[1]

    @pl.when((slot == 0) & (step == 0))
    def _():
        sum_ref[...] = first_ref[...]

    @pl.when(slot < slots_ref[0])
    def _():
        at = pl.multiple_of(step * ROWS, ROWS)
        sum_ref[pl.ds(at, ROWS), :] += lax.dot_general(
            tile_ref[0], vec_ref[0, :, :width], CONTRACT_LANES, preferred_element_type=F32
        )

    @pl.when((slot == pl.num_programs(0) - 1) & (step == pl.num_programs(1) - 1))
    def _():
        rhs = rhs_ref[...]
        image = image_ref[...]
        total = jnp.sum(tails_ref[...].astype(F32), axis=0)
        norm = total[:, 0:1] + total[:, 1:2] + total[:, 2:3]
        curve = total[:, 3:4] + total[:, 4:5] + total[:, 5:6]
        length = norm / curve
        second = (var_ref[...] + DIAGONAL) * image + SCALE * jnp.transpose(sum_ref[...])
        res = rhs - length * image
        res_image = image - length * second
        rows_ref[0:8] = rhs
        rows_ref[8:16] = res
        rows_ref[16:24] = image
        rows_ref[24:32] = res_image
        lane = lax.broadcasted_iota(jnp.int32, (rhs.shape[0], TAIL), 1)
        dots = jnp.zeros((rhs.shape[0], TAIL), F32)
        for place, product in enumerate((res * res, res * res_image, res * image, rhs * res_image)):
            dots = jnp.where(lane == place, jnp.sum(product, axis=1, keepdims=True), dots)
        dots_ref[...] = dots
        step_ref[...] = jnp.where(lane == 0, norm, jnp.where(lane == 1, curve, 0.0))


def order_kernel(rows_ref, perm_ref, out_ref):
    rows = rows_ref[...]
    count, width = rows.shape
    pieces = jnp.concatenate([piece for piece in split_three(rows)], axis=0).astype(BF16)
    perm = perm_ref[...]
    chunk = 256
    for col in range(0, width, chunk):
        total = jnp.zeros((3 * count, chunk), F32)
        for at in range(0, width, chunk):
            index = lax.broadcasted_iota(jnp.int32, (chunk, chunk), 0) + at
            pick = jnp.where(index == perm[:, col : col + chunk], 1.0, 0.0).astype(BF16)
            total += jnp.dot(pieces[:, at : at + chunk], pick, preferred_element_type=F32)
        out_ref[:, col : col + chunk] = total[:count] + total[count : 2 * count] + total[2 * count :]


def swap(value, mask, count):
    return lax.ppermute(value, "row", [(i, i ^ mask) for i in range(count)])


def levels(count, sizes):
    bits = count.bit_length() - 1
    out = []
    sizes = list(sizes)
    while bits:
        take = min(sizes.pop(0) if sizes else 1, bits)
        bits -= take
        out.append([mask << bits for mask in range(1, 1 << take)])
    return out


def tree_sum(value, count):
    for masks in levels(count, [2, 2, 2]):
        others = [swap(value, mask, count) for mask in masks]
        if len(masks) == 3:
            value = (value + others[0]) + (others[1] + others[2])
        else:
            value = value + others[0]
    return value


def tree_gather(value, count):
    blocks, places = value[None], [0]
    for masks in levels(count, [2] if count <= 16 else [2, 2]):
        blocks = jnp.concatenate([blocks] + [swap(blocks, mask, count) for mask in masks], axis=0)
        places = places + [place ^ mask for mask in masks for place in places]
    return blocks, places


def partners(tile_list, count):
    most = tile_list.shape[1]
    me = lax.axis_index("row")
    lists, places = tree_gather(tile_list[0, :, 1], count)
    number = me ^ jnp.asarray(places, jnp.int32)
    lower = jnp.any(lists == me, axis=1)
    upper = jnp.any(tile_list[0, :, 1][None, :] == number[:, None], axis=1)
    valid = lower | upper
    before = jnp.sum((valid[None, :] & (number[None, :] < number[:, None])).astype(jnp.int32), axis=1)
    total = jnp.sum(valid.astype(jnp.int32))
    place = jnp.minimum(jnp.arange(most), jnp.maximum(total - 1, 0))
    hit = valid[None, :] & (before[None, :] == place[:, None])
    picked = jnp.sum(jnp.where(hit, number[None, :], 0), axis=1)
    where = jnp.sum(jnp.where(hit, jnp.arange(count)[None, :], 0), axis=1)
    return jnp.concatenate([total[None], picked, where]).astype(jnp.int32)


def local(features, right_side, variance, hilbert_order, tile_list):
    width = features.shape[1]
    rhs_count = right_side.shape[0]
    count = lax.axis_size("row")
    most = tile_list.shape[1]
    steps = width // COLS
    row_steps = width // ROWS
    shape = jax.ShapeDtypeStruct
    params = pltpu.CompilerParams(vmem_limit_bytes=40 * 1024 * 1024)
    var_row = variance[None, :]

    payload = jnp.concatenate([features, right_side.astype(BF16)], axis=0)
    slots = partners(tile_list, count)
    every = lax.all_gather(payload, "row", axis=0)
    scratch = [
        pltpu.VMEM((width, KDIM), BF16),
        pltpu.VMEM((KDIM, width), BF16),
        pltpu.VMEM((rhs_count, width), BF16),
    ]
    sum_shape = (width, rhs_count)
    whole = lambda *ignored: (0, 0)
    own_tile, own_sum = pl.pallas_call(
        own_kernel,
        grid=(steps,),
        in_specs=[pl.BlockSpec(payload.shape, whole)],
        out_specs=[
            pl.BlockSpec((width, COLS), lambda i: (0, i)),
            pl.BlockSpec(sum_shape, whole),
        ],
        out_shape=[shape((width, width), BF16), shape(sum_shape, F32)],
        scratch_shapes=scratch,
        compiler_params=params,
        name="own_tile",
    )(payload)

    def tile_out(k, i, s):
        live = k < s[0]
        return (jnp.minimum(k, jnp.maximum(s[0] - 1, 0)), 0, jnp.where(live, i, steps - 1))

    def tile_in(k, i, s):
        live = k < s[0]
        return (jnp.minimum(k, jnp.maximum(s[0] - 1, 0)), jnp.where(live, i, row_steps - 1), 0)

    row_spec = pl.BlockSpec(right_side.shape, whole)
    var_spec = pl.BlockSpec(var_row.shape, whole)
    sum_spec = pl.BlockSpec(sum_shape, whole)
    send_shape = (rhs_count, width + TAIL)
    pair_tiles, image, send = pl.pallas_call(
        pair_kernel,
        grid_spec=pltpu.PrefetchScalarGridSpec(
            num_scalar_prefetch=1,
            grid=(most, steps),
            in_specs=[
                pl.BlockSpec(payload.shape, whole),
                pl.BlockSpec((1,) + payload.shape, lambda k, i, s: (s[1 + k], 0, 0)),
                sum_spec,
                row_spec,
                var_spec,
            ],
            out_specs=[
                pl.BlockSpec((1, width, COLS), tile_out),
                row_spec,
                pl.BlockSpec(send_shape, whole),
            ],
            scratch_shapes=scratch + [pltpu.VMEM(sum_shape, F32)],
        ),
        out_shape=[
            shape((most, width, width), BF16),
            shape(right_side.shape, F32),
            shape(send_shape, BF16),
        ],
        compiler_params=params,
        name="pair_tiles",
    )(slots, payload, every, own_sum, right_side, var_row)

    every_send, _ = tree_gather(send, count)
    own_again = pl.pallas_call(
        own_again_kernel,
        grid=(row_steps,),
        in_specs=[
            pl.BlockSpec((ROWS, width), lambda i: (i, 0)),
            pl.BlockSpec(send_shape, whole),
        ],
        out_specs=pl.BlockSpec((ROWS, rhs_count), lambda i: (i, 0)),
        out_shape=shape(sum_shape, F32),
        compiler_params=params,
        name="own_again",
    )(own_tile, send)
    dots_spec = pl.BlockSpec((rhs_count, TAIL), whole)
    rows, dots, steps_one = pl.pallas_call(
        again_kernel,
        grid_spec=pltpu.PrefetchScalarGridSpec(
            num_scalar_prefetch=1,
            grid=(most, row_steps),
            in_specs=[
                pl.BlockSpec((1, ROWS, width), tile_in),
                pl.BlockSpec((1,) + send_shape, lambda k, i, s: (s[1 + most + k], 0, 0)),
                pl.BlockSpec((count, rhs_count, TAIL), lambda k, i, s: (0, 0, width // TAIL)),
                sum_spec,
                row_spec,
                var_spec,
                row_spec,
            ],
            out_specs=[
                pl.BlockSpec((4 * rhs_count, width), whole),
                dots_spec,
                dots_spec,
            ],
            scratch_shapes=[pltpu.VMEM(sum_shape, F32)],
        ),
        out_shape=[
            shape((4 * rhs_count, width), F32),
            shape((rhs_count, TAIL), F32),
            shape((rhs_count, TAIL), F32),
        ],
        compiler_params=params,
        name="pair_again",
    )(slots, pair_tiles, every_send, every_send, own_again, right_side, var_row, image)

    dots = tree_sum(dots, count)
    ordered = pl.pallas_call(
        order_kernel,
        out_shape=shape(rows.shape, F32),
        compiler_params=params,
        name="curve_order",
    )(rows, hilbert_order)
    norm, curve = steps_one[:, 0:1], steps_one[:, 1:2]
    length = norm / curve
    norm_next = dots[:, 0:1]
    ratio = norm_next / norm
    curve_next = dots[:, 1:2] + ratio * (dots[:, 2:3] + dots[:, 3:4]) + ratio * ratio * curve
    length_next = norm_next / curve_next
    rhs_o, res_o, image_o, res_image_o = [ordered[at : at + 8] for at in range(0, 32, 8)]
    solved = length * rhs_o + length_next * (res_o + ratio * rhs_o)
    residual = res_o - length_next * (res_image_o + ratio * image_o)
    return (solved, residual)


def solution(mesh):
    in_specs = (
        P(None, ("group", "row")),
        P(None, ("group", "row")),
        P(("group", "row")),
        P(("group", "row"), None),
        P(("group", "row"), None, None),
    )
    out_specs = (P(None, ("group", "row")), P(None, ("group", "row")))
    return jax.shard_map(local, mesh=mesh, in_specs=in_specs, out_specs=out_specs, check_vma=False)
```

```python
import jax
import jax.numpy as jnp
import numpy as np
from jax import lax
from jax.experimental import pallas as pl
from jax.experimental.pallas import tpu as pltpu
from jax.sharding import PartitionSpec as P

SHRINK = 0.95
SCALE = 20.0 * (20.0 / 19.0) ** 19
DIAGONAL = float(1.0 - SCALE * float(np.float32(1.0 / SCALE).astype(jnp.bfloat16)))
KDIM = 128
ROWS = 512
UNIT = 256
SUB = 64
TAIL = 128
BF16 = jnp.bfloat16
F32 = jnp.float32


def split_three(value):
    high = value.astype(BF16).astype(F32)
    rest = value - high
    middle = rest.astype(BF16).astype(F32)
    return high, middle, rest - middle


def norm_rows(norm, first):
    high, middle, low = split_three(norm)
    row = lax.broadcasted_iota(jnp.int32, (32, norm.shape[1]), 0)
    out = jnp.where(row < 6, 1.0, 0.0)
    out = jnp.where(row == first, high, out)
    out = jnp.where(row == first + 1, middle, out)
    return jnp.where(row == first + 2, low, out).astype(BF16)


def own_factor(feat):
    wide = feat.astype(F32)
    norm = jnp.sum(wide * wide, axis=0, keepdims=True) * (SHRINK * SHRINK)
    pieces = split_three(wide * (-2.0 * SHRINK * SHRINK))
    return jnp.concatenate([piece.astype(BF16) for piece in pieces] + [norm_rows(norm, 0)], axis=0)


def other_factor(feat):
    wide = feat.astype(F32)
    norm = jnp.sum(wide * wide, axis=0, keepdims=True) * (SHRINK * SHRINK)
    return jnp.transpose(jnp.concatenate([feat, feat, feat, norm_rows(norm, 3)], axis=0))


def psi_tile(dist):
    dist = jnp.maximum(dist, 1e-30)
    radius = dist * lax.rsqrt(dist)
    u = jnp.maximum(SHRINK - radius, 0.0)
    two = u * u
    four = two * two
    eight = four * four
    sixteen = eight * eight
    return (sixteen * two * (u - two)).astype(BF16)


def tile_rows(left_ref, right_ref, vec_ref, begin, tile_ref, sum_ref, dist_refs):
    width = right_ref.shape[1]
    units = width // UNIT

    def gram(row, unit, dist_ref):
        col = unit * UNIT
        dist_ref[...] = jnp.dot(
            left_ref[pl.ds(pl.multiple_of(row, UNIT), UNIT), :],
            right_ref[:, col : col + UNIT],
            preferred_element_type=F32,
        )

    def product(vec, at, unit):
        col = unit * UNIT
        sum_ref[:, col : col + UNIT] += jnp.dot(
            vec, tile_ref[pl.ds(at, UNIT), col : col + UNIT], preferred_element_type=F32
        )

    gram(begin, 0, dist_refs[0])

    def step(index, carry):
        at = pl.multiple_of(index * UNIT, UNIT)
        row = begin + at
        following = begin + jnp.minimum(at + UNIT, ROWS - UNIT)
        vec = vec_ref[:, pl.ds(pl.multiple_of(row, UNIT), UNIT)]
        for unit in range(units):
            if unit + 1 < units:
                gram(row, unit + 1, dist_refs[(unit + 1) % 2])
            else:
                gram(following, 0, dist_refs[(unit + 1) % 2])
            col = unit * UNIT
            for sub in range(0, UNIT, SUB):
                tile_ref[pl.ds(at + sub, SUB), col : col + UNIT] = psi_tile(
                    dist_refs[unit % 2][sub : sub + SUB, :]
                )
            if unit:
                product(vec, at, unit - 1)
        product(vec, at, units - 1)
        return carry

    lax.fori_loop(0, ROWS // UNIT, step, 0)


def own_kernel(pay_ref, tile_ref, sum_ref, left_ref, right_ref, vec_ref, *dist_refs):
    step = pl.program_id(0)

    @pl.when(step == 0)
    def _():
        pay = pay_ref[...]
        left_ref[...] = other_factor(pay[:32])
        right_ref[...] = own_factor(pay[:32])
        vec_ref[...] = pay[32:40]
        sum_ref[...] = jnp.zeros_like(sum_ref)

    tile_rows(left_ref, right_ref, vec_ref, step * ROWS, tile_ref, sum_ref, dist_refs)


def pair_kernel(
    slots_ref, own_ref, pay_ref, first_ref, rhs_ref, var_ref,
    tile_ref, image_ref, send_ref,
    left_ref, right_ref, vec_ref, dist_zero_ref, dist_one_ref, sum_ref,
):
    slot, step = pl.program_id(0), pl.program_id(1)

    @pl.when((slot == 0) & (step == 0))
    def _():
        right_ref[...] = own_factor(own_ref[...][:32])
        sum_ref[...] = first_ref[...]

    @pl.when(slot < slots_ref[0])
    def _():
        @pl.when(step == 0)
        def _():
            pay = pay_ref[0]
            left_ref[...] = other_factor(pay[:32])
            vec_ref[...] = pay[32:40]

        tile_rows(
            left_ref, right_ref, vec_ref, step * ROWS, tile_ref.at[0], sum_ref,
            (dist_zero_ref, dist_one_ref),
        )

    @pl.when((slot == pl.num_programs(0) - 1) & (step == pl.num_programs(1) - 1))
    def _():
        rhs = rhs_ref[...]
        width = rhs.shape[1]
        image = (var_ref[...] + DIAGONAL) * rhs + SCALE * sum_ref[...]
        image_ref[...] = image
        send_ref[:, :width] = image.astype(BF16)
        pieces = split_three(jnp.sum(rhs * rhs, axis=1, keepdims=True))
        pieces += split_three(jnp.sum(rhs * image, axis=1, keepdims=True))
        lane = lax.broadcasted_iota(jnp.int32, (rhs.shape[0], TAIL), 1)
        tail = jnp.zeros((rhs.shape[0], TAIL), F32)
        for place, piece in enumerate(pieces):
            tail = jnp.where(lane == place, piece, tail)
        send_ref[:, width:] = tail.astype(BF16)


def own_again_kernel(tile_ref, vec_ref, sum_ref):
    step = pl.program_id(0)

    @pl.when(step == 0)
    def _():
        sum_ref[...] = jnp.zeros_like(sum_ref)

    at = pl.multiple_of(step * ROWS, ROWS)
    sum_ref[...] += jnp.dot(
        vec_ref[:, pl.ds(at, ROWS)], tile_ref[...], preferred_element_type=F32
    )


def again_kernel(
    slots_ref, tile_ref, vec_ref, tails_ref, first_ref, rhs_ref, var_ref, image_ref,
    rows_ref, dots_ref, step_ref,
    sum_ref,
):
    slot, step = pl.program_id(0), pl.program_id(1)

    @pl.when((slot == 0) & (step == 0))
    def _():
        sum_ref[...] = first_ref[...]

    @pl.when(slot < slots_ref[0])
    def _():
        at = pl.multiple_of(step * ROWS, ROWS)
        sum_ref[...] += jnp.dot(
            vec_ref[0, :, pl.ds(at, ROWS)], tile_ref[0], preferred_element_type=F32
        )

    @pl.when((slot == pl.num_programs(0) - 1) & (step == pl.num_programs(1) - 1))
    def _():
        rhs = rhs_ref[...]
        image = image_ref[...]
        total = jnp.sum(tails_ref[...].astype(F32), axis=0)
        norm = total[:, 0:1] + total[:, 1:2] + total[:, 2:3]
        curve = total[:, 3:4] + total[:, 4:5] + total[:, 5:6]
        length = norm / curve
        second = (var_ref[...] + DIAGONAL) * image + SCALE * sum_ref[...]
        res = rhs - length * image
        res_image = image - length * second
        rows_ref[0:8] = rhs
        rows_ref[8:16] = res
        rows_ref[16:24] = image
        rows_ref[24:32] = res_image
        lane = lax.broadcasted_iota(jnp.int32, (rhs.shape[0], TAIL), 1)
        dots = jnp.zeros((rhs.shape[0], TAIL), F32)
        for place, product in enumerate((res * res, res * res_image, res * image, rhs * res_image)):
            dots = jnp.where(lane == place, jnp.sum(product, axis=1, keepdims=True), dots)
        dots_ref[...] = dots
        step_ref[...] = jnp.where(lane == 0, norm, jnp.where(lane == 1, curve, 0.0))


def order_kernel(rows_ref, perm_ref, out_ref):
    rows = rows_ref[...]
    count, width = rows.shape
    pieces = jnp.concatenate([piece for piece in split_three(rows)], axis=0).astype(BF16)
    perm = perm_ref[...]
    chunk = 256
    for col in range(0, width, chunk):
        total = jnp.zeros((3 * count, chunk), F32)
        for at in range(0, width, chunk):
            index = lax.broadcasted_iota(jnp.int32, (chunk, chunk), 0) + at
            pick = jnp.where(index == perm[:, col : col + chunk], 1.0, 0.0).astype(BF16)
            total += jnp.dot(pieces[:, at : at + chunk], pick, preferred_element_type=F32)
        out_ref[:, col : col + chunk] = total[:count] + total[count : 2 * count] + total[2 * count :]


def swap(value, mask, count):
    return lax.ppermute(value, "row", [(i, i ^ mask) for i in range(count)])


def levels(count, sizes):
    bits = count.bit_length() - 1
    out = []
    sizes = list(sizes)
    while bits:
        take = min(sizes.pop(0) if sizes else 1, bits)
        bits -= take
        out.append([mask << bits for mask in range(1, 1 << take)])
    return out


def tree_sum(value, count):
    for masks in levels(count, [2, 2, 2]):
        others = [swap(value, mask, count) for mask in masks]
        if len(masks) == 3:
            value = (value + others[0]) + (others[1] + others[2])
        else:
            value = value + others[0]
    return value


def tree_gather(value, count):
    blocks, places = value[None], [0]
    for masks in levels(count, [2] if count <= 16 else [2, 2]):
        blocks = jnp.concatenate([blocks] + [swap(blocks, mask, count) for mask in masks], axis=0)
        places = places + [place ^ mask for mask in masks for place in places]
    return blocks, places


def partners(tile_list, count):
    most = tile_list.shape[1]
    me = lax.axis_index("row")
    lists, places = tree_gather(tile_list[0, :, 1], count)
    number = me ^ jnp.asarray(places, jnp.int32)
    lower = jnp.any(lists == me, axis=1)
    upper = jnp.any(tile_list[0, :, 1][None, :] == number[:, None], axis=1)
    valid = lower | upper
    before = jnp.sum((valid[None, :] & (number[None, :] < number[:, None])).astype(jnp.int32), axis=1)
    total = jnp.sum(valid.astype(jnp.int32))
    place = jnp.minimum(jnp.arange(most), jnp.maximum(total - 1, 0))
    hit = valid[None, :] & (before[None, :] == place[:, None])
    picked = jnp.sum(jnp.where(hit, number[None, :], 0), axis=1)
    where = jnp.sum(jnp.where(hit, jnp.arange(count)[None, :], 0), axis=1)
    return jnp.concatenate([total[None], picked, where]).astype(jnp.int32)


def local(features, right_side, variance, hilbert_order, tile_list):
    width = features.shape[1]
    rhs_count = right_side.shape[0]
    count = lax.axis_size("row")
    most = tile_list.shape[1]
    steps = width // ROWS
    shape = jax.ShapeDtypeStruct
    params = pltpu.CompilerParams(vmem_limit_bytes=24 * 1024 * 1024)
    var_row = variance[None, :]

    payload = jnp.concatenate([features, right_side.astype(BF16)], axis=0)
    slots = partners(tile_list, count)
    every = lax.all_gather(payload, "row", axis=0)
    scratch = [
        pltpu.VMEM((width, KDIM), BF16),
        pltpu.VMEM((KDIM, width), BF16),
        pltpu.VMEM((rhs_count, width), BF16),
        pltpu.VMEM((UNIT, UNIT), F32),
        pltpu.VMEM((UNIT, UNIT), F32),
    ]
    whole = lambda *ignored: (0, 0)
    row_spec = pl.BlockSpec(right_side.shape, whole)
    var_spec = pl.BlockSpec(var_row.shape, whole)
    own_tile, own_sum = pl.pallas_call(
        own_kernel,
        grid=(steps,),
        in_specs=[pl.BlockSpec(payload.shape, whole)],
        out_specs=[pl.BlockSpec((ROWS, width), lambda i: (i, 0)), row_spec],
        out_shape=[shape((width, width), BF16), shape(right_side.shape, F32)],
        scratch_shapes=scratch,
        compiler_params=params,
        name="own_tile",
    )(payload)

    def tile_at(k, i, s):
        live = k < s[0]
        return (jnp.minimum(k, jnp.maximum(s[0] - 1, 0)), jnp.where(live, i, steps - 1), 0)

    send_shape = (rhs_count, width + TAIL)
    pair_tiles, image, send = pl.pallas_call(
        pair_kernel,
        grid_spec=pltpu.PrefetchScalarGridSpec(
            num_scalar_prefetch=1,
            grid=(most, steps),
            in_specs=[
                pl.BlockSpec(payload.shape, whole),
                pl.BlockSpec((1,) + payload.shape, lambda k, i, s: (s[1 + k], 0, 0)),
                row_spec,
                row_spec,
                var_spec,
            ],
            out_specs=[
                pl.BlockSpec((1, ROWS, width), tile_at),
                row_spec,
                pl.BlockSpec(send_shape, whole),
            ],
            scratch_shapes=scratch + [pltpu.VMEM(right_side.shape, F32)],
        ),
        out_shape=[
            shape((most, width, width), BF16),
            shape(right_side.shape, F32),
            shape(send_shape, BF16),
        ],
        compiler_params=params,
        name="pair_tiles",
    )(slots, payload, every, own_sum, right_side, var_row)

    every_send, _ = tree_gather(send, count)
    own_again = pl.pallas_call(
        own_again_kernel,
        grid=(steps,),
        in_specs=[
            pl.BlockSpec((ROWS, width), lambda i: (i, 0)),
            pl.BlockSpec(send_shape, whole),
        ],
        out_specs=row_spec,
        out_shape=shape(right_side.shape, F32),
        compiler_params=params,
        name="own_again",
    )(own_tile, send)
    dots_spec = pl.BlockSpec((rhs_count, TAIL), whole)
    rows, dots, steps_one = pl.pallas_call(
        again_kernel,
        grid_spec=pltpu.PrefetchScalarGridSpec(
            num_scalar_prefetch=1,
            grid=(most, steps),
            in_specs=[
                pl.BlockSpec((1, ROWS, width), tile_at),
                pl.BlockSpec((1,) + send_shape, lambda k, i, s: (s[1 + most + k], 0, 0)),
                pl.BlockSpec((count, rhs_count, TAIL), lambda k, i, s: (0, 0, width // TAIL)),
                row_spec,
                row_spec,
                var_spec,
                row_spec,
            ],
            out_specs=[
                pl.BlockSpec((4 * rhs_count, width), whole),
                dots_spec,
                dots_spec,
            ],
            scratch_shapes=[pltpu.VMEM(right_side.shape, F32)],
        ),
        out_shape=[
            shape((4 * rhs_count, width), F32),
            shape((rhs_count, TAIL), F32),
            shape((rhs_count, TAIL), F32),
        ],
        compiler_params=params,
        name="pair_again",
    )(slots, pair_tiles, every_send, every_send, own_again, right_side, var_row, image)

    dots = tree_sum(dots, count)
    ordered = pl.pallas_call(
        order_kernel,
        out_shape=shape(rows.shape, F32),
        compiler_params=params,
        name="curve_order",
    )(rows, hilbert_order)
    norm, curve = steps_one[:, 0:1], steps_one[:, 1:2]
    length = norm / curve
    norm_next = dots[:, 0:1]
    ratio = norm_next / norm
    curve_next = dots[:, 1:2] + ratio * (dots[:, 2:3] + dots[:, 3:4]) + ratio * ratio * curve
    length_next = norm_next / curve_next
    rhs_o, res_o, image_o, res_image_o = [ordered[at : at + 8] for at in range(0, 32, 8)]
    solved = length * rhs_o + length_next * (res_o + ratio * rhs_o)
    residual = res_o - length_next * (res_image_o + ratio * image_o)
    return (solved, residual)


def solution(mesh):
    in_specs = (
        P(None, ("group", "row")),
        P(None, ("group", "row")),
        P(("group", "row")),
        P(("group", "row"), None),
        P(("group", "row"), None, None),
    )
    out_specs = (P(None, ("group", "row")), P(None, ("group", "row")))
    return jax.shard_map(local, mesh=mesh, in_specs=in_specs, out_specs=out_specs, check_vma=False)
```

```python
import jax
import jax.numpy as jnp
import numpy as np
from jax import lax
from jax.experimental import pallas as pl
from jax.experimental.pallas import tpu as pltpu
from jax.sharding import PartitionSpec as P

SHRINK = 0.95
GRAM = SHRINK * SHRINK / 4.0
SCALE = 20.0 * (20.0 / 19.0) ** 19
DIAGONAL = float(1.0 - SCALE * float(np.float32(1.0 / SCALE).astype(jnp.bfloat16)))
KDIM = 128
ROWS = 512
UNIT = 256
SUB = 64
FRONT = 3
HELD = 4
TAIL = 128
BF16 = jnp.bfloat16
F32 = jnp.float32


def split_three(value):
    high = value.astype(BF16).astype(F32)
    rest = value - high
    middle = rest.astype(BF16).astype(F32)
    return high, middle, rest - middle


def norm_rows(norm, first):
    high, middle, low = split_three(norm)
    row = lax.broadcasted_iota(jnp.int32, (32, norm.shape[1]), 0)
    out = jnp.where(row < 6, 1.0, 0.0)
    out = jnp.where(row == first, high, out)
    out = jnp.where(row == first + 1, middle, out)
    return jnp.where(row == first + 2, low, out).astype(BF16)


def own_factor(feat):
    wide = feat.astype(F32)
    norm = jnp.sum(wide * wide, axis=0, keepdims=True) * GRAM
    pieces = split_three(wide * (-2.0 * GRAM))
    return jnp.concatenate([piece.astype(BF16) for piece in pieces] + [norm_rows(norm, 0)], axis=0)


def other_factor(feat):
    wide = feat.astype(F32)
    norm = jnp.sum(wide * wide, axis=0, keepdims=True) * GRAM
    return jnp.transpose(jnp.concatenate([feat, feat, feat, norm_rows(norm, 3)], axis=0))


def psi_tile(quarter):
    quarter = jnp.maximum(quarter, 1e-30)
    start = lax.rsqrt(quarter.astype(BF16)).astype(F32)
    w = quarter * start
    u = jnp.maximum(SHRINK + w * (w * start - 3.0), 0.0)
    two = u * u
    four = two * two
    eight = four * four
    sixteen = eight * eight
    return (sixteen * two * (u - two)).astype(BF16)


def tile_rows(left_ref, right_ref, vec_ref, begin, tile_ref, sum_ref, dist_refs):
    width = right_ref.shape[1]
    units = width // UNIT

    def gram(row, unit, dist_ref):
        col = unit * UNIT
        dist_ref[...] = jnp.dot(
            left_ref[pl.ds(pl.multiple_of(row, UNIT), UNIT), :],
            right_ref[:, col : col + UNIT],
            preferred_element_type=F32,
        )

    def product(vec, at, unit):
        col = unit * UNIT
        sum_ref[:, col : col + UNIT] += jnp.dot(
            vec, tile_ref[pl.ds(at, UNIT), col : col + UNIT], preferred_element_type=F32
        )

    gram(begin, 0, dist_refs[0])

    def step(index, carry):
        at = pl.multiple_of(index * UNIT, UNIT)
        row = begin + at
        following = begin + jnp.minimum(at + UNIT, ROWS - UNIT)
        vec = vec_ref[:, pl.ds(pl.multiple_of(row, UNIT), UNIT)]
        for unit in range(units):
            if unit + 1 < units:
                gram(row, unit + 1, dist_refs[(unit + 1) % 2])
            else:
                gram(following, 0, dist_refs[(unit + 1) % 2])
            col = unit * UNIT
            for sub in range(0, UNIT, SUB):
                tile_ref[pl.ds(at + sub, SUB), col : col + UNIT] = psi_tile(
                    dist_refs[unit % 2][sub : sub + SUB, :]
                )
            if unit:
                product(vec, at, unit - 1)
        product(vec, at, units - 1)
        return carry

    lax.fori_loop(0, ROWS // UNIT, step, 0)


def unpack(pay):
    half = pay.shape[1]
    return jnp.concatenate([pay[:32], pay[32:64]], axis=1), jnp.concatenate([pay[64:72], pay[72:80]], axis=1)


def own_kernel(pay_ref, tile_ref, sum_ref, left_ref, right_ref, vec_ref, *dist_refs):
    step = pl.program_id(0)

    @pl.when(step == 0)
    def _():
        feat, vec = unpack(pay_ref[...])
        left_ref[...] = other_factor(feat)
        right_ref[...] = own_factor(feat)
        vec_ref[...] = vec
        sum_ref[...] = jnp.zeros_like(sum_ref)

    tile_rows(left_ref, right_ref, vec_ref, step * ROWS, tile_ref, sum_ref, dist_refs)


def pair_kernel(slots_ref, own_ref, first_ref, rhs_ref, var_ref, *refs):
    block_refs = refs[:-11]
    front_ref, back_ref, image_ref, send_ref = refs[-11:-7]
    left_ref, right_ref, vec_ref, dist_zero_ref, dist_one_ref, pay_ref, sem_ref = refs[-7:]
    slot, step = pl.program_id(0), pl.program_id(1)
    sum_ref = image_ref

    def fetch(which):
        place = slots_ref[1 + which]
        for at, block_ref in enumerate(block_refs):
            @pl.when(place == at)
            def _():
                pltpu.make_async_copy(
                    block_ref, pay_ref.at[which % 2], sem_ref.at[which % 2]
                ).start()

    @pl.when((slot == 0) & (step == 0))
    def _():
        right_ref[...] = own_factor(unpack(own_ref[...])[0])
        sum_ref[...] = first_ref[...]

        @pl.when(slots_ref[0] > 0)
        def _():
            fetch(0)

    @pl.when(slot < slots_ref[0])
    def _():
        @pl.when(step == 0)
        def _():
            pltpu.make_async_copy(
                block_refs[0], pay_ref.at[slot % 2], sem_ref.at[slot % 2]
            ).wait()

            @pl.when(slot + 1 < slots_ref[0])
            def _():
                fetch(slot + 1)

            feat, vec = unpack(pay_ref[slot % 2])
            left_ref[...] = other_factor(feat)
            vec_ref[...] = vec

        for tile_ref, here in ((front_ref, slot < FRONT), (back_ref, slot >= FRONT)):
            @pl.when(here)
            def _():
                tile_rows(
                    left_ref, right_ref, vec_ref, step * ROWS, tile_ref.at[0], sum_ref,
                    (dist_zero_ref, dist_one_ref),
                )

    @pl.when((slot == pl.num_programs(0) - 1) & (step == pl.num_programs(1) - 1))
    def _():
        rhs = rhs_ref[...]
        width = rhs.shape[1]
        image = (var_ref[...] + DIAGONAL) * rhs + SCALE * sum_ref[...]
        image_ref[...] = image
        send_ref[:, :width] = image.astype(BF16)
        pieces = split_three(jnp.sum(rhs * rhs, axis=1, keepdims=True))
        pieces += split_three(jnp.sum(rhs * image, axis=1, keepdims=True))
        lane = lax.broadcasted_iota(jnp.int32, (rhs.shape[0], TAIL), 1)
        tail = jnp.zeros((rhs.shape[0], TAIL), F32)
        for place, piece in enumerate(pieces):
            tail = jnp.where(lane == place, piece, tail)
        send_ref[:, width:] = tail.astype(BF16)


def own_again_kernel(tile_ref, vec_ref, sum_ref):
    step = pl.program_id(0)

    @pl.when(step == 0)
    def _():
        sum_ref[...] = jnp.zeros_like(sum_ref)

    at = pl.multiple_of(step * ROWS, ROWS)
    sum_ref[...] += jnp.dot(
        vec_ref[:, pl.ds(at, ROWS)], tile_ref[...], preferred_element_type=F32
    )


def again_kernel(
    slots_ref, front_ref, back_ref, vec_ref, tails_ref, first_ref, rhs_ref, var_ref, image_ref,
    rows_ref, dots_ref, step_ref,
    sum_ref, held_ref, sem_ref,
):
    slot, step = pl.program_id(0), pl.program_id(1)
    width = rhs_ref.shape[1]

    steps = width // ROWS
    parts = (slots_ref[0] - FRONT) * steps

    def fetch(part):
        at = pl.ds(pl.multiple_of((part % steps) * ROWS, ROWS), ROWS)
        return pltpu.make_async_copy(
            back_ref.at[part // steps, at], held_ref.at[part % HELD], sem_ref.at[part % HELD]
        )

    @pl.when((slot == 0) & (step == 0))
    def _():
        sum_ref[...] = first_ref[...]
        for part in range(HELD):
            @pl.when(part < parts)
            def _():
                fetch(part).start()

    @pl.when(slot < slots_ref[0])
    def _():
        at = pl.multiple_of(step * ROWS, ROWS)

        @pl.when(slot < FRONT)
        def _():
            sum_ref[...] += jnp.dot(
                vec_ref[0, :, pl.ds(at, ROWS)], front_ref[0], preferred_element_type=F32
            )

        @pl.when(slot >= FRONT)
        def _():
            part = (slot - FRONT) * steps + step
            fetch(part).wait()
            sum_ref[...] += jnp.dot(
                vec_ref[0, :, pl.ds(at, ROWS)], held_ref[part % HELD], preferred_element_type=F32
            )

            @pl.when(part + HELD < parts)
            def _():
                fetch(part + HELD).start()

    @pl.when((slot == pl.num_programs(0) - 1) & (step == pl.num_programs(1) - 1))
    def _():
        rhs = rhs_ref[...]
        image = image_ref[...]
        total = jnp.sum(tails_ref[...].astype(F32), axis=0)
        norm = total[:, 0:1] + total[:, 1:2] + total[:, 2:3]
        curve = total[:, 3:4] + total[:, 4:5] + total[:, 5:6]
        length = norm / curve
        second = (var_ref[...] + DIAGONAL) * image + SCALE * sum_ref[...]
        res = rhs - length * image
        res_image = image - length * second
        rows_ref[0:8] = rhs
        rows_ref[8:16] = res
        rows_ref[16:24] = image
        rows_ref[24:32] = res_image
        lane = lax.broadcasted_iota(jnp.int32, (rhs.shape[0], TAIL), 1)
        dots = jnp.zeros((rhs.shape[0], TAIL), F32)
        for place, product in enumerate((res * res, res * res_image, res * image, rhs * res_image)):
            dots = jnp.where(lane == place, jnp.sum(product, axis=1, keepdims=True), dots)
        dots_ref[...] = dots
        step_ref[...] = jnp.where(lane == 0, norm, jnp.where(lane == 1, curve, 0.0))


def order_kernel(rows_ref, perm_ref, out_ref):
    rows = rows_ref[...]
    count, width = rows.shape
    pieces = jnp.concatenate([piece for piece in split_three(rows)], axis=0).astype(BF16)
    perm = perm_ref[...]
    chunk = 256
    for col in range(0, width, chunk):
        total = jnp.zeros((3 * count, chunk), F32)
        for at in range(0, width, chunk):
            index = lax.broadcasted_iota(jnp.int32, (chunk, chunk), 0) + at
            pick = jnp.where(index == perm[:, col : col + chunk], 1.0, 0.0).astype(BF16)
            total += jnp.dot(pieces[:, at : at + chunk], pick, preferred_element_type=F32)
        out_ref[:, col : col + chunk] = total[:count] + total[count : 2 * count] + total[2 * count :]


def swap(value, mask, count):
    return lax.ppermute(value, "row", [(i, i ^ mask) for i in range(count)])


def levels(count, sizes):
    bits = count.bit_length() - 1
    out = []
    sizes = list(sizes)
    while bits:
        take = min(sizes.pop(0) if sizes else 1, bits)
        bits -= take
        out.append([mask << bits for mask in range(1, 1 << take)])
    return out


def tree_sum(value, count):
    for masks in levels(count, [2, 2, 2]):
        others = [swap(value, mask, count) for mask in masks]
        if len(masks) == 3:
            value = (value + others[0]) + (others[1] + others[2])
        else:
            value = value + others[0]
    return value


def gather_levels(count):
    return levels(count, [2] if count <= 16 else [2, 2])


def gather_places(count):
    places = [0]
    for masks in gather_levels(count):
        places = places + [place ^ mask for mask in masks for place in places]
    return places


def tree_gather(value, count):
    blocks = value[None]
    for masks in gather_levels(count):
        blocks = jnp.concatenate([blocks] + [swap(blocks, mask, count) for mask in masks], axis=0)
    return blocks


def pass_on(value, count):
    blocks = [value]
    for masks in gather_levels(count):
        blocks = blocks + [swap(block, mask, count) for mask in masks for block in blocks]
    return blocks


def partners(tile_list, count):
    most = tile_list.shape[1]
    me = lax.axis_index("row")
    lists = tree_gather(tile_list[0, :, 1], count)
    number = me ^ jnp.asarray(gather_places(count), jnp.int32)
    lower = jnp.any(lists == me, axis=1)
    upper = jnp.any(tile_list[0, :, 1][None, :] == number[:, None], axis=1)
    valid = lower | upper
    earlier = np.tri(count, k=-1, dtype=bool)
    before = jnp.sum((valid[None, :] & earlier).astype(jnp.int32), axis=1)
    total = jnp.sum(valid.astype(jnp.int32))
    slot = jnp.minimum(jnp.arange(most), jnp.maximum(total - 1, 0))
    hit = valid[None, :] & (before[None, :] == slot[:, None])
    where = jnp.sum(jnp.where(hit, jnp.arange(count)[None, :], 0), axis=1)
    return jnp.concatenate([total[None], where]).astype(jnp.int32)


def local(features, right_side, variance, hilbert_order, tile_list):
    width = features.shape[1]
    rhs_count = right_side.shape[0]
    count = lax.axis_size("row")
    most = tile_list.shape[1]
    steps = width // ROWS
    shape = jax.ShapeDtypeStruct
    params = pltpu.CompilerParams(vmem_limit_bytes=10 * 1024 * 1024)
    var_row = variance[None, :]

    rounded = right_side.astype(BF16)
    half = width // 2
    payload = jnp.concatenate(
        [features[:, :half], features[:, half:], rounded[:, :half], rounded[:, half:]], axis=0
    )
    every = pass_on(payload, count)
    slots = partners(tile_list, count)
    scratch = [
        pltpu.VMEM((width, KDIM), BF16),
        pltpu.VMEM((KDIM, width), BF16),
        pltpu.VMEM((rhs_count, width), BF16),
        pltpu.VMEM((UNIT, UNIT), F32),
        pltpu.VMEM((UNIT, UNIT), F32),
    ]
    whole = lambda *ignored: (0, 0)
    row_spec = pl.BlockSpec(right_side.shape, whole)
    var_spec = pl.BlockSpec(var_row.shape, whole)
    own_tile, own_sum = pl.pallas_call(
        own_kernel,
        grid=(steps,),
        in_specs=[pl.BlockSpec(payload.shape, whole)],
        out_specs=[pl.BlockSpec((ROWS, width), lambda i: (i, 0)), row_spec],
        out_shape=[pltpu.HBM((width, width), BF16), shape(right_side.shape, F32)],
        scratch_shapes=scratch,
        compiler_params=params,
        name="own_tile",
    )(payload)

    def front_at(k, i, s):
        return (jnp.minimum(k, FRONT - 1), jnp.where(k < FRONT, i, steps - 1), 0)

    def back_at(k, i, s):
        return (jnp.maximum(k - FRONT, 0), jnp.where(k < FRONT, 0, i), 0)

    tile_specs = [pl.BlockSpec((1, ROWS, width), front_at), pl.BlockSpec((1, ROWS, width), back_at)]
    send_shape = (rhs_count, width + TAIL)
    front_tiles, back_tiles, image, send = pl.pallas_call(
        pair_kernel,
        grid_spec=pltpu.PrefetchScalarGridSpec(
            num_scalar_prefetch=1,
            grid=(most, steps),
            in_specs=[
                pl.BlockSpec(payload.shape, whole),
                row_spec,
                row_spec,
                var_spec,
            ]
            + [pl.BlockSpec(memory_space=pl.ANY)] * count,
            out_specs=tile_specs
            + [
                row_spec,
                pl.BlockSpec(send_shape, whole),
            ],
            scratch_shapes=scratch
            + [pltpu.VMEM((2,) + payload.shape, BF16), pltpu.SemaphoreType.DMA((2,))],
        ),
        out_shape=[
            pltpu.VMEM((FRONT, width, width), BF16),
            pltpu.HBM((most - FRONT, width, width), BF16),
            shape(right_side.shape, F32),
            shape(send_shape, BF16),
        ],
        compiler_params=params,
        name="pair_tiles",
    )(slots, payload, own_sum, right_side, var_row, *every)
    front_tiles = pltpu.with_memory_space_constraint(front_tiles, pltpu.VMEM)
    back_tiles = pltpu.with_memory_space_constraint(back_tiles, pltpu.HBM)

    every_send = tree_gather(send, count)
    own_again = pl.pallas_call(
        own_again_kernel,
        grid=(steps,),
        in_specs=[
            pl.BlockSpec((ROWS, width), lambda i: (i, 0)),
            pl.BlockSpec(send_shape, whole),
        ],
        out_specs=row_spec,
        out_shape=shape(right_side.shape, F32),
        compiler_params=params,
        name="own_again",
    )(pltpu.with_memory_space_constraint(own_tile, pltpu.HBM), send)
    dots_spec = pl.BlockSpec((rhs_count, TAIL), whole)
    rows, dots, steps_one = pl.pallas_call(
        again_kernel,
        grid_spec=pltpu.PrefetchScalarGridSpec(
            num_scalar_prefetch=1,
            grid=(most, steps),
            in_specs=[
                tile_specs[0],
                pl.BlockSpec(memory_space=pl.ANY),
                pl.BlockSpec((1,) + send_shape, lambda k, i, s: (s[1 + k], 0, 0)),
                pl.BlockSpec((count, rhs_count, TAIL), lambda k, i, s: (0, 0, width // TAIL)),
                row_spec,
                row_spec,
                var_spec,
                row_spec,
            ],
            out_specs=[
                pl.BlockSpec((4 * rhs_count, width), whole),
                dots_spec,
                dots_spec,
            ],
            scratch_shapes=[
                pltpu.VMEM(right_side.shape, F32),
                pltpu.VMEM((HELD, ROWS, width), BF16),
                pltpu.SemaphoreType.DMA((HELD,)),
            ],
        ),
        out_shape=[
            shape((4 * rhs_count, width), F32),
            shape((rhs_count, TAIL), F32),
            shape((rhs_count, TAIL), F32),
        ],
        compiler_params=params,
        name="pair_again",
    )(slots, front_tiles, back_tiles, every_send, every_send, own_again, right_side, var_row, image)

    dots = tree_sum(dots, count)
    ordered = pl.pallas_call(
        order_kernel,
        out_shape=shape(rows.shape, F32),
        compiler_params=params,
        name="curve_order",
    )(rows, hilbert_order)
    norm, curve = steps_one[:, 0:1], steps_one[:, 1:2]
    length = norm / curve
    norm_next = dots[:, 0:1]
    ratio = norm_next / norm
    curve_next = dots[:, 1:2] + ratio * (dots[:, 2:3] + dots[:, 3:4]) + ratio * ratio * curve
    length_next = norm_next / curve_next
    rhs_o, res_o, image_o, res_image_o = [ordered[at : at + 8] for at in range(0, 32, 8)]
    solved = length * rhs_o + length_next * (res_o + ratio * rhs_o)
    residual = res_o - length_next * (res_image_o + ratio * image_o)
    return (solved, residual)


def solution(mesh):
    in_specs = (
        P(None, ("group", "row")),
        P(None, ("group", "row")),
        P(("group", "row")),
        P(("group", "row"), None),
        P(("group", "row"), None, None),
    )
    out_specs = (P(None, ("group", "row")), P(None, ("group", "row")))
    return jax.shard_map(local, mesh=mesh, in_specs=in_specs, out_specs=out_specs, check_vma=False)
```

```python
import functools

import jax
import jax.numpy as jnp
import numpy as np
from jax import lax
from jax.experimental import pallas as pl
from jax.experimental.pallas import tpu as pltpu
from jax.sharding import PartitionSpec as P

SHRINK = 0.95
GRAM = SHRINK * SHRINK
SCALE = 20.0 * (20.0 / 19.0) ** 19
DIAGONAL = float(1.0 - SCALE * float(np.float32(1.0 / SCALE).astype(jnp.bfloat16)))
KDIM = 128
ROWS = 512
PARTS = 4
UNIT = 256
FRONT = 3
HELD = 4
TAIL = 128
BF16 = jnp.bfloat16
F32 = jnp.float32


def split_three(value):
    high = value.astype(BF16).astype(F32)
    rest = value - high
    middle = rest.astype(BF16).astype(F32)
    return high, middle, rest - middle


def norm_rows(norm, first):
    high, middle, low = split_three(norm)
    row = lax.broadcasted_iota(jnp.int32, (32, norm.shape[1]), 0)
    out = jnp.where(row < 6, 1.0, 0.0)
    out = jnp.where(row == first, high, out)
    out = jnp.where(row == first + 1, middle, out)
    return jnp.where(row == first + 2, low, out).astype(BF16)


def own_factor(feat):
    wide = feat.astype(F32)
    norm = jnp.sum(wide * wide, axis=0, keepdims=True) * GRAM
    pieces = split_three(wide * (-2.0 * GRAM))
    return jnp.concatenate([piece.astype(BF16) for piece in pieces] + [norm_rows(norm, 0)], axis=0)


def other_factor(feat):
    wide = feat.astype(F32)
    norm = jnp.sum(wide * wide, axis=0, keepdims=True) * GRAM
    return jnp.transpose(jnp.concatenate([feat, feat, feat, norm_rows(norm, 3)], axis=0))


def psi_chain(dist):
    dist = jnp.maximum(dist, 1e-30)
    radius = dist * lax.rsqrt(dist)
    u = jnp.maximum(SHRINK - radius, 0.0)
    two = u * u
    four = two * two
    eight = four * four
    sixteen = eight * eight
    return (sixteen * two * (u - two)).astype(BF16)


def psi_power(dist):
    dist = jnp.maximum(dist, 1e-30)
    radius = dist * lax.rsqrt(dist)
    u = jnp.maximum(SHRINK - radius, 1e-30)
    return (jnp.exp2(19.0 * lax.log2(u)) * (1.0 - u)).astype(BF16)


def tile_rows(left_ref, right_ref, vec_ref, begin, tile_ref, sum_ref, dist_refs, psi, rows_at_once):
    width = right_ref.shape[1]
    units = width // UNIT

    def gram(row, unit, dist_ref):
        col = unit * UNIT
        dist_ref[...] = jnp.dot(
            left_ref[pl.ds(pl.multiple_of(row, UNIT), UNIT), :],
            right_ref[:, col : col + UNIT],
            preferred_element_type=F32,
        )

    def product(vec, at, unit):
        col = unit * UNIT
        sum_ref[:, col : col + UNIT] += jnp.dot(
            vec, tile_ref[pl.ds(at, UNIT), col : col + UNIT], preferred_element_type=F32
        )

    gram(begin, 0, dist_refs[0])

    def step(index, carry):
        at = pl.multiple_of(index * UNIT, UNIT)
        row = begin + at
        following = begin + jnp.minimum(at + UNIT, ROWS - UNIT)
        vec = vec_ref[:, pl.ds(pl.multiple_of(row, UNIT), UNIT)]
        for unit in range(units):
            if unit + 1 < units:
                gram(row, unit + 1, dist_refs[(unit + 1) % 2])
            else:
                gram(following, 0, dist_refs[(unit + 1) % 2])
            col = unit * UNIT
            for sub in range(0, UNIT, rows_at_once):
                tile_ref[pl.ds(at + sub, rows_at_once), col : col + UNIT] = psi(
                    dist_refs[unit % 2][sub : sub + rows_at_once, :]
                )
            if unit:
                product(vec, at, unit - 1)
        product(vec, at, units - 1)
        return carry

    lax.fori_loop(0, ROWS // UNIT, step, 0)


def unpack(pay):
    half = pay.shape[1]
    return jnp.concatenate([pay[:32], pay[32:64]], axis=1), jnp.concatenate([pay[64:72], pay[72:80]], axis=1)


def own_kernel(part, pay_ref, right_in_ref, arrived_ref, tile_ref, sum_ref, left_ref, vec_ref, *dist_refs):
    feat, vec = unpack(pay_ref[...])
    begin = part * ROWS
    left_ref[...] = other_factor(feat[:, begin : begin + ROWS])
    vec_ref[...] = vec[:, begin : begin + ROWS]
    sum_ref[...] = jnp.zeros_like(sum_ref)
    tile_rows(left_ref, right_in_ref, vec_ref, 0, tile_ref, sum_ref, dist_refs, psi_chain, 16)


def factor_kernel(pay_ref, list_ref, right_ref, list_out_ref):
    right_ref[...] = own_factor(unpack(pay_ref[...])[0])
    list_out_ref[...] = list_ref[...]


def pair_kernel(slots_ref, right_ref, rhs_ref, var_ref, *refs):
    first_refs = refs[:PARTS]
    block_refs = refs[PARTS:-10]
    front_ref, back_ref, image_ref, send_ref = refs[-10:-6]
    left_ref, vec_ref, dist_zero_ref, dist_one_ref, pay_ref, sem_ref = refs[-6:]
    slot, step = pl.program_id(0), pl.program_id(1)
    sum_ref = image_ref

    def fetch(which):
        place = slots_ref[1 + which]
        for at, block_ref in enumerate(block_refs):
            @pl.when(place == at)
            def _():
                pltpu.make_async_copy(
                    block_ref, pay_ref.at[which % 2], sem_ref.at[which % 2]
                ).start()

    @pl.when((slot == 0) & (step == 0))
    def _():
        sum_ref[...] = functools.reduce(jnp.add, [first_ref[...] for first_ref in first_refs])

        @pl.when(slots_ref[0] > 0)
        def _():
            fetch(0)

    @pl.when(slot < slots_ref[0])
    def _():
        @pl.when(step == 0)
        def _():
            pltpu.make_async_copy(
                block_refs[0], pay_ref.at[slot % 2], sem_ref.at[slot % 2]
            ).wait()

            @pl.when(slot + 1 < slots_ref[0])
            def _():
                fetch(slot + 1)

            feat, vec = unpack(pay_ref[slot % 2])
            left_ref[...] = other_factor(feat)
            vec_ref[...] = vec

        for tile_ref, here in ((front_ref, slot < FRONT), (back_ref, slot >= FRONT)):
            @pl.when(here)
            def _():
                tile_rows(
                    left_ref, right_ref, vec_ref, step * ROWS, tile_ref.at[0], sum_ref,
                    (dist_zero_ref, dist_one_ref), psi_power, 64,
                )

    @pl.when((slot == pl.num_programs(0) - 1) & (step == pl.num_programs(1) - 1))
    def _():
        rhs = rhs_ref[...]
        width = rhs.shape[1]
        image = (var_ref[...] + DIAGONAL) * rhs + SCALE * sum_ref[...]
        image_ref[...] = image
        send_ref[:, :width] = image.astype(BF16)
        pieces = split_three(jnp.sum(rhs * rhs, axis=1, keepdims=True))
        pieces += split_three(jnp.sum(rhs * image, axis=1, keepdims=True))
        lane = lax.broadcasted_iota(jnp.int32, (rhs.shape[0], TAIL), 1)
        tail = jnp.zeros((rhs.shape[0], TAIL), F32)
        for place, piece in enumerate(pieces):
            tail = jnp.where(lane == place, piece, tail)
        send_ref[:, width:] = tail.astype(BF16)


def own_again_kernel(*refs):
    tile_refs, (vec_ref, sum_ref) = refs[:PARTS], refs[PARTS:]
    step = pl.program_id(0)
    rows = tile_refs[0].shape[0]

    @pl.when(step == 0)
    def _():
        sum_ref[...] = jnp.zeros_like(sum_ref)

    for part, tile_ref in enumerate(tile_refs):
        at = pl.multiple_of(part * ROWS + step * rows, rows)
        sum_ref[...] += jnp.dot(
            vec_ref[:, pl.ds(at, rows)], tile_ref[...], preferred_element_type=F32
        )


def again_kernel(
    slots_ref, front_ref, back_ref, vec_ref, tails_ref, first_ref, rhs_ref, var_ref, image_ref,
    rows_ref, dots_ref, step_ref,
    sum_ref, held_ref, sem_ref,
):
    slot, step = pl.program_id(0), pl.program_id(1)
    width = rhs_ref.shape[1]

    steps = width // ROWS
    parts = (slots_ref[0] - FRONT) * steps

    def fetch(part):
        at = pl.ds(pl.multiple_of((part % steps) * ROWS, ROWS), ROWS)
        return pltpu.make_async_copy(
            back_ref.at[part // steps, at], held_ref.at[part % HELD], sem_ref.at[part % HELD]
        )

    @pl.when((slot == 0) & (step == 0))
    def _():
        sum_ref[...] = first_ref[...]
        for part in range(HELD):
            @pl.when(part < parts)
            def _():
                fetch(part).start()

    @pl.when(slot < slots_ref[0])
    def _():
        at = pl.multiple_of(step * ROWS, ROWS)

        @pl.when(slot < FRONT)
        def _():
            sum_ref[...] += jnp.dot(
                vec_ref[0, :, pl.ds(at, ROWS)], front_ref[0], preferred_element_type=F32
            )

        @pl.when(slot >= FRONT)
        def _():
            part = (slot - FRONT) * steps + step
            fetch(part).wait()
            sum_ref[...] += jnp.dot(
                vec_ref[0, :, pl.ds(at, ROWS)], held_ref[part % HELD], preferred_element_type=F32
            )

            @pl.when(part + HELD < parts)
            def _():
                fetch(part + HELD).start()

    @pl.when((slot == pl.num_programs(0) - 1) & (step == pl.num_programs(1) - 1))
    def _():
        rhs = rhs_ref[...]
        image = image_ref[...]
        total = jnp.sum(tails_ref[...].astype(F32), axis=0)
        norm = total[:, 0:1] + total[:, 1:2] + total[:, 2:3]
        curve = total[:, 3:4] + total[:, 4:5] + total[:, 5:6]
        length = norm / curve
        second = (var_ref[...] + DIAGONAL) * image + SCALE * sum_ref[...]
        res = rhs - length * image
        res_image = image - length * second
        rows_ref[0:8] = rhs
        rows_ref[8:16] = res
        rows_ref[16:24] = image
        rows_ref[24:32] = res_image
        lane = lax.broadcasted_iota(jnp.int32, (rhs.shape[0], TAIL), 1)
        dots = jnp.zeros((rhs.shape[0], TAIL), F32)
        for place, product in enumerate((res * res, res * res_image, res * image, rhs * res_image)):
            dots = jnp.where(lane == place, jnp.sum(product, axis=1, keepdims=True), dots)
        dots_ref[...] = dots
        step_ref[...] = jnp.where(lane == 0, norm, jnp.where(lane == 1, curve, 0.0))


def order_kernel(rows_ref, perm_ref, out_ref):
    rows = rows_ref[...]
    count, width = rows.shape
    pieces = jnp.concatenate([piece for piece in split_three(rows)], axis=0).astype(BF16)
    perm = perm_ref[...]
    chunk = 256
    for col in range(0, width, chunk):
        total = jnp.zeros((3 * count, chunk), F32)
        for at in range(0, width, chunk):
            index = lax.broadcasted_iota(jnp.int32, (chunk, chunk), 0) + at
            pick = jnp.where(index == perm[:, col : col + chunk], 1.0, 0.0).astype(BF16)
            total += jnp.dot(pieces[:, at : at + chunk], pick, preferred_element_type=F32)
        out_ref[:, col : col + chunk] = total[:count] + total[count : 2 * count] + total[2 * count :]


def swap(value, mask, count):
    return lax.ppermute(value, "row", [(i, i ^ mask) for i in range(count)])


def levels(count, sizes):
    bits = count.bit_length() - 1
    out = []
    sizes = list(sizes)
    while bits:
        take = min(sizes.pop(0) if sizes else 1, bits)
        bits -= take
        out.append([mask << bits for mask in range(1, 1 << take)])
    return out


def tree_sum(value, count):
    for masks in levels(count, [2, 2, 2]):
        others = [swap(value, mask, count) for mask in masks]
        if len(masks) == 3:
            value = (value + others[0]) + (others[1] + others[2])
        else:
            value = value + others[0]
    return value


def gather_levels(count):
    return levels(count, [2] if count <= 16 else [2, 2])


def gather_places(count):
    places = [0]
    for masks in gather_levels(count):
        places = places + [place ^ mask for mask in masks for place in places]
    return places


def tree_gather(value, count):
    blocks = value[None]
    for masks in gather_levels(count):
        blocks = jnp.concatenate([blocks] + [swap(blocks, mask, count) for mask in masks], axis=0)
    return blocks


def pass_on(value, count):
    blocks = [value]
    for masks in gather_levels(count):
        blocks = blocks + [swap(block, mask, count) for mask in masks for block in blocks]
    return blocks


def partners(coupled, count):
    most = coupled.shape[1]
    me = lax.axis_index("row")
    lists = tree_gather(coupled[0], count)
    number = me ^ jnp.asarray(gather_places(count), jnp.int32)
    lower = jnp.any(lists == me, axis=1)
    upper = jnp.any(coupled == number[:, None], axis=1)
    valid = lower | upper
    earlier = np.tri(count, k=-1, dtype=bool)
    before = jnp.sum((valid[None, :] & earlier).astype(jnp.int32), axis=1)
    total = jnp.sum(valid.astype(jnp.int32))
    slot = jnp.minimum(jnp.arange(most), jnp.maximum(total - 1, 0))
    hit = valid[None, :] & (before[None, :] == slot[:, None])
    where = jnp.sum(jnp.where(hit, jnp.arange(count)[None, :], 0), axis=1)
    return jnp.concatenate([total[None], where]).astype(jnp.int32)


def local(features, right_side, variance, hilbert_order, tile_list):
    width = features.shape[1]
    rhs_count = right_side.shape[0]
    count = lax.axis_size("row")
    most = tile_list.shape[1]
    steps = width // ROWS
    shape = jax.ShapeDtypeStruct
    params = pltpu.CompilerParams(vmem_limit_bytes=10 * 1024 * 1024)
    var_row = variance[None, :]

    rounded = right_side.astype(BF16)
    half = width // 2
    payload = jnp.concatenate(
        [features[:, :half], features[:, half:], rounded[:, :half], rounded[:, half:]], axis=0
    )
    every = pass_on(payload, count)
    dist_scratch = [pltpu.VMEM((UNIT, UNIT), F32)] * 2
    whole = lambda *ignored: (0, 0)
    row_spec = pl.BlockSpec(right_side.shape, whole)
    var_spec = pl.BlockSpec(var_row.shape, whole)
    right, coupled = pl.pallas_call(
        factor_kernel,
        out_shape=[shape((KDIM, width), BF16), shape((1, most), jnp.int32)],
        compiler_params=params,
        name="own_factor",
    )(payload, tile_list[:, :, 1])
    slots = partners(coupled, count)
    own_parts = [
        pl.pallas_call(
            functools.partial(own_kernel, part),
            in_specs=[
                pl.BlockSpec(payload.shape, lambda: (0, 0)),
                pl.BlockSpec(right.shape, lambda: (0, 0)),
                pl.BlockSpec(memory_space=pl.ANY),
            ],
            out_shape=[pltpu.HBM((ROWS, width), BF16), shape(right_side.shape, F32)],
            scratch_shapes=[pltpu.VMEM((ROWS, KDIM), BF16), pltpu.VMEM((rhs_count, ROWS), BF16)]
            + dist_scratch,
            compiler_params=params,
            cost_estimate=pl.CostEstimate(
                flops=4_000_000_000, bytes_accessed=2 * ROWS * width, transcendentals=0
            ),
            name=f"own_tile_{part}",
        )(payload, right, every[part])
        for part in range(PARTS)
    ]
    own_tiles = [part[0] for part in own_parts]
    own_sums = [part[1] for part in own_parts]

    def front_at(k, i, s):
        return (jnp.minimum(k, FRONT - 1), jnp.where(k < FRONT, i, steps - 1), 0)

    def back_at(k, i, s):
        return (jnp.maximum(k - FRONT, 0), jnp.where(k < FRONT, 0, i), 0)

    tile_specs = [pl.BlockSpec((1, ROWS, width), front_at), pl.BlockSpec((1, ROWS, width), back_at)]
    send_shape = (rhs_count, width + TAIL)
    front_tiles, back_tiles, image, send = pl.pallas_call(
        pair_kernel,
        grid_spec=pltpu.PrefetchScalarGridSpec(
            num_scalar_prefetch=1,
            grid=(most, steps),
            in_specs=[
                pl.BlockSpec(right.shape, whole),
                row_spec,
                var_spec,
            ]
            + [row_spec] * PARTS
            + [pl.BlockSpec(memory_space=pl.ANY)] * count,
            out_specs=tile_specs
            + [
                row_spec,
                pl.BlockSpec(send_shape, whole),
            ],
            scratch_shapes=[pltpu.VMEM((width, KDIM), BF16), pltpu.VMEM((rhs_count, width), BF16)]
            + dist_scratch
            + [pltpu.VMEM((2,) + payload.shape, BF16), pltpu.SemaphoreType.DMA((2,))],
        ),
        out_shape=[
            pltpu.VMEM((FRONT, width, width), BF16),
            pltpu.HBM((most - FRONT, width, width), BF16),
            shape(right_side.shape, F32),
            shape(send_shape, BF16),
        ],
        compiler_params=params,
        name="pair_tiles",
    )(slots, right, right_side, var_row, *own_sums, *every)
    front_tiles = pltpu.with_memory_space_constraint(front_tiles, pltpu.VMEM)
    back_tiles = pltpu.with_memory_space_constraint(back_tiles, pltpu.HBM)

    every_send = tree_gather(send, count)
    own_again = pl.pallas_call(
        own_again_kernel,
        grid=(2,),
        in_specs=[pl.BlockSpec((ROWS // 2, width), lambda i: (i, 0))] * PARTS
        + [pl.BlockSpec(send_shape, whole)],
        out_specs=row_spec,
        out_shape=shape(right_side.shape, F32),
        compiler_params=params,
        name="own_again",
    )(*[pltpu.with_memory_space_constraint(tile, pltpu.HBM) for tile in own_tiles], send)
    dots_spec = pl.BlockSpec((rhs_count, TAIL), whole)
    rows, dots, steps_one = pl.pallas_call(
        again_kernel,
        grid_spec=pltpu.PrefetchScalarGridSpec(
            num_scalar_prefetch=1,
            grid=(most, steps),
            in_specs=[
                tile_specs[0],
                pl.BlockSpec(memory_space=pl.ANY),
                pl.BlockSpec((1,) + send_shape, lambda k, i, s: (s[1 + k], 0, 0)),
                pl.BlockSpec((count, rhs_count, TAIL), lambda k, i, s: (0, 0, width // TAIL)),
                row_spec,
                row_spec,
                var_spec,
                row_spec,
            ],
            out_specs=[
                pl.BlockSpec((4 * rhs_count, width), whole),
                dots_spec,
                dots_spec,
            ],
            scratch_shapes=[
                pltpu.VMEM(right_side.shape, F32),
                pltpu.VMEM((HELD, ROWS, width), BF16),
                pltpu.SemaphoreType.DMA((HELD,)),
            ],
        ),
        out_shape=[
            shape((4 * rhs_count, width), F32),
            shape((rhs_count, TAIL), F32),
            shape((rhs_count, TAIL), F32),
        ],
        compiler_params=params,
        name="pair_again",
    )(slots, front_tiles, back_tiles, every_send, every_send, own_again, right_side, var_row, image)

    dots = tree_sum(dots, count)
    ordered = pl.pallas_call(
        order_kernel,
        out_shape=shape(rows.shape, F32),
        compiler_params=params,
        name="curve_order",
    )(rows, hilbert_order)
    norm, curve = steps_one[:, 0:1], steps_one[:, 1:2]
    length = norm / curve
    norm_next = dots[:, 0:1]
    ratio = norm_next / norm
    curve_next = dots[:, 1:2] + ratio * (dots[:, 2:3] + dots[:, 3:4]) + ratio * ratio * curve
    length_next = norm_next / curve_next
    rhs_o, res_o, image_o, res_image_o = [ordered[at : at + 8] for at in range(0, 32, 8)]
    solved = length * rhs_o + length_next * (res_o + ratio * rhs_o)
    residual = res_o - length_next * (res_image_o + ratio * image_o)
    return (solved, residual)


def solution(mesh):
    in_specs = (
        P(None, ("group", "row")),
        P(None, ("group", "row")),
        P(("group", "row")),
        P(("group", "row"), None),
        P(("group", "row"), None, None),
    )
    out_specs = (P(None, ("group", "row")), P(None, ("group", "row")))
    return jax.shard_map(local, mesh=mesh, in_specs=in_specs, out_specs=out_specs, check_vma=False)
```

```python
import functools

import jax
import jax.numpy as jnp
import numpy as np
from jax import lax
from jax.experimental import pallas as pl
from jax.experimental.pallas import tpu as pltpu
from jax.sharding import PartitionSpec as P

SHRINK = 0.95
GRAM = SHRINK * SHRINK
SCALE = 20.0 * (20.0 / 19.0) ** 19
DIAGONAL = float(1.0 - SCALE * float(np.float32(1.0 / SCALE).astype(jnp.bfloat16)))
KDIM = 128
ROWS = 512
PARTS = 4
COLS = 512
FRONT = 3
HELD = 4
TAIL = 128
BF16 = jnp.bfloat16
F32 = jnp.float32


def split_three(value):
    high = value.astype(BF16).astype(F32)
    rest = value - high
    middle = rest.astype(BF16).astype(F32)
    return high, middle, rest - middle


def norm_rows(norm, first):
    high, middle, low = split_three(norm)
    row = lax.broadcasted_iota(jnp.int32, (32, norm.shape[1]), 0)
    out = jnp.where(row < 6, 1.0, 0.0)
    out = jnp.where(row == first, high, out)
    out = jnp.where(row == first + 1, middle, out)
    return jnp.where(row == first + 2, low, out).astype(BF16)


def own_factor(feat):
    wide = feat.astype(F32)
    norm = jnp.sum(wide * wide, axis=0, keepdims=True) * GRAM
    pieces = split_three(wide * (-2.0 * GRAM))
    return jnp.concatenate([piece.astype(BF16) for piece in pieces] + [norm_rows(norm, 0)], axis=0)


def other_factor(feat):
    wide = feat.astype(F32)
    norm = jnp.sum(wide * wide, axis=0, keepdims=True) * GRAM
    return jnp.transpose(jnp.concatenate([feat, feat, feat, norm_rows(norm, 3)], axis=0))


def psi_power(dist):
    dist = jnp.maximum(dist, 1e-30)
    radius = dist * lax.rsqrt(dist)
    u = jnp.maximum(SHRINK - radius, 1e-30)
    return (jnp.exp2(19.0 * lax.log2(u)) * (1.0 - u)).astype(BF16)


def tile_rows(left_ref, right_ref, vec_ref, begin, tile_ref, sum_ref, rows_at_once):
    at = pl.multiple_of(begin, ROWS)
    left = left_ref[pl.ds(at, ROWS), :]
    vec = vec_ref[:, pl.ds(at, ROWS)]

    def step(index, carry):
        cols = pl.ds(pl.multiple_of(index * COLS, COLS), COLS)
        dist = jnp.dot(left, right_ref[:, cols], preferred_element_type=F32)
        parts = []
        for sub in range(0, ROWS, rows_at_once):
            part = psi_power(dist[sub : sub + rows_at_once])
            tile_ref[sub : sub + rows_at_once, cols] = part
            parts.append(part)
        sum_ref[:, cols] += jnp.dot(
            vec, jnp.concatenate(parts, axis=0), preferred_element_type=F32
        )
        return carry

    lax.fori_loop(0, right_ref.shape[1] // COLS, step, 0)


def unpack(pay):
    half = pay.shape[1]
    return jnp.concatenate([pay[:32], pay[32:64]], axis=1), jnp.concatenate([pay[64:72], pay[72:80]], axis=1)


def own_kernel(part, pay_ref, right_ref, arrived_ref, tile_ref, sum_ref, left_ref, vec_ref):
    feat, vec = unpack(pay_ref[...])
    begin = part * ROWS
    left_ref[...] = other_factor(feat[:, begin : begin + ROWS])
    vec_ref[...] = vec[:, begin : begin + ROWS]
    sum_ref[...] = jnp.zeros_like(sum_ref)
    tile_rows(left_ref, right_ref, vec_ref, 0, tile_ref, sum_ref, 128)


def factor_kernel(pay_ref, right_ref):
    right_ref[...] = own_factor(unpack(pay_ref[...])[0])


def pair_kernel(slots_ref, right_ref, rhs_ref, var_ref, *refs):
    first_refs = refs[:PARTS]
    block_refs = refs[PARTS:-8]
    front_ref, back_ref, image_ref, send_ref = refs[-8:-4]
    left_ref, vec_ref, pay_ref, sem_ref = refs[-4:]
    slot, step = pl.program_id(0), pl.program_id(1)
    sum_ref = image_ref

    def fetch(which):
        place = slots_ref[1 + which]
        for at, block_ref in enumerate(block_refs):
            @pl.when(place == at)
            def _():
                pltpu.make_async_copy(
                    block_ref, pay_ref.at[which % 2], sem_ref.at[which % 2]
                ).start()

    @pl.when((slot == 0) & (step == 0))
    def _():
        sum_ref[...] = functools.reduce(jnp.add, [first_ref[...] for first_ref in first_refs])

        @pl.when(slots_ref[0] > 0)
        def _():
            fetch(0)

    @pl.when(slot < slots_ref[0])
    def _():
        @pl.when(step == 0)
        def _():
            pltpu.make_async_copy(
                block_refs[0], pay_ref.at[slot % 2], sem_ref.at[slot % 2]
            ).wait()

            @pl.when(slot + 1 < slots_ref[0])
            def _():
                fetch(slot + 1)

            feat, vec = unpack(pay_ref[slot % 2])
            left_ref[...] = other_factor(feat)
            vec_ref[...] = vec

        for tile_ref, here in ((front_ref, slot < FRONT), (back_ref, slot >= FRONT)):
            @pl.when(here)
            def _():
                tile_rows(
                    left_ref, right_ref, vec_ref, step * ROWS, tile_ref.at[0], sum_ref, 64
                )

    @pl.when((slot == pl.num_programs(0) - 1) & (step == pl.num_programs(1) - 1))
    def _():
        rhs = rhs_ref[...]
        width = rhs.shape[1]
        image = (var_ref[...] + DIAGONAL) * rhs + SCALE * sum_ref[...]
        image_ref[...] = image
        send_ref[:, :width] = image.astype(BF16)
        pieces = split_three(jnp.sum(rhs * rhs, axis=1, keepdims=True))
        pieces += split_three(jnp.sum(rhs * image, axis=1, keepdims=True))
        lane = lax.broadcasted_iota(jnp.int32, (rhs.shape[0], TAIL), 1)
        tail = jnp.zeros((rhs.shape[0], TAIL), F32)
        for place, piece in enumerate(pieces):
            tail = jnp.where(lane == place, piece, tail)
        send_ref[:, width:] = tail.astype(BF16)


def own_again_kernel(*refs):
    tile_refs, (vec_ref, sum_ref) = refs[:PARTS], refs[PARTS:]
    step = pl.program_id(0)
    rows = tile_refs[0].shape[0]

    @pl.when(step == 0)
    def _():
        sum_ref[...] = jnp.zeros_like(sum_ref)

    for part, tile_ref in enumerate(tile_refs):
        at = pl.multiple_of(part * ROWS + step * rows, rows)
        sum_ref[...] += jnp.dot(
            vec_ref[:, pl.ds(at, rows)], tile_ref[...], preferred_element_type=F32
        )


def again_kernel(
    slots_ref, front_ref, back_ref, vec_ref, tails_ref, first_ref, rhs_ref, var_ref, image_ref,
    rows_ref, dots_ref, step_ref,
    sum_ref, held_ref, sem_ref,
):
    slot, step = pl.program_id(0), pl.program_id(1)
    width = rhs_ref.shape[1]

    steps = width // ROWS
    parts = (slots_ref[0] - FRONT) * steps

    def fetch(part):
        at = pl.ds(pl.multiple_of((part % steps) * ROWS, ROWS), ROWS)
        return pltpu.make_async_copy(
            back_ref.at[part // steps, at], held_ref.at[part % HELD], sem_ref.at[part % HELD]
        )

    @pl.when((slot == 0) & (step == 0))
    def _():
        sum_ref[...] = first_ref[...]
        for part in range(HELD):
            @pl.when(part < parts)
            def _():
                fetch(part).start()

    @pl.when(slot < slots_ref[0])
    def _():
        at = pl.multiple_of(step * ROWS, ROWS)

        @pl.when(slot < FRONT)
        def _():
            sum_ref[...] += jnp.dot(
                vec_ref[0, :, pl.ds(at, ROWS)], front_ref[0], preferred_element_type=F32
            )

        @pl.when(slot >= FRONT)
        def _():
            part = (slot - FRONT) * steps + step
            fetch(part).wait()
            sum_ref[...] += jnp.dot(
                vec_ref[0, :, pl.ds(at, ROWS)], held_ref[part % HELD], preferred_element_type=F32
            )

            @pl.when(part + HELD < parts)
            def _():
                fetch(part + HELD).start()

    @pl.when((slot == pl.num_programs(0) - 1) & (step == pl.num_programs(1) - 1))
    def _():
        rhs = rhs_ref[...]
        image = image_ref[...]
        total = jnp.sum(tails_ref[...].astype(F32), axis=0)
        norm = total[:, 0:1] + total[:, 1:2] + total[:, 2:3]
        curve = total[:, 3:4] + total[:, 4:5] + total[:, 5:6]
        length = norm / curve
        second = (var_ref[...] + DIAGONAL) * image + SCALE * sum_ref[...]
        res = rhs - length * image
        res_image = image - length * second
        rows_ref[0:8] = rhs
        rows_ref[8:16] = res
        rows_ref[16:24] = image
        rows_ref[24:32] = res_image
        lane = lax.broadcasted_iota(jnp.int32, (rhs.shape[0], TAIL), 1)
        dots = jnp.zeros((rhs.shape[0], TAIL), F32)
        for place, product in enumerate((res * res, res * res_image, res * image, rhs * res_image)):
            dots = jnp.where(lane == place, jnp.sum(product, axis=1, keepdims=True), dots)
        dots_ref[...] = dots
        step_ref[...] = jnp.where(lane == 0, norm, jnp.where(lane == 1, curve, 0.0))


def order_kernel(rows_ref, perm_ref, out_ref):
    rows = rows_ref[...]
    count, width = rows.shape
    pieces = jnp.concatenate([piece for piece in split_three(rows)], axis=0).astype(BF16)
    perm = perm_ref[...]
    chunk = 256
    for col in range(0, width, chunk):
        total = jnp.zeros((3 * count, chunk), F32)
        for at in range(0, width, chunk):
            index = lax.broadcasted_iota(jnp.int32, (chunk, chunk), 0) + at
            pick = jnp.where(index == perm[:, col : col + chunk], 1.0, 0.0).astype(BF16)
            total += jnp.dot(pieces[:, at : at + chunk], pick, preferred_element_type=F32)
        out_ref[:, col : col + chunk] = total[:count] + total[count : 2 * count] + total[2 * count :]


def swap(value, mask, count):
    return lax.ppermute(value, "row", [(i, i ^ mask) for i in range(count)])


def levels(count, sizes):
    bits = count.bit_length() - 1
    out = []
    sizes = list(sizes)
    while bits:
        take = min(sizes.pop(0) if sizes else 1, bits)
        bits -= take
        out.append([mask << bits for mask in range(1, 1 << take)])
    return out


def tree_sum(value, count):
    for masks in levels(count, [2, 2, 2]):
        others = [swap(value, mask, count) for mask in masks]
        if len(masks) == 3:
            value = (value + others[0]) + (others[1] + others[2])
        else:
            value = value + others[0]
    return value


def gather_levels(count):
    return levels(count, [2] if count <= 16 else [2, 2])


def gather_places(count):
    places = [0]
    for masks in gather_levels(count):
        places = places + [place ^ mask for mask in masks for place in places]
    return places


def tree_gather(value, count):
    blocks = value[None]
    for masks in gather_levels(count):
        blocks = jnp.concatenate([blocks] + [swap(blocks, mask, count) for mask in masks], axis=0)
    return blocks


def pass_on(value, count):
    blocks = [value]
    for masks in gather_levels(count):
        blocks = blocks + [swap(block, mask, count) for mask in masks for block in blocks]
    return blocks


def partners(coupled, count):
    most = coupled.shape[1]
    me = lax.axis_index("row")
    lists = tree_gather(coupled[0], count)
    number = me ^ jnp.asarray(gather_places(count), jnp.int32)
    lower = jnp.any(lists == me, axis=1)
    upper = jnp.any(coupled == number[:, None], axis=1)
    valid = lower | upper
    earlier = np.tri(count, k=-1, dtype=bool)
    before = jnp.sum((valid[None, :] & earlier).astype(jnp.int32), axis=1)
    total = jnp.sum(valid.astype(jnp.int32))
    slot = jnp.minimum(jnp.arange(most), jnp.maximum(total - 1, 0))
    hit = valid[None, :] & (before[None, :] == slot[:, None])
    where = jnp.sum(jnp.where(hit, jnp.arange(count)[None, :], 0), axis=1)
    return jnp.concatenate([total[None], where]).astype(jnp.int32)


def local(features, right_side, variance, hilbert_order, tile_list):
    width = features.shape[1]
    rhs_count = right_side.shape[0]
    count = lax.axis_size("row")
    most = tile_list.shape[1]
    steps = width // ROWS
    shape = jax.ShapeDtypeStruct
    params = pltpu.CompilerParams(vmem_limit_bytes=10 * 1024 * 1024)
    var_row = variance[None, :]

    rounded = right_side.astype(BF16)
    half = width // 2
    payload = jnp.concatenate(
        [features[:, :half], features[:, half:], rounded[:, :half], rounded[:, half:]], axis=0
    )
    every = pass_on(payload, count)
    whole = lambda *ignored: (0, 0)
    row_spec = pl.BlockSpec(right_side.shape, whole)
    var_spec = pl.BlockSpec(var_row.shape, whole)
    right = pl.pallas_call(
        factor_kernel,
        out_shape=shape((KDIM, width), BF16),
        compiler_params=params,
        name="own_factor",
    )(payload)
    slots = partners(tile_list[:, :, 1], count)
    own_parts = [
        pl.pallas_call(
            functools.partial(own_kernel, part),
            in_specs=[
                pl.BlockSpec(payload.shape, lambda: (0, 0)),
                pl.BlockSpec(right.shape, lambda: (0, 0)),
                pl.BlockSpec(memory_space=pl.ANY),
            ],
            out_shape=[pltpu.HBM((ROWS, width), BF16), shape(right_side.shape, F32)],
            scratch_shapes=[pltpu.VMEM((ROWS, KDIM), BF16), pltpu.VMEM((rhs_count, ROWS), BF16)],
            compiler_params=params,
            cost_estimate=pl.CostEstimate(
                flops=4_000_000_000, bytes_accessed=2 * ROWS * width, transcendentals=0
            ),
            name=f"own_tile_{part}",
        )(payload, right, every[part or PARTS])
        for part in range(PARTS)
    ]
    own_tiles = [part[0] for part in own_parts]
    own_sums = [part[1] for part in own_parts]

    def front_at(k, i, s):
        return (jnp.minimum(k, FRONT - 1), jnp.where(k < FRONT, i, steps - 1), 0)

    def back_at(k, i, s):
        return (jnp.maximum(k - FRONT, 0), jnp.where(k < FRONT, 0, i), 0)

    tile_specs = [pl.BlockSpec((1, ROWS, width), front_at), pl.BlockSpec((1, ROWS, width), back_at)]
    send_shape = (rhs_count, width + TAIL)
    front_tiles, back_tiles, image, send = pl.pallas_call(
        pair_kernel,
        grid_spec=pltpu.PrefetchScalarGridSpec(
            num_scalar_prefetch=1,
            grid=(most, steps),
            in_specs=[
                pl.BlockSpec(right.shape, whole),
                row_spec,
                var_spec,
            ]
            + [row_spec] * PARTS
            + [pl.BlockSpec(memory_space=pl.ANY)] * count,
            out_specs=tile_specs
            + [
                row_spec,
                pl.BlockSpec(send_shape, whole),
            ],
            scratch_shapes=[pltpu.VMEM((width, KDIM), BF16), pltpu.VMEM((rhs_count, width), BF16)]
            + [pltpu.VMEM((2,) + payload.shape, BF16), pltpu.SemaphoreType.DMA((2,))],
        ),
        out_shape=[
            pltpu.VMEM((FRONT, width, width), BF16),
            pltpu.HBM((most - FRONT, width, width), BF16),
            shape(right_side.shape, F32),
            shape(send_shape, BF16),
        ],
        compiler_params=params,
        name="pair_tiles",
    )(slots, right, right_side, var_row, *own_sums, *every)
    front_tiles = pltpu.with_memory_space_constraint(front_tiles, pltpu.VMEM)
    back_tiles = pltpu.with_memory_space_constraint(back_tiles, pltpu.HBM)

    every_send = tree_gather(send, count)
    own_again = pl.pallas_call(
        own_again_kernel,
        grid=(2,),
        in_specs=[pl.BlockSpec((ROWS // 2, width), lambda i: (i, 0))] * PARTS
        + [pl.BlockSpec(send_shape, whole)],
        out_specs=row_spec,
        out_shape=shape(right_side.shape, F32),
        compiler_params=params,
        name="own_again",
    )(*[pltpu.with_memory_space_constraint(tile, pltpu.HBM) for tile in own_tiles], send)
    dots_spec = pl.BlockSpec((rhs_count, TAIL), whole)
    rows, dots, steps_one = pl.pallas_call(
        again_kernel,
        grid_spec=pltpu.PrefetchScalarGridSpec(
            num_scalar_prefetch=1,
            grid=(most, steps),
            in_specs=[
                tile_specs[0],
                pl.BlockSpec(memory_space=pl.ANY),
                pl.BlockSpec((1,) + send_shape, lambda k, i, s: (s[1 + k], 0, 0)),
                pl.BlockSpec((count, rhs_count, TAIL), lambda k, i, s: (0, 0, width // TAIL)),
                row_spec,
                row_spec,
                var_spec,
                row_spec,
            ],
            out_specs=[
                pl.BlockSpec((4 * rhs_count, width), whole),
                dots_spec,
                dots_spec,
            ],
            scratch_shapes=[
                pltpu.VMEM(right_side.shape, F32),
                pltpu.VMEM((HELD, ROWS, width), BF16),
                pltpu.SemaphoreType.DMA((HELD,)),
            ],
        ),
        out_shape=[
            shape((4 * rhs_count, width), F32),
            shape((rhs_count, TAIL), F32),
            shape((rhs_count, TAIL), F32),
        ],
        compiler_params=params,
        name="pair_again",
    )(slots, front_tiles, back_tiles, every_send, every_send, own_again, right_side, var_row, image)

    dots = tree_sum(dots, count)
    ordered = pl.pallas_call(
        order_kernel,
        out_shape=shape(rows.shape, F32),
        compiler_params=params,
        name="curve_order",
    )(rows, hilbert_order)
    norm, curve = steps_one[:, 0:1], steps_one[:, 1:2]
    length = norm / curve
    norm_next = dots[:, 0:1]
    ratio = norm_next / norm
    curve_next = dots[:, 1:2] + ratio * (dots[:, 2:3] + dots[:, 3:4]) + ratio * ratio * curve
    length_next = norm_next / curve_next
    rhs_o, res_o, image_o, res_image_o = [ordered[at : at + 8] for at in range(0, 32, 8)]
    solved = length * rhs_o + length_next * (res_o + ratio * rhs_o)
    residual = res_o - length_next * (res_image_o + ratio * image_o)
    return (solved, residual)


def solution(mesh):
    in_specs = (
        P(None, ("group", "row")),
        P(None, ("group", "row")),
        P(("group", "row")),
        P(("group", "row"), None),
        P(("group", "row"), None, None),
    )
    out_specs = (P(None, ("group", "row")), P(None, ("group", "row")))
    return jax.shard_map(local, mesh=mesh, in_specs=in_specs, out_specs=out_specs, check_vma=False)
```

```python
import functools

import jax
import jax.numpy as jnp
import numpy as np
from jax import lax
from jax.experimental import pallas as pl
from jax.experimental.pallas import tpu as pltpu
from jax.sharding import PartitionSpec as P

SHRINK = 0.95
GRAM = SHRINK * SHRINK
SCALE = 20.0 * (20.0 / 19.0) ** 19
DIAGONAL = float(1.0 - SCALE * float(np.float32(1.0 / SCALE).astype(jnp.bfloat16)))
KDIM = 128
ROWS = 512
PARTS = 4
COLS = 512
SUB = 64
FRONT = 3
HELD = 4
TAIL = 128
BF16 = jnp.bfloat16
F32 = jnp.float32


def split_three(value):
    high = value.astype(BF16).astype(F32)
    rest = value - high
    middle = rest.astype(BF16).astype(F32)
    return high, middle, rest - middle


def norm_rows(norm, first):
    high, middle, low = split_three(norm)
    row = lax.broadcasted_iota(jnp.int32, (32, norm.shape[1]), 0)
    out = jnp.where(row < 6, 1.0, 0.0)
    out = jnp.where(row == first, high, out)
    out = jnp.where(row == first + 1, middle, out)
    return jnp.where(row == first + 2, low, out).astype(BF16)


def own_factor(feat):
    wide = feat.astype(F32)
    norm = jnp.sum(wide * wide, axis=0, keepdims=True) * GRAM
    pieces = split_three(wide * (-2.0 * GRAM))
    return jnp.concatenate([piece.astype(BF16) for piece in pieces] + [norm_rows(norm, 0)], axis=0)


def other_factor(feat):
    wide = feat.astype(F32)
    norm = jnp.sum(wide * wide, axis=0, keepdims=True) * GRAM
    return jnp.transpose(jnp.concatenate([feat, feat, feat, norm_rows(norm, 3)], axis=0))


def psi_chain(dist):
    dist = jnp.maximum(dist, 1e-30)
    radius = dist * lax.rsqrt(dist)
    u = jnp.maximum(SHRINK - radius, 0.0)
    two = u * u
    four = two * two
    eight = four * four
    sixteen = eight * eight
    return (sixteen * two * (u - two)).astype(BF16)


def psi_power(dist):
    dist = jnp.maximum(dist, 1e-30)
    radius = dist * lax.rsqrt(dist)
    u = jnp.maximum(SHRINK - radius, 1e-30)
    return (jnp.exp2(19.0 * lax.log2(u)) * (1.0 - u)).astype(BF16)


def tile_unit(left, right, vec, psis, tile_ref):
    dist = jnp.dot(left, right, preferred_element_type=F32)
    parts = []
    for index, sub in enumerate(range(0, left.shape[0], SUB)):
        part = psis[index % len(psis)](dist[sub : sub + SUB])
        tile_ref[sub : sub + SUB, :] = part
        parts.append(part)
    return jnp.dot(vec, jnp.concatenate(parts, axis=0), preferred_element_type=F32)


def unpack(pay):
    half = pay.shape[1]
    return jnp.concatenate([pay[:32], pay[32:64]], axis=1), jnp.concatenate([pay[64:72], pay[72:80]], axis=1)


def own_kernel(part, pay_ref, right_ref, arrived_ref, tile_ref, sum_ref, left_ref, vec_ref):
    @pl.when(pl.program_id(0) == 0)
    def _():
        feat, vec = unpack(pay_ref[...])
        begin = part * ROWS
        left_ref[...] = other_factor(feat[:, begin : begin + ROWS])
        vec_ref[...] = vec[:, begin : begin + ROWS]

    sum_ref[...] = tile_unit(
        left_ref[...], right_ref[...], vec_ref[...], (psi_power, psi_chain), tile_ref
    )


def factor_kernel(pay_ref, right_ref):
    right_ref[...] = own_factor(unpack(pay_ref[...])[0])


def find_partners(lists_ref, me, slots_ref):
    count, most = lists_ref.shape
    for at in range(slots_ref.shape[0]):
        slots_ref[at] = 0
    total = jnp.int32(0)
    for at, place in enumerate(gather_places(count)):
        if at == 0:
            continue
        hit = jnp.bool_(False)
        for entry in range(most):
            hit = hit | (lists_ref[at, entry] == me) | (lists_ref[0, entry] == (me ^ place))
        slots_ref[1 + total] = jnp.where(hit, at, 0)
        total = total + hit.astype(jnp.int32)
    slots_ref[0] = total


def pair_kernel(lists_ref, me_ref, right_ref, rhs_ref, var_ref, *refs):
    first_refs = refs[:PARTS]
    block_refs = refs[PARTS:-9]
    front_ref, back_ref, image_ref, send_ref, slots_ref = refs[-9:-4]
    left_ref, vec_ref, pay_ref, sem_ref = refs[-4:]
    slot, step = pl.program_id(0), pl.program_id(1)
    sum_ref = image_ref

    def fetch(which):
        place = slots_ref[1 + which]
        for at, block_ref in enumerate(block_refs):
            @pl.when(place == at)
            def _():
                pltpu.make_async_copy(
                    block_ref, pay_ref.at[which % 2], sem_ref.at[which % 2]
                ).start()

    @pl.when((slot == 0) & (step == 0))
    def _():
        find_partners(lists_ref, me_ref[0], slots_ref)
        sum_ref[...] = functools.reduce(jnp.add, [first_ref[...] for first_ref in first_refs])

        @pl.when(slots_ref[0] > 0)
        def _():
            fetch(0)

    @pl.when(slot < slots_ref[0])
    def _():
        @pl.when(step == 0)
        def _():
            pltpu.make_async_copy(
                block_refs[0], pay_ref.at[slot % 2], sem_ref.at[slot % 2]
            ).wait()

            @pl.when(slot + 1 < slots_ref[0])
            def _():
                fetch(slot + 1)

            feat, vec = unpack(pay_ref[slot % 2])
            left_ref[...] = other_factor(feat)
            vec_ref[...] = vec

        for tile_ref, here in ((front_ref, slot < FRONT), (back_ref, slot >= FRONT)):
            @pl.when(here)
            def _():
                rows = pl.ds(pl.multiple_of(step * ROWS, ROWS), ROWS)
                left, vec = left_ref[rows, :], vec_ref[:, rows]

                def unit(index, carry):
                    cols = pl.ds(pl.multiple_of(index * COLS, COLS), COLS)
                    sum_ref[:, cols] += tile_unit(
                        left, right_ref[:, cols], vec, (psi_power,), tile_ref.at[0, :, cols]
                    )
                    return carry

                lax.fori_loop(0, right_ref.shape[1] // COLS, unit, 0)

    @pl.when((slot == pl.num_programs(0) - 1) & (step == pl.num_programs(1) - 1))
    def _():
        rhs = rhs_ref[...]
        width = rhs.shape[1]
        image = (var_ref[...] + DIAGONAL) * rhs + SCALE * sum_ref[...]
        image_ref[...] = image
        send_ref[:, :width] = image.astype(BF16)
        pieces = split_three(jnp.sum(rhs * rhs, axis=1, keepdims=True))
        pieces += split_three(jnp.sum(rhs * image, axis=1, keepdims=True))
        lane = lax.broadcasted_iota(jnp.int32, (rhs.shape[0], TAIL), 1)
        tail = jnp.zeros((rhs.shape[0], TAIL), F32)
        for place, piece in enumerate(pieces):
            tail = jnp.where(lane == place, piece, tail)
        send_ref[:, width:] = tail.astype(BF16)


def own_again_kernel(part, tile_ref, vec_ref, sum_ref):
    step = pl.program_id(0)
    rows = tile_ref.shape[0]

    @pl.when(step == 0)
    def _():
        sum_ref[...] = jnp.zeros_like(sum_ref)

    at = pl.multiple_of(part * ROWS + step * rows, rows)
    sum_ref[...] += jnp.dot(vec_ref[:, pl.ds(at, rows)], tile_ref[...], preferred_element_type=F32)


def again_kernel(
    slots_ref, front_ref, back_ref, vec_ref, tails_ref, rhs_ref, var_ref, image_ref, *refs
):
    first_refs = refs[:PARTS]
    rows_ref, dots_ref, step_ref, sum_ref, held_ref, sem_ref = refs[PARTS:]
    slot, step = pl.program_id(0), pl.program_id(1)
    width = rhs_ref.shape[1]

    steps = width // ROWS
    parts = (slots_ref[0] - FRONT) * steps

    def fetch(part):
        at = pl.ds(pl.multiple_of((part % steps) * ROWS, ROWS), ROWS)
        return pltpu.make_async_copy(
            back_ref.at[part // steps, at], held_ref.at[part % HELD], sem_ref.at[part % HELD]
        )

    @pl.when((slot == 0) & (step == 0))
    def _():
        sum_ref[...] = functools.reduce(jnp.add, [first_ref[...] for first_ref in first_refs])
        for part in range(HELD):
            @pl.when(part < parts)
            def _():
                fetch(part).start()

    @pl.when(slot < slots_ref[0])
    def _():
        at = pl.multiple_of(step * ROWS, ROWS)

        @pl.when(slot < FRONT)
        def _():
            sum_ref[...] += jnp.dot(
                vec_ref[0, :, pl.ds(at, ROWS)], front_ref[0], preferred_element_type=F32
            )

        @pl.when(slot >= FRONT)
        def _():
            part = (slot - FRONT) * steps + step
            fetch(part).wait()
            sum_ref[...] += jnp.dot(
                vec_ref[0, :, pl.ds(at, ROWS)], held_ref[part % HELD], preferred_element_type=F32
            )

            @pl.when(part + HELD < parts)
            def _():
                fetch(part + HELD).start()

    @pl.when((slot == pl.num_programs(0) - 1) & (step == pl.num_programs(1) - 1))
    def _():
        rhs = rhs_ref[...]
        image = image_ref[...]
        total = jnp.sum(tails_ref[...].astype(F32), axis=0)
        norm = total[:, 0:1] + total[:, 1:2] + total[:, 2:3]
        curve = total[:, 3:4] + total[:, 4:5] + total[:, 5:6]
        length = norm / curve
        second = (var_ref[...] + DIAGONAL) * image + SCALE * sum_ref[...]
        res = rhs - length * image
        res_image = image - length * second
        rows_ref[0:8] = rhs
        rows_ref[8:16] = res
        rows_ref[16:24] = image
        rows_ref[24:32] = res_image
        lane = lax.broadcasted_iota(jnp.int32, (rhs.shape[0], TAIL), 1)
        dots = jnp.zeros((rhs.shape[0], TAIL), F32)
        for place, product in enumerate((res * res, res * res_image, res * image, rhs * res_image)):
            dots = jnp.where(lane == place, jnp.sum(product, axis=1, keepdims=True), dots)
        dots_ref[...] = dots
        step_ref[...] = jnp.where(lane == 0, norm, jnp.where(lane == 1, curve, 0.0))


def order_kernel(rows_ref, perm_ref, out_ref):
    rows = rows_ref[...]
    count, width = rows.shape
    pieces = jnp.concatenate([piece for piece in split_three(rows)], axis=0).astype(BF16)
    perm = perm_ref[...]
    chunk = 256
    for col in range(0, width, chunk):
        total = jnp.zeros((3 * count, chunk), F32)
        for at in range(0, width, chunk):
            index = lax.broadcasted_iota(jnp.int32, (chunk, chunk), 0) + at
            pick = jnp.where(index == perm[:, col : col + chunk], 1.0, 0.0).astype(BF16)
            total += jnp.dot(pieces[:, at : at + chunk], pick, preferred_element_type=F32)
        out_ref[:, col : col + chunk] = total[:count] + total[count : 2 * count] + total[2 * count :]


def swap(value, mask, count):
    return lax.ppermute(value, "row", [(i, i ^ mask) for i in range(count)])


def levels(count, sizes):
    bits = count.bit_length() - 1
    out = []
    sizes = list(sizes)
    while bits:
        take = min(sizes.pop(0) if sizes else 1, bits)
        bits -= take
        out.append([mask << bits for mask in range(1, 1 << take)])
    return out


def tree_sum(value, count):
    for masks in levels(count, [2, 2, 2]):
        others = [swap(value, mask, count) for mask in masks]
        if len(masks) == 3:
            value = (value + others[0]) + (others[1] + others[2])
        else:
            value = value + others[0]
    return value


def gather_levels(count):
    return levels(count, [2] if count <= 16 else [2, 2])


def gather_places(count):
    places = [0]
    for masks in gather_levels(count):
        places = places + [place ^ mask for mask in masks for place in places]
    return places


def tree_gather(value, count):
    blocks = value[None]
    for masks in gather_levels(count):
        blocks = jnp.concatenate([blocks] + [swap(blocks, mask, count) for mask in masks], axis=0)
    return blocks


def pass_on(value, count):
    blocks = [value]
    for masks in gather_levels(count):
        blocks = blocks + [swap(block, mask, count) for mask in masks for block in blocks]
    return blocks


def local(features, right_side, variance, hilbert_order, tile_list):
    width = features.shape[1]
    rhs_count = right_side.shape[0]
    count = lax.axis_size("row")
    most = tile_list.shape[1]
    steps = width // ROWS
    shape = jax.ShapeDtypeStruct
    params = pltpu.CompilerParams(vmem_limit_bytes=10 * 1024 * 1024)
    var_row = variance[None, :]

    rounded = right_side.astype(BF16)
    half = width // 2
    payload = jnp.concatenate(
        [features[:, :half], features[:, half:], rounded[:, :half], rounded[:, half:]], axis=0
    )
    every = pass_on(payload, count)
    whole = lambda *ignored: (0, 0)
    row_spec = pl.BlockSpec(right_side.shape, whole)
    var_spec = pl.BlockSpec(var_row.shape, whole)
    right = pl.pallas_call(
        factor_kernel,
        out_shape=shape((KDIM, width), BF16),
        compiler_params=params,
        name="own_factor",
    )(payload)
    lists = tree_gather(tile_list[0, :, 1], count)
    me = jnp.full((1,), lax.axis_index("row"), jnp.int32)
    own_parts = [
        pl.pallas_call(
            functools.partial(own_kernel, part),
            grid=(width // COLS,),
            in_specs=[
                pl.BlockSpec(payload.shape, whole),
                pl.BlockSpec((KDIM, COLS), lambda i: (0, i)),
                pl.BlockSpec(memory_space=pl.ANY),
            ],
            out_specs=[
                pl.BlockSpec((ROWS, COLS), lambda i: (0, i)),
                pl.BlockSpec((rhs_count, COLS), lambda i: (0, i)),
            ],
            out_shape=[pltpu.HBM((ROWS, width), BF16), shape(right_side.shape, F32)],
            scratch_shapes=[pltpu.VMEM((ROWS, KDIM), BF16), pltpu.VMEM((rhs_count, ROWS), BF16)],
            compiler_params=params,
            cost_estimate=pl.CostEstimate(
                flops=4_000_000_000, bytes_accessed=2 * ROWS * width, transcendentals=0
            ),
            name=f"own_tile_{part}",
        )(payload, right, every[part or PARTS])
        for part in range(PARTS)
    ]
    own_tiles = [part[0] for part in own_parts]
    own_sums = [part[1] for part in own_parts]

    def front_at(k, i, *ignored):
        return (jnp.minimum(k, FRONT - 1), jnp.where(k < FRONT, i, steps - 1), 0)

    def back_at(k, i, *ignored):
        return (jnp.maximum(k - FRONT, 0), jnp.where(k < FRONT, 0, i), 0)

    tile_specs = [pl.BlockSpec((1, ROWS, width), front_at), pl.BlockSpec((1, ROWS, width), back_at)]
    send_shape = (rhs_count, width + TAIL)
    front_tiles, back_tiles, image, send, slots = pl.pallas_call(
        pair_kernel,
        grid_spec=pltpu.PrefetchScalarGridSpec(
            num_scalar_prefetch=2,
            grid=(most, steps),
            in_specs=[
                pl.BlockSpec(right.shape, whole),
                row_spec,
                var_spec,
            ]
            + [row_spec] * PARTS
            + [pl.BlockSpec(memory_space=pl.ANY)] * count,
            out_specs=tile_specs
            + [
                row_spec,
                pl.BlockSpec(send_shape, whole),
                pl.BlockSpec(memory_space=pltpu.SMEM),
            ],
            scratch_shapes=[pltpu.VMEM((width, KDIM), BF16), pltpu.VMEM((rhs_count, width), BF16)]
            + [pltpu.VMEM((2,) + payload.shape, BF16), pltpu.SemaphoreType.DMA((2,))],
        ),
        out_shape=[
            pltpu.VMEM((FRONT, width, width), BF16),
            pltpu.HBM((most - FRONT, width, width), BF16),
            shape(right_side.shape, F32),
            shape(send_shape, BF16),
            shape((most + 2,), jnp.int32),
        ],
        compiler_params=params,
        name="pair_tiles",
    )(lists, me, right, right_side, var_row, *own_sums, *every)
    front_tiles = pltpu.with_memory_space_constraint(front_tiles, pltpu.VMEM)
    back_tiles = pltpu.with_memory_space_constraint(back_tiles, pltpu.HBM)

    every_send = tree_gather(send, count)
    own_again = [
        pl.pallas_call(
            functools.partial(own_again_kernel, part),
            grid=(2,),
            in_specs=[
                pl.BlockSpec((ROWS // 2, width), lambda i: (i, 0)),
                pl.BlockSpec(send_shape, whole),
            ],
            out_specs=row_spec,
            out_shape=shape(right_side.shape, F32),
            compiler_params=params,
            cost_estimate=pl.CostEstimate(
                flops=3_000_000_000, bytes_accessed=2 * ROWS * width, transcendentals=0
            ),
            name=f"own_again_{part}",
        )(pltpu.with_memory_space_constraint(tile, pltpu.HBM), send)
        for part, tile in enumerate(own_tiles)
    ]
    dots_spec = pl.BlockSpec((rhs_count, TAIL), whole)
    rows, dots, steps_one = pl.pallas_call(
        again_kernel,
        grid_spec=pltpu.PrefetchScalarGridSpec(
            num_scalar_prefetch=1,
            grid=(most, steps),
            in_specs=[
                tile_specs[0],
                pl.BlockSpec(memory_space=pl.ANY),
                pl.BlockSpec((1,) + send_shape, lambda k, i, s: (s[1 + k], 0, 0)),
                pl.BlockSpec((count, rhs_count, TAIL), lambda k, i, s: (0, 0, width // TAIL)),
                row_spec,
                var_spec,
                row_spec,
            ]
            + [row_spec] * PARTS,
            out_specs=[
                pl.BlockSpec((4 * rhs_count, width), whole),
                dots_spec,
                dots_spec,
            ],
            scratch_shapes=[
                pltpu.VMEM(right_side.shape, F32),
                pltpu.VMEM((HELD, ROWS, width), BF16),
                pltpu.SemaphoreType.DMA((HELD,)),
            ],
        ),
        out_shape=[
            shape((4 * rhs_count, width), F32),
            shape((rhs_count, TAIL), F32),
            shape((rhs_count, TAIL), F32),
        ],
        compiler_params=params,
        name="pair_again",
    )(slots, front_tiles, back_tiles, every_send, every_send, right_side, var_row, image, *own_again)

    dots = tree_sum(dots, count)
    ordered = pl.pallas_call(
        order_kernel,
        out_shape=shape(rows.shape, F32),
        compiler_params=params,
        name="curve_order",
    )(rows, hilbert_order)
    norm, curve = steps_one[:, 0:1], steps_one[:, 1:2]
    length = norm / curve
    norm_next = dots[:, 0:1]
    ratio = norm_next / norm
    curve_next = dots[:, 1:2] + ratio * (dots[:, 2:3] + dots[:, 3:4]) + ratio * ratio * curve
    length_next = norm_next / curve_next
    rhs_o, res_o, image_o, res_image_o = [ordered[at : at + 8] for at in range(0, 32, 8)]
    solved = length * rhs_o + length_next * (res_o + ratio * rhs_o)
    residual = res_o - length_next * (res_image_o + ratio * image_o)
    return (solved, residual)


def solution(mesh):
    in_specs = (
        P(None, ("group", "row")),
        P(None, ("group", "row")),
        P(("group", "row")),
        P(("group", "row"), None),
        P(("group", "row"), None, None),
    )
    out_specs = (P(None, ("group", "row")), P(None, ("group", "row")))
    return jax.shard_map(local, mesh=mesh, in_specs=in_specs, out_specs=out_specs, check_vma=False)
```

```python
import functools

import jax
import jax.numpy as jnp
import numpy as np
from jax import lax
from jax.experimental import pallas as pl
from jax.experimental.pallas import tpu as pltpu
from jax.sharding import PartitionSpec as P

SHRINK = 0.95
GRAM = SHRINK * SHRINK
SCALE = 20.0 * (20.0 / 19.0) ** 19
DIAGONAL = float(1.0 - SCALE * float(np.float32(1.0 / SCALE).astype(jnp.bfloat16)))
KDIM = 128
ROWS = 512
PARTS = 2
COLS = 512
SUB = 64
FRONT = 3
HELD = 4
TAIL = 128
BF16 = jnp.bfloat16
F32 = jnp.float32
CONTRACT_LANES = (((1,), (1,)), ((), ()))


def split_three(value):
    high = value.astype(BF16).astype(F32)
    rest = value - high
    middle = rest.astype(BF16).astype(F32)
    return high, middle, rest - middle


def norm_rows(norm, first):
    high, middle, low = split_three(norm)
    row = lax.broadcasted_iota(jnp.int32, (32, norm.shape[1]), 0)
    out = jnp.where(row < 6, 1.0, 0.0)
    out = jnp.where(row == first, high, out)
    out = jnp.where(row == first + 1, middle, out)
    return jnp.where(row == first + 2, low, out).astype(BF16)


def own_factor(feat):
    wide = feat.astype(F32)
    norm = jnp.sum(wide * wide, axis=0, keepdims=True) * GRAM
    pieces = split_three(wide * (-2.0 * GRAM))
    return jnp.concatenate([piece.astype(BF16) for piece in pieces] + [norm_rows(norm, 0)], axis=0)


def other_factor(feat):
    wide = feat.astype(F32)
    norm = jnp.sum(wide * wide, axis=0, keepdims=True) * GRAM
    return jnp.transpose(jnp.concatenate([feat, feat, feat, norm_rows(norm, 3)], axis=0))


def psi_power(dist):
    dist = jnp.maximum(dist, 1e-30)
    radius = dist * lax.rsqrt(dist)
    u = jnp.maximum(SHRINK - radius, 1e-30)
    return (jnp.exp2(19.0 * lax.log2(u)) * (1.0 - u)).astype(BF16)


def tile_unit(left, right, vec, tile_ref):
    dist = jnp.dot(left, right, preferred_element_type=F32)
    parts = []
    for sub in range(0, left.shape[0], SUB):
        part = psi_power(dist[sub : sub + SUB])
        tile_ref[sub : sub + SUB, :] = part
        parts.append(part)
    return jnp.dot(vec, jnp.concatenate(parts, axis=0), preferred_element_type=F32)


def unpack(pay):
    return jnp.concatenate([pay[:32], pay[32:64]], axis=1), jnp.concatenate([pay[64:72], pay[72:80]], axis=1)


def own_blocks(count):
    return [(row, col) for row in range(count) for col in range(row, count)]


def own_kernel(
    pay_ref, right_ref, list_ref, out_ref, sum_ref, list_out_ref,
    left_ref, vec_ref, tile_ref, sem_ref,
):
    list_out_ref[...] = list_ref[...]
    feat, vec = unpack(pay_ref[...])
    left_ref[...] = other_factor(feat)
    vec_ref[...] = vec
    sum_ref[...] = jnp.zeros_like(sum_ref)
    count = feat.shape[1] // ROWS
    piece = lambda index: pl.ds(pl.multiple_of(index * ROWS, ROWS), ROWS)
    save = lambda at: pltpu.make_async_copy(tile_ref.at[at], out_ref.at[at], sem_ref.at[at])

    def row_step(row, at):
        def col_step(col, at):
            sum_ref[:, piece(col)] += tile_unit(
                left_ref[piece(row), :], right_ref[:, piece(col)], vec_ref[:, piece(row)],
                tile_ref.at[at],
            )
            save(at).start()

            @pl.when(row != col)
            def _():
                sum_ref[:, piece(row)] += lax.dot_general(
                    vec_ref[:, piece(col)], tile_ref[at], CONTRACT_LANES,
                    preferred_element_type=F32,
                )

            return at + 1

        return lax.fori_loop(row, count, col_step, at)

    lax.fori_loop(0, count, row_step, 0)
    for at in range(tile_ref.shape[0]):
        save(at).wait()


def own_again_kernel(first, blocks, in_ref, vec_ref, sum_ref, tile_ref, sem_ref):
    load = lambda index: pltpu.make_async_copy(
        in_ref.at[first + index], tile_ref.at[index], sem_ref.at[index]
    )
    for index in range(len(blocks)):
        load(index).start()
    sum_ref[...] = jnp.zeros_like(sum_ref)
    piece = lambda index: slice(index * ROWS, (index + 1) * ROWS)
    for index, (row, col) in enumerate(blocks):
        load(index).wait()
        sum_ref[:, piece(col)] += jnp.dot(
            vec_ref[:, piece(row)], tile_ref[index], preferred_element_type=F32
        )
        if row != col:
            sum_ref[:, piece(row)] += lax.dot_general(
                vec_ref[:, piece(col)], tile_ref[index], CONTRACT_LANES, preferred_element_type=F32
            )


def payload_kernel(feat_ref, rhs_ref, pay_ref, right_ref):
    half = feat_ref.shape[1] // 2
    feat = feat_ref[...]
    rounded = rhs_ref[...].astype(BF16)
    pay_ref[:32] = feat[:, :half]
    pay_ref[32:64] = feat[:, half:]
    pay_ref[64:80] = jnp.concatenate([rounded[:, :half], rounded[:, half:]], axis=0)
    right_ref[...] = own_factor(feat)


def find_partners(lists_ref, me, slots_ref):
    count, most = lists_ref.shape
    for at in range(slots_ref.shape[0]):
        slots_ref[at] = 0
    total = jnp.int32(0)
    for at, place in enumerate(gather_places(count)):
        if at == 0:
            continue
        hit = jnp.bool_(False)
        for entry in range(most):
            hit = hit | (lists_ref[at, entry] == me) | (lists_ref[0, entry] == (me ^ place))
        slots_ref[1 + total] = jnp.where(hit, at, 0)
        total = total + hit.astype(jnp.int32)
    slots_ref[0] = total


def pair_kernel(block_at, lists_ref, me_ref, right_ref, rhs_ref, var_ref, *refs):
    first_ref, block_refs = refs[0], refs[1:-9]
    front_ref, back_ref, image_ref, send_ref, slots_ref = refs[-9:-4]
    left_ref, vec_ref, pay_ref, sem_ref = refs[-4:]
    slot, step = pl.program_id(0), pl.program_id(1)
    sum_ref = image_ref

    def fetch(which):
        place = slots_ref[1 + which]
        for at, (index, row) in enumerate(block_at):
            @pl.when(place == at)
            def _():
                pltpu.make_async_copy(
                    block_refs[index].at[pl.ds(row, pay_ref.shape[1])],
                    pay_ref.at[which % 2],
                    sem_ref.at[which % 2],
                ).start()

    @pl.when((slot == 0) & (step == 0))
    def _():
        find_partners(lists_ref, me_ref[0], slots_ref)
        sum_ref[...] = first_ref[...]

        @pl.when(slots_ref[0] > 0)
        def _():
            fetch(0)

    @pl.when(slot < slots_ref[0])
    def _():
        @pl.when(step == 0)
        def _():
            pltpu.make_async_copy(
                block_refs[0], pay_ref.at[slot % 2], sem_ref.at[slot % 2]
            ).wait()

            @pl.when(slot + 1 < slots_ref[0])
            def _():
                fetch(slot + 1)

            feat, vec = unpack(pay_ref[slot % 2])
            left_ref[...] = other_factor(feat)
            vec_ref[...] = vec

        for tile_ref, here in ((front_ref, slot < FRONT), (back_ref, slot >= FRONT)):
            @pl.when(here)
            def _():
                rows = pl.ds(pl.multiple_of(step * ROWS, ROWS), ROWS)
                left, vec = left_ref[rows, :], vec_ref[:, rows]

                def unit(index, carry):
                    cols = pl.ds(pl.multiple_of(index * COLS, COLS), COLS)
                    sum_ref[:, cols] += tile_unit(
                        left, right_ref[:, cols], vec, tile_ref.at[0, :, cols]
                    )
                    return carry

                lax.fori_loop(0, right_ref.shape[1] // COLS, unit, 0)

    @pl.when((slot == pl.num_programs(0) - 1) & (step == pl.num_programs(1) - 1))
    def _():
        rhs = rhs_ref[...]
        width = rhs.shape[1]
        image = (var_ref[...] + DIAGONAL) * rhs + SCALE * sum_ref[...]
        image_ref[...] = image
        send_ref[:, :width] = image.astype(BF16)
        pieces = split_three(jnp.sum(rhs * rhs, axis=1, keepdims=True))
        pieces += split_three(jnp.sum(rhs * image, axis=1, keepdims=True))
        lane = lax.broadcasted_iota(jnp.int32, (rhs.shape[0], TAIL), 1)
        tail = jnp.zeros((rhs.shape[0], TAIL), F32)
        for place, piece in enumerate(pieces):
            tail = jnp.where(lane == place, piece, tail)
        send_ref[:, width:] = tail.astype(BF16)


def again_kernel(
    slots_ref, front_ref, back_ref, vec_ref, tails_ref, rhs_ref, var_ref, image_ref, *refs
):
    first_refs = refs[:PARTS]
    rows_ref, dots_ref, step_ref, sum_ref, held_ref, sem_ref = refs[PARTS:]
    slot, step = pl.program_id(0), pl.program_id(1)
    width = rhs_ref.shape[1]

    steps = width // ROWS
    parts = (slots_ref[0] - FRONT) * steps

    def fetch(part):
        at = pl.ds(pl.multiple_of((part % steps) * ROWS, ROWS), ROWS)
        return pltpu.make_async_copy(
            back_ref.at[part // steps, at], held_ref.at[part % HELD], sem_ref.at[part % HELD]
        )

    @pl.when((slot == 0) & (step == 0))
    def _():
        sum_ref[...] = functools.reduce(jnp.add, [first_ref[...] for first_ref in first_refs])
        for part in range(HELD):
            @pl.when(part < parts)
            def _():
                fetch(part).start()

    @pl.when(slot < slots_ref[0])
    def _():
        at = pl.multiple_of(step * ROWS, ROWS)

        @pl.when(slot < FRONT)
        def _():
            sum_ref[...] += jnp.dot(
                vec_ref[0, :, pl.ds(at, ROWS)], front_ref[0], preferred_element_type=F32
            )

        @pl.when(slot >= FRONT)
        def _():
            part = (slot - FRONT) * steps + step
            fetch(part).wait()
            sum_ref[...] += jnp.dot(
                vec_ref[0, :, pl.ds(at, ROWS)], held_ref[part % HELD], preferred_element_type=F32
            )

            @pl.when(part + HELD < parts)
            def _():
                fetch(part + HELD).start()

    @pl.when((slot == pl.num_programs(0) - 1) & (step == pl.num_programs(1) - 1))
    def _():
        rhs = rhs_ref[...]
        image = image_ref[...]
        total = jnp.sum(tails_ref[...].astype(F32), axis=0)
        norm = total[:, 0:1] + total[:, 1:2] + total[:, 2:3]
        curve = total[:, 3:4] + total[:, 4:5] + total[:, 5:6]
        length = norm / curve
        second = (var_ref[...] + DIAGONAL) * image + SCALE * sum_ref[...]
        res = rhs - length * image
        res_image = image - length * second
        rows_ref[0:8] = rhs
        rows_ref[8:16] = res
        rows_ref[16:24] = image
        rows_ref[24:32] = res_image
        lane = lax.broadcasted_iota(jnp.int32, (rhs.shape[0], TAIL), 1)
        dots = jnp.zeros((rhs.shape[0], TAIL), F32)
        for place, product in enumerate((res * res, res * res_image, res * image, rhs * res_image)):
            dots = jnp.where(lane == place, jnp.sum(product, axis=1, keepdims=True), dots)
        dots_ref[...] = dots
        step_ref[...] = jnp.where(lane == 0, norm, jnp.where(lane == 1, curve, 0.0))


def order_kernel(rows_ref, perm_ref, out_ref):
    rows = rows_ref[...]
    count, width = rows.shape
    pieces = jnp.concatenate([piece for piece in split_three(rows)], axis=0).astype(BF16)
    perm = perm_ref[...]
    chunk = 256
    for col in range(0, width, chunk):
        total = jnp.zeros((3 * count, chunk), F32)
        for at in range(0, width, chunk):
            index = lax.broadcasted_iota(jnp.int32, (chunk, chunk), 0) + at
            pick = jnp.where(index == perm[:, col : col + chunk], 1.0, 0.0).astype(BF16)
            total += jnp.dot(pieces[:, at : at + chunk], pick, preferred_element_type=F32)
        out_ref[:, col : col + chunk] = total[:count] + total[count : 2 * count] + total[2 * count :]


def swap(value, mask, count):
    return lax.ppermute(value, "row", [(i, i ^ mask) for i in range(count)])


def levels(count, sizes):
    bits = count.bit_length() - 1
    out = []
    sizes = list(sizes)
    while bits:
        take = min(sizes.pop(0) if sizes else 1, bits)
        bits -= take
        out.append([mask << bits for mask in range(1, 1 << take)])
    return out


def tree_sum(value, count):
    for masks in levels(count, [2, 2, 2]):
        others = [swap(value, mask, count) for mask in masks]
        if len(masks) == 3:
            value = (value + others[0]) + (others[1] + others[2])
        else:
            value = value + others[0]
    return value


def gather_levels(count):
    return levels(count, [2] if count <= 16 else [2, 2])


def gather_places(count):
    places = [0]
    for masks in gather_levels(count):
        places = places + [place ^ mask for mask in masks for place in places]
    return places


def tree_gather(value, count):
    blocks, out = value[None], []
    for masks in gather_levels(count):
        blocks = jnp.concatenate([blocks] + [swap(blocks, mask, count) for mask in masks], axis=0)
        out.append(blocks)
    return out


def gate(block, *behind):
    return pl.pallas_call(
        lambda *refs: None,
        in_specs=[pl.BlockSpec(memory_space=pl.ANY)] * (1 + len(behind)),
        out_specs=pl.BlockSpec(memory_space=pl.ANY),
        out_shape=jax.ShapeDtypeStruct(block.shape, block.dtype),
        input_output_aliases={0: 0},
        name="gate",
    )(block, *behind)


def pass_on(value, behind, lists, count):
    rows = value.shape[0]
    *early, (mask,) = gather_levels(count)
    blocks = [value]
    for level, masks in enumerate(early):
        blocks = blocks + [swap(block, other, count) for other in masks for block in blocks]
        if level == 0:
            blocks = blocks[:2] + [gate(block, behind) for block in blocks[2:]]
    blocks[-1] = gate(blocks[-1], lists[-2])
    places = [(block, 0) for block in blocks] + [None] * len(blocks)
    for kinds in ((0, 1), (2,), (3,)):
        group = [index for index in range(len(blocks)) if index % 4 in kinds]
        arrived = swap(jnp.concatenate([blocks[index] for index in group], axis=0), mask, count)
        for at, index in enumerate(group):
            places[len(blocks) + index] = (arrived, at * rows)
    return places


def local(features, right_side, variance, hilbert_order, tile_list):
    width = features.shape[1]
    rhs_count = right_side.shape[0]
    count = lax.axis_size("row")
    most = tile_list.shape[1]
    steps = width // ROWS
    shape = jax.ShapeDtypeStruct
    params = pltpu.CompilerParams(vmem_limit_bytes=10 * 1024 * 1024)
    var_row = variance[None, :]

    whole = lambda *ignored: (0, 0)
    row_spec = pl.BlockSpec(right_side.shape, whole)
    var_spec = pl.BlockSpec(var_row.shape, whole)
    pay_shape = (80, width // 2)
    payload, right = pl.pallas_call(
        payload_kernel,
        out_shape=[shape(pay_shape, BF16), shape((KDIM, width), BF16)],
        compiler_params=params,
        name="payload",
    )(features, right_side)
    any_spec = pl.BlockSpec(memory_space=pl.ANY)
    blocks = own_blocks(width // ROWS)
    coupled = tile_list[:, :, 1]
    list_spec = pl.BlockSpec(coupled.shape, whole)
    own_tiles, own_sum, coupled = pl.pallas_call(
        own_kernel,
        in_specs=[pl.BlockSpec(payload.shape, whole), pl.BlockSpec(right.shape, whole), list_spec],
        out_specs=[any_spec, row_spec, list_spec],
        out_shape=[
            pltpu.HBM((len(blocks), ROWS, ROWS), BF16),
            shape(right_side.shape, F32),
            shape(coupled.shape, jnp.int32),
        ],
        scratch_shapes=[
            pltpu.VMEM((width, KDIM), BF16),
            pltpu.VMEM((rhs_count, width), BF16),
            pltpu.VMEM((len(blocks), ROWS, ROWS), BF16),
            pltpu.SemaphoreType.DMA((len(blocks),)),
        ],
        compiler_params=params,
        cost_estimate=pl.CostEstimate(
            flops=9_000_000_000, bytes_accessed=2 * len(blocks) * ROWS * ROWS, transcendentals=0
        ),
        name="own_tile",
    )(payload, right, coupled)
    lists = tree_gather(coupled[0], count)
    places = pass_on(payload, own_sum, lists, count)
    arrays = list({id(array): array for array, _ in places}.values())
    block_at = [([id(array) for array in arrays].index(id(array)), row) for array, row in places]
    me = jnp.full((1,), lax.axis_index("row"), jnp.int32)

    def front_at(k, i, *ignored):
        return (jnp.minimum(k, FRONT - 1), jnp.where(k < FRONT, i, steps - 1), 0)

    def back_at(k, i, *ignored):
        return (jnp.maximum(k - FRONT, 0), jnp.where(k < FRONT, 0, i), 0)

    tile_specs = [pl.BlockSpec((1, ROWS, width), front_at), pl.BlockSpec((1, ROWS, width), back_at)]
    send_shape = (rhs_count, width + TAIL)
    front_tiles, back_tiles, image, send, slots = pl.pallas_call(
        functools.partial(pair_kernel, block_at),
        grid_spec=pltpu.PrefetchScalarGridSpec(
            num_scalar_prefetch=2,
            grid=(most, steps),
            in_specs=[
                pl.BlockSpec(right.shape, whole),
                row_spec,
                var_spec,
            ]
            + [row_spec]
            + [any_spec] * len(arrays),
            out_specs=tile_specs
            + [
                row_spec,
                pl.BlockSpec(send_shape, whole),
                pl.BlockSpec(memory_space=pltpu.SMEM),
            ],
            scratch_shapes=[pltpu.VMEM((width, KDIM), BF16), pltpu.VMEM((rhs_count, width), BF16)]
            + [pltpu.VMEM((2,) + payload.shape, BF16), pltpu.SemaphoreType.DMA((2,))],
        ),
        out_shape=[
            pltpu.VMEM((FRONT, width, width), BF16),
            pltpu.HBM((most - FRONT, width, width), BF16),
            shape(right_side.shape, F32),
            shape(send_shape, BF16),
            shape((most + 2,), jnp.int32),
        ],
        compiler_params=params,
        name="pair_tiles",
    )(lists[-1], me, right, right_side, var_row, own_sum, *arrays)
    front_tiles = pltpu.with_memory_space_constraint(front_tiles, pltpu.VMEM)
    back_tiles = pltpu.with_memory_space_constraint(back_tiles, pltpu.HBM)

    every_send = tree_gather(send, count)[-1]
    own_again = []
    part = -(-len(blocks) // PARTS)
    for first in range(0, len(blocks), part):
        here = blocks[first : first + part]
        own_again.append(
            pl.pallas_call(
                functools.partial(own_again_kernel, first, here),
                in_specs=[any_spec, pl.BlockSpec(send_shape, whole)],
                out_specs=row_spec,
                out_shape=shape(right_side.shape, F32),
                scratch_shapes=[
                    pltpu.VMEM((len(here), ROWS, ROWS), BF16),
                    pltpu.SemaphoreType.DMA((len(here),)),
                ],
                compiler_params=params,
                cost_estimate=pl.CostEstimate(
                    flops=5_000_000_000, bytes_accessed=2 * len(here) * ROWS * ROWS, transcendentals=0
                ),
                name=f"own_again_{first}",
            )(pltpu.with_memory_space_constraint(own_tiles, pltpu.HBM), send)
        )
    dots_spec = pl.BlockSpec((rhs_count, TAIL), whole)
    rows, dots, steps_one = pl.pallas_call(
        again_kernel,
        grid_spec=pltpu.PrefetchScalarGridSpec(
            num_scalar_prefetch=1,
            grid=(most, steps),
            in_specs=[
                tile_specs[0],
                any_spec,
                pl.BlockSpec((1,) + send_shape, lambda k, i, s: (s[1 + k], 0, 0)),
                pl.BlockSpec((count, rhs_count, TAIL), lambda k, i, s: (0, 0, width // TAIL)),
                row_spec,
                var_spec,
                row_spec,
            ]
            + [row_spec] * PARTS,
            out_specs=[
                pl.BlockSpec((4 * rhs_count, width), whole),
                dots_spec,
                dots_spec,
            ],
            scratch_shapes=[
                pltpu.VMEM(right_side.shape, F32),
                pltpu.VMEM((HELD, ROWS, width), BF16),
                pltpu.SemaphoreType.DMA((HELD,)),
            ],
        ),
        out_shape=[
            shape((4 * rhs_count, width), F32),
            shape((rhs_count, TAIL), F32),
            shape((rhs_count, TAIL), F32),
        ],
        compiler_params=params,
        name="pair_again",
    )(slots, front_tiles, back_tiles, every_send, every_send, right_side, var_row, image, *own_again)

    dots = tree_sum(dots, count)
    ordered = pl.pallas_call(
        order_kernel,
        out_shape=shape(rows.shape, F32),
        compiler_params=params,
        name="curve_order",
    )(rows, hilbert_order)
    norm, curve = steps_one[:, 0:1], steps_one[:, 1:2]
    length = norm / curve
    norm_next = dots[:, 0:1]
    ratio = norm_next / norm
    curve_next = dots[:, 1:2] + ratio * (dots[:, 2:3] + dots[:, 3:4]) + ratio * ratio * curve
    length_next = norm_next / curve_next
    rhs_o, res_o, image_o, res_image_o = [ordered[at : at + 8] for at in range(0, 32, 8)]
    solved = length * rhs_o + length_next * (res_o + ratio * rhs_o)
    residual = res_o - length_next * (res_image_o + ratio * image_o)
    return (solved, residual)


def solution(mesh):
    in_specs = (
        P(None, ("group", "row")),
        P(None, ("group", "row")),
        P(("group", "row")),
        P(("group", "row"), None),
        P(("group", "row"), None, None),
    )
    out_specs = (P(None, ("group", "row")), P(None, ("group", "row")))
    return jax.shard_map(local, mesh=mesh, in_specs=in_specs, out_specs=out_specs, check_vma=False)
```

```python
import functools

import jax
import jax.numpy as jnp
import numpy as np
from jax import lax
from jax.experimental import pallas as pl
from jax.experimental.pallas import tpu as pltpu
from jax.sharding import PartitionSpec as P

SHRINK = 0.95
GRAM = SHRINK * SHRINK
SCALE = 20.0 * (20.0 / 19.0) ** 19
DIAGONAL = float(1.0 - SCALE * float(np.float32(1.0 / SCALE).astype(jnp.bfloat16)))
KDIM = 128
ROWS = 512
PARTS = 2
COLS = 512
SUB = 64
FRONT = 3
HELD = 4
TAIL = 128
BF16 = jnp.bfloat16
F32 = jnp.float32
CONTRACT_LANES = (((1,), (1,)), ((), ()))


def split_three(value):
    high = value.astype(BF16).astype(F32)
    rest = value - high
    middle = rest.astype(BF16).astype(F32)
    return high, middle, rest - middle


def norm_rows(norm, first):
    high, middle, low = split_three(norm)
    row = lax.broadcasted_iota(jnp.int32, (32, norm.shape[1]), 0)
    out = jnp.where(row < 6, 1.0, 0.0)
    out = jnp.where(row == first, high, out)
    out = jnp.where(row == first + 1, middle, out)
    return jnp.where(row == first + 2, low, out).astype(BF16)


def own_factor(feat):
    wide = feat.astype(F32)
    norm = jnp.sum(wide * wide, axis=0, keepdims=True) * GRAM
    pieces = split_three(wide * (-2.0 * GRAM))
    return jnp.concatenate([piece.astype(BF16) for piece in pieces] + [norm_rows(norm, 0)], axis=0)


def other_factor(feat):
    wide = feat.astype(F32)
    norm = jnp.sum(wide * wide, axis=0, keepdims=True) * GRAM
    return jnp.transpose(jnp.concatenate([feat, feat, feat, norm_rows(norm, 3)], axis=0))


def psi_power(dist):
    dist = jnp.maximum(dist, 1e-30)
    radius = dist * lax.rsqrt(dist)
    u = jnp.maximum(SHRINK - radius, 1e-30)
    return (jnp.exp2(19.0 * lax.log2(u)) * (1.0 - u)).astype(BF16)


def tile_unit(left, right, vec, tile_ref):
    dist = jnp.dot(left, right, preferred_element_type=F32)
    parts = []
    for sub in range(0, left.shape[0], SUB):
        part = psi_power(dist[sub : sub + SUB])
        tile_ref[sub : sub + SUB, :] = part
        parts.append(part)
    return jnp.dot(vec, jnp.concatenate(parts, axis=0), preferred_element_type=F32)


def unpack(pay):
    return jnp.concatenate([pay[:32], pay[32:64]], axis=1), jnp.concatenate([pay[64:72], pay[72:80]], axis=1)


def own_blocks(count):
    return [(row, col) for row in range(count) for col in range(row, count)]


def own_kernel(
    feat_ref, rhs_ref, right_ref, out_ref, sum_ref, left_ref, vec_ref, tile_ref, sem_ref
):
    feat = feat_ref[...]
    left_ref[...] = other_factor(feat)
    vec_ref[...] = rhs_ref[...].astype(BF16)
    sum_ref[...] = jnp.zeros_like(sum_ref)
    count = feat.shape[1] // ROWS
    piece = lambda index: pl.ds(pl.multiple_of(index * ROWS, ROWS), ROWS)
    save = lambda at: pltpu.make_async_copy(tile_ref.at[at], out_ref.at[at], sem_ref.at[at])

    def row_step(row, at):
        def col_step(col, at):
            sum_ref[:, piece(col)] += tile_unit(
                left_ref[piece(row), :], right_ref[:, piece(col)], vec_ref[:, piece(row)],
                tile_ref.at[at],
            )
            save(at).start()

            @pl.when(row != col)
            def _():
                sum_ref[:, piece(row)] += lax.dot_general(
                    vec_ref[:, piece(col)], tile_ref[at], CONTRACT_LANES,
                    preferred_element_type=F32,
                )

            return at + 1

        return lax.fori_loop(row, count, col_step, at)

    lax.fori_loop(0, count, row_step, 0)
    for at in range(tile_ref.shape[0]):
        save(at).wait()


def own_again_kernel(first, blocks, in_ref, vec_ref, sum_ref, tile_ref, sem_ref):
    load = lambda index: pltpu.make_async_copy(
        in_ref.at[first + index], tile_ref.at[index], sem_ref.at[index]
    )
    for index in range(len(blocks)):
        load(index).start()
    sum_ref[...] = jnp.zeros_like(sum_ref)
    piece = lambda index: slice(index * ROWS, (index + 1) * ROWS)
    for index, (row, col) in enumerate(blocks):
        load(index).wait()
        sum_ref[:, piece(col)] += jnp.dot(
            vec_ref[:, piece(row)], tile_ref[index], preferred_element_type=F32
        )
        if row != col:
            sum_ref[:, piece(row)] += lax.dot_general(
                vec_ref[:, piece(col)], tile_ref[index], CONTRACT_LANES, preferred_element_type=F32
            )


def payload_kernel(feat_ref, rhs_ref, pay_zero_ref, pay_one_ref, right_ref):
    feat = feat_ref[...]
    rounded = rhs_ref[...].astype(BF16)
    quarter = feat.shape[1] // 4
    for half, pay_ref in enumerate((pay_zero_ref, pay_one_ref)):
        first, second = [slice(at * quarter, (at + 1) * quarter) for at in (2 * half, 2 * half + 1)]
        pay_ref[:32] = feat[:, first]
        pay_ref[32:64] = feat[:, second]
        pay_ref[64:80] = jnp.concatenate([rounded[:, first], rounded[:, second]], axis=0)
    right_ref[...] = own_factor(feat)


def find_partners(lists_ref, me, slots_ref):
    count, most = lists_ref.shape
    for at in range(slots_ref.shape[0]):
        slots_ref[at] = 0
    total = jnp.int32(0)
    for at, place in enumerate(gather_places(count)):
        if at == 0:
            continue
        number = me ^ place
        hit = jnp.bool_(False)
        for entry in range(most):
            hit = hit | (lists_ref[at, entry] == me) | (lists_ref[0, entry] == number)
        slots_ref[1 + total] = jnp.where(hit, at, 0)
        slots_ref[most + 2 + total] = jnp.where(hit, number, 0)
        total = total + hit.astype(jnp.int32)
    slots_ref[0] = total


def half_tiles(slots_ref, right_ref, every_ref, front_ref, back_ref, sum_ref, left_ref, vec_ref, pay_ref, sem_ref):
    slot, step = pl.program_id(0), pl.program_id(1)
    numbers = pl.num_programs(0) + 2

    def fetch(which):
        return pltpu.make_async_copy(
            every_ref.at[slots_ref[numbers + which]], pay_ref.at[which % 2], sem_ref.at[which % 2]
        )

    @pl.when((slot == 0) & (step == 0) & (slots_ref[0] > 0))
    def _():
        fetch(0).start()

    @pl.when(slot < slots_ref[0])
    def _():
        @pl.when(step == 0)
        def _():
            fetch(slot).wait()

            @pl.when(slot + 1 < slots_ref[0])
            def _():
                fetch(slot + 1).start()

            feat, vec = unpack(pay_ref[slot % 2])
            left_ref[...] = other_factor(feat)
            vec_ref[...] = vec

        rows = pl.ds(pl.multiple_of(step * ROWS, ROWS), ROWS)
        left, vec = left_ref[rows, :], vec_ref[:, rows]
        for tile_ref, here in ((front_ref, slot < FRONT), (back_ref, slot >= FRONT)):
            @pl.when(here)
            def _():
                def unit(index, carry):
                    cols = pl.ds(pl.multiple_of(index * COLS, COLS), COLS)
                    sum_ref[:, cols] += tile_unit(
                        left, right_ref[:, cols], vec, tile_ref.at[0, :, cols]
                    )
                    return carry

                lax.fori_loop(0, right_ref.shape[1] // COLS, unit, 0)


def pair_zero_kernel(
    lists_ref, me_ref, right_ref, first_ref, every_ref, front_ref, back_ref, sum_ref, slots_ref, *refs
):
    @pl.when((pl.program_id(0) == 0) & (pl.program_id(1) == 0))
    def _():
        find_partners(lists_ref, me_ref[0], slots_ref)
        sum_ref[...] = first_ref[...]

    half_tiles(slots_ref, right_ref, every_ref, front_ref, back_ref, sum_ref, *refs)


def pair_one_kernel(
    slots_ref, right_ref, first_ref, every_ref, rhs_ref, var_ref,
    front_ref, back_ref, image_ref, send_ref, *refs
):
    slot, step = pl.program_id(0), pl.program_id(1)

    @pl.when((slot == 0) & (step == 0))
    def _():
        image_ref[...] = first_ref[...]

    half_tiles(slots_ref, right_ref, every_ref, front_ref, back_ref, image_ref, *refs)

    @pl.when((slot == pl.num_programs(0) - 1) & (step == pl.num_programs(1) - 1))
    def _():
        rhs = rhs_ref[...]
        width = rhs.shape[1]
        image = (var_ref[...] + DIAGONAL) * rhs + SCALE * image_ref[...]
        image_ref[...] = image
        send_ref[:, :width] = image.astype(BF16)
        pieces = split_three(jnp.sum(rhs * rhs, axis=1, keepdims=True))
        pieces += split_three(jnp.sum(rhs * image, axis=1, keepdims=True))
        lane = lax.broadcasted_iota(jnp.int32, (rhs.shape[0], TAIL), 1)
        tail = jnp.zeros((rhs.shape[0], TAIL), F32)
        for place, piece in enumerate(pieces):
            tail = jnp.where(lane == place, piece, tail)
        send_ref[:, width:] = tail.astype(BF16)


def again_kernel(
    slots_ref, front_zero_ref, front_one_ref, back_zero_ref, back_one_ref,
    vec_ref, tails_ref, rhs_ref, var_ref, image_ref, *refs
):
    first_refs = refs[:PARTS]
    rows_ref, dots_ref, step_ref, sum_ref, held_ref, sem_ref = refs[PARTS:]
    slot, step = pl.program_id(0), pl.program_id(1)
    width = rhs_ref.shape[1]
    steps = width // ROWS
    half = steps // 2
    parts = (slots_ref[0] - FRONT) * steps

    def fetch(part, back_ref, first):
        at = pl.ds(pl.multiple_of((part % steps - first) * ROWS, ROWS), ROWS)
        return pltpu.make_async_copy(
            back_ref.at[part // steps, at], held_ref.at[part % HELD], sem_ref.at[part % HELD]
        )

    def start(part):
        @pl.when((part < parts) & (part % steps < half))
        def _():
            fetch(part, back_zero_ref, 0).start()

        @pl.when((part < parts) & (part % steps >= half))
        def _():
            fetch(part, back_one_ref, half).start()

    @pl.when((slot == 0) & (step == 0))
    def _():
        sum_ref[...] = functools.reduce(jnp.add, [first_ref[...] for first_ref in first_refs])
        for part in range(HELD):
            start(part)

    @pl.when(slot < slots_ref[0])
    def _():
        at = pl.multiple_of(step * ROWS, ROWS)
        for front_ref, here in ((front_zero_ref, step < half), (front_one_ref, step >= half)):
            @pl.when((slot < FRONT) & here)
            def _():
                sum_ref[...] += jnp.dot(
                    vec_ref[0, :, pl.ds(at, ROWS)], front_ref[0], preferred_element_type=F32
                )

        @pl.when(slot >= FRONT)
        def _():
            part = (slot - FRONT) * steps + step
            fetch(part % HELD, back_zero_ref, part % HELD // half * half).wait()
            sum_ref[...] += jnp.dot(
                vec_ref[0, :, pl.ds(at, ROWS)], held_ref[part % HELD], preferred_element_type=F32
            )
            start(part + HELD)

    @pl.when((slot == pl.num_programs(0) - 1) & (step == pl.num_programs(1) - 1))
    def _():
        rhs = rhs_ref[...]
        image = image_ref[...]
        total = jnp.sum(tails_ref[...].astype(F32), axis=0)
        norm = total[:, 0:1] + total[:, 1:2] + total[:, 2:3]
        curve = total[:, 3:4] + total[:, 4:5] + total[:, 5:6]
        length = norm / curve
        second = (var_ref[...] + DIAGONAL) * image + SCALE * sum_ref[...]
        res = rhs - length * image
        res_image = image - length * second
        rows_ref[0:8] = rhs
        rows_ref[8:16] = res
        rows_ref[16:24] = image
        rows_ref[24:32] = res_image
        lane = lax.broadcasted_iota(jnp.int32, (rhs.shape[0], TAIL), 1)
        dots = jnp.zeros((rhs.shape[0], TAIL), F32)
        for place, product in enumerate((res * res, res * res_image, res * image, rhs * res_image)):
            dots = jnp.where(lane == place, jnp.sum(product, axis=1, keepdims=True), dots)
        dots_ref[...] = dots
        step_ref[...] = jnp.where(lane == 0, norm, jnp.where(lane == 1, curve, 0.0))


def order_kernel(rows_ref, perm_ref, out_ref):
    rows = rows_ref[...]
    count, width = rows.shape
    pieces = jnp.concatenate([piece for piece in split_three(rows)], axis=0).astype(BF16)
    perm = perm_ref[...]
    chunk = 256
    for col in range(0, width, chunk):
        total = jnp.zeros((3 * count, chunk), F32)
        for at in range(0, width, chunk):
            index = lax.broadcasted_iota(jnp.int32, (chunk, chunk), 0) + at
            pick = jnp.where(index == perm[:, col : col + chunk], 1.0, 0.0).astype(BF16)
            total += jnp.dot(pieces[:, at : at + chunk], pick, preferred_element_type=F32)
        out_ref[:, col : col + chunk] = total[:count] + total[count : 2 * count] + total[2 * count :]


def swap(value, mask, count):
    return lax.ppermute(value, "row", [(i, i ^ mask) for i in range(count)])


def levels(count, sizes):
    bits = count.bit_length() - 1
    out = []
    sizes = list(sizes)
    while bits:
        take = min(sizes.pop(0) if sizes else 1, bits)
        bits -= take
        out.append([mask << bits for mask in range(1, 1 << take)])
    return out


def tree_sum(value, count):
    for masks in levels(count, [2, 2, 2]):
        others = [swap(value, mask, count) for mask in masks]
        if len(masks) == 3:
            value = (value + others[0]) + (others[1] + others[2])
        else:
            value = value + others[0]
    return value


def gather_levels(count):
    return levels(count, [2] if count <= 16 else [2, 2])


def gather_places(count):
    places = [0]
    for masks in gather_levels(count):
        places = places + [place ^ mask for mask in masks for place in places]
    return places


def tree_gather(value, count):
    blocks, out = value[None], []
    for masks in gather_levels(count):
        blocks = jnp.concatenate([blocks] + [swap(blocks, mask, count) for mask in masks], axis=0)
        out.append(blocks)
    return out


def local(features, right_side, variance, hilbert_order, tile_list):
    width = features.shape[1]
    rhs_count = right_side.shape[0]
    count = lax.axis_size("row")
    most = tile_list.shape[1]
    steps = width // ROWS
    shape = jax.ShapeDtypeStruct
    params = pltpu.CompilerParams(vmem_limit_bytes=10 * 1024 * 1024)
    var_row = variance[None, :]

    whole = lambda *ignored: (0, 0)
    row_spec = pl.BlockSpec(right_side.shape, whole)
    var_spec = pl.BlockSpec(var_row.shape, whole)
    pay_shape = (80, width // 4)
    pay_zero, pay_one, right = pl.pallas_call(
        payload_kernel,
        out_shape=[shape(pay_shape, BF16), shape(pay_shape, BF16), shape((KDIM, width), BF16)],
        compiler_params=params,
        name="payload",
    )(features, right_side)
    in_hbm = lambda array: pltpu.with_memory_space_constraint(array, pltpu.HBM)
    every_zero = in_hbm(lax.all_gather(pay_zero, "row", axis=0))
    every_one = in_hbm(lax.all_gather(pay_one, "row", axis=0))
    lists = tree_gather(tile_list[0, :, 1], count)
    me = jnp.full((1,), lax.axis_index("row"), jnp.int32)
    any_spec = pl.BlockSpec(memory_space=pl.ANY)
    blocks = own_blocks(width // ROWS)
    own_tiles, own_sum = pl.pallas_call(
        own_kernel,
        out_specs=[any_spec, pl.BlockSpec(memory_space=pltpu.VMEM)],
        out_shape=[pltpu.HBM((len(blocks), ROWS, ROWS), BF16), shape(right_side.shape, F32)],
        scratch_shapes=[
            pltpu.VMEM((width, KDIM), BF16),
            pltpu.VMEM((rhs_count, width), BF16),
            pltpu.VMEM((len(blocks), ROWS, ROWS), BF16),
            pltpu.SemaphoreType.DMA((len(blocks),)),
        ],
        compiler_params=params,
        cost_estimate=pl.CostEstimate(
            flops=9_000_000_000, bytes_accessed=2 * len(blocks) * ROWS * ROWS, transcendentals=0
        ),
        name="own_tile",
    )(features, right_side, right)

    half = steps // 2

    def front_at(k, i, *ignored):
        return (jnp.minimum(k, FRONT - 1), jnp.where(k < FRONT, i, half - 1), 0)

    def back_at(k, i, *ignored):
        return (jnp.maximum(k - FRONT, 0), jnp.where(k < FRONT, 0, i), 0)

    half_specs = [pl.BlockSpec((1, ROWS, width), front_at), pl.BlockSpec((1, ROWS, width), back_at)]
    half_shapes = [
        pltpu.VMEM((FRONT, width // 2, width), BF16),
        pltpu.HBM((most - FRONT, width // 2, width), BF16),
    ]
    half_scratch = [
        pltpu.VMEM((width // 2, KDIM), BF16),
        pltpu.VMEM((rhs_count, width // 2), BF16),
        pltpu.VMEM((2,) + pay_shape, BF16),
        pltpu.SemaphoreType.DMA((2,)),
    ]
    right_spec = pl.BlockSpec(right.shape, whole)
    send_shape = (rhs_count, width + TAIL)
    front_zero, back_zero, half_sum, slots = pl.pallas_call(
        pair_zero_kernel,
        grid_spec=pltpu.PrefetchScalarGridSpec(
            num_scalar_prefetch=2,
            grid=(most, half),
            in_specs=[right_spec, row_spec, any_spec],
            out_specs=half_specs + [row_spec, pl.BlockSpec(memory_space=pltpu.SMEM)],
            scratch_shapes=half_scratch,
        ),
        out_shape=half_shapes
        + [shape(right_side.shape, F32), shape((2 * (most + 2),), jnp.int32)],
        compiler_params=params,
        name="pair_zero",
    )(lists[-1], me, right, own_sum, every_zero)
    front_one, back_one, image, send = pl.pallas_call(
        pair_one_kernel,
        grid_spec=pltpu.PrefetchScalarGridSpec(
            num_scalar_prefetch=1,
            grid=(most, half),
            in_specs=[right_spec, row_spec, any_spec, row_spec, var_spec],
            out_specs=half_specs + [row_spec, pl.BlockSpec(send_shape, whole)],
            scratch_shapes=half_scratch,
        ),
        out_shape=half_shapes + [shape(right_side.shape, F32), shape(send_shape, BF16)],
        compiler_params=params,
        name="pair_one",
    )(slots, right, half_sum, every_one, right_side, var_row)
    fronts = [pltpu.with_memory_space_constraint(part, pltpu.VMEM) for part in (front_zero, front_one)]
    backs = [pltpu.with_memory_space_constraint(part, pltpu.HBM) for part in (back_zero, back_one)]

    def front_zero_at(k, i, *ignored):
        return (jnp.minimum(k, FRONT - 1), jnp.where(k < FRONT, jnp.minimum(i, half - 1), half - 1), 0)

    def front_one_at(k, i, *ignored):
        return (jnp.minimum(k, FRONT - 1), jnp.where(k < FRONT, jnp.maximum(i - half, 0), half - 1), 0)

    every_send = tree_gather(send, count)[-1]
    own_again = []
    part = -(-len(blocks) // PARTS)
    for first in range(0, len(blocks), part):
        here = blocks[first : first + part]
        own_again.append(
            pl.pallas_call(
                functools.partial(own_again_kernel, first, here),
                in_specs=[any_spec, pl.BlockSpec(send_shape, whole)],
                out_specs=row_spec,
                out_shape=shape(right_side.shape, F32),
                scratch_shapes=[
                    pltpu.VMEM((len(here), ROWS, ROWS), BF16),
                    pltpu.SemaphoreType.DMA((len(here),)),
                ],
                compiler_params=params,
                cost_estimate=pl.CostEstimate(
                    flops=5_000_000_000, bytes_accessed=2 * len(here) * ROWS * ROWS, transcendentals=0
                ),
                name=f"own_again_{first}",
            )(pltpu.with_memory_space_constraint(own_tiles, pltpu.HBM), send)
        )
    dots_spec = pl.BlockSpec((rhs_count, TAIL), whole)
    rows, dots, steps_one = pl.pallas_call(
        again_kernel,
        grid_spec=pltpu.PrefetchScalarGridSpec(
            num_scalar_prefetch=1,
            grid=(most, steps),
            in_specs=[
                pl.BlockSpec((1, ROWS, width), front_zero_at),
                pl.BlockSpec((1, ROWS, width), front_one_at),
                any_spec,
                any_spec,
                pl.BlockSpec((1,) + send_shape, lambda k, i, s: (s[1 + k], 0, 0)),
                pl.BlockSpec((count, rhs_count, TAIL), lambda k, i, s: (0, 0, width // TAIL)),
                row_spec,
                var_spec,
                row_spec,
            ]
            + [row_spec] * PARTS,
            out_specs=[
                pl.BlockSpec((4 * rhs_count, width), whole),
                dots_spec,
                dots_spec,
            ],
            scratch_shapes=[
                pltpu.VMEM(right_side.shape, F32),
                pltpu.VMEM((HELD, ROWS, width), BF16),
                pltpu.SemaphoreType.DMA((HELD,)),
            ],
        ),
        out_shape=[
            shape((4 * rhs_count, width), F32),
            shape((rhs_count, TAIL), F32),
            shape((rhs_count, TAIL), F32),
        ],
        compiler_params=params,
        name="pair_again",
    )(slots, *fronts, *backs, every_send, every_send, right_side, var_row, image, *own_again)

    dots = tree_sum(dots, count)
    ordered = pl.pallas_call(
        order_kernel,
        out_shape=shape(rows.shape, F32),
        compiler_params=params,
        name="curve_order",
    )(rows, hilbert_order)
    norm, curve = steps_one[:, 0:1], steps_one[:, 1:2]
    length = norm / curve
    norm_next = dots[:, 0:1]
    ratio = norm_next / norm
    curve_next = dots[:, 1:2] + ratio * (dots[:, 2:3] + dots[:, 3:4]) + ratio * ratio * curve
    length_next = norm_next / curve_next
    rhs_o, res_o, image_o, res_image_o = [ordered[at : at + 8] for at in range(0, 32, 8)]
    solved = length * rhs_o + length_next * (res_o + ratio * rhs_o)
    residual = res_o - length_next * (res_image_o + ratio * image_o)
    return (solved, residual)


def solution(mesh):
    in_specs = (
        P(None, ("group", "row")),
        P(None, ("group", "row")),
        P(("group", "row")),
        P(("group", "row"), None),
        P(("group", "row"), None, None),
    )
    out_specs = (P(None, ("group", "row")), P(None, ("group", "row")))
    return jax.shard_map(local, mesh=mesh, in_specs=in_specs, out_specs=out_specs, check_vma=False)
```

```python
import functools

import jax
import jax.numpy as jnp
import numpy as np
from jax import lax
from jax.experimental import pallas as pl
from jax.experimental.pallas import tpu as pltpu
from jax.sharding import PartitionSpec as P

SHRINK = 0.95
GRAM = SHRINK * SHRINK
SCALE = 20.0 * (20.0 / 19.0) ** 19
DIAGONAL = float(1.0 - SCALE * float(np.float32(1.0 / SCALE).astype(jnp.bfloat16)))
KDIM = 128
ROWS = 512
PARTS = 2
COLS = 512
SUB = 64
FRONT = 3
HELD = 4
TAIL = 128
BF16 = jnp.bfloat16
F32 = jnp.float32
CONTRACT_LANES = (((1,), (1,)), ((), ()))


def split_three(value):
    high = value.astype(BF16).astype(F32)
    rest = value - high
    middle = rest.astype(BF16).astype(F32)
    return high, middle, rest - middle


def norm_rows(norm, first):
    high, middle, low = split_three(norm)
    row = lax.broadcasted_iota(jnp.int32, (32, norm.shape[1]), 0)
    out = jnp.where(row < 6, 1.0, 0.0)
    out = jnp.where(row == first, high, out)
    out = jnp.where(row == first + 1, middle, out)
    return jnp.where(row == first + 2, low, out).astype(BF16)


def own_factor(feat):
    wide = feat.astype(F32)
    norm = jnp.sum(wide * wide, axis=0, keepdims=True) * GRAM
    pieces = split_three(wide * (-2.0 * GRAM))
    return jnp.concatenate([piece.astype(BF16) for piece in pieces] + [norm_rows(norm, 0)], axis=0)


def other_factor(feat):
    wide = feat.astype(F32)
    norm = jnp.sum(wide * wide, axis=0, keepdims=True) * GRAM
    return jnp.transpose(jnp.concatenate([feat, feat, feat, norm_rows(norm, 3)], axis=0))


def psi_power(dist):
    dist = jnp.maximum(dist, 1e-30)
    radius = dist * lax.rsqrt(dist)
    u = jnp.maximum(SHRINK - radius, 1e-30)
    return (jnp.exp2(19.0 * lax.log2(u)) * (1.0 - u)).astype(BF16)


def tile_unit(left, right, vec, tile_ref):
    dist = jnp.dot(left, right, preferred_element_type=F32)
    parts = []
    for sub in range(0, left.shape[0], SUB):
        part = psi_power(dist[sub : sub + SUB])
        tile_ref[sub : sub + SUB, :] = part
        parts.append(part)
    return jnp.dot(vec, jnp.concatenate(parts, axis=0), preferred_element_type=F32)


def unpack(pay):
    return jnp.concatenate([pay[:32], pay[32:64]], axis=1), jnp.concatenate([pay[64:72], pay[72:80]], axis=1)


def own_blocks(rows, count):
    return [(row, col) for row in rows for col in range(row, count)]


def own_kernel(
    rows, feat_ref, rhs_ref, right_ref, arrived_ref, out_ref, sum_ref,
    left_ref, vec_ref, tile_ref, sem_ref,
):
    feat = feat_ref[...]
    left_ref[...] = other_factor(feat)
    vec_ref[...] = rhs_ref[...].astype(BF16)
    sum_ref[...] = jnp.zeros_like(sum_ref)
    count = feat.shape[1] // ROWS
    piece = lambda index: pl.ds(pl.multiple_of(index * ROWS, ROWS), ROWS)
    save = lambda at: pltpu.make_async_copy(tile_ref.at[at], out_ref.at[at], sem_ref.at[at])

    def row_step(row, at):
        def col_step(col, at):
            sum_ref[:, piece(col)] += tile_unit(
                left_ref[piece(row), :], right_ref[:, piece(col)], vec_ref[:, piece(row)],
                tile_ref.at[at],
            )
            save(at).start()

            @pl.when(row != col)
            def _():
                sum_ref[:, piece(row)] += lax.dot_general(
                    vec_ref[:, piece(col)], tile_ref[at], CONTRACT_LANES,
                    preferred_element_type=F32,
                )

            return at + 1

        return lax.fori_loop(row, count, col_step, at)

    lax.fori_loop(rows[0], rows[-1] + 1, row_step, 0)
    for at in range(tile_ref.shape[0]):
        save(at).wait()


def own_again_kernel(blocks, in_ref, vec_ref, sum_ref, tile_ref, sem_ref):
    load = lambda index: pltpu.make_async_copy(
        in_ref.at[index], tile_ref.at[index], sem_ref.at[index]
    )
    for index in range(len(blocks)):
        load(index).start()
    sum_ref[...] = jnp.zeros_like(sum_ref)
    piece = lambda index: slice(index * ROWS, (index + 1) * ROWS)
    for index, (row, col) in enumerate(blocks):
        load(index).wait()
        sum_ref[:, piece(col)] += jnp.dot(
            vec_ref[:, piece(row)], tile_ref[index], preferred_element_type=F32
        )
        if row != col:
            sum_ref[:, piece(row)] += lax.dot_general(
                vec_ref[:, piece(col)], tile_ref[index], CONTRACT_LANES, preferred_element_type=F32
            )


def payload_kernel(list_ref, feat_ref, rhs_ref, pay_zero_ref, pay_one_ref, right_ref):
    feat = feat_ref[...]
    rounded = rhs_ref[...].astype(BF16)
    quarter = feat.shape[1] // 4
    for half, pay_ref in enumerate((pay_zero_ref, pay_one_ref)):
        first, second = [slice(at * quarter, (at + 1) * quarter) for at in (2 * half, 2 * half + 1)]
        pay_ref[:32] = feat[:, first]
        pay_ref[32:64] = feat[:, second]
        pay_ref[64:80] = jnp.concatenate([rounded[:, first], rounded[:, second]], axis=0)
    lane = lax.broadcasted_iota(jnp.int32, (16, quarter), 1)
    numbers = jnp.full(lane.shape, -1, jnp.int32)
    for entry in range(list_ref.shape[1]):
        numbers = jnp.where(lane == entry, list_ref[0, entry, 1], numbers)
    pay_zero_ref[80:96] = numbers.astype(F32).astype(BF16)
    right_ref[...] = own_factor(feat)


def find_partners(lists_ref, me, slots_ref):
    count, most = lists_ref.shape[0], slots_ref.shape[0] // 2 - 2
    for at in range(slots_ref.shape[0]):
        slots_ref[at] = 0
    total = jnp.int32(0)
    for at, place in enumerate(gather_places(count)):
        if at == 0:
            continue
        number = me ^ place
        hit = jnp.bool_(False)
        for entry in range(most):
            hit = hit | (lists_ref[at, entry] == me) | (lists_ref[0, entry] == number)
        slots_ref[1 + total] = jnp.where(hit, at, 0)
        slots_ref[most + 2 + total] = jnp.where(hit, number, 0)
        total = total + hit.astype(jnp.int32)
    slots_ref[0] = total


def half_tiles(slots_ref, right_ref, fetch, front_ref, back_ref, sum_ref, left_ref, vec_ref, pay_ref, sem_ref):
    slot, step = pl.program_id(0), pl.program_id(1)

    @pl.when((slot == 0) & (step == 0) & (slots_ref[0] > 0))
    def _():
        fetch(0)

    @pl.when(slot < slots_ref[0])
    def _():
        @pl.when(step == 0)
        def _():
            pltpu.make_async_copy(
                pay_ref.at[(slot + 1) % 2], pay_ref.at[slot % 2], sem_ref.at[slot % 2]
            ).wait()

            @pl.when(slot + 1 < slots_ref[0])
            def _():
                fetch(slot + 1)

            feat, vec = unpack(pay_ref[slot % 2])
            left_ref[...] = other_factor(feat)
            vec_ref[...] = vec

        rows = pl.ds(pl.multiple_of(step * ROWS, ROWS), ROWS)
        left, vec = left_ref[rows, :], vec_ref[:, rows]
        for tile_ref, here in ((front_ref, slot < FRONT), (back_ref, slot >= FRONT)):
            @pl.when(here)
            def _():
                def unit(index, carry):
                    cols = pl.ds(pl.multiple_of(index * COLS, COLS), COLS)
                    sum_ref[:, cols] += tile_unit(
                        left, right_ref[:, cols], vec, tile_ref.at[0, :, cols]
                    )
                    return carry

                lax.fori_loop(0, right_ref.shape[1] // COLS, unit, 0)


def pair_zero_kernel(block_at, me_ref, right_ref, *refs):
    first_refs, block_refs = refs[:PARTS], refs[PARTS:-12]
    front_ref, back_ref, sum_ref, slots_ref = refs[-12:-8]
    left_ref, vec_ref, pay_ref, sem_ref, strip_ref, list_ref, lists_ref, strip_sem_ref = refs[-8:]

    @pl.when((pl.program_id(0) == 0) & (pl.program_id(1) == 0))
    def _():
        strips = [
            pltpu.make_async_copy(
                block_refs[index].at[pl.ds(row + 80, 16), pl.ds(0, 128)],
                strip_ref.at[at],
                strip_sem_ref.at[at],
            )
            for at, (index, row) in enumerate(block_at)
        ]
        for strip in strips:
            strip.start()
        sum_ref[...] = functools.reduce(jnp.add, [first_ref[...] for first_ref in first_refs])
        for at, strip in enumerate(strips):
            strip.wait()
            list_ref[at : at + 1, :] = strip_ref[at].astype(F32)[:1].astype(jnp.int32)
        numbers = pltpu.make_async_copy(list_ref, lists_ref, strip_sem_ref.at[0])
        numbers.start()
        numbers.wait()
        find_partners(lists_ref, me_ref[0], slots_ref)

    def fetch(which):
        for at, (index, row) in enumerate(block_at):
            @pl.when(slots_ref[1 + which] == at)
            def _():
                pltpu.make_async_copy(
                    block_refs[index].at[pl.ds(row, 80)],
                    pay_ref.at[which % 2],
                    sem_ref.at[which % 2],
                ).start()

    half_tiles(
        slots_ref, right_ref, fetch, front_ref, back_ref, sum_ref, left_ref, vec_ref, pay_ref, sem_ref
    )


def pair_one_kernel(
    slots_ref, right_ref, first_ref, every_ref, rhs_ref, var_ref,
    front_ref, back_ref, image_ref, send_ref, left_ref, vec_ref, pay_ref, sem_ref,
):
    slot, step = pl.program_id(0), pl.program_id(1)

    @pl.when((slot == 0) & (step == 0))
    def _():
        image_ref[...] = first_ref[...]

    def fetch(which):
        number = slots_ref[pl.num_programs(0) + 2 + which]
        pltpu.make_async_copy(
            every_ref.at[number], pay_ref.at[which % 2], sem_ref.at[which % 2]
        ).start()

    half_tiles(
        slots_ref, right_ref, fetch, front_ref, back_ref, image_ref, left_ref, vec_ref, pay_ref, sem_ref
    )

    @pl.when((slot == pl.num_programs(0) - 1) & (step == pl.num_programs(1) - 1))
    def _():
        rhs = rhs_ref[...]
        width = rhs.shape[1]
        image = (var_ref[...] + DIAGONAL) * rhs + SCALE * image_ref[...]
        image_ref[...] = image
        send_ref[:, :width] = image.astype(BF16)
        pieces = split_three(jnp.sum(rhs * rhs, axis=1, keepdims=True))
        pieces += split_three(jnp.sum(rhs * image, axis=1, keepdims=True))
        lane = lax.broadcasted_iota(jnp.int32, (rhs.shape[0], TAIL), 1)
        tail = jnp.zeros((rhs.shape[0], TAIL), F32)
        for place, piece in enumerate(pieces):
            tail = jnp.where(lane == place, piece, tail)
        send_ref[:, width:] = tail.astype(BF16)


def again_kernel(
    slots_ref, front_zero_ref, front_one_ref, back_zero_ref, back_one_ref,
    vec_ref, tails_ref, rhs_ref, var_ref, image_ref, *refs
):
    first_refs = refs[:PARTS]
    rows_ref, dots_ref, step_ref, sum_ref, held_ref, sem_ref = refs[PARTS:]
    slot, step = pl.program_id(0), pl.program_id(1)
    width = rhs_ref.shape[1]
    steps = width // ROWS
    half = steps // 2
    parts = (slots_ref[0] - FRONT) * steps

    def fetch(part, back_ref, first):
        at = pl.ds(pl.multiple_of((part % steps - first) * ROWS, ROWS), ROWS)
        return pltpu.make_async_copy(
            back_ref.at[part // steps, at], held_ref.at[part % HELD], sem_ref.at[part % HELD]
        )

    def start(part):
        @pl.when((part < parts) & (part % steps < half))
        def _():
            fetch(part, back_zero_ref, 0).start()

        @pl.when((part < parts) & (part % steps >= half))
        def _():
            fetch(part, back_one_ref, half).start()

    @pl.when((slot == 0) & (step == 0))
    def _():
        sum_ref[...] = functools.reduce(jnp.add, [first_ref[...] for first_ref in first_refs])
        for part in range(HELD):
            start(part)

    @pl.when(slot < slots_ref[0])
    def _():
        at = pl.multiple_of(step * ROWS, ROWS)
        for front_ref, here in ((front_zero_ref, step < half), (front_one_ref, step >= half)):
            @pl.when((slot < FRONT) & here)
            def _():
                sum_ref[...] += jnp.dot(
                    vec_ref[0, :, pl.ds(at, ROWS)], front_ref[0], preferred_element_type=F32
                )

        @pl.when(slot >= FRONT)
        def _():
            part = (slot - FRONT) * steps + step
            fetch(part % HELD, back_zero_ref, part % HELD // half * half).wait()
            sum_ref[...] += jnp.dot(
                vec_ref[0, :, pl.ds(at, ROWS)], held_ref[part % HELD], preferred_element_type=F32
            )
            start(part + HELD)

    @pl.when((slot == pl.num_programs(0) - 1) & (step == pl.num_programs(1) - 1))
    def _():
        rhs = rhs_ref[...]
        image = image_ref[...]
        total = jnp.sum(tails_ref[...].astype(F32), axis=0)
        norm = total[:, 0:1] + total[:, 1:2] + total[:, 2:3]
        curve = total[:, 3:4] + total[:, 4:5] + total[:, 5:6]
        length = norm / curve
        second = (var_ref[...] + DIAGONAL) * image + SCALE * sum_ref[...]
        res = rhs - length * image
        res_image = image - length * second
        rows_ref[0:8] = rhs
        rows_ref[8:16] = res
        rows_ref[16:24] = image
        rows_ref[24:32] = res_image
        lane = lax.broadcasted_iota(jnp.int32, (rhs.shape[0], TAIL), 1)
        dots = jnp.zeros((rhs.shape[0], TAIL), F32)
        for place, product in enumerate((res * res, res * res_image, res * image, rhs * res_image)):
            dots = jnp.where(lane == place, jnp.sum(product, axis=1, keepdims=True), dots)
        dots_ref[...] = dots
        step_ref[...] = jnp.where(lane == 0, norm, jnp.where(lane == 1, curve, 0.0))


def order_kernel(rows_ref, perm_ref, out_ref):
    rows = rows_ref[...]
    count, width = rows.shape
    pieces = jnp.concatenate([piece for piece in split_three(rows)], axis=0).astype(BF16)
    perm = perm_ref[...]
    chunk = 256
    for col in range(0, width, chunk):
        total = jnp.zeros((3 * count, chunk), F32)
        for at in range(0, width, chunk):
            index = lax.broadcasted_iota(jnp.int32, (chunk, chunk), 0) + at
            pick = jnp.where(index == perm[:, col : col + chunk], 1.0, 0.0).astype(BF16)
            total += jnp.dot(pieces[:, at : at + chunk], pick, preferred_element_type=F32)
        out_ref[:, col : col + chunk] = total[:count] + total[count : 2 * count] + total[2 * count :]


def swap(value, mask, count):
    return lax.ppermute(value, "row", [(i, i ^ mask) for i in range(count)])


def levels(count, sizes):
    bits = count.bit_length() - 1
    out = []
    sizes = list(sizes)
    while bits:
        take = min(sizes.pop(0) if sizes else 1, bits)
        bits -= take
        out.append([mask << bits for mask in range(1, 1 << take)])
    return out


def tree_sum(value, count):
    for masks in levels(count, [2, 2, 2]):
        others = [swap(value, mask, count) for mask in masks]
        if len(masks) == 3:
            value = (value + others[0]) + (others[1] + others[2])
        else:
            value = value + others[0]
    return value


def gather_levels(count):
    return levels(count, [2] if count <= 16 else [2, 2])


def gather_places(count):
    places = [0]
    for masks in gather_levels(count):
        places = places + [place ^ mask for mask in masks for place in places]
    return places


def tree_gather(value, count):
    blocks, out = value[None], []
    for masks in gather_levels(count):
        blocks = jnp.concatenate([blocks] + [swap(blocks, mask, count) for mask in masks], axis=0)
        out.append(blocks)
    return out


def gate(block, behind):
    return pl.pallas_call(
        lambda *refs: None,
        in_specs=[pl.BlockSpec(memory_space=pl.ANY)] * 2,
        out_specs=pl.BlockSpec(memory_space=pl.ANY),
        out_shape=jax.ShapeDtypeStruct(block.shape, block.dtype),
        input_output_aliases={0: 0},
        name="gate",
    )(block, behind)


def local(features, right_side, variance, hilbert_order, tile_list):
    width = features.shape[1]
    rhs_count = right_side.shape[0]
    count = lax.axis_size("row")
    most = tile_list.shape[1]
    steps = width // ROWS
    shape = jax.ShapeDtypeStruct
    params = pltpu.CompilerParams(vmem_limit_bytes=10 * 1024 * 1024)
    var_row = variance[None, :]

    whole = lambda *ignored: (0, 0)
    row_spec = pl.BlockSpec(right_side.shape, whole)
    var_spec = pl.BlockSpec(var_row.shape, whole)
    pay_shape = (80, width // 4)
    smem = pl.BlockSpec(memory_space=pltpu.SMEM)
    vmem = pl.BlockSpec(memory_space=pltpu.VMEM)
    pay_zero, pay_one, right = pl.pallas_call(
        payload_kernel,
        in_specs=[smem, vmem, vmem],
        out_shape=[
            shape((96, width // 4), BF16),
            shape(pay_shape, BF16),
            shape((KDIM, width), BF16),
        ],
        compiler_params=params,
        name="payload",
    )(tile_list, features, right_side)
    in_hbm = lambda array: pltpu.with_memory_space_constraint(array, pltpu.HBM)
    every_one = in_hbm(lax.all_gather(pay_one, "row", axis=0))
    me = jnp.full((1,), lax.axis_index("row"), jnp.int32)
    any_spec = pl.BlockSpec(memory_space=pl.ANY)

    def own_part(rows, arrived):
        blocks = own_blocks(rows, steps)
        tiles, sums = pl.pallas_call(
            functools.partial(own_kernel, rows),
            in_specs=[vmem, vmem, vmem, any_spec],
            out_specs=[any_spec, vmem],
            out_shape=[pltpu.HBM((len(blocks), ROWS, ROWS), BF16), shape(right_side.shape, F32)],
            scratch_shapes=[
                pltpu.VMEM((width, KDIM), BF16),
                pltpu.VMEM((rhs_count, width), BF16),
                pltpu.VMEM((len(blocks), ROWS, ROWS), BF16),
                pltpu.SemaphoreType.DMA((len(blocks),)),
            ],
            compiler_params=params,
            cost_estimate=pl.CostEstimate(
                flops=5_000_000_000, bytes_accessed=2 * len(blocks) * ROWS * ROWS, transcendentals=0
            ),
            name=f"own_tile_{rows[0]}",
        )(features, right_side, right, arrived)
        return blocks, tiles, sums

    first_masks, *later = gather_levels(count)
    near = jnp.concatenate([pay_zero] + [swap(pay_zero, mask, count) for mask in first_masks], axis=0)
    own_parts = [own_part(range(1), right)]
    near = gate(near, own_parts[0][2])
    own_parts.append(own_part(range(1, steps), near))
    arrays = [near]
    for level, masks in enumerate(later):
        arrays = arrays + [swap(array, mask, count) for mask in masks for array in arrays]
        if level == 0:
            arrays[-1] = gate(arrays[-1], own_parts[1][2])
    block_at = [(at, row * 96) for at in range(len(arrays)) for row in range(len(first_masks) + 1)]

    half = steps // 2

    def front_at(k, i, *ignored):
        return (jnp.minimum(k, FRONT - 1), jnp.where(k < FRONT, i, half - 1), 0)

    def back_at(k, i, *ignored):
        return (jnp.maximum(k - FRONT, 0), jnp.where(k < FRONT, 0, i), 0)

    half_specs = [pl.BlockSpec((1, ROWS, width), front_at), pl.BlockSpec((1, ROWS, width), back_at)]
    half_shapes = [
        pltpu.VMEM((FRONT, width // 2, width), BF16),
        pltpu.HBM((most - FRONT, width // 2, width), BF16),
    ]
    half_scratch = [
        pltpu.VMEM((width // 2, KDIM), BF16),
        pltpu.VMEM((rhs_count, width // 2), BF16),
        pltpu.VMEM((2,) + pay_shape, BF16),
        pltpu.SemaphoreType.DMA((2,)),
    ]
    right_spec = pl.BlockSpec(right.shape, whole)
    send_shape = (rhs_count, width + TAIL)
    front_zero, back_zero, half_sum, slots = pl.pallas_call(
        functools.partial(pair_zero_kernel, block_at),
        grid_spec=pltpu.PrefetchScalarGridSpec(
            num_scalar_prefetch=1,
            grid=(most, half),
            in_specs=[right_spec] + [row_spec] * PARTS + [any_spec] * len(arrays),
            out_specs=half_specs + [row_spec, smem],
            scratch_shapes=half_scratch
            + [
                pltpu.VMEM((count, 16, 128), BF16),
                pltpu.VMEM((count, 128), jnp.int32),
                pltpu.SMEM((count, 128), jnp.int32),
                pltpu.SemaphoreType.DMA((count,)),
            ],
        ),
        out_shape=half_shapes
        + [shape(right_side.shape, F32), shape((2 * (most + 2),), jnp.int32)],
        compiler_params=params,
        name="pair_zero",
    )(me, right, *[part[2] for part in own_parts], *arrays)
    front_one, back_one, image, send = pl.pallas_call(
        pair_one_kernel,
        grid_spec=pltpu.PrefetchScalarGridSpec(
            num_scalar_prefetch=1,
            grid=(most, half),
            in_specs=[right_spec, row_spec, any_spec, row_spec, var_spec],
            out_specs=half_specs + [row_spec, pl.BlockSpec(send_shape, whole)],
            scratch_shapes=half_scratch,
        ),
        out_shape=half_shapes + [shape(right_side.shape, F32), shape(send_shape, BF16)],
        compiler_params=params,
        name="pair_one",
    )(slots, right, half_sum, every_one, right_side, var_row)
    fronts = [pltpu.with_memory_space_constraint(part, pltpu.VMEM) for part in (front_zero, front_one)]
    backs = [pltpu.with_memory_space_constraint(part, pltpu.HBM) for part in (back_zero, back_one)]

    def front_zero_at(k, i, *ignored):
        return (jnp.minimum(k, FRONT - 1), jnp.where(k < FRONT, jnp.minimum(i, half - 1), half - 1), 0)

    def front_one_at(k, i, *ignored):
        return (jnp.minimum(k, FRONT - 1), jnp.where(k < FRONT, jnp.maximum(i - half, 0), half - 1), 0)

    every_send = tree_gather(send, count)[-1]
    own_again = [
        pl.pallas_call(
            functools.partial(own_again_kernel, blocks),
            in_specs=[any_spec, pl.BlockSpec(send_shape, whole)],
            out_specs=row_spec,
            out_shape=shape(right_side.shape, F32),
            scratch_shapes=[
                pltpu.VMEM((len(blocks), ROWS, ROWS), BF16),
                pltpu.SemaphoreType.DMA((len(blocks),)),
            ],
            compiler_params=params,
            cost_estimate=pl.CostEstimate(
                flops=5_000_000_000, bytes_accessed=2 * len(blocks) * ROWS * ROWS, transcendentals=0
            ),
            name=f"own_again_{part}",
        )(in_hbm(tiles), send)
        for part, (blocks, tiles, _) in enumerate(own_parts)
    ]
    dots_spec = pl.BlockSpec((rhs_count, TAIL), whole)
    rows, dots, steps_one = pl.pallas_call(
        again_kernel,
        grid_spec=pltpu.PrefetchScalarGridSpec(
            num_scalar_prefetch=1,
            grid=(most, steps),
            in_specs=[
                pl.BlockSpec((1, ROWS, width), front_zero_at),
                pl.BlockSpec((1, ROWS, width), front_one_at),
                any_spec,
                any_spec,
                pl.BlockSpec((1,) + send_shape, lambda k, i, s: (s[1 + k], 0, 0)),
                pl.BlockSpec((count, rhs_count, TAIL), lambda k, i, s: (0, 0, width // TAIL)),
                row_spec,
                var_spec,
                row_spec,
            ]
            + [row_spec] * PARTS,
            out_specs=[
                pl.BlockSpec((4 * rhs_count, width), whole),
                dots_spec,
                dots_spec,
            ],
            scratch_shapes=[
                pltpu.VMEM(right_side.shape, F32),
                pltpu.VMEM((HELD, ROWS, width), BF16),
                pltpu.SemaphoreType.DMA((HELD,)),
            ],
        ),
        out_shape=[
            shape((4 * rhs_count, width), F32),
            shape((rhs_count, TAIL), F32),
            shape((rhs_count, TAIL), F32),
        ],
        compiler_params=params,
        name="pair_again",
    )(slots, *fronts, *backs, every_send, every_send, right_side, var_row, image, *own_again)

    dots = tree_sum(dots, count)
    ordered = pl.pallas_call(
        order_kernel,
        out_shape=shape(rows.shape, F32),
        compiler_params=params,
        name="curve_order",
    )(rows, hilbert_order)
    norm, curve = steps_one[:, 0:1], steps_one[:, 1:2]
    length = norm / curve
    norm_next = dots[:, 0:1]
    ratio = norm_next / norm
    curve_next = dots[:, 1:2] + ratio * (dots[:, 2:3] + dots[:, 3:4]) + ratio * ratio * curve
    length_next = norm_next / curve_next
    rhs_o, res_o, image_o, res_image_o = [ordered[at : at + 8] for at in range(0, 32, 8)]
    solved = length * rhs_o + length_next * (res_o + ratio * rhs_o)
    residual = res_o - length_next * (res_image_o + ratio * image_o)
    return (solved, residual)


def solution(mesh):
    in_specs = (
        P(None, ("group", "row")),
        P(None, ("group", "row")),
        P(("group", "row")),
        P(("group", "row"), None),
        P(("group", "row"), None, None),
    )
    out_specs = (P(None, ("group", "row")), P(None, ("group", "row")))
    return jax.shard_map(local, mesh=mesh, in_specs=in_specs, out_specs=out_specs, check_vma=False)
```

```python
import functools

import jax
import jax.numpy as jnp
import numpy as np
from jax import lax
from jax.experimental import pallas as pl
from jax.experimental.pallas import tpu as pltpu
from jax.sharding import PartitionSpec as P

SHRINK = 0.95
GRAM = SHRINK * SHRINK
SCALE = 20.0 * (20.0 / 19.0) ** 19
DIAGONAL = float(1.0 - SCALE * float(np.float32(1.0 / SCALE).astype(jnp.bfloat16)))
KDIM = 128
ROWS = 512
PARTS = 2
COLS = 512
SUB = 64
FRONT = 3
HELD = 4
TAIL = 128
BF16 = jnp.bfloat16
F32 = jnp.float32
CONTRACT_LANES = (((1,), (1,)), ((), ()))


def split_three(value):
    high = value.astype(BF16).astype(F32)
    rest = value - high
    middle = rest.astype(BF16).astype(F32)
    return high, middle, rest - middle


def norm_rows(norm, first):
    high, middle, low = split_three(norm)
    row = lax.broadcasted_iota(jnp.int32, (32, norm.shape[1]), 0)
    out = jnp.where(row < 6, 1.0, 0.0)
    out = jnp.where(row == first, high, out)
    out = jnp.where(row == first + 1, middle, out)
    return jnp.where(row == first + 2, low, out).astype(BF16)


def own_factor(feat):
    wide = feat.astype(F32)
    norm = jnp.sum(wide * wide, axis=0, keepdims=True) * GRAM
    pieces = split_three(wide * (-2.0 * GRAM))
    return jnp.concatenate([piece.astype(BF16) for piece in pieces] + [norm_rows(norm, 0)], axis=0)


def other_factor(feat):
    wide = feat.astype(F32)
    norm = jnp.sum(wide * wide, axis=0, keepdims=True) * GRAM
    return jnp.transpose(jnp.concatenate([feat, feat, feat, norm_rows(norm, 3)], axis=0))


def psi_power(dist):
    dist = jnp.maximum(dist, 1e-30)
    radius = dist * lax.rsqrt(dist)
    u = jnp.maximum(SHRINK - radius, 1e-30)
    return (jnp.exp2(19.0 * lax.log2(u)) * (1.0 - u)).astype(BF16)


def tile_unit(left, right, vec, tile_ref):
    dist = jnp.dot(left, right, preferred_element_type=F32)
    parts = []
    for sub in range(0, left.shape[0], SUB):
        part = psi_power(dist[sub : sub + SUB])
        tile_ref[sub : sub + SUB, :] = part
        parts.append(part)
    return jnp.dot(vec, jnp.concatenate(parts, axis=0), preferred_element_type=F32)


def unpack(pay):
    return jnp.concatenate([pay[:32], pay[32:64]], axis=1), jnp.concatenate([pay[64:72], pay[72:80]], axis=1)


def own_blocks(rows, count):
    return [(row, col) for row in rows for col in range(row, count)]


def own_kernel(
    rows, left_ref, right_ref, vec_ref, arrived_ref, out_ref, sum_ref, tile_ref, sem_ref
):
    sum_ref[...] = jnp.zeros_like(sum_ref)
    count = vec_ref.shape[1] // ROWS
    piece = lambda index: pl.ds(pl.multiple_of(index * ROWS, ROWS), ROWS)
    save = lambda at: pltpu.make_async_copy(tile_ref.at[at], out_ref.at[at], sem_ref.at[at])

    def row_step(row, at):
        def col_step(col, at):
            sum_ref[:, piece(col)] += tile_unit(
                left_ref[piece(row), :], right_ref[:, piece(col)], vec_ref[:, piece(row)],
                tile_ref.at[at],
            )
            save(at).start()

            @pl.when(row != col)
            def _():
                sum_ref[:, piece(row)] += lax.dot_general(
                    vec_ref[:, piece(col)], tile_ref[at], CONTRACT_LANES,
                    preferred_element_type=F32,
                )

            return at + 1

        return lax.fori_loop(row, count, col_step, at)

    lax.fori_loop(rows[0], rows[-1] + 1, row_step, 0)
    for at in range(tile_ref.shape[0]):
        save(at).wait()


def own_again_kernel(blocks, in_ref, vec_ref, sum_ref, tile_ref, sem_ref):
    load = lambda index: pltpu.make_async_copy(
        in_ref.at[index], tile_ref.at[index], sem_ref.at[index]
    )
    for index in range(len(blocks)):
        load(index).start()
    sum_ref[...] = jnp.zeros_like(sum_ref)
    piece = lambda index: slice(index * ROWS, (index + 1) * ROWS)
    for index, (row, col) in enumerate(blocks):
        load(index).wait()
        sum_ref[:, piece(col)] += jnp.dot(
            vec_ref[:, piece(row)], tile_ref[index], preferred_element_type=F32
        )
        if row != col:
            sum_ref[:, piece(row)] += lax.dot_general(
                vec_ref[:, piece(col)], tile_ref[index], CONTRACT_LANES, preferred_element_type=F32
            )


def payload_kernel(
    list_ref, feat_ref, rhs_ref, pay_zero_ref, pay_one_ref, right_ref, left_ref, vec_ref
):
    feat = feat_ref[...]
    rounded = rhs_ref[...].astype(BF16)
    quarter = feat.shape[1] // 4
    for half, pay_ref in enumerate((pay_zero_ref, pay_one_ref)):
        first, second = [slice(at * quarter, (at + 1) * quarter) for at in (2 * half, 2 * half + 1)]
        pay_ref[:32] = feat[:, first]
        pay_ref[32:64] = feat[:, second]
        pay_ref[64:80] = jnp.concatenate([rounded[:, first], rounded[:, second]], axis=0)
    lane = lax.broadcasted_iota(jnp.int32, (16, quarter), 1)
    numbers = jnp.full(lane.shape, -1, jnp.int32)
    for entry in range(list_ref.shape[1]):
        numbers = jnp.where(lane == entry, list_ref[0, entry, 1], numbers)
    pay_zero_ref[80:96] = numbers.astype(F32).astype(BF16)
    right_ref[...] = own_factor(feat)
    left_ref[...] = other_factor(feat)
    vec_ref[...] = rounded


def find_partners(lists_ref, me, slots_ref):
    count, most = lists_ref.shape[0], slots_ref.shape[0] - 2
    for at in range(slots_ref.shape[0]):
        slots_ref[at] = 0
    total = jnp.int32(0)
    for at, place in enumerate(gather_places(count)):
        if at == 0:
            continue
        number = me ^ place
        hit = jnp.bool_(False)
        for entry in range(most):
            hit = hit | (lists_ref[at, entry] == me) | (lists_ref[0, entry] == number)
        slots_ref[1 + total] = jnp.where(hit, at, 0)
        total = total + hit.astype(jnp.int32)
    slots_ref[0] = total


def fetch_from(block_at, block_refs, slots_ref, pay_ref, sem_ref):
    def fetch(which):
        for at, (index, row) in enumerate(block_at):
            @pl.when(slots_ref[1 + which] == at)
            def _():
                pltpu.make_async_copy(
                    block_refs[index].at[pl.ds(row, 80)],
                    pay_ref.at[which % 2],
                    sem_ref.at[which % 2],
                ).start()

    return fetch


def half_tiles(slots_ref, right_ref, fetch, front_ref, back_ref, sum_ref, left_ref, vec_ref, pay_ref, sem_ref):
    slot, step = pl.program_id(0), pl.program_id(1)

    @pl.when((slot == 0) & (step == 0) & (slots_ref[0] > 0))
    def _():
        fetch(0)

    @pl.when(slot < slots_ref[0])
    def _():
        @pl.when(step == 0)
        def _():
            pltpu.make_async_copy(
                pay_ref.at[(slot + 1) % 2], pay_ref.at[slot % 2], sem_ref.at[slot % 2]
            ).wait()

            @pl.when(slot + 1 < slots_ref[0])
            def _():
                fetch(slot + 1)

            feat, vec = unpack(pay_ref[slot % 2])
            left_ref[...] = other_factor(feat)
            vec_ref[...] = vec

        rows = pl.ds(pl.multiple_of(step * ROWS, ROWS), ROWS)
        left, vec = left_ref[rows, :], vec_ref[:, rows]
        for tile_ref, here in ((front_ref, slot < FRONT), (back_ref, slot >= FRONT)):
            @pl.when(here)
            def _():
                def unit(index, carry):
                    cols = pl.ds(pl.multiple_of(index * COLS, COLS), COLS)
                    sum_ref[:, cols] += tile_unit(
                        left, right_ref[:, cols], vec, tile_ref.at[0, :, cols]
                    )
                    return carry

                lax.fori_loop(0, right_ref.shape[1] // COLS, unit, 0)


def pair_zero_kernel(block_at, me_ref, right_ref, *refs):
    first_refs, block_refs = refs[:PARTS], refs[PARTS:-12]
    front_ref, back_ref, sum_ref, slots_ref = refs[-12:-8]
    left_ref, vec_ref, pay_ref, sem_ref, strip_ref, list_ref, lists_ref, strip_sem_ref = refs[-8:]

    @pl.when((pl.program_id(0) == 0) & (pl.program_id(1) == 0))
    def _():
        strips = [
            pltpu.make_async_copy(
                block_refs[index].at[pl.ds(row + 80, 16), pl.ds(0, 128)],
                strip_ref.at[at],
                strip_sem_ref.at[at],
            )
            for at, (index, row) in enumerate(block_at)
        ]
        for strip in strips:
            strip.start()
        sum_ref[...] = functools.reduce(jnp.add, [first_ref[...] for first_ref in first_refs])
        for at, strip in enumerate(strips):
            strip.wait()
            list_ref[at : at + 1, :] = strip_ref[at].astype(F32)[:1].astype(jnp.int32)
        numbers = pltpu.make_async_copy(list_ref, lists_ref, strip_sem_ref.at[0])
        numbers.start()
        numbers.wait()
        find_partners(lists_ref, me_ref[0], slots_ref)

    fetch = fetch_from(block_at, block_refs, slots_ref, pay_ref, sem_ref)
    half_tiles(
        slots_ref, right_ref, fetch, front_ref, back_ref, sum_ref, left_ref, vec_ref, pay_ref, sem_ref
    )


def pair_one_kernel(block_at, slots_ref, right_ref, first_ref, rhs_ref, var_ref, *refs):
    block_refs = refs[:-8]
    front_ref, back_ref, image_ref, send_ref, left_ref, vec_ref, pay_ref, sem_ref = refs[-8:]
    slot, step = pl.program_id(0), pl.program_id(1)

    @pl.when((slot == 0) & (step == 0))
    def _():
        image_ref[...] = first_ref[...]

    fetch = fetch_from(block_at, block_refs, slots_ref, pay_ref, sem_ref)
    half_tiles(
        slots_ref, right_ref, fetch, front_ref, back_ref, image_ref, left_ref, vec_ref, pay_ref, sem_ref
    )

    @pl.when((slot == pl.num_programs(0) - 1) & (step == pl.num_programs(1) - 1))
    def _():
        rhs = rhs_ref[...]
        width = rhs.shape[1]
        image = (var_ref[...] + DIAGONAL) * rhs + SCALE * image_ref[...]
        image_ref[...] = image
        send_ref[:, :width] = image.astype(BF16)
        pieces = split_three(jnp.sum(rhs * rhs, axis=1, keepdims=True))
        pieces += split_three(jnp.sum(rhs * image, axis=1, keepdims=True))
        lane = lax.broadcasted_iota(jnp.int32, (rhs.shape[0], TAIL), 1)
        tail = jnp.zeros((rhs.shape[0], TAIL), F32)
        for place, piece in enumerate(pieces):
            tail = jnp.where(lane == place, piece, tail)
        send_ref[:, width:] = tail.astype(BF16)


def again_kernel(
    slots_ref, front_zero_ref, front_one_ref, back_zero_ref, back_one_ref,
    vec_ref, tails_ref, rhs_ref, var_ref, image_ref, *refs
):
    first_refs = refs[:PARTS]
    rows_ref, dots_ref, step_ref, sum_ref, held_ref, sem_ref = refs[PARTS:]
    slot, step = pl.program_id(0), pl.program_id(1)
    width = rhs_ref.shape[1]
    steps = width // ROWS
    half = steps // 2
    parts = (slots_ref[0] - FRONT) * steps

    def fetch(part, back_ref, first):
        at = pl.ds(pl.multiple_of((part % steps - first) * ROWS, ROWS), ROWS)
        return pltpu.make_async_copy(
            back_ref.at[part // steps, at], held_ref.at[part % HELD], sem_ref.at[part % HELD]
        )

    def start(part):
        @pl.when((part < parts) & (part % steps < half))
        def _():
            fetch(part, back_zero_ref, 0).start()

        @pl.when((part < parts) & (part % steps >= half))
        def _():
            fetch(part, back_one_ref, half).start()

    @pl.when((slot == 0) & (step == 0))
    def _():
        sum_ref[...] = functools.reduce(jnp.add, [first_ref[...] for first_ref in first_refs])
        for part in range(HELD):
            start(part)

    @pl.when(slot < slots_ref[0])
    def _():
        at = pl.multiple_of(step * ROWS, ROWS)
        for front_ref, here in ((front_zero_ref, step < half), (front_one_ref, step >= half)):
            @pl.when((slot < FRONT) & here)
            def _():
                sum_ref[...] += jnp.dot(
                    vec_ref[0, :, pl.ds(at, ROWS)], front_ref[0], preferred_element_type=F32
                )

        @pl.when(slot >= FRONT)
        def _():
            part = (slot - FRONT) * steps + step
            fetch(part % HELD, back_zero_ref, part % HELD // half * half).wait()
            sum_ref[...] += jnp.dot(
                vec_ref[0, :, pl.ds(at, ROWS)], held_ref[part % HELD], preferred_element_type=F32
            )
            start(part + HELD)

    @pl.when((slot == pl.num_programs(0) - 1) & (step == pl.num_programs(1) - 1))
    def _():
        rhs = rhs_ref[...]
        image = image_ref[...]
        total = jnp.sum(tails_ref[...].astype(F32), axis=0)
        norm = total[:, 0:1] + total[:, 1:2] + total[:, 2:3]
        curve = total[:, 3:4] + total[:, 4:5] + total[:, 5:6]
        length = norm / curve
        second = (var_ref[...] + DIAGONAL) * image + SCALE * sum_ref[...]
        res = rhs - length * image
        res_image = image - length * second
        rows_ref[0:8] = rhs
        rows_ref[8:16] = res
        rows_ref[16:24] = image
        rows_ref[24:32] = res_image
        lane = lax.broadcasted_iota(jnp.int32, (rhs.shape[0], TAIL), 1)
        dots = jnp.zeros((rhs.shape[0], TAIL), F32)
        for place, product in enumerate((res * res, res * res_image, res * image, rhs * res_image)):
            dots = jnp.where(lane == place, jnp.sum(product, axis=1, keepdims=True), dots)
        dots_ref[...] = dots
        step_ref[...] = jnp.where(lane == 0, norm, jnp.where(lane == 1, curve, 0.0))


def order_kernel(rows_ref, perm_ref, out_ref):
    rows = rows_ref[...]
    count, width = rows.shape
    pieces = jnp.concatenate([piece for piece in split_three(rows)], axis=0).astype(BF16)
    perm = perm_ref[...]
    chunk = 256
    for col in range(0, width, chunk):
        total = jnp.zeros((3 * count, chunk), F32)
        for at in range(0, width, chunk):
            index = lax.broadcasted_iota(jnp.int32, (chunk, chunk), 0) + at
            pick = jnp.where(index == perm[:, col : col + chunk], 1.0, 0.0).astype(BF16)
            total += jnp.dot(pieces[:, at : at + chunk], pick, preferred_element_type=F32)
        out_ref[:, col : col + chunk] = total[:count] + total[count : 2 * count] + total[2 * count :]


def swap(value, mask, count):
    return lax.ppermute(value, "row", [(i, i ^ mask) for i in range(count)])


def levels(count, sizes):
    bits = count.bit_length() - 1
    out = []
    sizes = list(sizes)
    while bits:
        take = min(sizes.pop(0) if sizes else 1, bits)
        bits -= take
        out.append([mask << bits for mask in range(1, 1 << take)])
    return out


def tree_sum(value, count):
    for masks in levels(count, [2, 2, 2]):
        others = [swap(value, mask, count) for mask in masks]
        if len(masks) == 3:
            value = (value + others[0]) + (others[1] + others[2])
        else:
            value = value + others[0]
    return value


def gather_levels(count):
    return levels(count, [2] if count <= 16 else [2, 2])


def gather_places(count):
    places = [0]
    for masks in gather_levels(count):
        places = places + [place ^ mask for mask in masks for place in places]
    return places


def tree_gather(value, count):
    blocks, out = value[None], []
    for masks in gather_levels(count):
        blocks = jnp.concatenate([blocks] + [swap(blocks, mask, count) for mask in masks], axis=0)
        out.append(blocks)
    return out


def gate(block, behind):
    return pl.pallas_call(
        lambda *refs: None,
        in_specs=[pl.BlockSpec(memory_space=pl.ANY)] * 2,
        out_specs=pl.BlockSpec(memory_space=pl.ANY),
        out_shape=jax.ShapeDtypeStruct(block.shape, block.dtype),
        input_output_aliases={0: 0},
        name="gate",
    )(block, behind)


def local(features, right_side, variance, hilbert_order, tile_list):
    width = features.shape[1]
    rhs_count = right_side.shape[0]
    count = lax.axis_size("row")
    most = tile_list.shape[1]
    steps = width // ROWS
    shape = jax.ShapeDtypeStruct
    params = pltpu.CompilerParams(vmem_limit_bytes=10 * 1024 * 1024)
    var_row = variance[None, :]

    whole = lambda *ignored: (0, 0)
    row_spec = pl.BlockSpec(right_side.shape, whole)
    var_spec = pl.BlockSpec(var_row.shape, whole)
    pay_shape = (80, width // 4)
    smem = pl.BlockSpec(memory_space=pltpu.SMEM)
    vmem = pl.BlockSpec(memory_space=pltpu.VMEM)
    in_hbm = lambda array: pltpu.with_memory_space_constraint(array, pltpu.HBM)
    pay_zero, pay_one, right, left, rounded = pl.pallas_call(
        payload_kernel,
        in_specs=[smem, vmem, vmem],
        out_shape=[
            shape((96, width // 4), BF16),
            shape(pay_shape, BF16),
            shape((KDIM, width), BF16),
            shape((width, KDIM), BF16),
            shape(right_side.shape, BF16),
        ],
        compiler_params=params,
        name="payload",
    )(tile_list, in_hbm(features), in_hbm(right_side))
    me = jnp.full((1,), lax.axis_index("row"), jnp.int32)
    any_spec = pl.BlockSpec(memory_space=pl.ANY)

    def own_part(rows, arrived):
        blocks = own_blocks(rows, steps)
        tiles, sums = pl.pallas_call(
            functools.partial(own_kernel, rows),
            in_specs=[vmem, vmem, vmem, any_spec],
            out_specs=[any_spec, vmem],
            out_shape=[pltpu.HBM((len(blocks), ROWS, ROWS), BF16), shape(right_side.shape, F32)],
            scratch_shapes=[
                pltpu.VMEM((len(blocks), ROWS, ROWS), BF16),
                pltpu.SemaphoreType.DMA((len(blocks),)),
            ],
            compiler_params=params,
            cost_estimate=pl.CostEstimate(
                flops=5_000_000_000, bytes_accessed=2 * len(blocks) * ROWS * ROWS, transcendentals=0
            ),
            name=f"own_tile_{rows[0]}",
        )(left, right, rounded, arrived)
        return blocks, tiles, sums

    first_masks, *later = gather_levels(count)
    first_level = lambda pay: jnp.concatenate(
        [pay] + [swap(pay, mask, count) for mask in first_masks], axis=0
    )
    near_zero = first_level(pay_zero)
    own_parts = [own_part(range(1), right)]
    near_zero = gate(near_zero, own_parts[0][2])
    near_one = first_level(gate(pay_one, own_parts[0][2]))
    own_parts.append(own_part(range(1, steps), near_zero))
    near_one = gate(near_one, own_parts[1][2])
    zero, places = [near_zero], [0]
    for level, masks in enumerate(later):
        zero = zero + [swap(array, mask, count) for mask in masks for array in zero]
        places = places + [mask ^ place for mask in masks for place in places]
        if level == 0:
            zero[-1] = gate(zero[-1], own_parts[1][2])
    one = [near_one] + [swap(near_one, place, count) for place in places[1:]]
    each = len(first_masks) + 1
    zero_at = [(at, row * 96) for at in range(len(zero)) for row in range(each)]
    one_at = [(at, row * 80) for at in range(len(one)) for row in range(each)]

    half = steps // 2

    def front_at(k, i, *ignored):
        return (jnp.minimum(k, FRONT - 1), jnp.where(k < FRONT, i, half - 1), 0)

    def back_at(k, i, *ignored):
        return (jnp.maximum(k - FRONT, 0), jnp.where(k < FRONT, 0, i), 0)

    half_specs = [pl.BlockSpec((1, ROWS, width), front_at), pl.BlockSpec((1, ROWS, width), back_at)]
    half_shapes = [
        pltpu.VMEM((FRONT, width // 2, width), BF16),
        pltpu.HBM((most - FRONT, width // 2, width), BF16),
    ]
    half_scratch = [
        pltpu.VMEM((width // 2, KDIM), BF16),
        pltpu.VMEM((rhs_count, width // 2), BF16),
        pltpu.VMEM((2,) + pay_shape, BF16),
        pltpu.SemaphoreType.DMA((2,)),
    ]
    right_spec = pl.BlockSpec(right.shape, whole)
    send_shape = (rhs_count, width + TAIL)
    front_zero, back_zero, half_sum, slots = pl.pallas_call(
        functools.partial(pair_zero_kernel, zero_at),
        grid_spec=pltpu.PrefetchScalarGridSpec(
            num_scalar_prefetch=1,
            grid=(most, half),
            in_specs=[right_spec] + [row_spec] * PARTS + [any_spec] * len(zero),
            out_specs=half_specs + [row_spec, smem],
            scratch_shapes=half_scratch
            + [
                pltpu.VMEM((count, 16, 128), BF16),
                pltpu.VMEM((count, 128), jnp.int32),
                pltpu.SMEM((count, 128), jnp.int32),
                pltpu.SemaphoreType.DMA((count,)),
            ],
        ),
        out_shape=half_shapes
        + [shape(right_side.shape, F32), shape((most + 2,), jnp.int32)],
        compiler_params=params,
        name="pair_zero",
    )(me, right, *[part[2] for part in own_parts], *zero)
    front_one, back_one, image, send = pl.pallas_call(
        functools.partial(pair_one_kernel, one_at),
        grid_spec=pltpu.PrefetchScalarGridSpec(
            num_scalar_prefetch=1,
            grid=(most, half),
            in_specs=[right_spec, row_spec, row_spec, var_spec] + [any_spec] * len(one),
            out_specs=half_specs + [row_spec, pl.BlockSpec(send_shape, whole)],
            scratch_shapes=half_scratch,
        ),
        out_shape=half_shapes + [shape(right_side.shape, F32), shape(send_shape, BF16)],
        compiler_params=params,
        name="pair_one",
    )(slots, right, half_sum, right_side, var_row, *one)
    fronts = [pltpu.with_memory_space_constraint(part, pltpu.VMEM) for part in (front_zero, front_one)]
    backs = [pltpu.with_memory_space_constraint(part, pltpu.HBM) for part in (back_zero, back_one)]

    def front_zero_at(k, i, *ignored):
        return (jnp.minimum(k, FRONT - 1), jnp.where(k < FRONT, jnp.minimum(i, half - 1), half - 1), 0)

    def front_one_at(k, i, *ignored):
        return (jnp.minimum(k, FRONT - 1), jnp.where(k < FRONT, jnp.maximum(i - half, 0), half - 1), 0)

    every_send = tree_gather(send, count)[-1]
    own_again = [
        pl.pallas_call(
            functools.partial(own_again_kernel, blocks),
            in_specs=[any_spec, pl.BlockSpec(send_shape, whole)],
            out_specs=row_spec,
            out_shape=shape(right_side.shape, F32),
            scratch_shapes=[
                pltpu.VMEM((len(blocks), ROWS, ROWS), BF16),
                pltpu.SemaphoreType.DMA((len(blocks),)),
            ],
            compiler_params=params,
            cost_estimate=pl.CostEstimate(
                flops=5_000_000_000, bytes_accessed=2 * len(blocks) * ROWS * ROWS, transcendentals=0
            ),
            name=f"own_again_{part}",
        )(in_hbm(tiles), send)
        for part, (blocks, tiles, _) in enumerate(own_parts)
    ]
    dots_spec = pl.BlockSpec((rhs_count, TAIL), whole)
    rows, dots, steps_one = pl.pallas_call(
        again_kernel,
        grid_spec=pltpu.PrefetchScalarGridSpec(
            num_scalar_prefetch=1,
            grid=(most, steps),
            in_specs=[
                pl.BlockSpec((1, ROWS, width), front_zero_at),
                pl.BlockSpec((1, ROWS, width), front_one_at),
                any_spec,
                any_spec,
                pl.BlockSpec((1,) + send_shape, lambda k, i, s: (s[1 + k], 0, 0)),
                pl.BlockSpec((count, rhs_count, TAIL), lambda k, i, s: (0, 0, width // TAIL)),
                row_spec,
                var_spec,
                row_spec,
            ]
            + [row_spec] * PARTS,
            out_specs=[
                pl.BlockSpec((4 * rhs_count, width), whole),
                dots_spec,
                dots_spec,
            ],
            scratch_shapes=[
                pltpu.VMEM(right_side.shape, F32),
                pltpu.VMEM((HELD, ROWS, width), BF16),
                pltpu.SemaphoreType.DMA((HELD,)),
            ],
        ),
        out_shape=[
            shape((4 * rhs_count, width), F32),
            shape((rhs_count, TAIL), F32),
            shape((rhs_count, TAIL), F32),
        ],
        compiler_params=params,
        name="pair_again",
    )(slots, *fronts, *backs, every_send, every_send, right_side, var_row, image, *own_again)

    dots = tree_sum(dots, count)
    ordered = pl.pallas_call(
        order_kernel,
        out_shape=shape(rows.shape, F32),
        compiler_params=params,
        name="curve_order",
    )(rows, hilbert_order)
    norm, curve = steps_one[:, 0:1], steps_one[:, 1:2]
    length = norm / curve
    norm_next = dots[:, 0:1]
    ratio = norm_next / norm
    curve_next = dots[:, 1:2] + ratio * (dots[:, 2:3] + dots[:, 3:4]) + ratio * ratio * curve
    length_next = norm_next / curve_next
    rhs_o, res_o, image_o, res_image_o = [ordered[at : at + 8] for at in range(0, 32, 8)]
    solved = length * rhs_o + length_next * (res_o + ratio * rhs_o)
    residual = res_o - length_next * (res_image_o + ratio * image_o)
    return (solved, residual)


def solution(mesh):
    in_specs = (
        P(None, ("group", "row")),
        P(None, ("group", "row")),
        P(("group", "row")),
        P(("group", "row"), None),
        P(("group", "row"), None, None),
    )
    out_specs = (P(None, ("group", "row")), P(None, ("group", "row")))
    return jax.shard_map(local, mesh=mesh, in_specs=in_specs, out_specs=out_specs, check_vma=False)
```

```python
import functools

import jax
import jax.numpy as jnp
import numpy as np
from jax import lax
from jax.experimental import pallas as pl
from jax.experimental.pallas import tpu as pltpu
from jax.sharding import PartitionSpec as P

SHRINK = 0.95
GRAM = SHRINK * SHRINK
SCALE = 20.0 * (20.0 / 19.0) ** 19
DIAGONAL = float(1.0 - SCALE * float(np.float32(1.0 / SCALE).astype(jnp.bfloat16)))
KDIM = 128
ROWS = 512
PARTS = 2
COLS = 512
SUB = 64
FRONT = 3
HELD = 4
TAIL = 128
BF16 = jnp.bfloat16
F32 = jnp.float32
CONTRACT_LANES = (((1,), (1,)), ((), ()))


def split_three(value):
    high = value.astype(BF16).astype(F32)
    rest = value - high
    middle = rest.astype(BF16).astype(F32)
    return high, middle, rest - middle


def norm_rows(norm, first):
    high, middle, low = split_three(norm)
    row = lax.broadcasted_iota(jnp.int32, (32, norm.shape[1]), 0)
    out = jnp.where(row < 6, 1.0, 0.0)
    out = jnp.where(row == first, high, out)
    out = jnp.where(row == first + 1, middle, out)
    return jnp.where(row == first + 2, low, out).astype(BF16)


def own_factor(feat):
    wide = feat.astype(F32)
    norm = jnp.sum(wide * wide, axis=0, keepdims=True) * GRAM
    pieces = split_three(wide * (-2.0 * GRAM))
    return jnp.concatenate([piece.astype(BF16) for piece in pieces] + [norm_rows(norm, 0)], axis=0)


def other_factor(feat):
    wide = feat.astype(F32)
    norm = jnp.sum(wide * wide, axis=0, keepdims=True) * GRAM
    return jnp.transpose(jnp.concatenate([feat, feat, feat, norm_rows(norm, 3)], axis=0))


def psi_power(dist):
    dist = jnp.maximum(dist, 1e-30)
    radius = dist * lax.rsqrt(dist)
    u = jnp.maximum(SHRINK - radius, 1e-30)
    return (jnp.exp2(19.0 * lax.log2(u)) * (1.0 - u)).astype(BF16)


def tile_unit(left, right, vec, tile_ref):
    dist = jnp.dot(left, right, preferred_element_type=F32)
    parts = []
    for sub in range(0, left.shape[0], SUB):
        part = psi_power(dist[sub : sub + SUB])
        tile_ref[sub : sub + SUB, :] = part
        parts.append(part)
    return jnp.dot(vec, jnp.concatenate(parts, axis=0), preferred_element_type=F32)


def unpack(pay):
    return jnp.concatenate([pay[:32], pay[32:64]], axis=1), jnp.concatenate([pay[64:72], pay[72:80]], axis=1)


def own_blocks(rows, count):
    return [(row, col) for row in rows for col in range(row, count)]


def own_kernel(
    rows, left_ref, right_ref, vec_ref, arrived_ref, out_ref, sum_ref, tile_ref, sem_ref
):
    sum_ref[...] = jnp.zeros_like(sum_ref)
    count = vec_ref.shape[1] // ROWS
    piece = lambda index: pl.ds(pl.multiple_of(index * ROWS, ROWS), ROWS)
    save = lambda at: pltpu.make_async_copy(tile_ref.at[at], out_ref.at[at], sem_ref.at[at])

    def row_step(row, at):
        def col_step(col, at):
            sum_ref[:, piece(col)] += tile_unit(
                left_ref[piece(row), :], right_ref[:, piece(col)], vec_ref[:, piece(row)],
                tile_ref.at[at],
            )
            save(at).start()

            @pl.when(row != col)
            def _():
                sum_ref[:, piece(row)] += lax.dot_general(
                    vec_ref[:, piece(col)], tile_ref[at], CONTRACT_LANES,
                    preferred_element_type=F32,
                )

            return at + 1

        return lax.fori_loop(row, count, col_step, at)

    lax.fori_loop(rows[0], rows[-1] + 1, row_step, 0)
    for at in range(tile_ref.shape[0]):
        save(at).wait()


def own_again_kernel(blocks, in_ref, vec_ref, sum_ref, tile_ref, sem_ref):
    load = lambda index: pltpu.make_async_copy(
        in_ref.at[index], tile_ref.at[index], sem_ref.at[index]
    )
    for index in range(len(blocks)):
        load(index).start()
    sum_ref[...] = jnp.zeros_like(sum_ref)
    piece = lambda index: slice(index * ROWS, (index + 1) * ROWS)
    for index, (row, col) in enumerate(blocks):
        load(index).wait()
        sum_ref[:, piece(col)] += jnp.dot(
            vec_ref[:, piece(row)], tile_ref[index], preferred_element_type=F32
        )
        if row != col:
            sum_ref[:, piece(row)] += lax.dot_general(
                vec_ref[:, piece(col)], tile_ref[index], CONTRACT_LANES, preferred_element_type=F32
            )


def payload_kernel(
    list_ref, feat_ref, rhs_ref, pay_zero_ref, pay_one_ref, right_ref, left_ref, vec_ref
):
    feat = feat_ref[...]
    rounded = rhs_ref[...].astype(BF16)
    quarter = feat.shape[1] // 4
    for half, pay_ref in enumerate((pay_zero_ref, pay_one_ref)):
        first, second = [slice(at * quarter, (at + 1) * quarter) for at in (2 * half, 2 * half + 1)]
        pay_ref[:32] = feat[:, first]
        pay_ref[32:64] = feat[:, second]
        pay_ref[64:80] = jnp.concatenate([rounded[:, first], rounded[:, second]], axis=0)
    lane = lax.broadcasted_iota(jnp.int32, (16, quarter), 1)
    numbers = jnp.full(lane.shape, -1, jnp.int32)
    for entry in range(list_ref.shape[1]):
        numbers = jnp.where(lane == entry, list_ref[0, entry, 1], numbers)
    pay_zero_ref[80:96] = numbers.astype(F32).astype(BF16)
    right_ref[...] = own_factor(feat)
    left_ref[...] = other_factor(feat)
    vec_ref[...] = rounded


def find_partners(lists_ref, me, slots_ref):
    count, most = lists_ref.shape[0], slots_ref.shape[0] - 2
    for at in range(slots_ref.shape[0]):
        slots_ref[at] = 0
    total = jnp.int32(0)
    for at, place in enumerate(gather_places(count)):
        if at == 0:
            continue
        number = me ^ place
        hit = jnp.bool_(False)
        for entry in range(most):
            hit = hit | (lists_ref[at, entry] == me) | (lists_ref[0, entry] == number)
        slots_ref[1 + total] = jnp.where(hit, at, 0)
        total = total + hit.astype(jnp.int32)
    slots_ref[0] = total


def fetch_from(block_at, block_refs, slots_ref, pay_ref, sem_ref):
    def fetch(which):
        for at, (index, row) in enumerate(block_at):
            @pl.when(slots_ref[1 + which] == at)
            def _():
                pltpu.make_async_copy(
                    block_refs[index].at[pl.ds(row, 80)],
                    pay_ref.at[which % 2],
                    sem_ref.at[which % 2],
                ).start()

    return fetch


def half_tiles(at_once, slots_ref, right_ref, fetch, front_ref, back_ref, sum_ref, left_ref, vec_ref, pay_ref, sem_ref):
    slot, step = pl.program_id(0), pl.program_id(1)

    @pl.when((slot == 0) & (step == 0) & (slots_ref[0] > 0))
    def _():
        fetch(0)

    @pl.when(slot < slots_ref[0])
    def _():
        @pl.when(step == 0)
        def _():
            pltpu.make_async_copy(
                pay_ref.at[(slot + 1) % 2], pay_ref.at[slot % 2], sem_ref.at[slot % 2]
            ).wait()

            @pl.when(slot + 1 < slots_ref[0])
            def _():
                fetch(slot + 1)

            feat, vec = unpack(pay_ref[slot % 2])
            left_ref[...] = other_factor(feat)
            vec_ref[...] = vec

        rows = pl.ds(pl.multiple_of(step * ROWS, ROWS), ROWS)
        left, vec = left_ref[rows, :], vec_ref[:, rows]
        for tile_ref, here in ((front_ref, slot < FRONT), (back_ref, slot >= FRONT)):
            @pl.when(here)
            def _():
                def unit(index, carry):
                    cols = pl.ds(pl.multiple_of(index * at_once, at_once), at_once)
                    sum_ref[:, cols] += tile_unit(
                        left, right_ref[:, cols], vec, tile_ref.at[0, :, cols]
                    )
                    return carry

                lax.fori_loop(0, right_ref.shape[1] // at_once, unit, 0)


def pair_zero_kernel(block_at, me_ref, right_ref, *refs):
    first_refs, block_refs = refs[:PARTS], refs[PARTS:-12]
    front_ref, back_ref, sum_ref, slots_ref = refs[-12:-8]
    left_ref, vec_ref, pay_ref, sem_ref, strip_ref, list_ref, lists_ref, strip_sem_ref = refs[-8:]

    @pl.when((pl.program_id(0) == 0) & (pl.program_id(1) == 0))
    def _():
        strips = [
            pltpu.make_async_copy(
                block_refs[index].at[pl.ds(row + 80, 16), pl.ds(0, 128)],
                strip_ref.at[at],
                strip_sem_ref.at[at],
            )
            for at, (index, row) in enumerate(block_at)
        ]
        for strip in strips:
            strip.start()
        sum_ref[...] = functools.reduce(jnp.add, [first_ref[...] for first_ref in first_refs])
        for at, strip in enumerate(strips):
            strip.wait()
            list_ref[at : at + 1, :] = strip_ref[at].astype(F32)[:1].astype(jnp.int32)
        numbers = pltpu.make_async_copy(list_ref, lists_ref, strip_sem_ref.at[0])
        numbers.start()
        numbers.wait()
        find_partners(lists_ref, me_ref[0], slots_ref)

    fetch = fetch_from(block_at, block_refs, slots_ref, pay_ref, sem_ref)
    half_tiles(
        2 * COLS, slots_ref, right_ref, fetch, front_ref, back_ref, sum_ref, left_ref, vec_ref, pay_ref, sem_ref
    )


def pair_one_kernel(block_at, slots_ref, right_ref, first_ref, rhs_ref, var_ref, *refs):
    block_refs = refs[:-8]
    front_ref, back_ref, image_ref, send_ref, left_ref, vec_ref, pay_ref, sem_ref = refs[-8:]
    slot, step = pl.program_id(0), pl.program_id(1)

    @pl.when((slot == 0) & (step == 0))
    def _():
        image_ref[...] = first_ref[...]

    fetch = fetch_from(block_at, block_refs, slots_ref, pay_ref, sem_ref)
    half_tiles(
        4 * COLS, slots_ref, right_ref, fetch, front_ref, back_ref, image_ref, left_ref, vec_ref, pay_ref, sem_ref
    )

    @pl.when((slot == pl.num_programs(0) - 1) & (step == pl.num_programs(1) - 1))
    def _():
        rhs = rhs_ref[...]
        width = rhs.shape[1]
        image = (var_ref[...] + DIAGONAL) * rhs + SCALE * image_ref[...]
        image_ref[...] = image
        send_ref[:, :width] = image.astype(BF16)
        pieces = split_three(jnp.sum(rhs * rhs, axis=1, keepdims=True))
        pieces += split_three(jnp.sum(rhs * image, axis=1, keepdims=True))
        lane = lax.broadcasted_iota(jnp.int32, (rhs.shape[0], TAIL), 1)
        tail = jnp.zeros((rhs.shape[0], TAIL), F32)
        for place, piece in enumerate(pieces):
            tail = jnp.where(lane == place, piece, tail)
        send_ref[:, width:] = tail.astype(BF16)


def again_kernel(
    slots_ref, front_zero_ref, front_one_ref, back_zero_ref, back_one_ref,
    vec_ref, tails_ref, rhs_ref, var_ref, image_ref, *refs
):
    first_refs = refs[:PARTS]
    rows_ref, dots_ref, step_ref, sum_ref, held_ref, sem_ref = refs[PARTS:]
    slot, step = pl.program_id(0), pl.program_id(1)
    width = rhs_ref.shape[1]
    steps = width // ROWS
    half = steps // 2
    parts = (slots_ref[0] - FRONT) * steps

    def fetch(part, back_ref, first):
        at = pl.ds(pl.multiple_of((part % steps - first) * ROWS, ROWS), ROWS)
        return pltpu.make_async_copy(
            back_ref.at[part // steps, at], held_ref.at[part % HELD], sem_ref.at[part % HELD]
        )

    def start(part):
        @pl.when((part < parts) & (part % steps < half))
        def _():
            fetch(part, back_zero_ref, 0).start()

        @pl.when((part < parts) & (part % steps >= half))
        def _():
            fetch(part, back_one_ref, half).start()

    @pl.when((slot == 0) & (step == 0))
    def _():
        sum_ref[...] = functools.reduce(jnp.add, [first_ref[...] for first_ref in first_refs])
        for part in range(HELD):
            start(part)

    @pl.when(slot < slots_ref[0])
    def _():
        at = pl.multiple_of(step * ROWS, ROWS)
        for front_ref, here in ((front_zero_ref, step < half), (front_one_ref, step >= half)):
            @pl.when((slot < FRONT) & here)
            def _():
                sum_ref[...] += jnp.dot(
                    vec_ref[0, :, pl.ds(at, ROWS)], front_ref[0], preferred_element_type=F32
                )

        @pl.when(slot >= FRONT)
        def _():
            part = (slot - FRONT) * steps + step
            fetch(part % HELD, back_zero_ref, part % HELD // half * half).wait()
            sum_ref[...] += jnp.dot(
                vec_ref[0, :, pl.ds(at, ROWS)], held_ref[part % HELD], preferred_element_type=F32
            )
            start(part + HELD)

    @pl.when((slot == pl.num_programs(0) - 1) & (step == pl.num_programs(1) - 1))
    def _():
        rhs = rhs_ref[...]
        image = image_ref[...]
        total = jnp.sum(tails_ref[...].astype(F32), axis=0)
        norm = total[:, 0:1] + total[:, 1:2] + total[:, 2:3]
        curve = total[:, 3:4] + total[:, 4:5] + total[:, 5:6]
        length = norm / curve
        second = (var_ref[...] + DIAGONAL) * image + SCALE * sum_ref[...]
        res = rhs - length * image
        res_image = image - length * second
        rows_ref[0:8] = rhs
        rows_ref[8:16] = res
        rows_ref[16:24] = image
        rows_ref[24:32] = res_image
        lane = lax.broadcasted_iota(jnp.int32, (rhs.shape[0], TAIL), 1)
        dots = jnp.zeros((rhs.shape[0], TAIL), F32)
        for place, product in enumerate((res * res, res * res_image, res * image, rhs * res_image)):
            dots = jnp.where(lane == place, jnp.sum(product, axis=1, keepdims=True), dots)
        dots_ref[...] = dots
        step_ref[...] = jnp.where(lane == 0, norm, jnp.where(lane == 1, curve, 0.0))


def order_kernel(rows_ref, perm_ref, out_ref):
    rows = rows_ref[...]
    count, width = rows.shape
    pieces = jnp.concatenate([piece for piece in split_three(rows)], axis=0).astype(BF16)
    perm = perm_ref[...]
    chunk = 256
    for col in range(0, width, chunk):
        total = jnp.zeros((3 * count, chunk), F32)
        for at in range(0, width, chunk):
            index = lax.broadcasted_iota(jnp.int32, (chunk, chunk), 0) + at
            pick = jnp.where(index == perm[:, col : col + chunk], 1.0, 0.0).astype(BF16)
            total += jnp.dot(pieces[:, at : at + chunk], pick, preferred_element_type=F32)
        out_ref[:, col : col + chunk] = total[:count] + total[count : 2 * count] + total[2 * count :]


def swap(value, mask, count):
    return lax.ppermute(value, "row", [(i, i ^ mask) for i in range(count)])


def levels(count, sizes):
    bits = count.bit_length() - 1
    out = []
    sizes = list(sizes)
    while bits:
        take = min(sizes.pop(0) if sizes else 1, bits)
        bits -= take
        out.append([mask << bits for mask in range(1, 1 << take)])
    return out


def tree_sum(value, count):
    for masks in levels(count, [2, 2, 2]):
        others = [swap(value, mask, count) for mask in masks]
        if len(masks) == 3:
            value = (value + others[0]) + (others[1] + others[2])
        else:
            value = value + others[0]
    return value


def gather_levels(count):
    return levels(count, [2] if count <= 16 else [2, 2])


def gather_places(count):
    places = [0]
    for masks in gather_levels(count):
        places = places + [place ^ mask for mask in masks for place in places]
    return places


def tree_gather(value, count):
    blocks, out = value[None], []
    for masks in gather_levels(count):
        blocks = jnp.concatenate([blocks] + [swap(blocks, mask, count) for mask in masks], axis=0)
        out.append(blocks)
    return out


def gate(block, behind):
    return pl.pallas_call(
        lambda *refs: None,
        in_specs=[pl.BlockSpec(memory_space=pl.ANY)] * 2,
        out_specs=pl.BlockSpec(memory_space=pl.ANY),
        out_shape=jax.ShapeDtypeStruct(block.shape, block.dtype),
        input_output_aliases={0: 0},
        compiler_params=pltpu.CompilerParams(vmem_limit_bytes=1024 * 1024),
        name="gate",
    )(block, behind)


def local(features, right_side, variance, hilbert_order, tile_list):
    width = features.shape[1]
    rhs_count = right_side.shape[0]
    count = lax.axis_size("row")
    most = tile_list.shape[1]
    steps = width // ROWS
    shape = jax.ShapeDtypeStruct
    params = pltpu.CompilerParams(vmem_limit_bytes=10 * 1024 * 1024)
    var_row = variance[None, :]

    whole = lambda *ignored: (0, 0)
    row_spec = pl.BlockSpec(right_side.shape, whole)
    var_spec = pl.BlockSpec(var_row.shape, whole)
    pay_shape = (80, width // 4)
    smem = pl.BlockSpec(memory_space=pltpu.SMEM)
    vmem = pl.BlockSpec(memory_space=pltpu.VMEM)
    in_hbm = lambda array: pltpu.with_memory_space_constraint(array, pltpu.HBM)
    pay_zero, pay_one, right, left, rounded = pl.pallas_call(
        payload_kernel,
        in_specs=[smem, vmem, vmem],
        out_shape=[
            shape((96, width // 4), BF16),
            shape(pay_shape, BF16),
            shape((KDIM, width), BF16),
            shape((width, KDIM), BF16),
            shape(right_side.shape, BF16),
        ],
        compiler_params=params,
        name="payload",
    )(tile_list, in_hbm(features), in_hbm(right_side))
    me = jnp.full((1,), lax.axis_index("row"), jnp.int32)
    any_spec = pl.BlockSpec(memory_space=pl.ANY)

    def own_part(rows, arrived):
        blocks = own_blocks(rows, steps)
        tiles, sums = pl.pallas_call(
            functools.partial(own_kernel, rows),
            in_specs=[vmem, vmem, vmem, any_spec],
            out_specs=[any_spec, vmem],
            out_shape=[pltpu.HBM((len(blocks), ROWS, ROWS), BF16), shape(right_side.shape, F32)],
            scratch_shapes=[
                pltpu.VMEM((len(blocks), ROWS, ROWS), BF16),
                pltpu.SemaphoreType.DMA((len(blocks),)),
            ],
            compiler_params=params,
            cost_estimate=pl.CostEstimate(
                flops=5_000_000_000, bytes_accessed=2 * len(blocks) * ROWS * ROWS, transcendentals=0
            ),
            name=f"own_tile_{rows[0]}",
        )(left, right, rounded, arrived)
        return blocks, tiles, sums

    first_masks, *later = gather_levels(count)
    first_level = lambda pay: jnp.concatenate(
        [pay] + [swap(pay, mask, count) for mask in first_masks], axis=0
    )
    near_zero = first_level(pay_zero)
    own_parts = [own_part(range(1), right)]
    near_zero = gate(near_zero, own_parts[0][2])
    near_one = first_level(gate(pay_one, own_parts[0][2]))
    own_parts.append(own_part(range(1, steps), near_zero))
    near_one = gate(near_one, own_parts[1][2])
    zero, places = [near_zero], [0]
    for level, masks in enumerate(later):
        zero = zero + [swap(array, mask, count) for mask in masks for array in zero]
        places = places + [mask ^ place for mask in masks for place in places]
        if level == 0:
            zero[-1] = gate(zero[-1], own_parts[1][2])
    one = [near_one] + [swap(near_one, place, count) for place in places[1:]]
    each = len(first_masks) + 1
    zero_at = [(at, row * 96) for at in range(len(zero)) for row in range(each)]
    one_at = [(at, row * 80) for at in range(len(one)) for row in range(each)]

    half = steps // 2

    def front_at(k, i, *ignored):
        return (jnp.minimum(k, FRONT - 1), jnp.where(k < FRONT, i, half - 1), 0)

    def back_at(k, i, *ignored):
        return (jnp.maximum(k - FRONT, 0), jnp.where(k < FRONT, 0, i), 0)

    half_specs = [pl.BlockSpec((1, ROWS, width), front_at), pl.BlockSpec((1, ROWS, width), back_at)]
    half_shapes = [
        pltpu.VMEM((FRONT, width // 2, width), BF16),
        pltpu.HBM((most - FRONT, width // 2, width), BF16),
    ]
    half_scratch = [
        pltpu.VMEM((width // 2, KDIM), BF16),
        pltpu.VMEM((rhs_count, width // 2), BF16),
        pltpu.VMEM((2,) + pay_shape, BF16),
        pltpu.SemaphoreType.DMA((2,)),
    ]
    right_spec = pl.BlockSpec(right.shape, whole)
    send_shape = (rhs_count, width + TAIL)
    front_zero, back_zero, half_sum, slots = pl.pallas_call(
        functools.partial(pair_zero_kernel, zero_at),
        grid_spec=pltpu.PrefetchScalarGridSpec(
            num_scalar_prefetch=1,
            grid=(most, half),
            in_specs=[right_spec] + [row_spec] * PARTS + [any_spec] * len(zero),
            out_specs=half_specs + [row_spec, smem],
            scratch_shapes=half_scratch
            + [
                pltpu.VMEM((count, 16, 128), BF16),
                pltpu.VMEM((count, 128), jnp.int32),
                pltpu.SMEM((count, 128), jnp.int32),
                pltpu.SemaphoreType.DMA((count,)),
            ],
        ),
        out_shape=half_shapes
        + [shape(right_side.shape, F32), shape((most + 2,), jnp.int32)],
        compiler_params=params,
        name="pair_zero",
    )(me, right, *[part[2] for part in own_parts], *zero)
    front_one, back_one, image, send = pl.pallas_call(
        functools.partial(pair_one_kernel, one_at),
        grid_spec=pltpu.PrefetchScalarGridSpec(
            num_scalar_prefetch=1,
            grid=(most, half),
            in_specs=[right_spec, row_spec, row_spec, var_spec] + [any_spec] * len(one),
            out_specs=half_specs + [row_spec, pl.BlockSpec(send_shape, whole)],
            scratch_shapes=half_scratch,
        ),
        out_shape=half_shapes + [shape(right_side.shape, F32), shape(send_shape, BF16)],
        compiler_params=params,
        name="pair_one",
    )(slots, right, half_sum, right_side, var_row, *one)
    fronts = [pltpu.with_memory_space_constraint(part, pltpu.VMEM) for part in (front_zero, front_one)]
    backs = [pltpu.with_memory_space_constraint(part, pltpu.HBM) for part in (back_zero, back_one)]

    def front_zero_at(k, i, *ignored):
        return (jnp.minimum(k, FRONT - 1), jnp.where(k < FRONT, jnp.minimum(i, half - 1), half - 1), 0)

    def front_one_at(k, i, *ignored):
        return (jnp.minimum(k, FRONT - 1), jnp.where(k < FRONT, jnp.maximum(i - half, 0), half - 1), 0)

    every_send = tree_gather(send, count)[-1]
    own_again = [
        pl.pallas_call(
            functools.partial(own_again_kernel, blocks),
            in_specs=[any_spec, pl.BlockSpec(send_shape, whole)],
            out_specs=row_spec,
            out_shape=shape(right_side.shape, F32),
            scratch_shapes=[
                pltpu.VMEM((len(blocks), ROWS, ROWS), BF16),
                pltpu.SemaphoreType.DMA((len(blocks),)),
            ],
            compiler_params=params,
            cost_estimate=pl.CostEstimate(
                flops=5_000_000_000, bytes_accessed=2 * len(blocks) * ROWS * ROWS, transcendentals=0
            ),
            name=f"own_again_{part}",
        )(in_hbm(tiles), send)
        for part, (blocks, tiles, _) in enumerate(own_parts)
    ]
    dots_spec = pl.BlockSpec((rhs_count, TAIL), whole)
    rows, dots, steps_one = pl.pallas_call(
        again_kernel,
        grid_spec=pltpu.PrefetchScalarGridSpec(
            num_scalar_prefetch=1,
            grid=(most, steps),
            in_specs=[
                pl.BlockSpec((1, ROWS, width), front_zero_at),
                pl.BlockSpec((1, ROWS, width), front_one_at),
                any_spec,
                any_spec,
                pl.BlockSpec((1,) + send_shape, lambda k, i, s: (s[1 + k], 0, 0)),
                pl.BlockSpec((count, rhs_count, TAIL), lambda k, i, s: (0, 0, width // TAIL)),
                row_spec,
                var_spec,
                row_spec,
            ]
            + [row_spec] * PARTS,
            out_specs=[
                pl.BlockSpec((4 * rhs_count, width), whole),
                dots_spec,
                dots_spec,
            ],
            scratch_shapes=[
                pltpu.VMEM(right_side.shape, F32),
                pltpu.VMEM((HELD, ROWS, width), BF16),
                pltpu.SemaphoreType.DMA((HELD,)),
            ],
        ),
        out_shape=[
            shape((4 * rhs_count, width), F32),
            shape((rhs_count, TAIL), F32),
            shape((rhs_count, TAIL), F32),
        ],
        compiler_params=params,
        name="pair_again",
    )(slots, *fronts, *backs, every_send, every_send, right_side, var_row, image, *own_again)

    dots = tree_sum(dots, count)
    ordered = pl.pallas_call(
        order_kernel,
        out_shape=shape(rows.shape, F32),
        compiler_params=params,
        name="curve_order",
    )(rows, hilbert_order)
    norm, curve = steps_one[:, 0:1], steps_one[:, 1:2]
    length = norm / curve
    norm_next = dots[:, 0:1]
    ratio = norm_next / norm
    curve_next = dots[:, 1:2] + ratio * (dots[:, 2:3] + dots[:, 3:4]) + ratio * ratio * curve
    length_next = norm_next / curve_next
    rhs_o, res_o, image_o, res_image_o = [ordered[at : at + 8] for at in range(0, 32, 8)]
    solved = length * rhs_o + length_next * (res_o + ratio * rhs_o)
    residual = res_o - length_next * (res_image_o + ratio * image_o)
    return (solved, residual)


def solution(mesh):
    in_specs = (
        P(None, ("group", "row")),
        P(None, ("group", "row")),
        P(("group", "row")),
        P(("group", "row"), None),
        P(("group", "row"), None, None),
    )
    out_specs = (P(None, ("group", "row")), P(None, ("group", "row")))
    return jax.shard_map(local, mesh=mesh, in_specs=in_specs, out_specs=out_specs, check_vma=False)
```

```python
import functools

import jax
import jax.numpy as jnp
import numpy as np
from jax import lax
from jax.experimental import pallas as pl
from jax.experimental.pallas import tpu as pltpu
from jax.sharding import PartitionSpec as P

SHRINK = 0.95
GRAM = SHRINK * SHRINK
SCALE = 20.0 * (20.0 / 19.0) ** 19
DIAGONAL = float(1.0 - SCALE * float(np.float32(1.0 / SCALE).astype(jnp.bfloat16)))
KDIM = 128
ROWS = 512
PARTS = 2
COLS = 1024
FRONT = 3
HELD = 4
TAIL = 128
BF16 = jnp.bfloat16
F32 = jnp.float32
CONTRACT_LANES = (((1,), (1,)), ((), ()))


def split_three(value):
    high = value.astype(BF16).astype(F32)
    rest = value - high
    middle = rest.astype(BF16).astype(F32)
    return high, middle, rest - middle


def norm_rows(norm, first):
    high, middle, low = split_three(norm)
    row = lax.broadcasted_iota(jnp.int32, (32, norm.shape[1]), 0)
    out = jnp.where(row < 6, 1.0, 0.0)
    out = jnp.where(row == first, high, out)
    out = jnp.where(row == first + 1, middle, out)
    return jnp.where(row == first + 2, low, out).astype(BF16)


def own_factor(feat):
    wide = feat.astype(F32)
    norm = jnp.sum(wide * wide, axis=0, keepdims=True) * GRAM
    pieces = split_three(wide * (-2.0 * GRAM))
    return jnp.concatenate([piece.astype(BF16) for piece in pieces] + [norm_rows(norm, 0)], axis=0)


def other_factor(feat):
    wide = feat.astype(F32)
    norm = jnp.sum(wide * wide, axis=0, keepdims=True) * GRAM
    return jnp.transpose(jnp.concatenate([feat, feat, feat, norm_rows(norm, 3)], axis=0))


def psi_chain(dist):
    dist = jnp.maximum(dist, 1e-30)
    radius = dist * lax.rsqrt(dist)
    u = jnp.maximum(SHRINK - radius, 0.0)
    two = u * u
    four = two * two
    eight = four * four
    return (eight * eight * two * (u - two)).astype(BF16)


def psi_power(dist):
    dist = jnp.maximum(dist, 1e-30)
    radius = dist * lax.rsqrt(dist)
    u = jnp.maximum(SHRINK - radius, 1e-30)
    return (jnp.exp2(19.0 * lax.log2(u)) * (1.0 - u)).astype(BF16)


def tile_unit(left, right, vec, tile_ref, psis, strip):
    dist = jnp.dot(left, right, preferred_element_type=F32)
    parts = []
    for index, sub in enumerate(range(0, left.shape[0], strip)):
        part = psis[index % len(psis)](dist[sub : sub + strip])
        tile_ref[sub : sub + strip, :] = part
        parts.append(part)
    return jnp.dot(vec, jnp.concatenate(parts, axis=0), preferred_element_type=F32)


def unpack(pay):
    return jnp.concatenate([pay[:32], pay[32:64]], axis=1), jnp.concatenate([pay[64:72], pay[72:80]], axis=1)


def own_blocks(rows, count):
    return [(row, col) for row in rows for col in range(row, count)]


def own_kernel(
    rows, left_ref, right_ref, vec_ref, arrived_ref, out_ref, sum_ref, tile_ref, sem_ref
):
    sum_ref[...] = jnp.zeros_like(sum_ref)
    count = vec_ref.shape[1] // ROWS
    piece = lambda index: pl.ds(pl.multiple_of(index * ROWS, ROWS), ROWS)
    save = lambda at: pltpu.make_async_copy(tile_ref.at[at], out_ref.at[at], sem_ref.at[at])

    def row_step(row, at):
        def col_step(col, at):
            sum_ref[:, piece(col)] += tile_unit(
                left_ref[piece(row), :], right_ref[:, piece(col)], vec_ref[:, piece(row)],
                tile_ref.at[at], (psi_power,), 64,
            )
            save(at).start()

            @pl.when(row != col)
            def _():
                sum_ref[:, piece(row)] += lax.dot_general(
                    vec_ref[:, piece(col)], tile_ref[at], CONTRACT_LANES,
                    preferred_element_type=F32,
                )

            return at + 1

        return lax.fori_loop(row, count, col_step, at)

    lax.fori_loop(rows[0], rows[-1] + 1, row_step, 0)
    for at in range(tile_ref.shape[0]):
        save(at).wait()


def own_again_kernel(blocks, in_ref, vec_ref, sum_ref, tile_ref, sem_ref):
    load = lambda index: pltpu.make_async_copy(
        in_ref.at[index], tile_ref.at[index], sem_ref.at[index]
    )
    for index in range(len(blocks)):
        load(index).start()
    sum_ref[...] = jnp.zeros_like(sum_ref)
    piece = lambda index: slice(index * ROWS, (index + 1) * ROWS)
    for index, (row, col) in enumerate(blocks):
        load(index).wait()
        sum_ref[:, piece(col)] += jnp.dot(
            vec_ref[:, piece(row)], tile_ref[index], preferred_element_type=F32
        )
        if row != col:
            sum_ref[:, piece(row)] += lax.dot_general(
                vec_ref[:, piece(col)], tile_ref[index], CONTRACT_LANES, preferred_element_type=F32
            )


def payload_kernel(
    list_ref, feat_ref, rhs_ref, pay_zero_ref, pay_one_ref, right_ref, left_ref, vec_ref
):
    feat = feat_ref[...]
    rounded = rhs_ref[...].astype(BF16)
    quarter = feat.shape[1] // 4
    for half, pay_ref in enumerate((pay_zero_ref, pay_one_ref)):
        first, second = [slice(at * quarter, (at + 1) * quarter) for at in (2 * half, 2 * half + 1)]
        pay_ref[:32] = feat[:, first]
        pay_ref[32:64] = feat[:, second]
        pay_ref[64:80] = jnp.concatenate([rounded[:, first], rounded[:, second]], axis=0)
    lane = lax.broadcasted_iota(jnp.int32, (16, quarter), 1)
    numbers = jnp.full(lane.shape, -1, jnp.int32)
    for entry in range(list_ref.shape[1]):
        numbers = jnp.where(lane == entry, list_ref[0, entry, 1], numbers)
    pay_zero_ref[80:96] = numbers.astype(F32).astype(BF16)
    right_ref[...] = own_factor(feat)
    left_ref[...] = other_factor(feat)
    vec_ref[...] = rounded


def find_partners(lists_ref, me, slots_ref):
    count, most = lists_ref.shape[0], slots_ref.shape[0] - 2
    for at in range(slots_ref.shape[0]):
        slots_ref[at] = 0
    total = jnp.int32(0)
    for at, place in enumerate(gather_places(count)):
        if at == 0:
            continue
        number = me ^ place
        hit = jnp.bool_(False)
        for entry in range(most):
            hit = hit | (lists_ref[at, entry] == me) | (lists_ref[0, entry] == number)
        slots_ref[1 + total] = jnp.where(hit, at, 0)
        total = total + hit.astype(jnp.int32)
    slots_ref[0] = total


def fetch_from(block_at, block_refs, slots_ref, pay_ref, sem_ref):
    def fetch(which):
        for at, (index, row) in enumerate(block_at):
            @pl.when(slots_ref[1 + which] == at)
            def _():
                pltpu.make_async_copy(
                    block_refs[index].at[pl.ds(row, 80)],
                    pay_ref.at[which % 2],
                    sem_ref.at[which % 2],
                ).start()

    return fetch


def half_tiles(psis, strip, slots_ref, right_ref, fetch, front_ref, back_ref, sum_ref, left_ref, vec_ref, pay_ref, sem_ref):
    slot, step = pl.program_id(0), pl.program_id(1)

    @pl.when((slot == 0) & (step == 0) & (slots_ref[0] > 0))
    def _():
        fetch(0)

    @pl.when(slot < slots_ref[0])
    def _():
        @pl.when(step == 0)
        def _():
            pltpu.make_async_copy(
                pay_ref.at[(slot + 1) % 2], pay_ref.at[slot % 2], sem_ref.at[slot % 2]
            ).wait()

            @pl.when(slot + 1 < slots_ref[0])
            def _():
                fetch(slot + 1)

            feat, vec = unpack(pay_ref[slot % 2])
            left_ref[...] = other_factor(feat)
            vec_ref[...] = vec

        rows = pl.ds(pl.multiple_of(step * ROWS, ROWS), ROWS)
        left, vec = left_ref[rows, :], vec_ref[:, rows]
        for tile_ref, here in ((front_ref, slot < FRONT), (back_ref, slot >= FRONT)):
            @pl.when(here)
            def _():
                def unit(index, carry):
                    cols = pl.ds(pl.multiple_of(index * COLS, COLS), COLS)
                    sum_ref[:, cols] += tile_unit(
                        left, right_ref[:, cols], vec, tile_ref.at[0, :, cols], psis, strip
                    )
                    return carry

                lax.fori_loop(0, right_ref.shape[1] // COLS, unit, 0)


def pair_zero_kernel(block_at, me_ref, right_ref, *refs):
    first_refs, block_refs = refs[:PARTS], refs[PARTS:-12]
    front_ref, back_ref, sum_ref, slots_ref = refs[-12:-8]
    left_ref, vec_ref, pay_ref, sem_ref, strip_ref, list_ref, lists_ref, strip_sem_ref = refs[-8:]

    @pl.when((pl.program_id(0) == 0) & (pl.program_id(1) == 0))
    def _():
        strips = [
            pltpu.make_async_copy(
                block_refs[index].at[pl.ds(row + 80, 16), pl.ds(0, 128)],
                strip_ref.at[at],
                strip_sem_ref.at[at],
            )
            for at, (index, row) in enumerate(block_at)
        ]
        for strip in strips:
            strip.start()
        sum_ref[...] = functools.reduce(jnp.add, [first_ref[...] for first_ref in first_refs])
        for at, strip in enumerate(strips):
            strip.wait()
            list_ref[at : at + 1, :] = strip_ref[at].astype(F32)[:1].astype(jnp.int32)
        numbers = pltpu.make_async_copy(list_ref, lists_ref, strip_sem_ref.at[0])
        numbers.start()
        numbers.wait()
        find_partners(lists_ref, me_ref[0], slots_ref)

    fetch = fetch_from(block_at, block_refs, slots_ref, pay_ref, sem_ref)
    half_tiles(
        (psi_power, psi_chain), 64, slots_ref, right_ref, fetch, front_ref, back_ref, sum_ref, left_ref, vec_ref, pay_ref, sem_ref
    )


def pair_one_kernel(block_at, slots_ref, right_ref, first_ref, rhs_ref, var_ref, *refs):
    block_refs = refs[:-8]
    front_ref, back_ref, image_ref, send_ref, left_ref, vec_ref, pay_ref, sem_ref = refs[-8:]
    slot, step = pl.program_id(0), pl.program_id(1)

    @pl.when((slot == 0) & (step == 0))
    def _():
        image_ref[...] = first_ref[...]

    fetch = fetch_from(block_at, block_refs, slots_ref, pay_ref, sem_ref)
    half_tiles(
        (psi_power,), 128, slots_ref, right_ref, fetch, front_ref, back_ref, image_ref, left_ref, vec_ref, pay_ref, sem_ref
    )

    @pl.when((slot == pl.num_programs(0) - 1) & (step == pl.num_programs(1) - 1))
    def _():
        rhs = rhs_ref[...]
        width = rhs.shape[1]
        image = (var_ref[...] + DIAGONAL) * rhs + SCALE * image_ref[...]
        image_ref[...] = image
        send_ref[:, :width] = image.astype(BF16)
        pieces = split_three(jnp.sum(rhs * rhs, axis=1, keepdims=True))
        pieces += split_three(jnp.sum(rhs * image, axis=1, keepdims=True))
        lane = lax.broadcasted_iota(jnp.int32, (rhs.shape[0], TAIL), 1)
        tail = jnp.zeros((rhs.shape[0], TAIL), F32)
        for place, piece in enumerate(pieces):
            tail = jnp.where(lane == place, piece, tail)
        send_ref[:, width:] = tail.astype(BF16)


def again_kernel(
    slots_ref, front_zero_ref, front_one_ref, back_zero_ref, back_one_ref,
    vec_ref, tails_ref, rhs_ref, var_ref, image_ref, *refs
):
    first_refs = refs[:PARTS]
    rows_ref, dots_ref, step_ref, sum_ref, held_ref, sem_ref = refs[PARTS:]
    slot, step = pl.program_id(0), pl.program_id(1)
    width = rhs_ref.shape[1]
    steps = width // ROWS
    half = steps // 2
    parts = (slots_ref[0] - FRONT) * steps

    def fetch(part, back_ref, first):
        at = pl.ds(pl.multiple_of((part % steps - first) * ROWS, ROWS), ROWS)
        return pltpu.make_async_copy(
            back_ref.at[part // steps, at], held_ref.at[part % HELD], sem_ref.at[part % HELD]
        )

    def start(part):
        @pl.when((part < parts) & (part % steps < half))
        def _():
            fetch(part, back_zero_ref, 0).start()

        @pl.when((part < parts) & (part % steps >= half))
        def _():
            fetch(part, back_one_ref, half).start()

    @pl.when((slot == 0) & (step == 0))
    def _():
        sum_ref[...] = functools.reduce(jnp.add, [first_ref[...] for first_ref in first_refs])
        for part in range(HELD):
            start(part)

    @pl.when(slot < slots_ref[0])
    def _():
        at = pl.multiple_of(step * ROWS, ROWS)
        for front_ref, here in ((front_zero_ref, step < half), (front_one_ref, step >= half)):
            @pl.when((slot < FRONT) & here)
            def _():
                sum_ref[...] += jnp.dot(
                    vec_ref[0, :, pl.ds(at, ROWS)], front_ref[0], preferred_element_type=F32
                )

        @pl.when(slot >= FRONT)
        def _():
            part = (slot - FRONT) * steps + step
            fetch(part % HELD, back_zero_ref, part % HELD // half * half).wait()
            sum_ref[...] += jnp.dot(
                vec_ref[0, :, pl.ds(at, ROWS)], held_ref[part % HELD], preferred_element_type=F32
            )
            start(part + HELD)

    @pl.when((slot == pl.num_programs(0) - 1) & (step == pl.num_programs(1) - 1))
    def _():
        rhs = rhs_ref[...]
        image = image_ref[...]
        total = jnp.sum(tails_ref[...].astype(F32), axis=0)
        norm = total[:, 0:1] + total[:, 1:2] + total[:, 2:3]
        curve = total[:, 3:4] + total[:, 4:5] + total[:, 5:6]
        length = norm / curve
        second = (var_ref[...] + DIAGONAL) * image + SCALE * sum_ref[...]
        res = rhs - length * image
        res_image = image - length * second
        rows_ref[0:8] = rhs
        rows_ref[8:16] = res
        rows_ref[16:24] = image
        rows_ref[24:32] = res_image
        lane = lax.broadcasted_iota(jnp.int32, (rhs.shape[0], TAIL), 1)
        dots = jnp.zeros((rhs.shape[0], TAIL), F32)
        for place, product in enumerate((res * res, res * res_image, res * image, rhs * res_image)):
            dots = jnp.where(lane == place, jnp.sum(product, axis=1, keepdims=True), dots)
        dots_ref[...] = dots
        step_ref[...] = jnp.where(lane == 0, norm, jnp.where(lane == 1, curve, 0.0))


def order_kernel(rows_ref, perm_ref, out_ref):
    rows = rows_ref[...]
    count, width = rows.shape
    pieces = jnp.concatenate([piece for piece in split_three(rows)], axis=0).astype(BF16)
    perm = perm_ref[...]
    chunk = 256
    for col in range(0, width, chunk):
        total = jnp.zeros((3 * count, chunk), F32)
        for at in range(0, width, chunk):
            index = lax.broadcasted_iota(jnp.int32, (chunk, chunk), 0) + at
            pick = jnp.where(index == perm[:, col : col + chunk], 1.0, 0.0).astype(BF16)
            total += jnp.dot(pieces[:, at : at + chunk], pick, preferred_element_type=F32)
        out_ref[:, col : col + chunk] = total[:count] + total[count : 2 * count] + total[2 * count :]


def swap(value, mask, count):
    return lax.ppermute(value, "row", [(i, i ^ mask) for i in range(count)])


def levels(count, sizes):
    bits = count.bit_length() - 1
    out = []
    sizes = list(sizes)
    while bits:
        take = min(sizes.pop(0) if sizes else 1, bits)
        bits -= take
        out.append([mask << bits for mask in range(1, 1 << take)])
    return out


def tree_sum(value, count):
    for masks in levels(count, [2, 2, 2]):
        others = [swap(value, mask, count) for mask in masks]
        if len(masks) == 3:
            value = (value + others[0]) + (others[1] + others[2])
        else:
            value = value + others[0]
    return value


def gather_levels(count):
    return levels(count, [2] if count <= 16 else [2, 2])


def gather_places(count):
    places = [0]
    for masks in gather_levels(count):
        places = places + [place ^ mask for mask in masks for place in places]
    return places


def tree_gather(value, count):
    blocks, out = value[None], []
    for masks in gather_levels(count):
        blocks = jnp.concatenate([blocks] + [swap(blocks, mask, count) for mask in masks], axis=0)
        out.append(blocks)
    return out


def gate(block, behind):
    return pl.pallas_call(
        lambda *refs: None,
        in_specs=[pl.BlockSpec(memory_space=pl.ANY)] * 2,
        out_specs=pl.BlockSpec(memory_space=pl.ANY),
        out_shape=jax.ShapeDtypeStruct(block.shape, block.dtype),
        input_output_aliases={0: 0},
        compiler_params=pltpu.CompilerParams(vmem_limit_bytes=1024 * 1024),
        name="gate",
    )(block, behind)


def local(features, right_side, variance, hilbert_order, tile_list):
    width = features.shape[1]
    rhs_count = right_side.shape[0]
    count = lax.axis_size("row")
    most = tile_list.shape[1]
    steps = width // ROWS
    shape = jax.ShapeDtypeStruct
    params = pltpu.CompilerParams(vmem_limit_bytes=10 * 1024 * 1024)
    var_row = variance[None, :]

    whole = lambda *ignored: (0, 0)
    row_spec = pl.BlockSpec(right_side.shape, whole)
    var_spec = pl.BlockSpec(var_row.shape, whole)
    pay_shape = (80, width // 4)
    smem = pl.BlockSpec(memory_space=pltpu.SMEM)
    vmem = pl.BlockSpec(memory_space=pltpu.VMEM)
    in_hbm = lambda array: pltpu.with_memory_space_constraint(array, pltpu.HBM)
    pay_zero, pay_one, right, left, rounded = pl.pallas_call(
        payload_kernel,
        in_specs=[smem, vmem, vmem],
        out_shape=[
            shape((96, width // 4), BF16),
            shape(pay_shape, BF16),
            shape((KDIM, width), BF16),
            shape((width, KDIM), BF16),
            shape(right_side.shape, BF16),
        ],
        compiler_params=params,
        name="payload",
    )(tile_list, in_hbm(features), in_hbm(right_side))
    me = jnp.full((1,), lax.axis_index("row"), jnp.int32)
    any_spec = pl.BlockSpec(memory_space=pl.ANY)

    def own_part(rows, arrived):
        blocks = own_blocks(rows, steps)
        tiles, sums = pl.pallas_call(
            functools.partial(own_kernel, rows),
            in_specs=[vmem, vmem, vmem, any_spec],
            out_specs=[any_spec, vmem],
            out_shape=[pltpu.HBM((len(blocks), ROWS, ROWS), BF16), shape(right_side.shape, F32)],
            scratch_shapes=[
                pltpu.VMEM((len(blocks), ROWS, ROWS), BF16),
                pltpu.SemaphoreType.DMA((len(blocks),)),
            ],
            compiler_params=params,
            cost_estimate=pl.CostEstimate(
                flops=5_000_000_000, bytes_accessed=2 * len(blocks) * ROWS * ROWS, transcendentals=0
            ),
            name=f"own_tile_{rows[0]}",
        )(left, right, rounded, arrived)
        return blocks, tiles, sums

    first_masks, *later = gather_levels(count)
    first_level = lambda pay: jnp.concatenate(
        [pay] + [swap(pay, mask, count) for mask in first_masks], axis=0
    )
    near_zero = first_level(pay_zero)
    own_parts = [own_part(range(1), right)]
    near_zero = gate(near_zero, own_parts[0][2])
    near_one = first_level(gate(pay_one, own_parts[0][2]))
    own_parts.append(own_part(range(1, steps), near_zero))
    near_one = gate(near_one, own_parts[1][2])
    zero, places = [near_zero], [0]
    for level, masks in enumerate(later):
        zero = zero + [swap(array, mask, count) for mask in masks for array in zero]
        places = places + [mask ^ place for mask in masks for place in places]
        if level == 0:
            zero[-1] = gate(zero[-1], own_parts[1][2])
    one = [near_one] + [swap(near_one, place, count) for place in places[1:]]
    each = len(first_masks) + 1
    zero_at = [(at, row * 96) for at in range(len(zero)) for row in range(each)]
    one_at = [(at, row * 80) for at in range(len(one)) for row in range(each)]

    half = steps // 2

    def front_at(k, i, *ignored):
        return (jnp.minimum(k, FRONT - 1), jnp.where(k < FRONT, i, half - 1), 0)

    def back_at(k, i, *ignored):
        return (jnp.maximum(k - FRONT, 0), jnp.where(k < FRONT, 0, i), 0)

    half_specs = [pl.BlockSpec((1, ROWS, width), front_at), pl.BlockSpec((1, ROWS, width), back_at)]
    half_shapes = [
        pltpu.VMEM((FRONT, width // 2, width), BF16),
        pltpu.HBM((most - FRONT, width // 2, width), BF16),
    ]
    half_scratch = [
        pltpu.VMEM((width // 2, KDIM), BF16),
        pltpu.VMEM((rhs_count, width // 2), BF16),
        pltpu.VMEM((2,) + pay_shape, BF16),
        pltpu.SemaphoreType.DMA((2,)),
    ]
    right_spec = pl.BlockSpec(right.shape, whole)
    send_shape = (rhs_count, width + TAIL)
    front_zero, back_zero, half_sum, slots = pl.pallas_call(
        functools.partial(pair_zero_kernel, zero_at),
        grid_spec=pltpu.PrefetchScalarGridSpec(
            num_scalar_prefetch=1,
            grid=(most, half),
            in_specs=[right_spec] + [row_spec] * PARTS + [any_spec] * len(zero),
            out_specs=half_specs + [row_spec, smem],
            scratch_shapes=half_scratch
            + [
                pltpu.VMEM((count, 16, 128), BF16),
                pltpu.VMEM((count, 128), jnp.int32),
                pltpu.SMEM((count, 128), jnp.int32),
                pltpu.SemaphoreType.DMA((count,)),
            ],
        ),
        out_shape=half_shapes
        + [shape(right_side.shape, F32), shape((most + 2,), jnp.int32)],
        compiler_params=params,
        name="pair_zero",
    )(me, right, *[part[2] for part in own_parts], *zero)
    front_one, back_one, image, send = pl.pallas_call(
        functools.partial(pair_one_kernel, one_at),
        grid_spec=pltpu.PrefetchScalarGridSpec(
            num_scalar_prefetch=1,
            grid=(most, half),
            in_specs=[right_spec, row_spec, row_spec, var_spec] + [any_spec] * len(one),
            out_specs=half_specs + [row_spec, pl.BlockSpec(send_shape, whole)],
            scratch_shapes=half_scratch,
        ),
        out_shape=half_shapes + [shape(right_side.shape, F32), shape(send_shape, BF16)],
        compiler_params=params,
        name="pair_one",
    )(slots, right, half_sum, right_side, var_row, *one)
    fronts = [pltpu.with_memory_space_constraint(part, pltpu.VMEM) for part in (front_zero, front_one)]
    backs = [pltpu.with_memory_space_constraint(part, pltpu.HBM) for part in (back_zero, back_one)]

    def front_zero_at(k, i, *ignored):
        return (jnp.minimum(k, FRONT - 1), jnp.where(k < FRONT, jnp.minimum(i, half - 1), half - 1), 0)

    def front_one_at(k, i, *ignored):
        return (jnp.minimum(k, FRONT - 1), jnp.where(k < FRONT, jnp.maximum(i - half, 0), half - 1), 0)

    every_send = tree_gather(send, count)[-1]
    own_again = [
        pl.pallas_call(
            functools.partial(own_again_kernel, blocks),
            in_specs=[any_spec, pl.BlockSpec(send_shape, whole)],
            out_specs=row_spec,
            out_shape=shape(right_side.shape, F32),
            scratch_shapes=[
                pltpu.VMEM((len(blocks), ROWS, ROWS), BF16),
                pltpu.SemaphoreType.DMA((len(blocks),)),
            ],
            compiler_params=params,
            cost_estimate=pl.CostEstimate(
                flops=5_000_000_000, bytes_accessed=2 * len(blocks) * ROWS * ROWS, transcendentals=0
            ),
            name=f"own_again_{part}",
        )(in_hbm(tiles), send)
        for part, (blocks, tiles, _) in enumerate(own_parts)
    ]
    dots_spec = pl.BlockSpec((rhs_count, TAIL), whole)
    rows, dots, steps_one = pl.pallas_call(
        again_kernel,
        grid_spec=pltpu.PrefetchScalarGridSpec(
            num_scalar_prefetch=1,
            grid=(most, steps),
            in_specs=[
                pl.BlockSpec((1, ROWS, width), front_zero_at),
                pl.BlockSpec((1, ROWS, width), front_one_at),
                any_spec,
                any_spec,
                pl.BlockSpec((1,) + send_shape, lambda k, i, s: (s[1 + k], 0, 0)),
                pl.BlockSpec((count, rhs_count, TAIL), lambda k, i, s: (0, 0, width // TAIL)),
                row_spec,
                var_spec,
                row_spec,
            ]
            + [row_spec] * PARTS,
            out_specs=[
                pl.BlockSpec((4 * rhs_count, width), whole),
                dots_spec,
                dots_spec,
            ],
            scratch_shapes=[
                pltpu.VMEM(right_side.shape, F32),
                pltpu.VMEM((HELD, ROWS, width), BF16),
                pltpu.SemaphoreType.DMA((HELD,)),
            ],
        ),
        out_shape=[
            shape((4 * rhs_count, width), F32),
            shape((rhs_count, TAIL), F32),
            shape((rhs_count, TAIL), F32),
        ],
        compiler_params=params,
        name="pair_again",
    )(slots, *fronts, *backs, every_send, every_send, right_side, var_row, image, *own_again)

    dots = tree_sum(dots, count)
    ordered = pl.pallas_call(
        order_kernel,
        out_shape=shape(rows.shape, F32),
        compiler_params=params,
        name="curve_order",
    )(rows, hilbert_order)
    norm, curve = steps_one[:, 0:1], steps_one[:, 1:2]
    length = norm / curve
    norm_next = dots[:, 0:1]
    ratio = norm_next / norm
    curve_next = dots[:, 1:2] + ratio * (dots[:, 2:3] + dots[:, 3:4]) + ratio * ratio * curve
    length_next = norm_next / curve_next
    rhs_o, res_o, image_o, res_image_o = [ordered[at : at + 8] for at in range(0, 32, 8)]
    solved = length * rhs_o + length_next * (res_o + ratio * rhs_o)
    residual = res_o - length_next * (res_image_o + ratio * image_o)
    return (solved, residual)


def solution(mesh):
    in_specs = (
        P(None, ("group", "row")),
        P(None, ("group", "row")),
        P(("group", "row")),
        P(("group", "row"), None),
        P(("group", "row"), None, None),
    )
    out_specs = (P(None, ("group", "row")), P(None, ("group", "row")))
    return jax.shard_map(local, mesh=mesh, in_specs=in_specs, out_specs=out_specs, check_vma=False)
```

```python
import functools

import jax
import jax.numpy as jnp
import numpy as np
from jax import lax
from jax.experimental import pallas as pl
from jax.experimental.pallas import tpu as pltpu
from jax.sharding import PartitionSpec as P

SHRINK = 0.95
GRAM = SHRINK * SHRINK
SCALE = 20.0 * (20.0 / 19.0) ** 19
DIAGONAL = float(1.0 - SCALE * float(np.float32(1.0 / SCALE).astype(jnp.bfloat16)))
KDIM = 128
ROWS = 512
PARTS = 2
PIECE = 256
STRIP = 64
FRONT = 3
HELD = 4
TAIL = 128
BF16 = jnp.bfloat16
F32 = jnp.float32
CONTRACT_LANES = (((1,), (1,)), ((), ()))


def split_three(value):
    high = value.astype(BF16).astype(F32)
    rest = value - high
    middle = rest.astype(BF16).astype(F32)
    return high, middle, rest - middle


def norm_rows(norm, first):
    high, middle, low = split_three(norm)
    row = lax.broadcasted_iota(jnp.int32, (32, norm.shape[1]), 0)
    out = jnp.where(row < 6, 1.0, 0.0)
    out = jnp.where(row == first, high, out)
    out = jnp.where(row == first + 1, middle, out)
    return jnp.where(row == first + 2, low, out).astype(BF16)


def own_factor(feat):
    wide = feat.astype(F32)
    norm = jnp.sum(wide * wide, axis=0, keepdims=True) * GRAM
    pieces = split_three(wide * (-2.0 * GRAM))
    return jnp.concatenate([piece.astype(BF16) for piece in pieces] + [norm_rows(norm, 0)], axis=0)


def other_factor(feat):
    wide = feat.astype(F32)
    norm = jnp.sum(wide * wide, axis=0, keepdims=True) * GRAM
    return jnp.transpose(jnp.concatenate([feat, feat, feat, norm_rows(norm, 3)], axis=0))


def psi_power(dist):
    dist = jnp.maximum(dist, 1e-30)
    radius = dist * lax.rsqrt(dist)
    u = jnp.maximum(SHRINK - radius, 1e-30)
    return (jnp.exp2(19.0 * lax.log2(u)) * (1.0 - u)).astype(BF16)


def tile_unit(left, right, vec, tile_ref, ahead):
    pieces = [slice(at, at + PIECE) for at in range(0, right.shape[1], PIECE)]
    gram = lambda piece: jnp.dot(left, right[:, piece], preferred_element_type=F32)
    product = lambda part: jnp.dot(vec, part, preferred_element_type=F32)
    dists = [gram(piece) for piece in pieces[:ahead]]
    parts, terms = [], []
    for index, piece in enumerate(pieces):
        if index + ahead < len(pieces):
            dists.append(gram(pieces[index + ahead]))
        dist = dists[index]
        strips = []
        for sub in range(0, left.shape[0], STRIP):
            strips.append(psi_power(dist[sub : sub + STRIP]))
            tile_ref[sub : sub + STRIP, piece] = strips[-1]
        parts.append(jnp.concatenate(strips, axis=0))
        if index >= ahead:
            terms.append(product(parts[index - ahead]))
    terms += [product(part) for part in parts[len(terms) :]]
    return jnp.concatenate(terms, axis=1)


def unpack(pay):
    return jnp.concatenate([pay[:32], pay[32:64]], axis=1), jnp.concatenate([pay[64:72], pay[72:80]], axis=1)


def own_blocks(rows, count):
    return [(row, col) for row in rows for col in range(row, count)]


def own_kernel(
    rows, left_ref, right_ref, vec_ref, arrived_ref, out_ref, sum_ref, tile_ref, sem_ref
):
    sum_ref[...] = jnp.zeros_like(sum_ref)
    count = vec_ref.shape[1] // ROWS
    piece = lambda index: pl.ds(pl.multiple_of(index * ROWS, ROWS), ROWS)
    save = lambda at: pltpu.make_async_copy(tile_ref.at[at], out_ref.at[at], sem_ref.at[at])

    def row_step(row, at):
        def col_step(col, at):
            sum_ref[:, piece(col)] += tile_unit(
                left_ref[piece(row), :], right_ref[:, piece(col)], vec_ref[:, piece(row)],
                tile_ref.at[at], 1,
            )
            save(at).start()

            @pl.when(row != col)
            def _():
                sum_ref[:, piece(row)] += lax.dot_general(
                    vec_ref[:, piece(col)], tile_ref[at], CONTRACT_LANES,
                    preferred_element_type=F32,
                )

            return at + 1

        return lax.fori_loop(row, count, col_step, at)

    lax.fori_loop(rows[0], rows[-1] + 1, row_step, 0)
    for at in range(tile_ref.shape[0]):
        save(at).wait()


def own_again_kernel(blocks, in_ref, vec_ref, sum_ref, tile_ref, sem_ref):
    load = lambda index: pltpu.make_async_copy(
        in_ref.at[index], tile_ref.at[index], sem_ref.at[index]
    )
    for index in range(len(blocks)):
        load(index).start()
    sum_ref[...] = jnp.zeros_like(sum_ref)
    piece = lambda index: slice(index * ROWS, (index + 1) * ROWS)
    for index, (row, col) in enumerate(blocks):
        load(index).wait()
        sum_ref[:, piece(col)] += jnp.dot(
            vec_ref[:, piece(row)], tile_ref[index], preferred_element_type=F32
        )
        if row != col:
            sum_ref[:, piece(row)] += lax.dot_general(
                vec_ref[:, piece(col)], tile_ref[index], CONTRACT_LANES, preferred_element_type=F32
            )


def payload_kernel(
    list_ref, feat_ref, rhs_ref, pay_zero_ref, pay_one_ref, right_ref, left_ref, vec_ref
):
    feat = feat_ref[...]
    rounded = rhs_ref[...].astype(BF16)
    quarter = feat.shape[1] // 4
    for half, pay_ref in enumerate((pay_zero_ref, pay_one_ref)):
        first, second = [slice(at * quarter, (at + 1) * quarter) for at in (2 * half, 2 * half + 1)]
        pay_ref[:32] = feat[:, first]
        pay_ref[32:64] = feat[:, second]
        pay_ref[64:80] = jnp.concatenate([rounded[:, first], rounded[:, second]], axis=0)
    lane = lax.broadcasted_iota(jnp.int32, (16, quarter), 1)
    numbers = jnp.full(lane.shape, -1, jnp.int32)
    for entry in range(list_ref.shape[1]):
        numbers = jnp.where(lane == entry, list_ref[0, entry, 1], numbers)
    pay_zero_ref[80:96] = numbers.astype(F32).astype(BF16)
    right_ref[...] = own_factor(feat)
    left_ref[...] = other_factor(feat)
    vec_ref[...] = rounded


def find_partners(lists_ref, me, slots_ref):
    count, most = lists_ref.shape[0], slots_ref.shape[0] - 2
    for at in range(slots_ref.shape[0]):
        slots_ref[at] = 0
    total = jnp.int32(0)
    for at, place in enumerate(gather_places(count)):
        if at == 0:
            continue
        number = me ^ place
        hit = jnp.bool_(False)
        for entry in range(most):
            hit = hit | (lists_ref[at, entry] == me) | (lists_ref[0, entry] == number)
        slots_ref[1 + total] = jnp.where(hit, at, 0)
        total = total + hit.astype(jnp.int32)
    slots_ref[0] = total


def fetch_from(block_at, block_refs, slots_ref, pay_ref, sem_ref):
    def fetch(which):
        for at, (index, row) in enumerate(block_at):
            @pl.when(slots_ref[1 + which] == at)
            def _():
                pltpu.make_async_copy(
                    block_refs[index].at[pl.ds(row, 80)],
                    pay_ref.at[which % 2],
                    sem_ref.at[which % 2],
                ).start()

    return fetch


def half_tiles(ahead, slots_ref, right_ref, fetch, front_ref, back_ref, sum_ref, left_ref, vec_ref, pay_ref, sem_ref):
    slot, step = pl.program_id(0), pl.program_id(1)

    @pl.when((slot == 0) & (step == 0) & (slots_ref[0] > 0))
    def _():
        fetch(0)

    @pl.when(slot < slots_ref[0])
    def _():
        @pl.when(step == 0)
        def _():
            pltpu.make_async_copy(
                pay_ref.at[(slot + 1) % 2], pay_ref.at[slot % 2], sem_ref.at[slot % 2]
            ).wait()

            @pl.when(slot + 1 < slots_ref[0])
            def _():
                fetch(slot + 1)

            feat, vec = unpack(pay_ref[slot % 2])
            left_ref[...] = other_factor(feat)
            vec_ref[...] = vec

        rows = pl.ds(pl.multiple_of(step * ROWS, ROWS), ROWS)
        left, vec = left_ref[rows, :], vec_ref[:, rows]
        for tile_ref, here in ((front_ref, slot < FRONT), (back_ref, slot >= FRONT)):
            @pl.when(here)
            def _():
                sum_ref[...] += tile_unit(left, right_ref[...], vec, tile_ref.at[0], ahead)


def pair_zero_kernel(block_at, me_ref, right_ref, *refs):
    first_refs, block_refs = refs[:PARTS], refs[PARTS:-12]
    front_ref, back_ref, sum_ref, slots_ref = refs[-12:-8]
    left_ref, vec_ref, pay_ref, sem_ref, strip_ref, list_ref, lists_ref, strip_sem_ref = refs[-8:]

    @pl.when((pl.program_id(0) == 0) & (pl.program_id(1) == 0))
    def _():
        strips = [
            pltpu.make_async_copy(
                block_refs[index].at[pl.ds(row + 80, 16), pl.ds(0, 128)],
                strip_ref.at[at],
                strip_sem_ref.at[at],
            )
            for at, (index, row) in enumerate(block_at)
        ]
        for strip in strips:
            strip.start()
        sum_ref[...] = functools.reduce(jnp.add, [first_ref[...] for first_ref in first_refs])
        for at, strip in enumerate(strips):
            strip.wait()
            list_ref[at : at + 1, :] = strip_ref[at].astype(F32)[:1].astype(jnp.int32)
        numbers = pltpu.make_async_copy(list_ref, lists_ref, strip_sem_ref.at[0])
        numbers.start()
        numbers.wait()
        find_partners(lists_ref, me_ref[0], slots_ref)

    fetch = fetch_from(block_at, block_refs, slots_ref, pay_ref, sem_ref)
    half_tiles(
        1, slots_ref, right_ref, fetch, front_ref, back_ref, sum_ref, left_ref, vec_ref, pay_ref, sem_ref
    )


def pair_one_kernel(block_at, slots_ref, right_ref, first_ref, rhs_ref, var_ref, *refs):
    block_refs = refs[:-8]
    front_ref, back_ref, image_ref, send_ref, left_ref, vec_ref, pay_ref, sem_ref = refs[-8:]
    slot, step = pl.program_id(0), pl.program_id(1)

    @pl.when((slot == 0) & (step == 0))
    def _():
        image_ref[...] = first_ref[...]

    fetch = fetch_from(block_at, block_refs, slots_ref, pay_ref, sem_ref)
    half_tiles(
        0, slots_ref, right_ref, fetch, front_ref, back_ref, image_ref, left_ref, vec_ref, pay_ref, sem_ref
    )

    @pl.when((slot == pl.num_programs(0) - 1) & (step == pl.num_programs(1) - 1))
    def _():
        rhs = rhs_ref[...]
        width = rhs.shape[1]
        image = (var_ref[...] + DIAGONAL) * rhs + SCALE * image_ref[...]
        image_ref[...] = image
        send_ref[:, :width] = image.astype(BF16)
        pieces = split_three(jnp.sum(rhs * rhs, axis=1, keepdims=True))
        pieces += split_three(jnp.sum(rhs * image, axis=1, keepdims=True))
        lane = lax.broadcasted_iota(jnp.int32, (rhs.shape[0], TAIL), 1)
        tail = jnp.zeros((rhs.shape[0], TAIL), F32)
        for place, piece in enumerate(pieces):
            tail = jnp.where(lane == place, piece, tail)
        send_ref[:, width:] = tail.astype(BF16)


def again_kernel(
    slots_ref, front_zero_ref, front_one_ref, back_zero_ref, back_one_ref,
    vec_ref, tails_ref, rhs_ref, var_ref, image_ref, *refs
):
    first_refs = refs[:PARTS]
    rows_ref, dots_ref, step_ref, sum_ref, held_ref, sem_ref = refs[PARTS:]
    slot, step = pl.program_id(0), pl.program_id(1)
    width = rhs_ref.shape[1]
    steps = width // ROWS
    half = steps // 2
    parts = (slots_ref[0] - FRONT) * steps

    def fetch(part, back_ref, first):
        at = pl.ds(pl.multiple_of((part % steps - first) * ROWS, ROWS), ROWS)
        return pltpu.make_async_copy(
            back_ref.at[part // steps, at], held_ref.at[part % HELD], sem_ref.at[part % HELD]
        )

    def start(part):
        @pl.when((part < parts) & (part % steps < half))
        def _():
            fetch(part, back_zero_ref, 0).start()

        @pl.when((part < parts) & (part % steps >= half))
        def _():
            fetch(part, back_one_ref, half).start()

    @pl.when((slot == 0) & (step == 0))
    def _():
        sum_ref[...] = functools.reduce(jnp.add, [first_ref[...] for first_ref in first_refs])
        for part in range(HELD):
            start(part)

    @pl.when(slot < slots_ref[0])
    def _():
        at = pl.multiple_of(step * ROWS, ROWS)
        for front_ref, here in ((front_zero_ref, step < half), (front_one_ref, step >= half)):
            @pl.when((slot < FRONT) & here)
            def _():
                sum_ref[...] += jnp.dot(
                    vec_ref[0, :, pl.ds(at, ROWS)], front_ref[0], preferred_element_type=F32
                )

        @pl.when(slot >= FRONT)
        def _():
            part = (slot - FRONT) * steps + step
            fetch(part % HELD, back_zero_ref, part % HELD // half * half).wait()
            sum_ref[...] += jnp.dot(
                vec_ref[0, :, pl.ds(at, ROWS)], held_ref[part % HELD], preferred_element_type=F32
            )
            start(part + HELD)

    @pl.when((slot == pl.num_programs(0) - 1) & (step == pl.num_programs(1) - 1))
    def _():
        rhs = rhs_ref[...]
        image = image_ref[...]
        total = jnp.sum(tails_ref[...].astype(F32), axis=0)
        norm = total[:, 0:1] + total[:, 1:2] + total[:, 2:3]
        curve = total[:, 3:4] + total[:, 4:5] + total[:, 5:6]
        length = norm / curve
        second = (var_ref[...] + DIAGONAL) * image + SCALE * sum_ref[...]
        res = rhs - length * image
        res_image = image - length * second
        rows_ref[0:8] = rhs
        rows_ref[8:16] = res
        rows_ref[16:24] = image
        rows_ref[24:32] = res_image
        lane = lax.broadcasted_iota(jnp.int32, (rhs.shape[0], TAIL), 1)
        dots = jnp.zeros((rhs.shape[0], TAIL), F32)
        for place, product in enumerate((res * res, res * res_image, res * image, rhs * res_image)):
            dots = jnp.where(lane == place, jnp.sum(product, axis=1, keepdims=True), dots)
        dots_ref[...] = dots
        step_ref[...] = jnp.where(lane == 0, norm, jnp.where(lane == 1, curve, 0.0))


def order_kernel(rows_ref, perm_ref, out_ref):
    rows = rows_ref[...]
    count, width = rows.shape
    pieces = jnp.concatenate([piece for piece in split_three(rows)], axis=0).astype(BF16)
    perm = perm_ref[...]
    chunk = 256
    for col in range(0, width, chunk):
        total = jnp.zeros((3 * count, chunk), F32)
        for at in range(0, width, chunk):
            index = lax.broadcasted_iota(jnp.int32, (chunk, chunk), 0) + at
            pick = jnp.where(index == perm[:, col : col + chunk], 1.0, 0.0).astype(BF16)
            total += jnp.dot(pieces[:, at : at + chunk], pick, preferred_element_type=F32)
        out_ref[:, col : col + chunk] = total[:count] + total[count : 2 * count] + total[2 * count :]


def swap(value, mask, count):
    return lax.ppermute(value, "row", [(i, i ^ mask) for i in range(count)])


def levels(count, sizes):
    bits = count.bit_length() - 1
    out = []
    sizes = list(sizes)
    while bits:
        take = min(sizes.pop(0) if sizes else 1, bits)
        bits -= take
        out.append([mask << bits for mask in range(1, 1 << take)])
    return out


def tree_sum(value, count):
    for masks in levels(count, [2, 2, 2]):
        others = [swap(value, mask, count) for mask in masks]
        if len(masks) == 3:
            value = (value + others[0]) + (others[1] + others[2])
        else:
            value = value + others[0]
    return value


def gather_levels(count):
    return levels(count, [2] if count <= 16 else [2, 2])


def gather_places(count):
    places = [0]
    for masks in gather_levels(count):
        places = places + [place ^ mask for mask in masks for place in places]
    return places


def tree_gather(value, count):
    blocks, out = value[None], []
    for masks in gather_levels(count):
        blocks = jnp.concatenate([blocks] + [swap(blocks, mask, count) for mask in masks], axis=0)
        out.append(blocks)
    return out


def gate(block, behind):
    return pl.pallas_call(
        lambda *refs: None,
        in_specs=[pl.BlockSpec(memory_space=pl.ANY)] * 2,
        out_specs=pl.BlockSpec(memory_space=pl.ANY),
        out_shape=jax.ShapeDtypeStruct(block.shape, block.dtype),
        input_output_aliases={0: 0},
        compiler_params=pltpu.CompilerParams(vmem_limit_bytes=1024 * 1024),
        name="gate",
    )(block, behind)


def local(features, right_side, variance, hilbert_order, tile_list):
    width = features.shape[1]
    rhs_count = right_side.shape[0]
    count = lax.axis_size("row")
    most = tile_list.shape[1]
    steps = width // ROWS
    shape = jax.ShapeDtypeStruct
    params = pltpu.CompilerParams(vmem_limit_bytes=10 * 1024 * 1024)
    var_row = variance[None, :]

    whole = lambda *ignored: (0, 0)
    row_spec = pl.BlockSpec(right_side.shape, whole)
    var_spec = pl.BlockSpec(var_row.shape, whole)
    pay_shape = (80, width // 4)
    smem = pl.BlockSpec(memory_space=pltpu.SMEM)
    vmem = pl.BlockSpec(memory_space=pltpu.VMEM)
    in_hbm = lambda array: pltpu.with_memory_space_constraint(array, pltpu.HBM)
    pay_zero, pay_one, right, left, rounded = pl.pallas_call(
        payload_kernel,
        in_specs=[smem, vmem, vmem],
        out_shape=[
            shape((96, width // 4), BF16),
            shape(pay_shape, BF16),
            shape((KDIM, width), BF16),
            shape((width, KDIM), BF16),
            shape(right_side.shape, BF16),
        ],
        compiler_params=params,
        name="payload",
    )(tile_list, in_hbm(features), in_hbm(right_side))
    me = jnp.full((1,), lax.axis_index("row"), jnp.int32)
    any_spec = pl.BlockSpec(memory_space=pl.ANY)

    def own_part(rows, arrived):
        blocks = own_blocks(rows, steps)
        tiles, sums = pl.pallas_call(
            functools.partial(own_kernel, rows),
            in_specs=[vmem, vmem, vmem, any_spec],
            out_specs=[any_spec, vmem],
            out_shape=[pltpu.HBM((len(blocks), ROWS, ROWS), BF16), shape(right_side.shape, F32)],
            scratch_shapes=[
                pltpu.VMEM((len(blocks), ROWS, ROWS), BF16),
                pltpu.SemaphoreType.DMA((len(blocks),)),
            ],
            compiler_params=params,
            cost_estimate=pl.CostEstimate(
                flops=5_000_000_000, bytes_accessed=2 * len(blocks) * ROWS * ROWS, transcendentals=0
            ),
            name=f"own_tile_{rows[0]}",
        )(left, right, rounded, arrived)
        return blocks, tiles, sums

    first_masks, *later = gather_levels(count)
    first_level = lambda pay: jnp.concatenate(
        [pay] + [swap(pay, mask, count) for mask in first_masks], axis=0
    )
    near_zero = first_level(pay_zero)
    own_parts = [own_part(range(1), right)]
    near_zero = gate(near_zero, own_parts[0][2])
    near_one = first_level(gate(pay_one, own_parts[0][2]))
    own_parts.append(own_part(range(1, steps), near_zero))
    near_one = gate(near_one, own_parts[1][2])
    zero, places = [near_zero], [0]
    for level, masks in enumerate(later):
        zero = zero + [swap(array, mask, count) for mask in masks for array in zero]
        places = places + [mask ^ place for mask in masks for place in places]
        if level == 0:
            zero[-1] = gate(zero[-1], own_parts[1][2])
    one = [near_one] + [swap(near_one, place, count) for place in places[1:]]
    each = len(first_masks) + 1
    zero_at = [(at, row * 96) for at in range(len(zero)) for row in range(each)]
    one_at = [(at, row * 80) for at in range(len(one)) for row in range(each)]

    half = steps // 2

    def front_at(k, i, *ignored):
        return (jnp.minimum(k, FRONT - 1), jnp.where(k < FRONT, i, half - 1), 0)

    def back_at(k, i, *ignored):
        return (jnp.maximum(k - FRONT, 0), jnp.where(k < FRONT, 0, i), 0)

    half_specs = [pl.BlockSpec((1, ROWS, width), front_at), pl.BlockSpec((1, ROWS, width), back_at)]
    half_shapes = [
        pltpu.VMEM((FRONT, width // 2, width), BF16),
        pltpu.HBM((most - FRONT, width // 2, width), BF16),
    ]
    half_scratch = [
        pltpu.VMEM((width // 2, KDIM), BF16),
        pltpu.VMEM((rhs_count, width // 2), BF16),
        pltpu.VMEM((2,) + pay_shape, BF16),
        pltpu.SemaphoreType.DMA((2,)),
    ]
    right_spec = pl.BlockSpec(right.shape, whole)
    send_shape = (rhs_count, width + TAIL)
    front_zero, back_zero, half_sum, slots = pl.pallas_call(
        functools.partial(pair_zero_kernel, zero_at),
        grid_spec=pltpu.PrefetchScalarGridSpec(
            num_scalar_prefetch=1,
            grid=(most, half),
            in_specs=[right_spec] + [row_spec] * PARTS + [any_spec] * len(zero),
            out_specs=half_specs + [row_spec, smem],
            scratch_shapes=half_scratch
            + [
                pltpu.VMEM((count, 16, 128), BF16),
                pltpu.VMEM((count, 128), jnp.int32),
                pltpu.SMEM((count, 128), jnp.int32),
                pltpu.SemaphoreType.DMA((count,)),
            ],
        ),
        out_shape=half_shapes
        + [shape(right_side.shape, F32), shape((most + 2,), jnp.int32)],
        compiler_params=params,
        name="pair_zero",
    )(me, right, *[part[2] for part in own_parts], *zero)
    front_one, back_one, image, send = pl.pallas_call(
        functools.partial(pair_one_kernel, one_at),
        grid_spec=pltpu.PrefetchScalarGridSpec(
            num_scalar_prefetch=1,
            grid=(most, half),
            in_specs=[right_spec, row_spec, row_spec, var_spec] + [any_spec] * len(one),
            out_specs=half_specs + [row_spec, pl.BlockSpec(send_shape, whole)],
            scratch_shapes=half_scratch,
        ),
        out_shape=half_shapes + [shape(right_side.shape, F32), shape(send_shape, BF16)],
        compiler_params=params,
        name="pair_one",
    )(slots, right, half_sum, right_side, var_row, *one)
    fronts = [pltpu.with_memory_space_constraint(part, pltpu.VMEM) for part in (front_zero, front_one)]
    backs = [pltpu.with_memory_space_constraint(part, pltpu.HBM) for part in (back_zero, back_one)]

    def front_zero_at(k, i, *ignored):
        return (jnp.minimum(k, FRONT - 1), jnp.where(k < FRONT, jnp.minimum(i, half - 1), half - 1), 0)

    def front_one_at(k, i, *ignored):
        return (jnp.minimum(k, FRONT - 1), jnp.where(k < FRONT, jnp.maximum(i - half, 0), half - 1), 0)

    every_send = tree_gather(send, count)[-1]
    own_again = [
        pl.pallas_call(
            functools.partial(own_again_kernel, blocks),
            in_specs=[any_spec, pl.BlockSpec(send_shape, whole)],
            out_specs=row_spec,
            out_shape=shape(right_side.shape, F32),
            scratch_shapes=[
                pltpu.VMEM((len(blocks), ROWS, ROWS), BF16),
                pltpu.SemaphoreType.DMA((len(blocks),)),
            ],
            compiler_params=params,
            cost_estimate=pl.CostEstimate(
                flops=5_000_000_000, bytes_accessed=2 * len(blocks) * ROWS * ROWS, transcendentals=0
            ),
            name=f"own_again_{part}",
        )(in_hbm(tiles), send)
        for part, (blocks, tiles, _) in enumerate(own_parts)
    ]
    dots_spec = pl.BlockSpec((rhs_count, TAIL), whole)
    rows, dots, steps_one = pl.pallas_call(
        again_kernel,
        grid_spec=pltpu.PrefetchScalarGridSpec(
            num_scalar_prefetch=1,
            grid=(most, steps),
            in_specs=[
                pl.BlockSpec((1, ROWS, width), front_zero_at),
                pl.BlockSpec((1, ROWS, width), front_one_at),
                any_spec,
                any_spec,
                pl.BlockSpec((1,) + send_shape, lambda k, i, s: (s[1 + k], 0, 0)),
                pl.BlockSpec((count, rhs_count, TAIL), lambda k, i, s: (0, 0, width // TAIL)),
                row_spec,
                var_spec,
                row_spec,
            ]
            + [row_spec] * PARTS,
            out_specs=[
                pl.BlockSpec((4 * rhs_count, width), whole),
                dots_spec,
                dots_spec,
            ],
            scratch_shapes=[
                pltpu.VMEM(right_side.shape, F32),
                pltpu.VMEM((HELD, ROWS, width), BF16),
                pltpu.SemaphoreType.DMA((HELD,)),
            ],
        ),
        out_shape=[
            shape((4 * rhs_count, width), F32),
            shape((rhs_count, TAIL), F32),
            shape((rhs_count, TAIL), F32),
        ],
        compiler_params=params,
        name="pair_again",
    )(slots, *fronts, *backs, every_send, every_send, right_side, var_row, image, *own_again)

    dots = tree_sum(dots, count)
    ordered = pl.pallas_call(
        order_kernel,
        out_shape=shape(rows.shape, F32),
        compiler_params=params,
        name="curve_order",
    )(rows, hilbert_order)
    norm, curve = steps_one[:, 0:1], steps_one[:, 1:2]
    length = norm / curve
    norm_next = dots[:, 0:1]
    ratio = norm_next / norm
    curve_next = dots[:, 1:2] + ratio * (dots[:, 2:3] + dots[:, 3:4]) + ratio * ratio * curve
    length_next = norm_next / curve_next
    rhs_o, res_o, image_o, res_image_o = [ordered[at : at + 8] for at in range(0, 32, 8)]
    solved = length * rhs_o + length_next * (res_o + ratio * rhs_o)
    residual = res_o - length_next * (res_image_o + ratio * image_o)
    return (solved, residual)


def solution(mesh):
    in_specs = (
        P(None, ("group", "row")),
        P(None, ("group", "row")),
        P(("group", "row")),
        P(("group", "row"), None),
        P(("group", "row"), None, None),
    )
    out_specs = (P(None, ("group", "row")), P(None, ("group", "row")))
    return jax.shard_map(local, mesh=mesh, in_specs=in_specs, out_specs=out_specs, check_vma=False)
```

```python
import functools

import jax
import jax.numpy as jnp
import numpy as np
from jax import lax
from jax.experimental import pallas as pl
from jax.experimental.pallas import tpu as pltpu
from jax.sharding import PartitionSpec as P

SHRINK = 0.95
GRAM = SHRINK * SHRINK
SCALE = 20.0 * (20.0 / 19.0) ** 19
DIAGONAL = float(1.0 - SCALE * float(np.float32(1.0 / SCALE).astype(jnp.bfloat16)))
KDIM = 128
ROWS = 512
PARTS = 2
PIECE = 256
STRIP = 64
FRONT = 3
HELD = 4
TAIL = 128
BF16 = jnp.bfloat16
F32 = jnp.float32
CONTRACT_LANES = (((1,), (1,)), ((), ()))


def split_three(value):
    high = value.astype(BF16).astype(F32)
    rest = value - high
    middle = rest.astype(BF16).astype(F32)
    return high, middle, rest - middle


def norm_rows(norm, first):
    high, middle, low = split_three(norm)
    row = lax.broadcasted_iota(jnp.int32, (32, norm.shape[1]), 0)
    out = jnp.where(row < 6, 1.0, 0.0)
    out = jnp.where(row == first, high, out)
    out = jnp.where(row == first + 1, middle, out)
    return jnp.where(row == first + 2, low, out).astype(BF16)


def own_factor(feat):
    wide = feat.astype(F32)
    norm = jnp.sum(wide * wide, axis=0, keepdims=True) * GRAM
    pieces = split_three(wide * (-2.0 * GRAM))
    return jnp.concatenate([piece.astype(BF16) for piece in pieces] + [norm_rows(norm, 0)], axis=0)


def other_factor(feat):
    wide = feat.astype(F32)
    norm = jnp.sum(wide * wide, axis=0, keepdims=True) * GRAM
    return jnp.transpose(jnp.concatenate([feat, feat, feat, norm_rows(norm, 3)], axis=0))


def psi_power(dist):
    dist = jnp.maximum(dist, 1e-30)
    radius = dist * lax.rsqrt(dist)
    u = jnp.maximum(SHRINK - radius, 1e-30)
    return (jnp.exp2(19.0 * lax.log2(u)) * (1.0 - u)).astype(BF16)


def tile_unit(left, right, vec, tile_ref, cuts):
    rows = left.shape[0]
    pieces = [slice(at, at + PIECE) for at in range(0, right.shape[1], PIECE)]
    part = rows // cuts
    strips = part // STRIP

    def gram(piece, cut):
        at = slice(cut * part, (cut + 1) * part)
        return jnp.dot(left[at], right[:, piece], preferred_element_type=F32)

    def product(done, cut):
        at = slice(cut * part, (cut + 1) * part)
        return jnp.dot(
            vec[:, at], jnp.concatenate(done[cut], axis=0), preferred_element_type=F32
        )

    dists = [gram(pieces[0], cut) for cut in range(cuts)]
    before, terms = None, []
    for index, piece in enumerate(pieces):
        following, done, term = [], [], 0.0
        for cut in range(cuts):
            if index + 1 < len(pieces):
                following.append(gram(pieces[index + 1], cut))
            done.append([])
            for strip in range(strips):
                at = strip * STRIP
                values = psi_power(dists[cut][at : at + STRIP])
                tile_ref[cut * part + at : cut * part + at + STRIP, piece] = values
                done[cut].append(values)
                if before is not None and strip == strips // 2:
                    term = term + product(before, cut)
        if before is not None:
            terms.append(term)
        dists, before = following, done
    terms.append(sum(product(before, cut) for cut in range(cuts)))
    return jnp.concatenate(terms, axis=1)


def unpack(pay):
    return jnp.concatenate([pay[:32], pay[32:64]], axis=1), jnp.concatenate([pay[64:72], pay[72:80]], axis=1)


def own_blocks(rows, count):
    return [(row, col) for row in rows for col in range(row, count)]


def own_kernel(
    rows, left_ref, right_ref, vec_ref, arrived_ref, out_ref, sum_ref, tile_ref, sem_ref
):
    sum_ref[...] = jnp.zeros_like(sum_ref)
    count = vec_ref.shape[1] // ROWS
    piece = lambda index: pl.ds(pl.multiple_of(index * ROWS, ROWS), ROWS)
    save = lambda at: pltpu.make_async_copy(tile_ref.at[at], out_ref.at[at], sem_ref.at[at])

    def row_step(row, at):
        def col_step(col, at):
            sum_ref[:, piece(col)] += tile_unit(
                left_ref[piece(row), :], right_ref[:, piece(col)], vec_ref[:, piece(row)],
                tile_ref.at[at], 1,
            )
            save(at).start()

            @pl.when(row != col)
            def _():
                sum_ref[:, piece(row)] += lax.dot_general(
                    vec_ref[:, piece(col)], tile_ref[at], CONTRACT_LANES,
                    preferred_element_type=F32,
                )

            return at + 1

        return lax.fori_loop(row, count, col_step, at)

    lax.fori_loop(rows[0], rows[-1] + 1, row_step, 0)
    for at in range(tile_ref.shape[0]):
        save(at).wait()


def own_again_kernel(blocks, in_ref, vec_ref, sum_ref, tile_ref, sem_ref):
    load = lambda index: pltpu.make_async_copy(
        in_ref.at[index], tile_ref.at[index], sem_ref.at[index]
    )
    for index in range(len(blocks)):
        load(index).start()
    sum_ref[...] = jnp.zeros_like(sum_ref)
    piece = lambda index: slice(index * ROWS, (index + 1) * ROWS)
    for index, (row, col) in enumerate(blocks):
        load(index).wait()
        sum_ref[:, piece(col)] += jnp.dot(
            vec_ref[:, piece(row)], tile_ref[index], preferred_element_type=F32
        )
        if row != col:
            sum_ref[:, piece(row)] += lax.dot_general(
                vec_ref[:, piece(col)], tile_ref[index], CONTRACT_LANES, preferred_element_type=F32
            )


def payload_kernel(
    list_ref, feat_ref, rhs_ref, pay_zero_ref, pay_one_ref, right_ref, left_ref, vec_ref
):
    feat = feat_ref[...]
    rounded = rhs_ref[...].astype(BF16)
    quarter = feat.shape[1] // 4
    for half, pay_ref in enumerate((pay_zero_ref, pay_one_ref)):
        first, second = [slice(at * quarter, (at + 1) * quarter) for at in (2 * half, 2 * half + 1)]
        pay_ref[:32] = feat[:, first]
        pay_ref[32:64] = feat[:, second]
        pay_ref[64:80] = jnp.concatenate([rounded[:, first], rounded[:, second]], axis=0)
    lane = lax.broadcasted_iota(jnp.int32, (16, quarter), 1)
    numbers = jnp.full(lane.shape, -1, jnp.int32)
    for entry in range(list_ref.shape[1]):
        numbers = jnp.where(lane == entry, list_ref[0, entry, 1], numbers)
    pay_zero_ref[80:96] = numbers.astype(F32).astype(BF16)
    right_ref[...] = own_factor(feat)
    left_ref[...] = other_factor(feat)
    vec_ref[...] = rounded


def find_partners(lists_ref, me, slots_ref):
    count, most = lists_ref.shape[0], slots_ref.shape[0] - 2
    for at in range(slots_ref.shape[0]):
        slots_ref[at] = 0
    total = jnp.int32(0)
    for at, place in enumerate(gather_places(count)):
        if at == 0:
            continue
        number = me ^ place
        hit = jnp.bool_(False)
        for entry in range(most):
            hit = hit | (lists_ref[at, entry] == me) | (lists_ref[0, entry] == number)
        slots_ref[1 + total] = jnp.where(hit, at, 0)
        total = total + hit.astype(jnp.int32)
    slots_ref[0] = total


def fetch_from(block_at, block_refs, slots_ref, pay_ref, sem_ref):
    def fetch(which):
        for at, (index, row) in enumerate(block_at):
            @pl.when(slots_ref[1 + which] == at)
            def _():
                pltpu.make_async_copy(
                    block_refs[index].at[pl.ds(row, 80)],
                    pay_ref.at[which % 2],
                    sem_ref.at[which % 2],
                ).start()

    return fetch


def half_tiles(cuts, slots_ref, right_ref, fetch, front_ref, back_ref, sum_ref, left_ref, vec_ref, pay_ref, sem_ref):
    slot, step = pl.program_id(0), pl.program_id(1)

    @pl.when((slot == 0) & (step == 0) & (slots_ref[0] > 0))
    def _():
        fetch(0)

    @pl.when(slot < slots_ref[0])
    def _():
        @pl.when(step == 0)
        def _():
            pltpu.make_async_copy(
                pay_ref.at[(slot + 1) % 2], pay_ref.at[slot % 2], sem_ref.at[slot % 2]
            ).wait()

            @pl.when(slot + 1 < slots_ref[0])
            def _():
                fetch(slot + 1)

            feat, vec = unpack(pay_ref[slot % 2])
            left_ref[...] = other_factor(feat)
            vec_ref[...] = vec

        rows = pl.ds(pl.multiple_of(step * ROWS, ROWS), ROWS)
        left, vec = left_ref[rows, :], vec_ref[:, rows]
        for tile_ref, here in ((front_ref, slot < FRONT), (back_ref, slot >= FRONT)):
            @pl.when(here)
            def _():
                sum_ref[...] += tile_unit(left, right_ref[...], vec, tile_ref.at[0], cuts)


def pair_zero_kernel(block_at, me_ref, right_ref, *refs):
    first_refs, block_refs = refs[:PARTS], refs[PARTS:-12]
    front_ref, back_ref, sum_ref, slots_ref = refs[-12:-8]
    left_ref, vec_ref, pay_ref, sem_ref, strip_ref, list_ref, lists_ref, strip_sem_ref = refs[-8:]

    @pl.when((pl.program_id(0) == 0) & (pl.program_id(1) == 0))
    def _():
        strips = [
            pltpu.make_async_copy(
                block_refs[index].at[pl.ds(row + 80, 16), pl.ds(0, 128)],
                strip_ref.at[at],
                strip_sem_ref.at[at],
            )
            for at, (index, row) in enumerate(block_at)
        ]
        for strip in strips:
            strip.start()
        sum_ref[...] = functools.reduce(jnp.add, [first_ref[...] for first_ref in first_refs])
        for at, strip in enumerate(strips):
            strip.wait()
            list_ref[at : at + 1, :] = strip_ref[at].astype(F32)[:1].astype(jnp.int32)
        numbers = pltpu.make_async_copy(list_ref, lists_ref, strip_sem_ref.at[0])
        numbers.start()
        numbers.wait()
        find_partners(lists_ref, me_ref[0], slots_ref)

    fetch = fetch_from(block_at, block_refs, slots_ref, pay_ref, sem_ref)
    half_tiles(
        2, slots_ref, right_ref, fetch, front_ref, back_ref, sum_ref, left_ref, vec_ref, pay_ref, sem_ref
    )


def pair_one_kernel(block_at, slots_ref, right_ref, first_ref, rhs_ref, var_ref, *refs):
    block_refs = refs[:-8]
    front_ref, back_ref, image_ref, send_ref, left_ref, vec_ref, pay_ref, sem_ref = refs[-8:]
    slot, step = pl.program_id(0), pl.program_id(1)

    @pl.when((slot == 0) & (step == 0))
    def _():
        image_ref[...] = first_ref[...]

    fetch = fetch_from(block_at, block_refs, slots_ref, pay_ref, sem_ref)
    half_tiles(
        1, slots_ref, right_ref, fetch, front_ref, back_ref, image_ref, left_ref, vec_ref, pay_ref, sem_ref
    )

    @pl.when((slot == pl.num_programs(0) - 1) & (step == pl.num_programs(1) - 1))
    def _():
        rhs = rhs_ref[...]
        width = rhs.shape[1]
        image = (var_ref[...] + DIAGONAL) * rhs + SCALE * image_ref[...]
        image_ref[...] = image
        send_ref[:, :width] = image.astype(BF16)
        pieces = split_three(jnp.sum(rhs * rhs, axis=1, keepdims=True))
        pieces += split_three(jnp.sum(rhs * image, axis=1, keepdims=True))
        lane = lax.broadcasted_iota(jnp.int32, (rhs.shape[0], TAIL), 1)
        tail = jnp.zeros((rhs.shape[0], TAIL), F32)
        for place, piece in enumerate(pieces):
            tail = jnp.where(lane == place, piece, tail)
        send_ref[:, width:] = tail.astype(BF16)


def again_kernel(
    slots_ref, front_zero_ref, front_one_ref, back_zero_ref, back_one_ref,
    vec_ref, tails_ref, rhs_ref, var_ref, image_ref, *refs
):
    first_refs = refs[:PARTS]
    rows_ref, dots_ref, step_ref, sum_ref, held_ref, sem_ref = refs[PARTS:]
    slot, step = pl.program_id(0), pl.program_id(1)
    width = rhs_ref.shape[1]
    steps = width // ROWS
    half = steps // 2
    parts = (slots_ref[0] - FRONT) * steps

    def fetch(part, back_ref, first):
        at = pl.ds(pl.multiple_of((part % steps - first) * ROWS, ROWS), ROWS)
        return pltpu.make_async_copy(
            back_ref.at[part // steps, at], held_ref.at[part % HELD], sem_ref.at[part % HELD]
        )

    def start(part):
        @pl.when((part < parts) & (part % steps < half))
        def _():
            fetch(part, back_zero_ref, 0).start()

        @pl.when((part < parts) & (part % steps >= half))
        def _():
            fetch(part, back_one_ref, half).start()

    @pl.when((slot == 0) & (step == 0))
    def _():
        sum_ref[...] = functools.reduce(jnp.add, [first_ref[...] for first_ref in first_refs])
        for part in range(HELD):
            start(part)

    @pl.when(slot < slots_ref[0])
    def _():
        at = pl.multiple_of(step * ROWS, ROWS)
        for front_ref, here in ((front_zero_ref, step < half), (front_one_ref, step >= half)):
            @pl.when((slot < FRONT) & here)
            def _():
                sum_ref[...] += jnp.dot(
                    vec_ref[0, :, pl.ds(at, ROWS)], front_ref[0], preferred_element_type=F32
                )

        @pl.when(slot >= FRONT)
        def _():
            part = (slot - FRONT) * steps + step
            fetch(part % HELD, back_zero_ref, part % HELD // half * half).wait()
            sum_ref[...] += jnp.dot(
                vec_ref[0, :, pl.ds(at, ROWS)], held_ref[part % HELD], preferred_element_type=F32
            )
            start(part + HELD)

    @pl.when((slot == pl.num_programs(0) - 1) & (step == pl.num_programs(1) - 1))
    def _():
        rhs = rhs_ref[...]
        image = image_ref[...]
        total = jnp.sum(tails_ref[...].astype(F32), axis=0)
        norm = total[:, 0:1] + total[:, 1:2] + total[:, 2:3]
        curve = total[:, 3:4] + total[:, 4:5] + total[:, 5:6]
        length = norm / curve
        second = (var_ref[...] + DIAGONAL) * image + SCALE * sum_ref[...]
        res = rhs - length * image
        res_image = image - length * second
        rows_ref[0:8] = rhs
        rows_ref[8:16] = res
        rows_ref[16:24] = image
        rows_ref[24:32] = res_image
        lane = lax.broadcasted_iota(jnp.int32, (rhs.shape[0], TAIL), 1)
        dots = jnp.zeros((rhs.shape[0], TAIL), F32)
        for place, product in enumerate((res * res, res * res_image, res * image, rhs * res_image)):
            dots = jnp.where(lane == place, jnp.sum(product, axis=1, keepdims=True), dots)
        dots_ref[...] = dots
        step_ref[...] = jnp.where(lane == 0, norm, jnp.where(lane == 1, curve, 0.0))


def order_kernel(rows_ref, perm_ref, out_ref):
    rows = rows_ref[...]
    count, width = rows.shape
    pieces = jnp.concatenate([piece for piece in split_three(rows)], axis=0).astype(BF16)
    perm = perm_ref[...]
    chunk = 256
    for col in range(0, width, chunk):
        total = jnp.zeros((3 * count, chunk), F32)
        for at in range(0, width, chunk):
            index = lax.broadcasted_iota(jnp.int32, (chunk, chunk), 0) + at
            pick = jnp.where(index == perm[:, col : col + chunk], 1.0, 0.0).astype(BF16)
            total += jnp.dot(pieces[:, at : at + chunk], pick, preferred_element_type=F32)
        out_ref[:, col : col + chunk] = total[:count] + total[count : 2 * count] + total[2 * count :]


def swap(value, mask, count):
    return lax.ppermute(value, "row", [(i, i ^ mask) for i in range(count)])


def levels(count, sizes):
    bits = count.bit_length() - 1
    out = []
    sizes = list(sizes)
    while bits:
        take = min(sizes.pop(0) if sizes else 1, bits)
        bits -= take
        out.append([mask << bits for mask in range(1, 1 << take)])
    return out


def tree_sum(value, count):
    for masks in levels(count, [2, 2, 2]):
        others = [swap(value, mask, count) for mask in masks]
        if len(masks) == 3:
            value = (value + others[0]) + (others[1] + others[2])
        else:
            value = value + others[0]
    return value


def gather_levels(count):
    return levels(count, [2] if count <= 16 else [2, 2])


def gather_places(count):
    places = [0]
    for masks in gather_levels(count):
        places = places + [place ^ mask for mask in masks for place in places]
    return places


def tree_gather(value, count):
    blocks, out = value[None], []
    for masks in gather_levels(count):
        blocks = jnp.concatenate([blocks] + [swap(blocks, mask, count) for mask in masks], axis=0)
        out.append(blocks)
    return out


def gate(block, behind):
    return pl.pallas_call(
        lambda *refs: None,
        in_specs=[pl.BlockSpec(memory_space=pl.ANY)] * 2,
        out_specs=pl.BlockSpec(memory_space=pl.ANY),
        out_shape=jax.ShapeDtypeStruct(block.shape, block.dtype),
        input_output_aliases={0: 0},
        compiler_params=pltpu.CompilerParams(vmem_limit_bytes=1024 * 1024),
        name="gate",
    )(block, behind)


def local(features, right_side, variance, hilbert_order, tile_list):
    width = features.shape[1]
    rhs_count = right_side.shape[0]
    count = lax.axis_size("row")
    most = tile_list.shape[1]
    steps = width // ROWS
    shape = jax.ShapeDtypeStruct
    params = pltpu.CompilerParams(vmem_limit_bytes=10 * 1024 * 1024)
    var_row = variance[None, :]

    whole = lambda *ignored: (0, 0)
    row_spec = pl.BlockSpec(right_side.shape, whole)
    var_spec = pl.BlockSpec(var_row.shape, whole)
    pay_shape = (80, width // 4)
    smem = pl.BlockSpec(memory_space=pltpu.SMEM)
    vmem = pl.BlockSpec(memory_space=pltpu.VMEM)
    in_hbm = lambda array: pltpu.with_memory_space_constraint(array, pltpu.HBM)
    pay_zero, pay_one, right, left, rounded = pl.pallas_call(
        payload_kernel,
        in_specs=[smem, vmem, vmem],
        out_shape=[
            shape((96, width // 4), BF16),
            shape(pay_shape, BF16),
            shape((KDIM, width), BF16),
            shape((width, KDIM), BF16),
            shape(right_side.shape, BF16),
        ],
        compiler_params=params,
        name="payload",
    )(tile_list, in_hbm(features), in_hbm(right_side))
    me = jnp.full((1,), lax.axis_index("row"), jnp.int32)
    any_spec = pl.BlockSpec(memory_space=pl.ANY)

    def own_part(rows, arrived):
        blocks = own_blocks(rows, steps)
        tiles, sums = pl.pallas_call(
            functools.partial(own_kernel, rows),
            in_specs=[vmem, vmem, vmem, any_spec],
            out_specs=[any_spec, vmem],
            out_shape=[pltpu.HBM((len(blocks), ROWS, ROWS), BF16), shape(right_side.shape, F32)],
            scratch_shapes=[
                pltpu.VMEM((len(blocks), ROWS, ROWS), BF16),
                pltpu.SemaphoreType.DMA((len(blocks),)),
            ],
            compiler_params=params,
            cost_estimate=pl.CostEstimate(
                flops=5_000_000_000, bytes_accessed=2 * len(blocks) * ROWS * ROWS, transcendentals=0
            ),
            name=f"own_tile_{rows[0]}",
        )(left, right, rounded, arrived)
        return blocks, tiles, sums

    first_masks, *later = gather_levels(count)
    first_level = lambda pay: jnp.concatenate(
        [pay] + [swap(pay, mask, count) for mask in first_masks], axis=0
    )
    near_zero = first_level(pay_zero)
    own_parts = [own_part(range(1), right)]
    near_zero = gate(near_zero, own_parts[0][2])
    near_one = first_level(gate(pay_one, own_parts[0][2]))
    own_parts.append(own_part(range(1, steps), near_zero))
    near_one = gate(near_one, own_parts[1][2])
    zero, places = [near_zero], [0]
    for level, masks in enumerate(later):
        zero = zero + [swap(array, mask, count) for mask in masks for array in zero]
        places = places + [mask ^ place for mask in masks for place in places]
        if level == 0:
            zero[-1] = gate(zero[-1], own_parts[1][2])
    one = [near_one] + [swap(near_one, place, count) for place in places[1:]]
    each = len(first_masks) + 1
    zero_at = [(at, row * 96) for at in range(len(zero)) for row in range(each)]
    one_at = [(at, row * 80) for at in range(len(one)) for row in range(each)]

    half = steps // 2

    def front_at(k, i, *ignored):
        return (jnp.minimum(k, FRONT - 1), jnp.where(k < FRONT, i, half - 1), 0)

    def back_at(k, i, *ignored):
        return (jnp.maximum(k - FRONT, 0), jnp.where(k < FRONT, 0, i), 0)

    half_specs = [pl.BlockSpec((1, ROWS, width), front_at), pl.BlockSpec((1, ROWS, width), back_at)]
    half_shapes = [
        pltpu.VMEM((FRONT, width // 2, width), BF16),
        pltpu.HBM((most - FRONT, width // 2, width), BF16),
    ]
    half_scratch = [
        pltpu.VMEM((width // 2, KDIM), BF16),
        pltpu.VMEM((rhs_count, width // 2), BF16),
        pltpu.VMEM((2,) + pay_shape, BF16),
        pltpu.SemaphoreType.DMA((2,)),
    ]
    right_spec = pl.BlockSpec(right.shape, whole)
    send_shape = (rhs_count, width + TAIL)
    front_zero, back_zero, half_sum, slots = pl.pallas_call(
        functools.partial(pair_zero_kernel, zero_at),
        grid_spec=pltpu.PrefetchScalarGridSpec(
            num_scalar_prefetch=1,
            grid=(most, half),
            in_specs=[right_spec] + [row_spec] * PARTS + [any_spec] * len(zero),
            out_specs=half_specs + [row_spec, smem],
            scratch_shapes=half_scratch
            + [
                pltpu.VMEM((count, 16, 128), BF16),
                pltpu.VMEM((count, 128), jnp.int32),
                pltpu.SMEM((count, 128), jnp.int32),
                pltpu.SemaphoreType.DMA((count,)),
            ],
        ),
        out_shape=half_shapes
        + [shape(right_side.shape, F32), shape((most + 2,), jnp.int32)],
        compiler_params=params,
        name="pair_zero",
    )(me, right, *[part[2] for part in own_parts], *zero)
    front_one, back_one, image, send = pl.pallas_call(
        functools.partial(pair_one_kernel, one_at),
        grid_spec=pltpu.PrefetchScalarGridSpec(
            num_scalar_prefetch=1,
            grid=(most, half),
            in_specs=[right_spec, row_spec, row_spec, var_spec] + [any_spec] * len(one),
            out_specs=half_specs + [row_spec, pl.BlockSpec(send_shape, whole)],
            scratch_shapes=half_scratch,
        ),
        out_shape=half_shapes + [shape(right_side.shape, F32), shape(send_shape, BF16)],
        compiler_params=params,
        name="pair_one",
    )(slots, right, half_sum, right_side, var_row, *one)
    fronts = [pltpu.with_memory_space_constraint(part, pltpu.VMEM) for part in (front_zero, front_one)]
    backs = [pltpu.with_memory_space_constraint(part, pltpu.HBM) for part in (back_zero, back_one)]

    def front_zero_at(k, i, *ignored):
        return (jnp.minimum(k, FRONT - 1), jnp.where(k < FRONT, jnp.minimum(i, half - 1), half - 1), 0)

    def front_one_at(k, i, *ignored):
        return (jnp.minimum(k, FRONT - 1), jnp.where(k < FRONT, jnp.maximum(i - half, 0), half - 1), 0)

    every_send = tree_gather(send, count)[-1]
    own_again = [
        pl.pallas_call(
            functools.partial(own_again_kernel, blocks),
            in_specs=[any_spec, pl.BlockSpec(send_shape, whole)],
            out_specs=row_spec,
            out_shape=shape(right_side.shape, F32),
            scratch_shapes=[
                pltpu.VMEM((len(blocks), ROWS, ROWS), BF16),
                pltpu.SemaphoreType.DMA((len(blocks),)),
            ],
            compiler_params=params,
            cost_estimate=pl.CostEstimate(
                flops=5_000_000_000, bytes_accessed=2 * len(blocks) * ROWS * ROWS, transcendentals=0
            ),
            name=f"own_again_{part}",
        )(in_hbm(tiles), send)
        for part, (blocks, tiles, _) in enumerate(own_parts)
    ]
    dots_spec = pl.BlockSpec((rhs_count, TAIL), whole)
    rows, dots, steps_one = pl.pallas_call(
        again_kernel,
        grid_spec=pltpu.PrefetchScalarGridSpec(
            num_scalar_prefetch=1,
            grid=(most, steps),
            in_specs=[
                pl.BlockSpec((1, ROWS, width), front_zero_at),
                pl.BlockSpec((1, ROWS, width), front_one_at),
                any_spec,
                any_spec,
                pl.BlockSpec((1,) + send_shape, lambda k, i, s: (s[1 + k], 0, 0)),
                pl.BlockSpec((count, rhs_count, TAIL), lambda k, i, s: (0, 0, width // TAIL)),
                row_spec,
                var_spec,
                row_spec,
            ]
            + [row_spec] * PARTS,
            out_specs=[
                pl.BlockSpec((4 * rhs_count, width), whole),
                dots_spec,
                dots_spec,
            ],
            scratch_shapes=[
                pltpu.VMEM(right_side.shape, F32),
                pltpu.VMEM((HELD, ROWS, width), BF16),
                pltpu.SemaphoreType.DMA((HELD,)),
            ],
        ),
        out_shape=[
            shape((4 * rhs_count, width), F32),
            shape((rhs_count, TAIL), F32),
            shape((rhs_count, TAIL), F32),
        ],
        compiler_params=params,
        name="pair_again",
    )(slots, *fronts, *backs, every_send, every_send, right_side, var_row, image, *own_again)

    dots = tree_sum(dots, count)
    ordered = pl.pallas_call(
        order_kernel,
        out_shape=shape(rows.shape, F32),
        compiler_params=params,
        name="curve_order",
    )(rows, hilbert_order)
    norm, curve = steps_one[:, 0:1], steps_one[:, 1:2]
    length = norm / curve
    norm_next = dots[:, 0:1]
    ratio = norm_next / norm
    curve_next = dots[:, 1:2] + ratio * (dots[:, 2:3] + dots[:, 3:4]) + ratio * ratio * curve
    length_next = norm_next / curve_next
    rhs_o, res_o, image_o, res_image_o = [ordered[at : at + 8] for at in range(0, 32, 8)]
    solved = length * rhs_o + length_next * (res_o + ratio * rhs_o)
    residual = res_o - length_next * (res_image_o + ratio * image_o)
    return (solved, residual)


def solution(mesh):
    in_specs = (
        P(None, ("group", "row")),
        P(None, ("group", "row")),
        P(("group", "row")),
        P(("group", "row"), None),
        P(("group", "row"), None, None),
    )
    out_specs = (P(None, ("group", "row")), P(None, ("group", "row")))
    return jax.shard_map(local, mesh=mesh, in_specs=in_specs, out_specs=out_specs, check_vma=False)
```

```python
import functools

import jax
import jax.numpy as jnp
import numpy as np
from jax import lax
from jax.experimental import pallas as pl
from jax.experimental.pallas import tpu as pltpu
from jax.sharding import PartitionSpec as P

SHRINK = 0.95
GRAM = SHRINK * SHRINK
SCALE = 20.0 * (20.0 / 19.0) ** 19
DIAGONAL = float(1.0 - SCALE * float(np.float32(1.0 / SCALE).astype(jnp.bfloat16)))
KDIM = 128
ROWS = 512
PARTS = 2
FRONT = 3
HELD = 4
TAIL = 128
BF16 = jnp.bfloat16
F32 = jnp.float32
CONTRACT_LANES = (((1,), (1,)), ((), ()))


def split_three(value):
    high = value.astype(BF16).astype(F32)
    rest = value - high
    middle = rest.astype(BF16).astype(F32)
    return high, middle, rest - middle


def norm_rows(norm, first):
    high, middle, low = split_three(norm)
    row = lax.broadcasted_iota(jnp.int32, (32, norm.shape[1]), 0)
    out = jnp.where(row < 6, 1.0, 0.0)
    out = jnp.where(row == first, high, out)
    out = jnp.where(row == first + 1, middle, out)
    return jnp.where(row == first + 2, low, out).astype(BF16)


def own_factor(feat):
    wide = feat.astype(F32)
    norm = jnp.sum(wide * wide, axis=0, keepdims=True) * GRAM
    pieces = split_three(wide * (-2.0 * GRAM))
    return jnp.concatenate([piece.astype(BF16) for piece in pieces] + [norm_rows(norm, 0)], axis=0)


def other_factor(feat):
    wide = feat.astype(F32)
    norm = jnp.sum(wide * wide, axis=0, keepdims=True) * GRAM
    return jnp.transpose(jnp.concatenate([feat, feat, feat, norm_rows(norm, 3)], axis=0))


def psi_power(dist):
    dist = jnp.maximum(dist, 1e-30)
    radius = dist * lax.rsqrt(dist)
    u = jnp.maximum(SHRINK - radius, 1e-30)
    return (jnp.exp2(19.0 * lax.log2(u)) * (1.0 - u)).astype(BF16)


def tile_unit(left, right, vec, tile_ref, width, strip):
    pieces = [slice(at, at + width) for at in range(0, right.shape[1], width)]
    gram = lambda piece: jnp.dot(left, right[:, piece], preferred_element_type=F32)
    product = lambda part: jnp.dot(vec, part, preferred_element_type=F32)
    dist, part, terms = gram(pieces[0]), None, []
    for index, piece in enumerate(pieces):
        following = gram(pieces[index + 1]) if index + 1 < len(pieces) else None
        strips = []
        for at in range(0, left.shape[0], strip):
            strips.append(psi_power(dist[at : at + strip]))
            tile_ref[at : at + strip, piece] = strips[-1]
        if part is not None:
            terms.append(product(part))
        dist, part = following, jnp.concatenate(strips, axis=0)
    return jnp.concatenate(terms + [product(part)], axis=1)


def unpack(pay):
    return jnp.concatenate([pay[:32], pay[32:64]], axis=1), jnp.concatenate([pay[64:72], pay[72:80]], axis=1)


def own_blocks(rows, count):
    return [(row, col) for row in rows for col in range(row, count)]


def own_kernel(
    rows, left_ref, right_ref, vec_ref, arrived_ref, out_ref, sum_ref, tile_ref, sem_ref
):
    sum_ref[...] = jnp.zeros_like(sum_ref)
    count = vec_ref.shape[1] // ROWS
    piece = lambda index: pl.ds(pl.multiple_of(index * ROWS, ROWS), ROWS)
    save = lambda at: pltpu.make_async_copy(tile_ref.at[at], out_ref.at[at], sem_ref.at[at])

    def row_step(row, at):
        def col_step(col, at):
            sum_ref[:, piece(col)] += tile_unit(
                left_ref[piece(row), :], right_ref[:, piece(col)], vec_ref[:, piece(row)],
                tile_ref.at[at], 256, 64,
            )
            save(at).start()

            @pl.when(row != col)
            def _():
                sum_ref[:, piece(row)] += lax.dot_general(
                    vec_ref[:, piece(col)], tile_ref[at], CONTRACT_LANES,
                    preferred_element_type=F32,
                )

            return at + 1

        return lax.fori_loop(row, count, col_step, at)

    lax.fori_loop(rows[0], rows[-1] + 1, row_step, 0)
    for at in range(tile_ref.shape[0]):
        save(at).wait()


def own_again_kernel(blocks, in_ref, vec_ref, sum_ref, tile_ref, sem_ref):
    load = lambda index: pltpu.make_async_copy(
        in_ref.at[index], tile_ref.at[index], sem_ref.at[index]
    )
    for index in range(len(blocks)):
        load(index).start()
    sum_ref[...] = jnp.zeros_like(sum_ref)
    piece = lambda index: slice(index * ROWS, (index + 1) * ROWS)
    for index, (row, col) in enumerate(blocks):
        load(index).wait()
        sum_ref[:, piece(col)] += jnp.dot(
            vec_ref[:, piece(row)], tile_ref[index], preferred_element_type=F32
        )
        if row != col:
            sum_ref[:, piece(row)] += lax.dot_general(
                vec_ref[:, piece(col)], tile_ref[index], CONTRACT_LANES, preferred_element_type=F32
            )


def payload_kernel(
    list_ref, feat_ref, rhs_ref, pay_zero_ref, pay_one_ref, right_ref, left_ref, vec_ref
):
    feat = feat_ref[...]
    rounded = rhs_ref[...].astype(BF16)
    quarter = feat.shape[1] // 4
    for half, pay_ref in enumerate((pay_zero_ref, pay_one_ref)):
        first, second = [slice(at * quarter, (at + 1) * quarter) for at in (2 * half, 2 * half + 1)]
        pay_ref[:32] = feat[:, first]
        pay_ref[32:64] = feat[:, second]
        pay_ref[64:80] = jnp.concatenate([rounded[:, first], rounded[:, second]], axis=0)
    lane = lax.broadcasted_iota(jnp.int32, (16, quarter), 1)
    numbers = jnp.full(lane.shape, -1, jnp.int32)
    for entry in range(list_ref.shape[1]):
        numbers = jnp.where(lane == entry, list_ref[0, entry, 1], numbers)
    pay_zero_ref[80:96] = numbers.astype(F32).astype(BF16)
    right_ref[...] = own_factor(feat)
    left_ref[...] = other_factor(feat)
    vec_ref[...] = rounded


def find_partners(lists_ref, me, slots_ref):
    count, most = lists_ref.shape[0], slots_ref.shape[0] - 2
    for at in range(slots_ref.shape[0]):
        slots_ref[at] = 0
    total = jnp.int32(0)
    for at, place in enumerate(gather_places(count)):
        if at == 0:
            continue
        number = me ^ place
        hit = jnp.bool_(False)
        for entry in range(most):
            hit = hit | (lists_ref[at, entry] == me) | (lists_ref[0, entry] == number)
        slots_ref[1 + total] = jnp.where(hit, at, 0)
        total = total + hit.astype(jnp.int32)
    slots_ref[0] = total


def fetch_from(block_at, block_refs, slots_ref, pay_ref, sem_ref):
    def fetch(which):
        for at, (index, row) in enumerate(block_at):
            @pl.when(slots_ref[1 + which] == at)
            def _():
                pltpu.make_async_copy(
                    block_refs[index].at[pl.ds(row, 80)],
                    pay_ref.at[which % 2],
                    sem_ref.at[which % 2],
                ).start()

    return fetch


def half_tiles(piece, strip, slots_ref, right_ref, fetch, front_ref, back_ref, sum_ref, left_ref, vec_ref, pay_ref, sem_ref):
    slot, step = pl.program_id(0), pl.program_id(1)

    @pl.when((slot == 0) & (step == 0) & (slots_ref[0] > 0))
    def _():
        fetch(0)

    @pl.when(slot < slots_ref[0])
    def _():
        @pl.when(step == 0)
        def _():
            pltpu.make_async_copy(
                pay_ref.at[(slot + 1) % 2], pay_ref.at[slot % 2], sem_ref.at[slot % 2]
            ).wait()

            @pl.when(slot + 1 < slots_ref[0])
            def _():
                fetch(slot + 1)

            feat, vec = unpack(pay_ref[slot % 2])
            left_ref[...] = other_factor(feat)
            vec_ref[...] = vec

        rows = pl.ds(pl.multiple_of(step * ROWS, ROWS), ROWS)
        left, vec = left_ref[rows, :], vec_ref[:, rows]
        for tile_ref, here in ((front_ref, slot < FRONT), (back_ref, slot >= FRONT)):
            @pl.when(here)
            def _():
                sum_ref[...] += tile_unit(left, right_ref[...], vec, tile_ref.at[0], piece, strip)


def pair_zero_kernel(block_at, me_ref, right_ref, *refs):
    first_refs, block_refs = refs[:PARTS], refs[PARTS:-12]
    front_ref, back_ref, sum_ref, slots_ref = refs[-12:-8]
    left_ref, vec_ref, pay_ref, sem_ref, strip_ref, list_ref, lists_ref, strip_sem_ref = refs[-8:]

    @pl.when((pl.program_id(0) == 0) & (pl.program_id(1) == 0))
    def _():
        strips = [
            pltpu.make_async_copy(
                block_refs[index].at[pl.ds(row + 80, 16), pl.ds(0, 128)],
                strip_ref.at[at],
                strip_sem_ref.at[at],
            )
            for at, (index, row) in enumerate(block_at)
        ]
        for strip in strips:
            strip.start()
        sum_ref[...] = functools.reduce(jnp.add, [first_ref[...] for first_ref in first_refs])
        for at, strip in enumerate(strips):
            strip.wait()
            list_ref[at : at + 1, :] = strip_ref[at].astype(F32)[:1].astype(jnp.int32)
        numbers = pltpu.make_async_copy(list_ref, lists_ref, strip_sem_ref.at[0])
        numbers.start()
        numbers.wait()
        find_partners(lists_ref, me_ref[0], slots_ref)

    fetch = fetch_from(block_at, block_refs, slots_ref, pay_ref, sem_ref)
    half_tiles(
        256, 128, slots_ref, right_ref, fetch, front_ref, back_ref, sum_ref, left_ref, vec_ref, pay_ref, sem_ref
    )


def pair_one_kernel(block_at, slots_ref, right_ref, first_ref, rhs_ref, var_ref, *refs):
    block_refs = refs[:-8]
    front_ref, back_ref, image_ref, send_ref, left_ref, vec_ref, pay_ref, sem_ref = refs[-8:]
    slot, step = pl.program_id(0), pl.program_id(1)

    @pl.when((slot == 0) & (step == 0))
    def _():
        image_ref[...] = first_ref[...]

    fetch = fetch_from(block_at, block_refs, slots_ref, pay_ref, sem_ref)
    half_tiles(
        512, 64, slots_ref, right_ref, fetch, front_ref, back_ref, image_ref, left_ref, vec_ref, pay_ref, sem_ref
    )

    @pl.when((slot == pl.num_programs(0) - 1) & (step == pl.num_programs(1) - 1))
    def _():
        rhs = rhs_ref[...]
        width = rhs.shape[1]
        image = (var_ref[...] + DIAGONAL) * rhs + SCALE * image_ref[...]
        image_ref[...] = image
        send_ref[:, :width] = image.astype(BF16)
        pieces = split_three(jnp.sum(rhs * rhs, axis=1, keepdims=True))
        pieces += split_three(jnp.sum(rhs * image, axis=1, keepdims=True))
        lane = lax.broadcasted_iota(jnp.int32, (rhs.shape[0], TAIL), 1)
        tail = jnp.zeros((rhs.shape[0], TAIL), F32)
        for place, piece in enumerate(pieces):
            tail = jnp.where(lane == place, piece, tail)
        send_ref[:, width:] = tail.astype(BF16)


def again_kernel(
    slots_ref, front_zero_ref, front_one_ref, back_zero_ref, back_one_ref,
    vec_ref, tails_ref, rhs_ref, var_ref, image_ref, *refs
):
    first_refs = refs[:PARTS]
    rows_ref, dots_ref, step_ref, sum_ref, held_ref, sem_ref = refs[PARTS:]
    slot = pl.program_id(0)
    width = rhs_ref.shape[1]
    steps = width // ROWS
    half = width // 2
    parts = (slots_ref[0] - FRONT) * steps

    def fetch(part, back_ref, first):
        at = pl.ds(pl.multiple_of((part % steps - first) * ROWS, ROWS), ROWS)
        return pltpu.make_async_copy(
            back_ref.at[part // steps, at], held_ref.at[part % HELD], sem_ref.at[part % HELD]
        )

    def start(part):
        @pl.when((part < parts) & (part % steps < steps // 2))
        def _():
            fetch(part, back_zero_ref, 0).start()

        @pl.when((part < parts) & (part % steps >= steps // 2))
        def _():
            fetch(part, back_one_ref, steps // 2).start()

    @pl.when(slot == 0)
    def _():
        sum_ref[...] = functools.reduce(jnp.add, [first_ref[...] for first_ref in first_refs])
        for part in range(HELD):
            start(part)

    @pl.when((slot < slots_ref[0]) & (slot < FRONT))
    def _():
        for index, front_ref in enumerate((front_zero_ref, front_one_ref)):
            sum_ref[...] += jnp.dot(
                vec_ref[0, :, index * half : (index + 1) * half], front_ref[0],
                preferred_element_type=F32,
            )

    @pl.when((slot < slots_ref[0]) & (slot >= FRONT))
    def _():
        for step in range(steps):
            part = (slot - FRONT) * steps + step
            fetch(part % HELD, back_zero_ref, part % HELD // (steps // 2) * (steps // 2)).wait()
            sum_ref[...] += jnp.dot(
                vec_ref[0, :, step * ROWS : (step + 1) * ROWS], held_ref[part % HELD],
                preferred_element_type=F32,
            )
            start(part + HELD)

    @pl.when(slot == pl.num_programs(0) - 1)
    def _():
        rhs = rhs_ref[...]
        image = image_ref[...]
        total = jnp.sum(tails_ref[...].astype(F32), axis=0)
        norm = total[:, 0:1] + total[:, 1:2] + total[:, 2:3]
        curve = total[:, 3:4] + total[:, 4:5] + total[:, 5:6]
        length = norm / curve
        second = (var_ref[...] + DIAGONAL) * image + SCALE * sum_ref[...]
        res = rhs - length * image
        res_image = image - length * second
        rows_ref[0:8] = rhs
        rows_ref[8:16] = res
        rows_ref[16:24] = image
        rows_ref[24:32] = res_image
        lane = lax.broadcasted_iota(jnp.int32, (rhs.shape[0], TAIL), 1)
        dots = jnp.zeros((rhs.shape[0], TAIL), F32)
        for place, product in enumerate((res * res, res * res_image, res * image, rhs * res_image)):
            dots = jnp.where(lane == place, jnp.sum(product, axis=1, keepdims=True), dots)
        dots_ref[...] = dots
        step_ref[...] = jnp.where(lane == 0, norm, jnp.where(lane == 1, curve, 0.0))


def order_kernel(rows_ref, perm_ref, out_ref):
    rows = rows_ref[...]
    count, width = rows.shape
    pieces = jnp.concatenate([piece for piece in split_three(rows)], axis=0).astype(BF16)
    perm = perm_ref[...]
    chunk = 256
    for col in range(0, width, chunk):
        total = jnp.zeros((3 * count, chunk), F32)
        for at in range(0, width, chunk):
            index = lax.broadcasted_iota(jnp.int32, (chunk, chunk), 0) + at
            pick = jnp.where(index == perm[:, col : col + chunk], 1.0, 0.0).astype(BF16)
            total += jnp.dot(pieces[:, at : at + chunk], pick, preferred_element_type=F32)
        out_ref[:, col : col + chunk] = total[:count] + total[count : 2 * count] + total[2 * count :]


def swap(value, mask, count):
    return lax.ppermute(value, "row", [(i, i ^ mask) for i in range(count)])


def levels(count, sizes):
    bits = count.bit_length() - 1
    out = []
    sizes = list(sizes)
    while bits:
        take = min(sizes.pop(0) if sizes else 1, bits)
        bits -= take
        out.append([mask << bits for mask in range(1, 1 << take)])
    return out


def tree_sum(value, count):
    for masks in levels(count, [2, 2, 2]):
        others = [swap(value, mask, count) for mask in masks]
        if len(masks) == 3:
            value = (value + others[0]) + (others[1] + others[2])
        else:
            value = value + others[0]
    return value


def gather_levels(count):
    return levels(count, [2] if count <= 16 else [2, 2])


def gather_places(count):
    places = [0]
    for masks in gather_levels(count):
        places = places + [place ^ mask for mask in masks for place in places]
    return places


def tree_gather(value, count):
    blocks, out = value[None], []
    for masks in gather_levels(count):
        blocks = jnp.concatenate([blocks] + [swap(blocks, mask, count) for mask in masks], axis=0)
        out.append(blocks)
    return out


def gate(block, behind):
    return pl.pallas_call(
        lambda *refs: None,
        in_specs=[pl.BlockSpec(memory_space=pl.ANY)] * 2,
        out_specs=pl.BlockSpec(memory_space=pl.ANY),
        out_shape=jax.ShapeDtypeStruct(block.shape, block.dtype),
        input_output_aliases={0: 0},
        compiler_params=pltpu.CompilerParams(vmem_limit_bytes=1024 * 1024),
        name="gate",
    )(block, behind)


def local(features, right_side, variance, hilbert_order, tile_list):
    width = features.shape[1]
    rhs_count = right_side.shape[0]
    count = lax.axis_size("row")
    most = tile_list.shape[1]
    steps = width // ROWS
    shape = jax.ShapeDtypeStruct
    params = pltpu.CompilerParams(vmem_limit_bytes=10 * 1024 * 1024)
    var_row = variance[None, :]

    whole = lambda *ignored: (0, 0)
    row_spec = pl.BlockSpec(right_side.shape, whole)
    var_spec = pl.BlockSpec(var_row.shape, whole)
    pay_shape = (80, width // 4)
    smem = pl.BlockSpec(memory_space=pltpu.SMEM)
    vmem = pl.BlockSpec(memory_space=pltpu.VMEM)
    in_hbm = lambda array: pltpu.with_memory_space_constraint(array, pltpu.HBM)
    pay_zero, pay_one, right, left, rounded = pl.pallas_call(
        payload_kernel,
        in_specs=[smem, vmem, vmem],
        out_shape=[
            shape((96, width // 4), BF16),
            shape(pay_shape, BF16),
            shape((KDIM, width), BF16),
            shape((width, KDIM), BF16),
            shape(right_side.shape, BF16),
        ],
        compiler_params=params,
        name="payload",
    )(tile_list, in_hbm(features), in_hbm(right_side))
    me = jnp.full((1,), lax.axis_index("row"), jnp.int32)
    any_spec = pl.BlockSpec(memory_space=pl.ANY)

    def own_part(rows, arrived):
        blocks = own_blocks(rows, steps)
        tiles, sums = pl.pallas_call(
            functools.partial(own_kernel, rows),
            in_specs=[vmem, vmem, vmem, any_spec],
            out_specs=[any_spec, vmem],
            out_shape=[pltpu.HBM((len(blocks), ROWS, ROWS), BF16), shape(right_side.shape, F32)],
            scratch_shapes=[
                pltpu.VMEM((len(blocks), ROWS, ROWS), BF16),
                pltpu.SemaphoreType.DMA((len(blocks),)),
            ],
            compiler_params=params,
            cost_estimate=pl.CostEstimate(
                flops=5_000_000_000, bytes_accessed=2 * len(blocks) * ROWS * ROWS, transcendentals=0
            ),
            name=f"own_tile_{rows[0]}",
        )(left, right, rounded, arrived)
        return blocks, tiles, sums

    first_masks, *later = gather_levels(count)
    first_level = lambda pay: jnp.concatenate(
        [pay] + [swap(pay, mask, count) for mask in first_masks], axis=0
    )
    near_zero = first_level(pay_zero)
    own_parts = [own_part(range(1), right)]
    near_zero = gate(near_zero, own_parts[0][2])
    near_one = first_level(gate(pay_one, own_parts[0][2]))
    own_parts.append(own_part(range(1, steps), near_zero))
    near_one = gate(near_one, own_parts[1][2])
    zero, places = [near_zero], [0]
    for level, masks in enumerate(later):
        zero = zero + [swap(array, mask, count) for mask in masks for array in zero]
        places = places + [mask ^ place for mask in masks for place in places]
        if level == 0:
            zero[-1] = gate(zero[-1], own_parts[1][2])
    one = [near_one] + [swap(near_one, place, count) for place in places[1:]]
    each = len(first_masks) + 1
    zero_at = [(at, row * 96) for at in range(len(zero)) for row in range(each)]
    one_at = [(at, row * 80) for at in range(len(one)) for row in range(each)]

    half = steps // 2

    def front_at(k, i, *ignored):
        return (jnp.minimum(k, FRONT - 1), jnp.where(k < FRONT, i, half - 1), 0)

    def back_at(k, i, *ignored):
        return (jnp.maximum(k - FRONT, 0), jnp.where(k < FRONT, 0, i), 0)

    half_specs = [pl.BlockSpec((1, ROWS, width), front_at), pl.BlockSpec((1, ROWS, width), back_at)]
    half_shapes = [
        pltpu.VMEM((FRONT, width // 2, width), BF16),
        pltpu.HBM((most - FRONT, width // 2, width), BF16),
    ]
    half_scratch = [
        pltpu.VMEM((width // 2, KDIM), BF16),
        pltpu.VMEM((rhs_count, width // 2), BF16),
        pltpu.VMEM((2,) + pay_shape, BF16),
        pltpu.SemaphoreType.DMA((2,)),
    ]
    right_spec = pl.BlockSpec(right.shape, whole)
    send_shape = (rhs_count, width + TAIL)
    front_zero, back_zero, half_sum, slots = pl.pallas_call(
        functools.partial(pair_zero_kernel, zero_at),
        grid_spec=pltpu.PrefetchScalarGridSpec(
            num_scalar_prefetch=1,
            grid=(most, half),
            in_specs=[right_spec] + [row_spec] * PARTS + [any_spec] * len(zero),
            out_specs=half_specs + [row_spec, smem],
            scratch_shapes=half_scratch
            + [
                pltpu.VMEM((count, 16, 128), BF16),
                pltpu.VMEM((count, 128), jnp.int32),
                pltpu.SMEM((count, 128), jnp.int32),
                pltpu.SemaphoreType.DMA((count,)),
            ],
        ),
        out_shape=half_shapes
        + [shape(right_side.shape, F32), shape((most + 2,), jnp.int32)],
        compiler_params=params,
        name="pair_zero",
    )(me, right, *[part[2] for part in own_parts], *zero)
    front_one, back_one, image, send = pl.pallas_call(
        functools.partial(pair_one_kernel, one_at),
        grid_spec=pltpu.PrefetchScalarGridSpec(
            num_scalar_prefetch=1,
            grid=(most, half),
            in_specs=[right_spec, row_spec, row_spec, var_spec] + [any_spec] * len(one),
            out_specs=half_specs + [row_spec, pl.BlockSpec(send_shape, whole)],
            scratch_shapes=half_scratch,
        ),
        out_shape=half_shapes + [shape(right_side.shape, F32), shape(send_shape, BF16)],
        compiler_params=params,
        name="pair_one",
    )(slots, right, half_sum, right_side, var_row, *one)
    fronts = [pltpu.with_memory_space_constraint(part, pltpu.VMEM) for part in (front_zero, front_one)]
    backs = [pltpu.with_memory_space_constraint(part, pltpu.HBM) for part in (back_zero, back_one)]

    every_send = tree_gather(send, count)[-1]
    own_again = [
        pl.pallas_call(
            functools.partial(own_again_kernel, blocks),
            in_specs=[any_spec, pl.BlockSpec(send_shape, whole)],
            out_specs=row_spec,
            out_shape=shape(right_side.shape, F32),
            scratch_shapes=[
                pltpu.VMEM((len(blocks), ROWS, ROWS), BF16),
                pltpu.SemaphoreType.DMA((len(blocks),)),
            ],
            compiler_params=params,
            cost_estimate=pl.CostEstimate(
                flops=5_000_000_000, bytes_accessed=2 * len(blocks) * ROWS * ROWS, transcendentals=0
            ),
            name=f"own_again_{part}",
        )(in_hbm(tiles), send)
        for part, (blocks, tiles, _) in enumerate(own_parts)
    ]
    dots_spec = pl.BlockSpec((rhs_count, TAIL), whole)
    rows, dots, steps_one = pl.pallas_call(
        again_kernel,
        grid_spec=pltpu.PrefetchScalarGridSpec(
            num_scalar_prefetch=1,
            grid=(most,),
            in_specs=[
                pl.BlockSpec((1, width // 2, width), lambda k, s: (jnp.minimum(k, FRONT - 1), 0, 0)),
                pl.BlockSpec((1, width // 2, width), lambda k, s: (jnp.minimum(k, FRONT - 1), 0, 0)),
                any_spec,
                any_spec,
                pl.BlockSpec((1,) + send_shape, lambda k, s: (s[1 + k], 0, 0)),
                pl.BlockSpec((count, rhs_count, TAIL), lambda k, s: (0, 0, width // TAIL)),
                row_spec,
                var_spec,
                row_spec,
            ]
            + [row_spec] * PARTS,
            out_specs=[
                pl.BlockSpec((4 * rhs_count, width), whole),
                dots_spec,
                dots_spec,
            ],
            scratch_shapes=[
                pltpu.VMEM(right_side.shape, F32),
                pltpu.VMEM((HELD, ROWS, width), BF16),
                pltpu.SemaphoreType.DMA((HELD,)),
            ],
        ),
        out_shape=[
            shape((4 * rhs_count, width), F32),
            shape((rhs_count, TAIL), F32),
            shape((rhs_count, TAIL), F32),
        ],
        compiler_params=params,
        name="pair_again",
    )(slots, *fronts, *backs, every_send, every_send, right_side, var_row, image, *own_again)

    dots = tree_sum(dots, count)
    ordered = pl.pallas_call(
        order_kernel,
        out_shape=shape(rows.shape, F32),
        compiler_params=params,
        name="curve_order",
    )(rows, hilbert_order)
    norm, curve = steps_one[:, 0:1], steps_one[:, 1:2]
    length = norm / curve
    norm_next = dots[:, 0:1]
    ratio = norm_next / norm
    curve_next = dots[:, 1:2] + ratio * (dots[:, 2:3] + dots[:, 3:4]) + ratio * ratio * curve
    length_next = norm_next / curve_next
    rhs_o, res_o, image_o, res_image_o = [ordered[at : at + 8] for at in range(0, 32, 8)]
    solved = length * rhs_o + length_next * (res_o + ratio * rhs_o)
    residual = res_o - length_next * (res_image_o + ratio * image_o)
    return (solved, residual)


def solution(mesh):
    in_specs = (
        P(None, ("group", "row")),
        P(None, ("group", "row")),
        P(("group", "row")),
        P(("group", "row"), None),
        P(("group", "row"), None, None),
    )
    out_specs = (P(None, ("group", "row")), P(None, ("group", "row")))
    return jax.shard_map(local, mesh=mesh, in_specs=in_specs, out_specs=out_specs, check_vma=False)
```

```python
import functools

import jax
import jax.numpy as jnp
import numpy as np
from jax import lax
from jax.experimental import pallas as pl
from jax.experimental.pallas import tpu as pltpu
from jax.sharding import PartitionSpec as P

SHRINK = 0.95
GRAM = SHRINK * SHRINK
SCALE = 20.0 * (20.0 / 19.0) ** 19
DIAGONAL = float(1.0 - SCALE * float(np.float32(1.0 / SCALE).astype(jnp.bfloat16)))
KDIM = 128
ROWS = 512
PARTS = 2
PIECE = 256
STRIP = 64
FRONT = 3
HELD = 4
TAIL = 128
BF16 = jnp.bfloat16
F32 = jnp.float32
CONTRACT_LANES = (((1,), (1,)), ((), ()))


def split_three(value):
    high = value.astype(BF16).astype(F32)
    rest = value - high
    middle = rest.astype(BF16).astype(F32)
    return high, middle, rest - middle


def norm_rows(norm, first):
    high, middle, low = split_three(norm)
    row = lax.broadcasted_iota(jnp.int32, (32, norm.shape[1]), 0)
    out = jnp.where(row < 6, 1.0, 0.0)
    out = jnp.where(row == first, high, out)
    out = jnp.where(row == first + 1, middle, out)
    return jnp.where(row == first + 2, low, out).astype(BF16)


def own_factor(feat):
    wide = feat.astype(F32)
    norm = jnp.sum(wide * wide, axis=0, keepdims=True) * GRAM
    pieces = split_three(wide * (-2.0 * GRAM))
    return jnp.concatenate([piece.astype(BF16) for piece in pieces] + [norm_rows(norm, 0)], axis=0)


def other_factor(feat):
    wide = feat.astype(F32)
    norm = jnp.sum(wide * wide, axis=0, keepdims=True) * GRAM
    return jnp.transpose(jnp.concatenate([feat, feat, feat, norm_rows(norm, 3)], axis=0))


def psi_power(dist):
    dist = jnp.maximum(dist, 1e-30)
    radius = dist * lax.rsqrt(dist)
    u = jnp.maximum(SHRINK - radius, 1e-30)
    return (jnp.exp2(19.0 * lax.log2(u)) * (1.0 - u)).astype(BF16)


def tile_unit(left, right, vec, tile_ref, edge, ahead):
    width = right.shape[1]
    begins = [0] + list(range(edge, width, PIECE)) + [width]
    pieces = [slice(begin, end) for begin, end in zip(begins, begins[1:])]
    gram = lambda piece: jnp.dot(left, right[:, piece], preferred_element_type=F32)
    product = lambda part: jnp.dot(vec, part, preferred_element_type=F32)
    dists, part, terms = [gram(piece) for piece in pieces[:ahead]], None, []
    for index, piece in enumerate(pieces):
        dists += [gram(later) for later in pieces[index + ahead : index + ahead + 1]]
        strips = []
        for at in range(0, left.shape[0], STRIP):
            strips.append(psi_power(dists[index][at : at + STRIP]))
            tile_ref[at : at + STRIP, piece] = strips[-1]
        if part is not None:
            terms.append(product(part))
        part = jnp.concatenate(strips, axis=0)
    return jnp.concatenate(terms + [product(part)], axis=1)


def unpack(pay):
    return jnp.concatenate([pay[:32], pay[32:64]], axis=1), jnp.concatenate([pay[64:72], pay[72:80]], axis=1)


def own_blocks(rows, count):
    return [(row, col) for row in rows for col in range(row, count)]


def own_kernel(
    rows, left_ref, right_ref, vec_ref, arrived_ref, out_ref, sum_ref, tile_ref, sem_ref
):
    sum_ref[...] = jnp.zeros_like(sum_ref)
    count = vec_ref.shape[1] // ROWS
    piece = lambda index: pl.ds(pl.multiple_of(index * ROWS, ROWS), ROWS)
    save = lambda at: pltpu.make_async_copy(tile_ref.at[at], out_ref.at[at], sem_ref.at[at])

    def row_step(row, at):
        def col_step(col, at):
            sum_ref[:, piece(col)] += tile_unit(
                left_ref[piece(row), :], right_ref[:, piece(col)], vec_ref[:, piece(row)],
                tile_ref.at[at], PIECE, 1,
            )
            save(at).start()

            @pl.when(row != col)
            def _():
                sum_ref[:, piece(row)] += lax.dot_general(
                    vec_ref[:, piece(col)], tile_ref[at], CONTRACT_LANES,
                    preferred_element_type=F32,
                )

            return at + 1

        return lax.fori_loop(row, count, col_step, at)

    lax.fori_loop(rows[0], rows[-1] + 1, row_step, 0)
    for at in range(tile_ref.shape[0]):
        save(at).wait()


def own_again_kernel(blocks, in_ref, vec_ref, sum_ref, tile_ref, sem_ref):
    load = lambda index: pltpu.make_async_copy(
        in_ref.at[index], tile_ref.at[index], sem_ref.at[index]
    )
    for index in range(len(blocks)):
        load(index).start()
    sum_ref[...] = jnp.zeros_like(sum_ref)
    piece = lambda index: slice(index * ROWS, (index + 1) * ROWS)
    for index, (row, col) in enumerate(blocks):
        load(index).wait()
        sum_ref[:, piece(col)] += jnp.dot(
            vec_ref[:, piece(row)], tile_ref[index], preferred_element_type=F32
        )
        if row != col:
            sum_ref[:, piece(row)] += lax.dot_general(
                vec_ref[:, piece(col)], tile_ref[index], CONTRACT_LANES, preferred_element_type=F32
            )


def payload_kernel(
    list_ref, feat_ref, rhs_ref, pay_zero_ref, pay_one_ref, right_ref, left_ref, vec_ref
):
    feat = feat_ref[...]
    rounded = rhs_ref[...].astype(BF16)
    quarter = feat.shape[1] // 4
    for half, pay_ref in enumerate((pay_zero_ref, pay_one_ref)):
        first, second = [slice(at * quarter, (at + 1) * quarter) for at in (2 * half, 2 * half + 1)]
        pay_ref[:32] = feat[:, first]
        pay_ref[32:64] = feat[:, second]
        pay_ref[64:80] = jnp.concatenate([rounded[:, first], rounded[:, second]], axis=0)
    lane = lax.broadcasted_iota(jnp.int32, (16, quarter), 1)
    numbers = jnp.full(lane.shape, -1, jnp.int32)
    for entry in range(list_ref.shape[1]):
        numbers = jnp.where(lane == entry, list_ref[0, entry, 1], numbers)
    pay_zero_ref[80:96] = numbers.astype(F32).astype(BF16)
    right_ref[...] = own_factor(feat)
    left_ref[...] = other_factor(feat)
    vec_ref[...] = rounded


def find_partners(lists_ref, me, slots_ref):
    count, most = lists_ref.shape[0], slots_ref.shape[0] - 2
    for at in range(slots_ref.shape[0]):
        slots_ref[at] = 0
    total = jnp.int32(0)
    for at, place in enumerate(gather_places(count)):
        if at == 0:
            continue
        number = me ^ place
        hit = jnp.bool_(False)
        for entry in range(most):
            hit = hit | (lists_ref[at, entry] == me) | (lists_ref[0, entry] == number)
        slots_ref[1 + total] = jnp.where(hit, at, 0)
        total = total + hit.astype(jnp.int32)
    slots_ref[0] = total


def fetch_from(block_at, block_refs, slots_ref, pay_ref, sem_ref):
    def fetch(which):
        for at, (index, row) in enumerate(block_at):
            @pl.when(slots_ref[1 + which] == at)
            def _():
                pltpu.make_async_copy(
                    block_refs[index].at[pl.ds(row, 80)],
                    pay_ref.at[which % 2],
                    sem_ref.at[which % 2],
                ).start()

    return fetch


def half_tiles(edge, ahead, slots_ref, right_ref, fetch, front_ref, back_ref, sum_ref, left_ref, vec_ref, pay_ref, sem_ref):
    slot, step = pl.program_id(0), pl.program_id(1)

    @pl.when((slot == 0) & (step == 0) & (slots_ref[0] > 0))
    def _():
        fetch(0)

    @pl.when(slot < slots_ref[0])
    def _():
        @pl.when(step == 0)
        def _():
            pltpu.make_async_copy(
                pay_ref.at[(slot + 1) % 2], pay_ref.at[slot % 2], sem_ref.at[slot % 2]
            ).wait()

            @pl.when(slot + 1 < slots_ref[0])
            def _():
                fetch(slot + 1)

            feat, vec = unpack(pay_ref[slot % 2])
            left_ref[...] = other_factor(feat)
            vec_ref[...] = vec

        rows = pl.ds(pl.multiple_of(step * ROWS, ROWS), ROWS)
        left, vec = left_ref[rows, :], vec_ref[:, rows]
        for tile_ref, here in ((front_ref, slot < FRONT), (back_ref, slot >= FRONT)):
            @pl.when(here)
            def _():
                sum_ref[...] += tile_unit(left, right_ref[...], vec, tile_ref.at[0], edge, ahead)


def pair_zero_kernel(block_at, me_ref, right_ref, *refs):
    first_refs, block_refs = refs[:PARTS], refs[PARTS:-12]
    front_ref, back_ref, sum_ref, slots_ref = refs[-12:-8]
    left_ref, vec_ref, pay_ref, sem_ref, strip_ref, list_ref, lists_ref, strip_sem_ref = refs[-8:]

    @pl.when((pl.program_id(0) == 0) & (pl.program_id(1) == 0))
    def _():
        strips = [
            pltpu.make_async_copy(
                block_refs[index].at[pl.ds(row + 80, 16), pl.ds(0, 128)],
                strip_ref.at[at],
                strip_sem_ref.at[at],
            )
            for at, (index, row) in enumerate(block_at)
        ]
        for strip in strips:
            strip.start()
        sum_ref[...] = functools.reduce(jnp.add, [first_ref[...] for first_ref in first_refs])
        for at, strip in enumerate(strips):
            strip.wait()
            list_ref[at : at + 1, :] = strip_ref[at].astype(F32)[:1].astype(jnp.int32)
        numbers = pltpu.make_async_copy(list_ref, lists_ref, strip_sem_ref.at[0])
        numbers.start()
        numbers.wait()
        find_partners(lists_ref, me_ref[0], slots_ref)

    fetch = fetch_from(block_at, block_refs, slots_ref, pay_ref, sem_ref)
    half_tiles(
        PIECE // 2, 1, slots_ref, right_ref, fetch, front_ref, back_ref, sum_ref, left_ref, vec_ref, pay_ref, sem_ref
    )


def pair_one_kernel(block_at, slots_ref, right_ref, first_ref, rhs_ref, var_ref, *refs):
    block_refs = refs[:-8]
    front_ref, back_ref, image_ref, send_ref, left_ref, vec_ref, pay_ref, sem_ref = refs[-8:]
    slot, step = pl.program_id(0), pl.program_id(1)

    @pl.when((slot == 0) & (step == 0))
    def _():
        image_ref[...] = first_ref[...]

    fetch = fetch_from(block_at, block_refs, slots_ref, pay_ref, sem_ref)
    half_tiles(
        PIECE, 2, slots_ref, right_ref, fetch, front_ref, back_ref, image_ref, left_ref, vec_ref, pay_ref, sem_ref
    )

    @pl.when((slot == pl.num_programs(0) - 1) & (step == pl.num_programs(1) - 1))
    def _():
        rhs = rhs_ref[...]
        width = rhs.shape[1]
        image = (var_ref[...] + DIAGONAL) * rhs + SCALE * image_ref[...]
        image_ref[...] = image
        send_ref[:, :width] = image.astype(BF16)
        pieces = split_three(jnp.sum(rhs * rhs, axis=1, keepdims=True))
        pieces += split_three(jnp.sum(rhs * image, axis=1, keepdims=True))
        lane = lax.broadcasted_iota(jnp.int32, (rhs.shape[0], TAIL), 1)
        tail = jnp.zeros((rhs.shape[0], TAIL), F32)
        for place, piece in enumerate(pieces):
            tail = jnp.where(lane == place, piece, tail)
        send_ref[:, width:] = tail.astype(BF16)


def again_kernel(
    slots_ref, front_zero_ref, front_one_ref, back_zero_ref, back_one_ref,
    vec_ref, tails_ref, rhs_ref, var_ref, image_ref, *refs
):
    first_refs = refs[:PARTS]
    rows_ref, dots_ref, step_ref, sum_ref, held_ref, sem_ref = refs[PARTS:]
    slot = pl.program_id(0)
    width = rhs_ref.shape[1]
    steps = width // ROWS
    half = width // 2
    parts = (slots_ref[0] - FRONT) * steps

    def fetch(part, back_ref, first):
        at = pl.ds(pl.multiple_of((part % steps - first) * ROWS, ROWS), ROWS)
        return pltpu.make_async_copy(
            back_ref.at[part // steps, at], held_ref.at[part % HELD], sem_ref.at[part % HELD]
        )

    def start(part):
        @pl.when((part < parts) & (part % steps < steps // 2))
        def _():
            fetch(part, back_zero_ref, 0).start()

        @pl.when((part < parts) & (part % steps >= steps // 2))
        def _():
            fetch(part, back_one_ref, steps // 2).start()

    @pl.when(slot == 0)
    def _():
        sum_ref[...] = functools.reduce(jnp.add, [first_ref[...] for first_ref in first_refs])
        for part in range(HELD):
            start(part)

    @pl.when((slot < slots_ref[0]) & (slot < FRONT))
    def _():
        for index, front_ref in enumerate((front_zero_ref, front_one_ref)):
            sum_ref[...] += jnp.dot(
                vec_ref[0, :, index * half : (index + 1) * half], front_ref[0],
                preferred_element_type=F32,
            )

    @pl.when((slot < slots_ref[0]) & (slot >= FRONT))
    def _():
        for step in range(steps):
            part = (slot - FRONT) * steps + step
            fetch(part % HELD, back_zero_ref, part % HELD // (steps // 2) * (steps // 2)).wait()
            sum_ref[...] += jnp.dot(
                vec_ref[0, :, step * ROWS : (step + 1) * ROWS], held_ref[part % HELD],
                preferred_element_type=F32,
            )
            start(part + HELD)

    @pl.when(slot == pl.num_programs(0) - 1)
    def _():
        rhs = rhs_ref[...]
        image = image_ref[...]
        total = jnp.sum(tails_ref[...].astype(F32), axis=0)
        norm = total[:, 0:1] + total[:, 1:2] + total[:, 2:3]
        curve = total[:, 3:4] + total[:, 4:5] + total[:, 5:6]
        length = norm / curve
        second = (var_ref[...] + DIAGONAL) * image + SCALE * sum_ref[...]
        res = rhs - length * image
        res_image = image - length * second
        rows_ref[0:8] = rhs
        rows_ref[8:16] = res
        rows_ref[16:24] = image
        rows_ref[24:32] = res_image
        lane = lax.broadcasted_iota(jnp.int32, (rhs.shape[0], TAIL), 1)
        dots = jnp.zeros((rhs.shape[0], TAIL), F32)
        for place, product in enumerate((res * res, res * res_image, res * image, rhs * res_image)):
            dots = jnp.where(lane == place, jnp.sum(product, axis=1, keepdims=True), dots)
        dots_ref[...] = dots
        step_ref[...] = jnp.where(lane == 0, norm, jnp.where(lane == 1, curve, 0.0))


def order_kernel(rows_ref, perm_ref, out_ref):
    rows = rows_ref[...]
    count, width = rows.shape
    pieces = jnp.concatenate([piece for piece in split_three(rows)], axis=0).astype(BF16)
    perm = perm_ref[...]
    chunk = 256
    for col in range(0, width, chunk):
        total = jnp.zeros((3 * count, chunk), F32)
        for at in range(0, width, chunk):
            index = lax.broadcasted_iota(jnp.int32, (chunk, chunk), 0) + at
            pick = jnp.where(index == perm[:, col : col + chunk], 1.0, 0.0).astype(BF16)
            total += jnp.dot(pieces[:, at : at + chunk], pick, preferred_element_type=F32)
        out_ref[:, col : col + chunk] = total[:count] + total[count : 2 * count] + total[2 * count :]


def swap(value, mask, count):
    return lax.ppermute(value, "row", [(i, i ^ mask) for i in range(count)])


def levels(count, sizes):
    bits = count.bit_length() - 1
    out = []
    sizes = list(sizes)
    while bits:
        take = min(sizes.pop(0) if sizes else 1, bits)
        bits -= take
        out.append([mask << bits for mask in range(1, 1 << take)])
    return out


def tree_sum(value, count):
    for masks in levels(count, [2, 2, 2]):
        others = [swap(value, mask, count) for mask in masks]
        if len(masks) == 3:
            value = (value + others[0]) + (others[1] + others[2])
        else:
            value = value + others[0]
    return value


def gather_levels(count):
    return levels(count, [2] if count <= 16 else [2, 2])


def gather_places(count):
    places = [0]
    for masks in gather_levels(count):
        places = places + [place ^ mask for mask in masks for place in places]
    return places


def tree_gather(value, count):
    blocks, out = value[None], []
    for masks in gather_levels(count):
        blocks = jnp.concatenate([blocks] + [swap(blocks, mask, count) for mask in masks], axis=0)
        out.append(blocks)
    return out


def gate(block, behind):
    return pl.pallas_call(
        lambda *refs: None,
        in_specs=[pl.BlockSpec(memory_space=pl.ANY)] * 2,
        out_specs=pl.BlockSpec(memory_space=pl.ANY),
        out_shape=jax.ShapeDtypeStruct(block.shape, block.dtype),
        input_output_aliases={0: 0},
        compiler_params=pltpu.CompilerParams(vmem_limit_bytes=1024 * 1024),
        name="gate",
    )(block, behind)


def local(features, right_side, variance, hilbert_order, tile_list):
    width = features.shape[1]
    rhs_count = right_side.shape[0]
    count = lax.axis_size("row")
    most = tile_list.shape[1]
    steps = width // ROWS
    shape = jax.ShapeDtypeStruct
    params = pltpu.CompilerParams(vmem_limit_bytes=10 * 1024 * 1024)
    var_row = variance[None, :]

    whole = lambda *ignored: (0, 0)
    row_spec = pl.BlockSpec(right_side.shape, whole)
    var_spec = pl.BlockSpec(var_row.shape, whole)
    pay_shape = (80, width // 4)
    smem = pl.BlockSpec(memory_space=pltpu.SMEM)
    vmem = pl.BlockSpec(memory_space=pltpu.VMEM)
    in_hbm = lambda array: pltpu.with_memory_space_constraint(array, pltpu.HBM)
    pay_zero, pay_one, right, left, rounded = pl.pallas_call(
        payload_kernel,
        in_specs=[smem, vmem, vmem],
        out_shape=[
            shape((96, width // 4), BF16),
            shape(pay_shape, BF16),
            shape((KDIM, width), BF16),
            shape((width, KDIM), BF16),
            shape(right_side.shape, BF16),
        ],
        compiler_params=params,
        name="payload",
    )(tile_list, in_hbm(features), in_hbm(right_side))
    me = jnp.full((1,), lax.axis_index("row"), jnp.int32)
    any_spec = pl.BlockSpec(memory_space=pl.ANY)

    def own_part(rows, arrived):
        blocks = own_blocks(rows, steps)
        tiles, sums = pl.pallas_call(
            functools.partial(own_kernel, rows),
            in_specs=[vmem, vmem, vmem, any_spec],
            out_specs=[any_spec, vmem],
            out_shape=[pltpu.HBM((len(blocks), ROWS, ROWS), BF16), shape(right_side.shape, F32)],
            scratch_shapes=[
                pltpu.VMEM((len(blocks), ROWS, ROWS), BF16),
                pltpu.SemaphoreType.DMA((len(blocks),)),
            ],
            compiler_params=params,
            cost_estimate=pl.CostEstimate(
                flops=5_000_000_000, bytes_accessed=2 * len(blocks) * ROWS * ROWS, transcendentals=0
            ),
            name=f"own_tile_{rows[0]}",
        )(left, right, rounded, arrived)
        return blocks, tiles, sums

    first_masks, *later = gather_levels(count)
    first_level = lambda pay: jnp.concatenate(
        [pay] + [swap(pay, mask, count) for mask in first_masks], axis=0
    )
    near_zero = first_level(pay_zero)
    own_parts = [own_part(range(1), right)]
    near_zero = gate(near_zero, own_parts[0][2])
    near_one = first_level(gate(pay_one, own_parts[0][2]))
    own_parts.append(own_part(range(1, steps), near_zero))
    near_one = gate(near_one, own_parts[1][2])
    zero, places = [near_zero], [0]
    for level, masks in enumerate(later):
        zero = zero + [swap(array, mask, count) for mask in masks for array in zero]
        places = places + [mask ^ place for mask in masks for place in places]
        if level == 0:
            zero[-1] = gate(zero[-1], own_parts[1][2])
    one = [near_one] + [swap(near_one, place, count) for place in places[1:]]
    each = len(first_masks) + 1
    zero_at = [(at, row * 96) for at in range(len(zero)) for row in range(each)]
    one_at = [(at, row * 80) for at in range(len(one)) for row in range(each)]

    half = steps // 2

    def front_at(k, i, *ignored):
        return (jnp.minimum(k, FRONT - 1), jnp.where(k < FRONT, i, half - 1), 0)

    def back_at(k, i, *ignored):
        return (jnp.maximum(k - FRONT, 0), jnp.where(k < FRONT, 0, i), 0)

    half_specs = [pl.BlockSpec((1, ROWS, width), front_at), pl.BlockSpec((1, ROWS, width), back_at)]
    half_shapes = [
        pltpu.VMEM((FRONT, width // 2, width), BF16),
        pltpu.HBM((most - FRONT, width // 2, width), BF16),
    ]
    half_scratch = [
        pltpu.VMEM((width // 2, KDIM), BF16),
        pltpu.VMEM((rhs_count, width // 2), BF16),
        pltpu.VMEM((2,) + pay_shape, BF16),
        pltpu.SemaphoreType.DMA((2,)),
    ]
    right_spec = pl.BlockSpec(right.shape, whole)
    send_shape = (rhs_count, width + TAIL)
    front_zero, back_zero, half_sum, slots = pl.pallas_call(
        functools.partial(pair_zero_kernel, zero_at),
        grid_spec=pltpu.PrefetchScalarGridSpec(
            num_scalar_prefetch=1,
            grid=(most, half),
            in_specs=[right_spec] + [row_spec] * PARTS + [any_spec] * len(zero),
            out_specs=half_specs + [row_spec, smem],
            scratch_shapes=half_scratch
            + [
                pltpu.VMEM((count, 16, 128), BF16),
                pltpu.VMEM((count, 128), jnp.int32),
                pltpu.SMEM((count, 128), jnp.int32),
                pltpu.SemaphoreType.DMA((count,)),
            ],
        ),
        out_shape=half_shapes
        + [shape(right_side.shape, F32), shape((most + 2,), jnp.int32)],
        compiler_params=params,
        name="pair_zero",
    )(me, right, *[part[2] for part in own_parts], *zero)
    front_one, back_one, image, send = pl.pallas_call(
        functools.partial(pair_one_kernel, one_at),
        grid_spec=pltpu.PrefetchScalarGridSpec(
            num_scalar_prefetch=1,
            grid=(most, half),
            in_specs=[right_spec, row_spec, row_spec, var_spec] + [any_spec] * len(one),
            out_specs=half_specs + [row_spec, pl.BlockSpec(send_shape, whole)],
            scratch_shapes=half_scratch,
        ),
        out_shape=half_shapes + [shape(right_side.shape, F32), shape(send_shape, BF16)],
        compiler_params=params,
        name="pair_one",
    )(slots, right, half_sum, right_side, var_row, *one)
    fronts = [pltpu.with_memory_space_constraint(part, pltpu.VMEM) for part in (front_zero, front_one)]
    backs = [pltpu.with_memory_space_constraint(part, pltpu.HBM) for part in (back_zero, back_one)]

    every_send = tree_gather(send, count)[-1]
    own_again = [
        pl.pallas_call(
            functools.partial(own_again_kernel, blocks),
            in_specs=[any_spec, pl.BlockSpec(send_shape, whole)],
            out_specs=row_spec,
            out_shape=shape(right_side.shape, F32),
            scratch_shapes=[
                pltpu.VMEM((len(blocks), ROWS, ROWS), BF16),
                pltpu.SemaphoreType.DMA((len(blocks),)),
            ],
            compiler_params=params,
            cost_estimate=pl.CostEstimate(
                flops=5_000_000_000, bytes_accessed=2 * len(blocks) * ROWS * ROWS, transcendentals=0
            ),
            name=f"own_again_{part}",
        )(in_hbm(tiles), send)
        for part, (blocks, tiles, _) in enumerate(own_parts)
    ]
    dots_spec = pl.BlockSpec((rhs_count, TAIL), whole)
    rows, dots, steps_one = pl.pallas_call(
        again_kernel,
        grid_spec=pltpu.PrefetchScalarGridSpec(
            num_scalar_prefetch=1,
            grid=(most,),
            in_specs=[
                pl.BlockSpec((1, width // 2, width), lambda k, s: (jnp.minimum(k, FRONT - 1), 0, 0)),
                pl.BlockSpec((1, width // 2, width), lambda k, s: (jnp.minimum(k, FRONT - 1), 0, 0)),
                any_spec,
                any_spec,
                pl.BlockSpec((1,) + send_shape, lambda k, s: (s[1 + k], 0, 0)),
                pl.BlockSpec((count, rhs_count, TAIL), lambda k, s: (0, 0, width // TAIL)),
                row_spec,
                var_spec,
                row_spec,
            ]
            + [row_spec] * PARTS,
            out_specs=[
                pl.BlockSpec((4 * rhs_count, width), whole),
                dots_spec,
                dots_spec,
            ],
            scratch_shapes=[
                pltpu.VMEM(right_side.shape, F32),
                pltpu.VMEM((HELD, ROWS, width), BF16),
                pltpu.SemaphoreType.DMA((HELD,)),
            ],
        ),
        out_shape=[
            shape((4 * rhs_count, width), F32),
            shape((rhs_count, TAIL), F32),
            shape((rhs_count, TAIL), F32),
        ],
        compiler_params=params,
        name="pair_again",
    )(slots, *fronts, *backs, every_send, every_send, right_side, var_row, image, *own_again)

    dots = tree_sum(dots, count)
    ordered = pl.pallas_call(
        order_kernel,
        out_shape=shape(rows.shape, F32),
        compiler_params=params,
        name="curve_order",
    )(rows, hilbert_order)
    norm, curve = steps_one[:, 0:1], steps_one[:, 1:2]
    length = norm / curve
    norm_next = dots[:, 0:1]
    ratio = norm_next / norm
    curve_next = dots[:, 1:2] + ratio * (dots[:, 2:3] + dots[:, 3:4]) + ratio * ratio * curve
    length_next = norm_next / curve_next
    rhs_o, res_o, image_o, res_image_o = [ordered[at : at + 8] for at in range(0, 32, 8)]
    solved = length * rhs_o + length_next * (res_o + ratio * rhs_o)
    residual = res_o - length_next * (res_image_o + ratio * image_o)
    return (solved, residual)


def solution(mesh):
    in_specs = (
        P(None, ("group", "row")),
        P(None, ("group", "row")),
        P(("group", "row")),
        P(("group", "row"), None),
        P(("group", "row"), None, None),
    )
    out_specs = (P(None, ("group", "row")), P(None, ("group", "row")))
    return jax.shard_map(local, mesh=mesh, in_specs=in_specs, out_specs=out_specs, check_vma=False)
```

```python
import functools

import jax
import jax.numpy as jnp
import numpy as np
from jax import lax
from jax.experimental import pallas as pl
from jax.experimental.pallas import tpu as pltpu
from jax.sharding import PartitionSpec as P

SHRINK = 0.95
GRAM = SHRINK * SHRINK
SCALE = 20.0 * (20.0 / 19.0) ** 19
DIAGONAL = float(1.0 - SCALE * float(np.float32(1.0 / SCALE).astype(jnp.bfloat16)))
KDIM = 128
ROWS = 512
PARTS = 2
PIECE = 256
STRIP = 64
FRONT = 3
HELD = 4
TAIL = 128
BF16 = jnp.bfloat16
F32 = jnp.float32
CONTRACT_LANES = (((1,), (1,)), ((), ()))


def split_three(value):
    high = value.astype(BF16).astype(F32)
    rest = value - high
    middle = rest.astype(BF16).astype(F32)
    return high, middle, rest - middle


def norm_rows(norm, first):
    high, middle, low = split_three(norm)
    row = lax.broadcasted_iota(jnp.int32, (32, norm.shape[1]), 0)
    out = jnp.where(row < 6, 1.0, 0.0)
    out = jnp.where(row == first, high, out)
    out = jnp.where(row == first + 1, middle, out)
    return jnp.where(row == first + 2, low, out).astype(BF16)


def own_factor(feat):
    wide = feat.astype(F32)
    norm = jnp.sum(wide * wide, axis=0, keepdims=True) * GRAM
    pieces = split_three(wide * (-2.0 * GRAM))
    return jnp.concatenate([piece.astype(BF16) for piece in pieces] + [norm_rows(norm, 0)], axis=0)


def other_factor(feat):
    wide = feat.astype(F32)
    norm = jnp.sum(wide * wide, axis=0, keepdims=True) * GRAM
    return jnp.transpose(jnp.concatenate([feat, feat, feat, norm_rows(norm, 3)], axis=0))


def psi_chain(dist):
    dist = jnp.maximum(dist, 1e-30)
    radius = dist * lax.rsqrt(dist)
    u = jnp.maximum(SHRINK - radius, 0.0)
    two = u * u
    four = two * two
    eight = four * four
    return (eight * eight * (two * (u - two))).astype(BF16)


def psi_power(dist):
    dist = jnp.maximum(dist, 1e-30)
    radius = dist * lax.rsqrt(dist)
    u = jnp.maximum(SHRINK - radius, 1e-30)
    return (jnp.exp2(19.0 * lax.log2(u)) * (1.0 - u)).astype(BF16)


def tile_unit(left, right, vec, tile_ref, psis):
    pieces = [slice(at, at + PIECE) for at in range(0, right.shape[1], PIECE)]
    gram = lambda piece: jnp.dot(left, right[:, piece], preferred_element_type=F32)
    product = lambda part: jnp.dot(vec, part, preferred_element_type=F32)
    dist, part, terms = gram(pieces[0]), None, []
    for index, piece in enumerate(pieces):
        following = gram(pieces[index + 1]) if index + 1 < len(pieces) else None
        strips = []
        for at in range(0, left.shape[0], STRIP):
            psi = psis[len(strips) % len(psis)]
            strips.append(psi(dist[at : at + STRIP]))
            tile_ref[at : at + STRIP, piece] = strips[-1]
        if part is not None:
            terms.append(product(part))
        dist, part = following, jnp.concatenate(strips, axis=0)
    return jnp.concatenate(terms + [product(part)], axis=1)


def unpack(pay):
    return jnp.concatenate([pay[:32], pay[32:64]], axis=1), jnp.concatenate([pay[64:72], pay[72:80]], axis=1)


def own_blocks(rows, count):
    return [(row, col) for row in rows for col in range(row, count)]


def own_kernel(
    rows, left_ref, right_ref, vec_ref, arrived_ref, out_ref, sum_ref, tile_ref, sem_ref
):
    sum_ref[...] = jnp.zeros_like(sum_ref)
    count = vec_ref.shape[1] // ROWS
    piece = lambda index: pl.ds(pl.multiple_of(index * ROWS, ROWS), ROWS)
    save = lambda at: pltpu.make_async_copy(tile_ref.at[at], out_ref.at[at], sem_ref.at[at])

    def row_step(row, at):
        def col_step(col, at):
            sum_ref[:, piece(col)] += tile_unit(
                left_ref[piece(row), :], right_ref[:, piece(col)], vec_ref[:, piece(row)],
                tile_ref.at[at], (psi_power,),
            )
            save(at).start()

            @pl.when(row != col)
            def _():
                sum_ref[:, piece(row)] += lax.dot_general(
                    vec_ref[:, piece(col)], tile_ref[at], CONTRACT_LANES,
                    preferred_element_type=F32,
                )

            return at + 1

        return lax.fori_loop(row, count, col_step, at)

    lax.fori_loop(rows[0], rows[-1] + 1, row_step, 0)
    for at in range(tile_ref.shape[0]):
        save(at).wait()


def own_again_kernel(blocks, in_ref, vec_ref, sum_ref, tile_ref, sem_ref):
    load = lambda index: pltpu.make_async_copy(
        in_ref.at[index], tile_ref.at[index], sem_ref.at[index]
    )
    for index in range(len(blocks)):
        load(index).start()
    sum_ref[...] = jnp.zeros_like(sum_ref)
    piece = lambda index: slice(index * ROWS, (index + 1) * ROWS)
    for index, (row, col) in enumerate(blocks):
        load(index).wait()
        sum_ref[:, piece(col)] += jnp.dot(
            vec_ref[:, piece(row)], tile_ref[index], preferred_element_type=F32
        )
        if row != col:
            sum_ref[:, piece(row)] += lax.dot_general(
                vec_ref[:, piece(col)], tile_ref[index], CONTRACT_LANES, preferred_element_type=F32
            )


def payload_kernel(
    list_ref, feat_ref, rhs_ref, pay_zero_ref, pay_one_ref, right_ref, left_ref, vec_ref
):
    feat = feat_ref[...]
    rounded = rhs_ref[...].astype(BF16)
    quarter = feat.shape[1] // 4
    for half, pay_ref in enumerate((pay_zero_ref, pay_one_ref)):
        first, second = [slice(at * quarter, (at + 1) * quarter) for at in (2 * half, 2 * half + 1)]
        pay_ref[:32] = feat[:, first]
        pay_ref[32:64] = feat[:, second]
        pay_ref[64:80] = jnp.concatenate([rounded[:, first], rounded[:, second]], axis=0)
    lane = lax.broadcasted_iota(jnp.int32, (16, quarter), 1)
    numbers = jnp.full(lane.shape, -1, jnp.int32)
    for entry in range(list_ref.shape[1]):
        numbers = jnp.where(lane == entry, list_ref[0, entry, 1], numbers)
    pay_zero_ref[80:96] = numbers.astype(F32).astype(BF16)
    right_ref[...] = own_factor(feat)
    left_ref[...] = other_factor(feat)
    vec_ref[...] = rounded


def find_partners(lists_ref, me, slots_ref):
    count, most = lists_ref.shape[0], slots_ref.shape[0] - 2
    for at in range(slots_ref.shape[0]):
        slots_ref[at] = 0
    total = jnp.int32(0)
    for at, place in enumerate(gather_places(count)):
        if at == 0:
            continue
        number = me ^ place
        hit = jnp.bool_(False)
        for entry in range(most):
            hit = hit | (lists_ref[at, entry] == me) | (lists_ref[0, entry] == number)
        slots_ref[1 + total] = jnp.where(hit, at, 0)
        total = total + hit.astype(jnp.int32)
    slots_ref[0] = total


def fetch_from(block_at, block_refs, slots_ref, pay_ref, sem_ref):
    def fetch(which):
        for at, (index, row) in enumerate(block_at):
            @pl.when(slots_ref[1 + which] == at)
            def _():
                pltpu.make_async_copy(
                    block_refs[index].at[pl.ds(row, 80)],
                    pay_ref.at[which % 2],
                    sem_ref.at[which % 2],
                ).start()

    return fetch


def half_tiles(psis, slots_ref, right_ref, fetch, front_ref, back_ref, sum_ref, left_ref, vec_ref, pay_ref, sem_ref):
    slot, step = pl.program_id(0), pl.program_id(1)

    @pl.when((slot == 0) & (step == 0) & (slots_ref[0] > 0))
    def _():
        fetch(0)

    @pl.when(slot < slots_ref[0])
    def _():
        @pl.when(step == 0)
        def _():
            pltpu.make_async_copy(
                pay_ref.at[(slot + 1) % 2], pay_ref.at[slot % 2], sem_ref.at[slot % 2]
            ).wait()

            @pl.when(slot + 1 < slots_ref[0])
            def _():
                fetch(slot + 1)

            feat, vec = unpack(pay_ref[slot % 2])
            left_ref[...] = other_factor(feat)
            vec_ref[...] = vec

        rows = pl.ds(pl.multiple_of(step * ROWS, ROWS), ROWS)
        left, vec = left_ref[rows, :], vec_ref[:, rows]
        for tile_ref, here in ((front_ref, slot < FRONT), (back_ref, slot >= FRONT)):
            @pl.when(here)
            def _():
                sum_ref[...] += tile_unit(left, right_ref[...], vec, tile_ref.at[0], psis)


def pair_zero_kernel(block_at, me_ref, right_ref, *refs):
    first_refs, block_refs = refs[:PARTS], refs[PARTS:-12]
    front_ref, back_ref, sum_ref, slots_ref = refs[-12:-8]
    left_ref, vec_ref, pay_ref, sem_ref, strip_ref, list_ref, lists_ref, strip_sem_ref = refs[-8:]

    @pl.when((pl.program_id(0) == 0) & (pl.program_id(1) == 0))
    def _():
        strips = [
            pltpu.make_async_copy(
                block_refs[index].at[pl.ds(row + 80, 16), pl.ds(0, 128)],
                strip_ref.at[at],
                strip_sem_ref.at[at],
            )
            for at, (index, row) in enumerate(block_at)
        ]
        for strip in strips:
            strip.start()
        sum_ref[...] = functools.reduce(jnp.add, [first_ref[...] for first_ref in first_refs])
        for at, strip in enumerate(strips):
            strip.wait()
            list_ref[at : at + 1, :] = strip_ref[at].astype(F32)[:1].astype(jnp.int32)
        numbers = pltpu.make_async_copy(list_ref, lists_ref, strip_sem_ref.at[0])
        numbers.start()
        numbers.wait()
        find_partners(lists_ref, me_ref[0], slots_ref)

    fetch = fetch_from(block_at, block_refs, slots_ref, pay_ref, sem_ref)
    half_tiles(
        (psi_power, psi_chain), slots_ref, right_ref, fetch, front_ref, back_ref, sum_ref, left_ref, vec_ref, pay_ref, sem_ref
    )


def pair_one_kernel(block_at, slots_ref, right_ref, first_ref, rhs_ref, var_ref, *refs):
    block_refs = refs[:-8]
    front_ref, back_ref, image_ref, send_ref, left_ref, vec_ref, pay_ref, sem_ref = refs[-8:]
    slot, step = pl.program_id(0), pl.program_id(1)

    @pl.when((slot == 0) & (step == 0))
    def _():
        image_ref[...] = first_ref[...]

    fetch = fetch_from(block_at, block_refs, slots_ref, pay_ref, sem_ref)
    half_tiles(
        (psi_chain,), slots_ref, right_ref, fetch, front_ref, back_ref, image_ref, left_ref, vec_ref, pay_ref, sem_ref
    )

    @pl.when((slot == pl.num_programs(0) - 1) & (step == pl.num_programs(1) - 1))
    def _():
        rhs = rhs_ref[...]
        width = rhs.shape[1]
        image = (var_ref[...] + DIAGONAL) * rhs + SCALE * image_ref[...]
        image_ref[...] = image
        send_ref[:, :width] = image.astype(BF16)
        pieces = split_three(jnp.sum(rhs * rhs, axis=1, keepdims=True))
        pieces += split_three(jnp.sum(rhs * image, axis=1, keepdims=True))
        lane = lax.broadcasted_iota(jnp.int32, (rhs.shape[0], TAIL), 1)
        tail = jnp.zeros((rhs.shape[0], TAIL), F32)
        for place, piece in enumerate(pieces):
            tail = jnp.where(lane == place, piece, tail)
        send_ref[:, width:] = tail.astype(BF16)


def again_kernel(
    slots_ref, front_zero_ref, front_one_ref, back_zero_ref, back_one_ref,
    vec_ref, tails_ref, rhs_ref, var_ref, image_ref, *refs
):
    first_refs = refs[:PARTS]
    rows_ref, dots_ref, step_ref, sum_ref, held_ref, sem_ref = refs[PARTS:]
    slot = pl.program_id(0)
    width = rhs_ref.shape[1]
    steps = width // ROWS
    half = width // 2
    parts = (slots_ref[0] - FRONT) * steps

    def fetch(part, back_ref, first):
        at = pl.ds(pl.multiple_of((part % steps - first) * ROWS, ROWS), ROWS)
        return pltpu.make_async_copy(
            back_ref.at[part // steps, at], held_ref.at[part % HELD], sem_ref.at[part % HELD]
        )

    def start(part):
        @pl.when((part < parts) & (part % steps < steps // 2))
        def _():
            fetch(part, back_zero_ref, 0).start()

        @pl.when((part < parts) & (part % steps >= steps // 2))
        def _():
            fetch(part, back_one_ref, steps // 2).start()

    @pl.when(slot == 0)
    def _():
        sum_ref[...] = functools.reduce(jnp.add, [first_ref[...] for first_ref in first_refs])
        for part in range(HELD):
            start(part)

    @pl.when((slot < slots_ref[0]) & (slot < FRONT))
    def _():
        for index, front_ref in enumerate((front_zero_ref, front_one_ref)):
            sum_ref[...] += jnp.dot(
                vec_ref[0, :, index * half : (index + 1) * half], front_ref[0],
                preferred_element_type=F32,
            )

    @pl.when((slot < slots_ref[0]) & (slot >= FRONT))
    def _():
        for step in range(steps):
            part = (slot - FRONT) * steps + step
            fetch(part % HELD, back_zero_ref, part % HELD // (steps // 2) * (steps // 2)).wait()
            sum_ref[...] += jnp.dot(
                vec_ref[0, :, step * ROWS : (step + 1) * ROWS], held_ref[part % HELD],
                preferred_element_type=F32,
            )
            start(part + HELD)

    @pl.when(slot == pl.num_programs(0) - 1)
    def _():
        rhs = rhs_ref[...]
        image = image_ref[...]
        total = jnp.sum(tails_ref[...].astype(F32), axis=0)
        norm = total[:, 0:1] + total[:, 1:2] + total[:, 2:3]
        curve = total[:, 3:4] + total[:, 4:5] + total[:, 5:6]
        length = norm / curve
        second = (var_ref[...] + DIAGONAL) * image + SCALE * sum_ref[...]
        res = rhs - length * image
        res_image = image - length * second
        rows_ref[0:8] = rhs
        rows_ref[8:16] = res
        rows_ref[16:24] = image
        rows_ref[24:32] = res_image
        lane = lax.broadcasted_iota(jnp.int32, (rhs.shape[0], TAIL), 1)
        dots = jnp.zeros((rhs.shape[0], TAIL), F32)
        for place, product in enumerate((res * res, res * res_image, res * image, rhs * res_image)):
            dots = jnp.where(lane == place, jnp.sum(product, axis=1, keepdims=True), dots)
        dots_ref[...] = dots
        step_ref[...] = jnp.where(lane == 0, norm, jnp.where(lane == 1, curve, 0.0))


def order_kernel(rows_ref, perm_ref, out_ref):
    rows = rows_ref[...]
    count, width = rows.shape
    pieces = jnp.concatenate([piece for piece in split_three(rows)], axis=0).astype(BF16)
    perm = perm_ref[...]
    chunk = 256
    for col in range(0, width, chunk):
        total = jnp.zeros((3 * count, chunk), F32)
        for at in range(0, width, chunk):
            index = lax.broadcasted_iota(jnp.int32, (chunk, chunk), 0) + at
            pick = jnp.where(index == perm[:, col : col + chunk], 1.0, 0.0).astype(BF16)
            total += jnp.dot(pieces[:, at : at + chunk], pick, preferred_element_type=F32)
        out_ref[:, col : col + chunk] = total[:count] + total[count : 2 * count] + total[2 * count :]


def swap(value, mask, count):
    return lax.ppermute(value, "row", [(i, i ^ mask) for i in range(count)])


def levels(count, sizes):
    bits = count.bit_length() - 1
    out = []
    sizes = list(sizes)
    while bits:
        take = min(sizes.pop(0) if sizes else 1, bits)
        bits -= take
        out.append([mask << bits for mask in range(1, 1 << take)])
    return out


def tree_sum(value, count):
    for masks in levels(count, [2, 2, 2]):
        others = [swap(value, mask, count) for mask in masks]
        if len(masks) == 3:
            value = (value + others[0]) + (others[1] + others[2])
        else:
            value = value + others[0]
    return value


def gather_levels(count):
    return levels(count, [2] if count <= 16 else [2, 2])


def gather_places(count):
    places = [0]
    for masks in gather_levels(count):
        places = places + [place ^ mask for mask in masks for place in places]
    return places


def tree_gather(value, count):
    blocks, out = value[None], []
    for masks in gather_levels(count):
        blocks = jnp.concatenate([blocks] + [swap(blocks, mask, count) for mask in masks], axis=0)
        out.append(blocks)
    return out


def gate(block, behind):
    return pl.pallas_call(
        lambda *refs: None,
        in_specs=[pl.BlockSpec(memory_space=pl.ANY)] * 2,
        out_specs=pl.BlockSpec(memory_space=pl.ANY),
        out_shape=jax.ShapeDtypeStruct(block.shape, block.dtype),
        input_output_aliases={0: 0},
        compiler_params=pltpu.CompilerParams(vmem_limit_bytes=1024 * 1024),
        name="gate",
    )(block, behind)


def local(features, right_side, variance, hilbert_order, tile_list):
    width = features.shape[1]
    rhs_count = right_side.shape[0]
    count = lax.axis_size("row")
    most = tile_list.shape[1]
    steps = width // ROWS
    shape = jax.ShapeDtypeStruct
    params = pltpu.CompilerParams(vmem_limit_bytes=10 * 1024 * 1024)
    var_row = variance[None, :]

    whole = lambda *ignored: (0, 0)
    row_spec = pl.BlockSpec(right_side.shape, whole)
    var_spec = pl.BlockSpec(var_row.shape, whole)
    pay_shape = (80, width // 4)
    smem = pl.BlockSpec(memory_space=pltpu.SMEM)
    vmem = pl.BlockSpec(memory_space=pltpu.VMEM)
    in_hbm = lambda array: pltpu.with_memory_space_constraint(array, pltpu.HBM)
    pay_zero, pay_one, right, left, rounded = pl.pallas_call(
        payload_kernel,
        in_specs=[smem, vmem, vmem],
        out_shape=[
            shape((96, width // 4), BF16),
            shape(pay_shape, BF16),
            shape((KDIM, width), BF16),
            shape((width, KDIM), BF16),
            shape(right_side.shape, BF16),
        ],
        compiler_params=params,
        name="payload",
    )(tile_list, in_hbm(features), in_hbm(right_side))
    me = jnp.full((1,), lax.axis_index("row"), jnp.int32)
    any_spec = pl.BlockSpec(memory_space=pl.ANY)

    def own_part(rows, arrived):
        blocks = own_blocks(rows, steps)
        tiles, sums = pl.pallas_call(
            functools.partial(own_kernel, rows),
            in_specs=[vmem, vmem, vmem, any_spec],
            out_specs=[any_spec, vmem],
            out_shape=[pltpu.HBM((len(blocks), ROWS, ROWS), BF16), shape(right_side.shape, F32)],
            scratch_shapes=[
                pltpu.VMEM((len(blocks), ROWS, ROWS), BF16),
                pltpu.SemaphoreType.DMA((len(blocks),)),
            ],
            compiler_params=params,
            cost_estimate=pl.CostEstimate(
                flops=5_000_000_000, bytes_accessed=2 * len(blocks) * ROWS * ROWS, transcendentals=0
            ),
            name=f"own_tile_{rows[0]}",
        )(left, right, rounded, arrived)
        return blocks, tiles, sums

    first_masks, *later = gather_levels(count)
    first_level = lambda pay: jnp.concatenate(
        [pay] + [swap(pay, mask, count) for mask in first_masks], axis=0
    )
    near_zero = first_level(pay_zero)
    own_parts = [own_part(range(1), right)]
    near_zero = gate(near_zero, own_parts[0][2])
    near_one = first_level(gate(pay_one, own_parts[0][2]))
    own_parts.append(own_part(range(1, steps), near_zero))
    near_one = gate(near_one, own_parts[1][2])
    zero, places = [near_zero], [0]
    for level, masks in enumerate(later):
        zero = zero + [swap(array, mask, count) for mask in masks for array in zero]
        places = places + [mask ^ place for mask in masks for place in places]
        if level == 0:
            zero[-1] = gate(zero[-1], own_parts[1][2])
    one = [near_one] + [swap(near_one, place, count) for place in places[1:]]
    each = len(first_masks) + 1
    zero_at = [(at, row * 96) for at in range(len(zero)) for row in range(each)]
    one_at = [(at, row * 80) for at in range(len(one)) for row in range(each)]

    half = steps // 2

    def front_at(k, i, *ignored):
        return (jnp.minimum(k, FRONT - 1), jnp.where(k < FRONT, i, half - 1), 0)

    def back_at(k, i, *ignored):
        return (jnp.maximum(k - FRONT, 0), jnp.where(k < FRONT, 0, i), 0)

    half_specs = [pl.BlockSpec((1, ROWS, width), front_at), pl.BlockSpec((1, ROWS, width), back_at)]
    half_shapes = [
        pltpu.VMEM((FRONT, width // 2, width), BF16),
        pltpu.HBM((most - FRONT, width // 2, width), BF16),
    ]
    half_scratch = [
        pltpu.VMEM((width // 2, KDIM), BF16),
        pltpu.VMEM((rhs_count, width // 2), BF16),
        pltpu.VMEM((2,) + pay_shape, BF16),
        pltpu.SemaphoreType.DMA((2,)),
    ]
    right_spec = pl.BlockSpec(right.shape, whole)
    send_shape = (rhs_count, width + TAIL)
    front_zero, back_zero, half_sum, slots = pl.pallas_call(
        functools.partial(pair_zero_kernel, zero_at),
        grid_spec=pltpu.PrefetchScalarGridSpec(
            num_scalar_prefetch=1,
            grid=(most, half),
            in_specs=[right_spec] + [row_spec] * PARTS + [any_spec] * len(zero),
            out_specs=half_specs + [row_spec, smem],
            scratch_shapes=half_scratch
            + [
                pltpu.VMEM((count, 16, 128), BF16),
                pltpu.VMEM((count, 128), jnp.int32),
                pltpu.SMEM((count, 128), jnp.int32),
                pltpu.SemaphoreType.DMA((count,)),
            ],
        ),
        out_shape=half_shapes
        + [shape(right_side.shape, F32), shape((most + 2,), jnp.int32)],
        compiler_params=params,
        name="pair_zero",
    )(me, right, *[part[2] for part in own_parts], *zero)
    front_one, back_one, image, send = pl.pallas_call(
        functools.partial(pair_one_kernel, one_at),
        grid_spec=pltpu.PrefetchScalarGridSpec(
            num_scalar_prefetch=1,
            grid=(most, half),
            in_specs=[right_spec, row_spec, row_spec, var_spec] + [any_spec] * len(one),
            out_specs=half_specs + [row_spec, pl.BlockSpec(send_shape, whole)],
            scratch_shapes=half_scratch,
        ),
        out_shape=half_shapes + [shape(right_side.shape, F32), shape(send_shape, BF16)],
        compiler_params=params,
        name="pair_one",
    )(slots, right, half_sum, right_side, var_row, *one)
    fronts = [pltpu.with_memory_space_constraint(part, pltpu.VMEM) for part in (front_zero, front_one)]
    backs = [pltpu.with_memory_space_constraint(part, pltpu.HBM) for part in (back_zero, back_one)]

    every_send = tree_gather(send, count)[-1]
    own_again = [
        pl.pallas_call(
            functools.partial(own_again_kernel, blocks),
            in_specs=[any_spec, pl.BlockSpec(send_shape, whole)],
            out_specs=row_spec,
            out_shape=shape(right_side.shape, F32),
            scratch_shapes=[
                pltpu.VMEM((len(blocks), ROWS, ROWS), BF16),
                pltpu.SemaphoreType.DMA((len(blocks),)),
            ],
            compiler_params=params,
            cost_estimate=pl.CostEstimate(
                flops=5_000_000_000, bytes_accessed=2 * len(blocks) * ROWS * ROWS, transcendentals=0
            ),
            name=f"own_again_{part}",
        )(in_hbm(tiles), send)
        for part, (blocks, tiles, _) in enumerate(own_parts)
    ]
    dots_spec = pl.BlockSpec((rhs_count, TAIL), whole)
    rows, dots, steps_one = pl.pallas_call(
        again_kernel,
        grid_spec=pltpu.PrefetchScalarGridSpec(
            num_scalar_prefetch=1,
            grid=(most,),
            in_specs=[
                pl.BlockSpec((1, width // 2, width), lambda k, s: (jnp.minimum(k, FRONT - 1), 0, 0)),
                pl.BlockSpec((1, width // 2, width), lambda k, s: (jnp.minimum(k, FRONT - 1), 0, 0)),
                any_spec,
                any_spec,
                pl.BlockSpec((1,) + send_shape, lambda k, s: (s[1 + k], 0, 0)),
                pl.BlockSpec((count, rhs_count, TAIL), lambda k, s: (0, 0, width // TAIL)),
                row_spec,
                var_spec,
                row_spec,
            ]
            + [row_spec] * PARTS,
            out_specs=[
                pl.BlockSpec((4 * rhs_count, width), whole),
                dots_spec,
                dots_spec,
            ],
            scratch_shapes=[
                pltpu.VMEM(right_side.shape, F32),
                pltpu.VMEM((HELD, ROWS, width), BF16),
                pltpu.SemaphoreType.DMA((HELD,)),
            ],
        ),
        out_shape=[
            shape((4 * rhs_count, width), F32),
            shape((rhs_count, TAIL), F32),
            shape((rhs_count, TAIL), F32),
        ],
        compiler_params=params,
        name="pair_again",
    )(slots, *fronts, *backs, every_send, every_send, right_side, var_row, image, *own_again)

    dots = tree_sum(dots, count)
    ordered = pl.pallas_call(
        order_kernel,
        out_shape=shape(rows.shape, F32),
        compiler_params=params,
        name="curve_order",
    )(rows, hilbert_order)
    norm, curve = steps_one[:, 0:1], steps_one[:, 1:2]
    length = norm / curve
    norm_next = dots[:, 0:1]
    ratio = norm_next / norm
    curve_next = dots[:, 1:2] + ratio * (dots[:, 2:3] + dots[:, 3:4]) + ratio * ratio * curve
    length_next = norm_next / curve_next
    rhs_o, res_o, image_o, res_image_o = [ordered[at : at + 8] for at in range(0, 32, 8)]
    solved = length * rhs_o + length_next * (res_o + ratio * rhs_o)
    residual = res_o - length_next * (res_image_o + ratio * image_o)
    return (solved, residual)


def solution(mesh):
    in_specs = (
        P(None, ("group", "row")),
        P(None, ("group", "row")),
        P(("group", "row")),
        P(("group", "row"), None),
        P(("group", "row"), None, None),
    )
    out_specs = (P(None, ("group", "row")), P(None, ("group", "row")))
    return jax.shard_map(local, mesh=mesh, in_specs=in_specs, out_specs=out_specs, check_vma=False)
```

```python
import functools

import jax
import jax.numpy as jnp
import numpy as np
from jax import lax
from jax.experimental import pallas as pl
from jax.experimental.pallas import tpu as pltpu
from jax.sharding import PartitionSpec as P

SHRINK = 0.95
GRAM = SHRINK * SHRINK
SCALE = 20.0 * (20.0 / 19.0) ** 19
DIAGONAL = float(1.0 - SCALE * float(np.float32(1.0 / SCALE).astype(jnp.bfloat16)))
KDIM = 128
ROWS = 512
PARTS = 2
PIECE = 256
STRIP = 64
FRONT = 3
HELD = 4
TAIL = 128
BF16 = jnp.bfloat16
F32 = jnp.float32
CONTRACT_LANES = (((1,), (1,)), ((), ()))


def split_three(value):
    high = value.astype(BF16).astype(F32)
    rest = value - high
    middle = rest.astype(BF16).astype(F32)
    return high, middle, rest - middle


def norm_rows(norm, first):
    high, middle, low = split_three(norm)
    row = lax.broadcasted_iota(jnp.int32, (32, norm.shape[1]), 0)
    out = jnp.where(row < 6, 1.0, 0.0)
    out = jnp.where(row == first, high, out)
    out = jnp.where(row == first + 1, middle, out)
    return jnp.where(row == first + 2, low, out).astype(BF16)


def own_factor(feat):
    wide = feat.astype(F32)
    norm = jnp.sum(wide * wide, axis=0, keepdims=True) * GRAM
    pieces = split_three(wide * (-2.0 * GRAM))
    return jnp.concatenate([piece.astype(BF16) for piece in pieces] + [norm_rows(norm, 0)], axis=0)


def other_factor(feat):
    wide = feat.astype(F32)
    norm = jnp.sum(wide * wide, axis=0, keepdims=True) * GRAM
    return jnp.transpose(jnp.concatenate([feat, feat, feat, norm_rows(norm, 3)], axis=0))


def psi_power(dist):
    dist = jnp.maximum(dist, 1e-30)
    radius = dist * lax.rsqrt(dist)
    u = jnp.maximum(SHRINK - radius, 1e-30)
    return (jnp.exp2(19.0 * lax.log2(u)) * (1.0 - u)).astype(BF16)


def tile_unit(left, right, vec, tile_ref, aside=None):
    pieces = [slice(at, at + PIECE) for at in range(0, right.shape[1], PIECE)]
    gram = lambda piece: jnp.dot(left, right[:, piece], preferred_element_type=F32)
    product = lambda part: jnp.dot(vec, part, preferred_element_type=F32)
    dist, part, terms = gram(pieces[0]), None, []
    for index, piece in enumerate(pieces):
        following = gram(pieces[index + 1]) if index + 1 < len(pieces) else None
        strips = []
        for at in range(0, left.shape[0], STRIP):
            strips.append(psi_power(dist[at : at + STRIP]))
            tile_ref[at : at + STRIP, piece] = strips[-1]
        if part is not None:
            terms.append(product(part))
        if index == 1 and aside is not None:
            aside()
        dist, part = following, jnp.concatenate(strips, axis=0)
    return jnp.concatenate(terms + [product(part)], axis=1)


def unpack(pay):
    return jnp.concatenate([pay[:32], pay[32:64]], axis=1), jnp.concatenate([pay[64:72], pay[72:80]], axis=1)


def own_blocks(rows, count):
    return [(row, col) for row in rows for col in range(row, count)]


def own_kernel(
    rows, left_ref, right_ref, vec_ref, arrived_ref, out_ref, sum_ref, tile_ref, sem_ref
):
    sum_ref[...] = jnp.zeros_like(sum_ref)
    count = vec_ref.shape[1] // ROWS
    piece = lambda index: pl.ds(pl.multiple_of(index * ROWS, ROWS), ROWS)
    save = lambda at: pltpu.make_async_copy(tile_ref.at[at], out_ref.at[at], sem_ref.at[at])

    def row_step(row, at):
        def col_step(col, at):
            sum_ref[:, piece(col)] += tile_unit(
                left_ref[piece(row), :], right_ref[:, piece(col)], vec_ref[:, piece(row)],
                tile_ref.at[at],
            )
            save(at).start()

            @pl.when(row != col)
            def _():
                sum_ref[:, piece(row)] += lax.dot_general(
                    vec_ref[:, piece(col)], tile_ref[at], CONTRACT_LANES,
                    preferred_element_type=F32,
                )

            return at + 1

        return lax.fori_loop(row, count, col_step, at)

    lax.fori_loop(rows[0], rows[-1] + 1, row_step, 0)
    for at in range(tile_ref.shape[0]):
        save(at).wait()


def own_again_kernel(blocks, in_ref, vec_ref, sum_ref, tile_ref, sem_ref):
    load = lambda index: pltpu.make_async_copy(
        in_ref.at[index], tile_ref.at[index], sem_ref.at[index]
    )
    for index in range(len(blocks)):
        load(index).start()
    sum_ref[...] = jnp.zeros_like(sum_ref)
    piece = lambda index: slice(index * ROWS, (index + 1) * ROWS)
    for index, (row, col) in enumerate(blocks):
        load(index).wait()
        sum_ref[:, piece(col)] += jnp.dot(
            vec_ref[:, piece(row)], tile_ref[index], preferred_element_type=F32
        )
        if row != col:
            sum_ref[:, piece(row)] += lax.dot_general(
                vec_ref[:, piece(col)], tile_ref[index], CONTRACT_LANES, preferred_element_type=F32
            )


def payload_kernel(
    list_ref, feat_ref, rhs_ref, pay_zero_ref, pay_one_ref, right_ref, left_ref, vec_ref
):
    feat = feat_ref[...]
    rounded = rhs_ref[...].astype(BF16)
    quarter = feat.shape[1] // 4
    for half, pay_ref in enumerate((pay_zero_ref, pay_one_ref)):
        first, second = [slice(at * quarter, (at + 1) * quarter) for at in (2 * half, 2 * half + 1)]
        pay_ref[:32] = feat[:, first]
        pay_ref[32:64] = feat[:, second]
        pay_ref[64:80] = jnp.concatenate([rounded[:, first], rounded[:, second]], axis=0)
    lane = lax.broadcasted_iota(jnp.int32, (16, quarter), 1)
    numbers = jnp.full(lane.shape, -1, jnp.int32)
    for entry in range(list_ref.shape[1]):
        numbers = jnp.where(lane == entry, list_ref[0, entry, 1], numbers)
    pay_zero_ref[80:96] = numbers.astype(F32).astype(BF16)
    right_ref[...] = own_factor(feat)
    left_ref[...] = other_factor(feat)
    vec_ref[...] = rounded


def find_partners(lists_ref, me, slots_ref):
    count, most = lists_ref.shape[0], slots_ref.shape[0] - 2
    for at in range(slots_ref.shape[0]):
        slots_ref[at] = 0
    total = jnp.int32(0)
    for at, place in enumerate(gather_places(count)):
        if at == 0:
            continue
        number = me ^ place
        hit = jnp.bool_(False)
        for entry in range(most):
            hit = hit | (lists_ref[at, entry] == me) | (lists_ref[0, entry] == number)
        slots_ref[1 + total] = jnp.where(hit, at, 0)
        total = total + hit.astype(jnp.int32)
    slots_ref[0] = total


def fetch_from(block_at, block_refs, slots_ref, pay_ref, sem_ref):
    def fetch(which):
        for at, (index, row) in enumerate(block_at):
            @pl.when(slots_ref[1 + which] == at)
            def _():
                pltpu.make_async_copy(
                    block_refs[index].at[pl.ds(row, 80)],
                    pay_ref.at[which % 2],
                    sem_ref.at[which % 2],
                ).start()

    return fetch


def half_tiles(early, slots_ref, right_ref, fetch, front_ref, back_ref, sum_ref, left_ref, vec_ref, pay_ref, sem_ref):
    slot, step = pl.program_id(0), pl.program_id(1)
    last = pl.num_programs(1) - 1

    def arrive(which):
        pltpu.make_async_copy(
            pay_ref.at[(which + 1) % 2], pay_ref.at[which % 2], sem_ref.at[which % 2]
        ).wait()

    def factor(which):
        feat, vec = unpack(pay_ref[which % 2])
        left_ref[which % 2] = other_factor(feat)
        vec_ref[which % 2] = vec

    @pl.when((slot == 0) & (step == 0) & (slots_ref[0] > 0))
    def _():
        fetch(0)

    @pl.when(slot < slots_ref[0])
    def _():
        @pl.when((step == 0) & ((slot == 0) | (not early)))
        def _():
            arrive(slot)
            factor(slot)

        @pl.when((step == 0) & (slot + 1 < slots_ref[0]))
        def _():
            fetch(slot + 1)

        if early:
            @pl.when((step == last) & (slot + 1 < slots_ref[0]))
            def _():
                arrive(slot + 1)

        rows = pl.ds(pl.multiple_of(step * ROWS, ROWS), ROWS)
        place = slot % 2
        left, vec = left_ref[place, rows, :], vec_ref[place, :, rows]
        for tile_ref, here in ((front_ref, slot < FRONT), (back_ref, slot >= FRONT)):
            for ends in (False, True) if early else (None,):
                @pl.when(here if ends is None else here & ((step == last) == ends))
                def _():
                    aside = (lambda: factor(slot + 1)) if ends else None
                    sum_ref[...] += tile_unit(left, right_ref[...], vec, tile_ref.at[0], aside)


def pair_zero_kernel(block_at, me_ref, right_ref, *refs):
    first_refs, block_refs = refs[:PARTS], refs[PARTS:-12]
    front_ref, back_ref, sum_ref, slots_ref = refs[-12:-8]
    left_ref, vec_ref, pay_ref, sem_ref, strip_ref, list_ref, lists_ref, strip_sem_ref = refs[-8:]

    @pl.when((pl.program_id(0) == 0) & (pl.program_id(1) == 0))
    def _():
        strips = [
            pltpu.make_async_copy(
                block_refs[index].at[pl.ds(row + 80, 16), pl.ds(0, 128)],
                strip_ref.at[at],
                strip_sem_ref.at[at],
            )
            for at, (index, row) in enumerate(block_at)
        ]
        for strip in strips:
            strip.start()
        sum_ref[...] = functools.reduce(jnp.add, [first_ref[...] for first_ref in first_refs])
        for at, strip in enumerate(strips):
            strip.wait()
            list_ref[at : at + 1, :] = strip_ref[at].astype(F32)[:1].astype(jnp.int32)
        numbers = pltpu.make_async_copy(list_ref, lists_ref, strip_sem_ref.at[0])
        numbers.start()
        numbers.wait()
        find_partners(lists_ref, me_ref[0], slots_ref)

    fetch = fetch_from(block_at, block_refs, slots_ref, pay_ref, sem_ref)
    half_tiles(
        True, slots_ref, right_ref, fetch, front_ref, back_ref, sum_ref, left_ref, vec_ref, pay_ref, sem_ref
    )


def pair_one_kernel(block_at, slots_ref, right_ref, first_ref, rhs_ref, var_ref, *refs):
    block_refs = refs[:-8]
    front_ref, back_ref, image_ref, send_ref, left_ref, vec_ref, pay_ref, sem_ref = refs[-8:]
    slot, step = pl.program_id(0), pl.program_id(1)

    @pl.when((slot == 0) & (step == 0))
    def _():
        image_ref[...] = first_ref[...]

    fetch = fetch_from(block_at, block_refs, slots_ref, pay_ref, sem_ref)
    half_tiles(
        False, slots_ref, right_ref, fetch, front_ref, back_ref, image_ref, left_ref, vec_ref, pay_ref, sem_ref
    )

    @pl.when((slot == pl.num_programs(0) - 1) & (step == pl.num_programs(1) - 1))
    def _():
        rhs = rhs_ref[...]
        width = rhs.shape[1]
        image = (var_ref[...] + DIAGONAL) * rhs + SCALE * image_ref[...]
        image_ref[...] = image
        send_ref[:, :width] = image.astype(BF16)
        pieces = split_three(jnp.sum(rhs * rhs, axis=1, keepdims=True))
        pieces += split_three(jnp.sum(rhs * image, axis=1, keepdims=True))
        lane = lax.broadcasted_iota(jnp.int32, (rhs.shape[0], TAIL), 1)
        tail = jnp.zeros((rhs.shape[0], TAIL), F32)
        for place, piece in enumerate(pieces):
            tail = jnp.where(lane == place, piece, tail)
        send_ref[:, width:] = tail.astype(BF16)


def again_kernel(
    slots_ref, front_zero_ref, front_one_ref, back_zero_ref, back_one_ref,
    vec_ref, tails_ref, rhs_ref, var_ref, image_ref, *refs
):
    first_refs = refs[:PARTS]
    rows_ref, dots_ref, step_ref, sum_ref, held_ref, sem_ref = refs[PARTS:]
    slot = pl.program_id(0)
    width = rhs_ref.shape[1]
    steps = width // ROWS
    half = width // 2
    parts = (slots_ref[0] - FRONT) * steps

    def fetch(part, back_ref, first):
        at = pl.ds(pl.multiple_of((part % steps - first) * ROWS, ROWS), ROWS)
        return pltpu.make_async_copy(
            back_ref.at[part // steps, at], held_ref.at[part % HELD], sem_ref.at[part % HELD]
        )

    def start(part):
        @pl.when((part < parts) & (part % steps < steps // 2))
        def _():
            fetch(part, back_zero_ref, 0).start()

        @pl.when((part < parts) & (part % steps >= steps // 2))
        def _():
            fetch(part, back_one_ref, steps // 2).start()

    @pl.when(slot == 0)
    def _():
        sum_ref[...] = functools.reduce(jnp.add, [first_ref[...] for first_ref in first_refs])
        for part in range(HELD):
            start(part)

    @pl.when((slot < slots_ref[0]) & (slot < FRONT))
    def _():
        for index, front_ref in enumerate((front_zero_ref, front_one_ref)):
            sum_ref[...] += jnp.dot(
                vec_ref[0, :, index * half : (index + 1) * half], front_ref[0],
                preferred_element_type=F32,
            )

    @pl.when((slot < slots_ref[0]) & (slot >= FRONT))
    def _():
        for step in range(steps):
            part = (slot - FRONT) * steps + step
            fetch(part % HELD, back_zero_ref, part % HELD // (steps // 2) * (steps // 2)).wait()
            sum_ref[...] += jnp.dot(
                vec_ref[0, :, step * ROWS : (step + 1) * ROWS], held_ref[part % HELD],
                preferred_element_type=F32,
            )
            start(part + HELD)

    @pl.when(slot == pl.num_programs(0) - 1)
    def _():
        rhs = rhs_ref[...]
        image = image_ref[...]
        total = jnp.sum(tails_ref[...].astype(F32), axis=0)
        norm = total[:, 0:1] + total[:, 1:2] + total[:, 2:3]
        curve = total[:, 3:4] + total[:, 4:5] + total[:, 5:6]
        length = norm / curve
        second = (var_ref[...] + DIAGONAL) * image + SCALE * sum_ref[...]
        res = rhs - length * image
        res_image = image - length * second
        rows_ref[0:8] = rhs
        rows_ref[8:16] = res
        rows_ref[16:24] = image
        rows_ref[24:32] = res_image
        lane = lax.broadcasted_iota(jnp.int32, (rhs.shape[0], TAIL), 1)
        dots = jnp.zeros((rhs.shape[0], TAIL), F32)
        for place, product in enumerate((res * res, res * res_image, res * image, rhs * res_image)):
            dots = jnp.where(lane == place, jnp.sum(product, axis=1, keepdims=True), dots)
        dots_ref[...] = dots
        step_ref[...] = jnp.where(lane == 0, norm, jnp.where(lane == 1, curve, 0.0))


def order_kernel(rows_ref, perm_ref, out_ref):
    rows = rows_ref[...]
    count, width = rows.shape
    pieces = jnp.concatenate([piece for piece in split_three(rows)], axis=0).astype(BF16)
    perm = perm_ref[...]
    chunk = 256
    for col in range(0, width, chunk):
        total = jnp.zeros((3 * count, chunk), F32)
        for at in range(0, width, chunk):
            index = lax.broadcasted_iota(jnp.int32, (chunk, chunk), 0) + at
            pick = jnp.where(index == perm[:, col : col + chunk], 1.0, 0.0).astype(BF16)
            total += jnp.dot(pieces[:, at : at + chunk], pick, preferred_element_type=F32)
        out_ref[:, col : col + chunk] = total[:count] + total[count : 2 * count] + total[2 * count :]


def swap(value, mask, count):
    return lax.ppermute(value, "row", [(i, i ^ mask) for i in range(count)])


def levels(count, sizes):
    bits = count.bit_length() - 1
    out = []
    sizes = list(sizes)
    while bits:
        take = min(sizes.pop(0) if sizes else 1, bits)
        bits -= take
        out.append([mask << bits for mask in range(1, 1 << take)])
    return out


def tree_sum(value, count):
    for masks in levels(count, [2, 2, 2]):
        others = [swap(value, mask, count) for mask in masks]
        if len(masks) == 3:
            value = (value + others[0]) + (others[1] + others[2])
        else:
            value = value + others[0]
    return value


def gather_levels(count):
    return levels(count, [2] if count <= 16 else [2, 2])


def gather_places(count):
    places = [0]
    for masks in gather_levels(count):
        places = places + [place ^ mask for mask in masks for place in places]
    return places


def tree_gather(value, count):
    blocks, out = value[None], []
    for masks in gather_levels(count):
        blocks = jnp.concatenate([blocks] + [swap(blocks, mask, count) for mask in masks], axis=0)
        out.append(blocks)
    return out


def gate(block, behind):
    return pl.pallas_call(
        lambda *refs: None,
        in_specs=[pl.BlockSpec(memory_space=pl.ANY)] * 2,
        out_specs=pl.BlockSpec(memory_space=pl.ANY),
        out_shape=jax.ShapeDtypeStruct(block.shape, block.dtype),
        input_output_aliases={0: 0},
        compiler_params=pltpu.CompilerParams(vmem_limit_bytes=1024 * 1024),
        name="gate",
    )(block, behind)


def local(features, right_side, variance, hilbert_order, tile_list):
    width = features.shape[1]
    rhs_count = right_side.shape[0]
    count = lax.axis_size("row")
    most = tile_list.shape[1]
    steps = width // ROWS
    shape = jax.ShapeDtypeStruct
    params = pltpu.CompilerParams(vmem_limit_bytes=10 * 1024 * 1024)
    var_row = variance[None, :]

    whole = lambda *ignored: (0, 0)
    row_spec = pl.BlockSpec(right_side.shape, whole)
    var_spec = pl.BlockSpec(var_row.shape, whole)
    pay_shape = (80, width // 4)
    smem = pl.BlockSpec(memory_space=pltpu.SMEM)
    vmem = pl.BlockSpec(memory_space=pltpu.VMEM)
    in_hbm = lambda array: pltpu.with_memory_space_constraint(array, pltpu.HBM)
    pay_zero, pay_one, right, left, rounded = pl.pallas_call(
        payload_kernel,
        in_specs=[smem, vmem, vmem],
        out_shape=[
            shape((96, width // 4), BF16),
            shape(pay_shape, BF16),
            shape((KDIM, width), BF16),
            shape((width, KDIM), BF16),
            shape(right_side.shape, BF16),
        ],
        compiler_params=params,
        name="payload",
    )(tile_list, in_hbm(features), in_hbm(right_side))
    me = jnp.full((1,), lax.axis_index("row"), jnp.int32)
    any_spec = pl.BlockSpec(memory_space=pl.ANY)

    def own_part(rows, arrived):
        blocks = own_blocks(rows, steps)
        tiles, sums = pl.pallas_call(
            functools.partial(own_kernel, rows),
            in_specs=[vmem, vmem, vmem, any_spec],
            out_specs=[any_spec, vmem],
            out_shape=[pltpu.HBM((len(blocks), ROWS, ROWS), BF16), shape(right_side.shape, F32)],
            scratch_shapes=[
                pltpu.VMEM((len(blocks), ROWS, ROWS), BF16),
                pltpu.SemaphoreType.DMA((len(blocks),)),
            ],
            compiler_params=params,
            cost_estimate=pl.CostEstimate(
                flops=5_000_000_000, bytes_accessed=2 * len(blocks) * ROWS * ROWS, transcendentals=0
            ),
            name=f"own_tile_{rows[0]}",
        )(left, right, rounded, arrived)
        return blocks, tiles, sums

    first_masks, *later = gather_levels(count)
    first_level = lambda pay: jnp.concatenate(
        [pay] + [swap(pay, mask, count) for mask in first_masks], axis=0
    )
    near_zero = first_level(pay_zero)
    own_parts = [own_part(range(1), right)]
    near_zero = gate(near_zero, own_parts[0][2])
    near_one = first_level(gate(pay_one, own_parts[0][2]))
    own_parts.append(own_part(range(1, steps), near_zero))
    near_one = gate(near_one, own_parts[1][2])
    zero, places = [near_zero], [0]
    for level, masks in enumerate(later):
        zero = zero + [swap(array, mask, count) for mask in masks for array in zero]
        places = places + [mask ^ place for mask in masks for place in places]
        if level == 0:
            zero[-1] = gate(zero[-1], own_parts[1][2])
    one = [near_one] + [swap(near_one, place, count) for place in places[1:]]
    each = len(first_masks) + 1
    zero_at = [(at, row * 96) for at in range(len(zero)) for row in range(each)]
    one_at = [(at, row * 80) for at in range(len(one)) for row in range(each)]

    half = steps // 2

    def front_at(k, i, *ignored):
        return (jnp.minimum(k, FRONT - 1), jnp.where(k < FRONT, i, half - 1), 0)

    def back_at(k, i, *ignored):
        return (jnp.maximum(k - FRONT, 0), jnp.where(k < FRONT, 0, i), 0)

    half_specs = [pl.BlockSpec((1, ROWS, width), front_at), pl.BlockSpec((1, ROWS, width), back_at)]
    half_shapes = [
        pltpu.VMEM((FRONT, width // 2, width), BF16),
        pltpu.HBM((most - FRONT, width // 2, width), BF16),
    ]
    half_scratch = [
        pltpu.VMEM((2, width // 2, KDIM), BF16),
        pltpu.VMEM((2, rhs_count, width // 2), BF16),
        pltpu.VMEM((2,) + pay_shape, BF16),
        pltpu.SemaphoreType.DMA((2,)),
    ]
    right_spec = pl.BlockSpec(right.shape, whole)
    send_shape = (rhs_count, width + TAIL)
    front_zero, back_zero, half_sum, slots = pl.pallas_call(
        functools.partial(pair_zero_kernel, zero_at),
        grid_spec=pltpu.PrefetchScalarGridSpec(
            num_scalar_prefetch=1,
            grid=(most, half),
            in_specs=[right_spec] + [row_spec] * PARTS + [any_spec] * len(zero),
            out_specs=half_specs + [row_spec, smem],
            scratch_shapes=half_scratch
            + [
                pltpu.VMEM((count, 16, 128), BF16),
                pltpu.VMEM((count, 128), jnp.int32),
                pltpu.SMEM((count, 128), jnp.int32),
                pltpu.SemaphoreType.DMA((count,)),
            ],
        ),
        out_shape=half_shapes
        + [shape(right_side.shape, F32), shape((most + 2,), jnp.int32)],
        compiler_params=params,
        name="pair_zero",
    )(me, right, *[part[2] for part in own_parts], *zero)
    front_one, back_one, image, send = pl.pallas_call(
        functools.partial(pair_one_kernel, one_at),
        grid_spec=pltpu.PrefetchScalarGridSpec(
            num_scalar_prefetch=1,
            grid=(most, half),
            in_specs=[right_spec, row_spec, row_spec, var_spec] + [any_spec] * len(one),
            out_specs=half_specs + [row_spec, pl.BlockSpec(send_shape, whole)],
            scratch_shapes=half_scratch,
        ),
        out_shape=half_shapes + [shape(right_side.shape, F32), shape(send_shape, BF16)],
        compiler_params=params,
        name="pair_one",
    )(slots, right, half_sum, right_side, var_row, *one)
    fronts = [pltpu.with_memory_space_constraint(part, pltpu.VMEM) for part in (front_zero, front_one)]
    backs = [pltpu.with_memory_space_constraint(part, pltpu.HBM) for part in (back_zero, back_one)]

    every_send = tree_gather(send, count)[-1]
    own_again = [
        pl.pallas_call(
            functools.partial(own_again_kernel, blocks),
            in_specs=[any_spec, pl.BlockSpec(send_shape, whole)],
            out_specs=row_spec,
            out_shape=shape(right_side.shape, F32),
            scratch_shapes=[
                pltpu.VMEM((len(blocks), ROWS, ROWS), BF16),
                pltpu.SemaphoreType.DMA((len(blocks),)),
            ],
            compiler_params=params,
            cost_estimate=pl.CostEstimate(
                flops=5_000_000_000, bytes_accessed=2 * len(blocks) * ROWS * ROWS, transcendentals=0
            ),
            name=f"own_again_{part}",
        )(in_hbm(tiles), send)
        for part, (blocks, tiles, _) in enumerate(own_parts)
    ]
    dots_spec = pl.BlockSpec((rhs_count, TAIL), whole)
    rows, dots, steps_one = pl.pallas_call(
        again_kernel,
        grid_spec=pltpu.PrefetchScalarGridSpec(
            num_scalar_prefetch=1,
            grid=(most,),
            in_specs=[
                pl.BlockSpec((1, width // 2, width), lambda k, s: (jnp.minimum(k, FRONT - 1), 0, 0)),
                pl.BlockSpec((1, width // 2, width), lambda k, s: (jnp.minimum(k, FRONT - 1), 0, 0)),
                any_spec,
                any_spec,
                pl.BlockSpec((1,) + send_shape, lambda k, s: (s[1 + k], 0, 0)),
                pl.BlockSpec((count, rhs_count, TAIL), lambda k, s: (0, 0, width // TAIL)),
                row_spec,
                var_spec,
                row_spec,
            ]
            + [row_spec] * PARTS,
            out_specs=[
                pl.BlockSpec((4 * rhs_count, width), whole),
                dots_spec,
                dots_spec,
            ],
            scratch_shapes=[
                pltpu.VMEM(right_side.shape, F32),
                pltpu.VMEM((HELD, ROWS, width), BF16),
                pltpu.SemaphoreType.DMA((HELD,)),
            ],
        ),
        out_shape=[
            shape((4 * rhs_count, width), F32),
            shape((rhs_count, TAIL), F32),
            shape((rhs_count, TAIL), F32),
        ],
        compiler_params=params,
        name="pair_again",
    )(slots, *fronts, *backs, every_send, every_send, right_side, var_row, image, *own_again)

    dots = tree_sum(dots, count)
    ordered = pl.pallas_call(
        order_kernel,
        out_shape=shape(rows.shape, F32),
        compiler_params=params,
        name="curve_order",
    )(rows, hilbert_order)
    norm, curve = steps_one[:, 0:1], steps_one[:, 1:2]
    length = norm / curve
    norm_next = dots[:, 0:1]
    ratio = norm_next / norm
    curve_next = dots[:, 1:2] + ratio * (dots[:, 2:3] + dots[:, 3:4]) + ratio * ratio * curve
    length_next = norm_next / curve_next
    rhs_o, res_o, image_o, res_image_o = [ordered[at : at + 8] for at in range(0, 32, 8)]
    solved = length * rhs_o + length_next * (res_o + ratio * rhs_o)
    residual = res_o - length_next * (res_image_o + ratio * image_o)
    return (solved, residual)


def solution(mesh):
    in_specs = (
        P(None, ("group", "row")),
        P(None, ("group", "row")),
        P(("group", "row")),
        P(("group", "row"), None),
        P(("group", "row"), None, None),
    )
    out_specs = (P(None, ("group", "row")), P(None, ("group", "row")))
    return jax.shard_map(local, mesh=mesh, in_specs=in_specs, out_specs=out_specs, check_vma=False)
```

```python
import functools

import jax
import jax.numpy as jnp
import numpy as np
from jax import lax
from jax.experimental import pallas as pl
from jax.experimental.pallas import tpu as pltpu
from jax.sharding import PartitionSpec as P

SHRINK = 0.95
GRAM = SHRINK * SHRINK
SCALE = 20.0 * (20.0 / 19.0) ** 19
DIAGONAL = float(1.0 - SCALE * float(np.float32(1.0 / SCALE).astype(jnp.bfloat16)))
KDIM = 128
ROWS = 512
PARTS = 2
PIECE = 256
STRIP = 64
FRONT = 3
HELD = 4
TAIL = 128
BF16 = jnp.bfloat16
F32 = jnp.float32
CONTRACT_LANES = (((1,), (1,)), ((), ()))


def split_three(value):
    high = value.astype(BF16).astype(F32)
    rest = value - high
    middle = rest.astype(BF16).astype(F32)
    return high, middle, rest - middle


def norm_rows(norm, first):
    high, middle, low = split_three(norm)
    row = lax.broadcasted_iota(jnp.int32, (32, norm.shape[1]), 0)
    out = jnp.where(row < 6, 1.0, 0.0)
    out = jnp.where(row == first, high, out)
    out = jnp.where(row == first + 1, middle, out)
    return jnp.where(row == first + 2, low, out).astype(BF16)


def own_factor(feat):
    wide = feat.astype(F32)
    norm = jnp.sum(wide * wide, axis=0, keepdims=True) * GRAM
    pieces = split_three(wide * (-2.0 * GRAM))
    return jnp.concatenate([piece.astype(BF16) for piece in pieces] + [norm_rows(norm, 0)], axis=0)


def other_factor(feat):
    wide = feat.astype(F32)
    norm = jnp.sum(wide * wide, axis=0, keepdims=True) * GRAM
    return jnp.transpose(jnp.concatenate([feat, feat, feat, norm_rows(norm, 3)], axis=0))


def psi_power(dist):
    dist = jnp.maximum(dist, 1e-30)
    radius = dist * lax.rsqrt(dist)
    u = jnp.maximum(SHRINK - radius, 1e-30)
    return (jnp.exp2(19.0 * lax.log2(u)) * (1.0 - u)).astype(BF16)


def tile_unit(left, right, vec, tile_ref, aside=None):
    cols = [slice(at, at + PIECE) for at in range(0, right.shape[1], PIECE)]
    pieces = [(row, col) for row in range(0, left.shape[0], ROWS) for col in range(len(cols))]
    gram = lambda row, col: jnp.dot(
        left[row : row + ROWS], right[:, cols[col]], preferred_element_type=F32
    )
    terms = [0.0] * len(cols)

    def product(row, col, part):
        terms[col] = terms[col] + jnp.dot(
            vec[:, row : row + ROWS], part, preferred_element_type=F32
        )

    dist, before = gram(*pieces[0]), None
    for index, (row, col) in enumerate(pieces):
        following = gram(*pieces[index + 1]) if index + 1 < len(pieces) else None
        strips = []
        for at in range(0, ROWS, STRIP):
            strips.append(psi_power(dist[at : at + STRIP]))
            tile_ref[row + at : row + at + STRIP, cols[col]] = strips[-1]
        if before is not None:
            product(*before)
        if index == 1 and aside is not None:
            aside()
        dist, before = following, (row, col, jnp.concatenate(strips, axis=0))
    product(*before)
    return jnp.concatenate(terms, axis=1)


def unpack(pay):
    return jnp.concatenate([pay[:32], pay[32:64]], axis=1), jnp.concatenate([pay[64:72], pay[72:80]], axis=1)


def own_blocks(rows, count):
    return [(row, col) for row in rows for col in range(row, count)]


def own_kernel(
    rows, left_ref, right_ref, vec_ref, arrived_ref, out_ref, sum_ref, tile_ref, sem_ref
):
    sum_ref[...] = jnp.zeros_like(sum_ref)
    count = vec_ref.shape[1] // ROWS
    piece = lambda index: pl.ds(pl.multiple_of(index * ROWS, ROWS), ROWS)
    save = lambda at: pltpu.make_async_copy(tile_ref.at[at], out_ref.at[at], sem_ref.at[at])

    def row_step(row, at):
        def col_step(col, at):
            sum_ref[:, piece(col)] += tile_unit(
                left_ref[piece(row), :], right_ref[:, piece(col)], vec_ref[:, piece(row)],
                tile_ref.at[at],
            )
            save(at).start()

            @pl.when(row != col)
            def _():
                sum_ref[:, piece(row)] += lax.dot_general(
                    vec_ref[:, piece(col)], tile_ref[at], CONTRACT_LANES,
                    preferred_element_type=F32,
                )

            return at + 1

        return lax.fori_loop(row, count, col_step, at)

    lax.fori_loop(rows[0], rows[-1] + 1, row_step, 0)
    for at in range(tile_ref.shape[0]):
        save(at).wait()


def own_again_kernel(blocks, in_ref, vec_ref, sum_ref, tile_ref, sem_ref):
    load = lambda index: pltpu.make_async_copy(
        in_ref.at[index], tile_ref.at[index], sem_ref.at[index]
    )
    for index in range(len(blocks)):
        load(index).start()
    sum_ref[...] = jnp.zeros_like(sum_ref)
    piece = lambda index: slice(index * ROWS, (index + 1) * ROWS)
    for index, (row, col) in enumerate(blocks):
        load(index).wait()
        sum_ref[:, piece(col)] += jnp.dot(
            vec_ref[:, piece(row)], tile_ref[index], preferred_element_type=F32
        )
        if row != col:
            sum_ref[:, piece(row)] += lax.dot_general(
                vec_ref[:, piece(col)], tile_ref[index], CONTRACT_LANES, preferred_element_type=F32
            )


def payload_kernel(
    list_ref, feat_ref, rhs_ref, pay_zero_ref, pay_one_ref, right_ref, left_ref, vec_ref
):
    feat = feat_ref[...]
    rounded = rhs_ref[...].astype(BF16)
    quarter = feat.shape[1] // 4
    for half, pay_ref in enumerate((pay_zero_ref, pay_one_ref)):
        first, second = [slice(at * quarter, (at + 1) * quarter) for at in (2 * half, 2 * half + 1)]
        pay_ref[:32] = feat[:, first]
        pay_ref[32:64] = feat[:, second]
        pay_ref[64:80] = jnp.concatenate([rounded[:, first], rounded[:, second]], axis=0)
    lane = lax.broadcasted_iota(jnp.int32, (16, quarter), 1)
    numbers = jnp.full(lane.shape, -1, jnp.int32)
    for entry in range(list_ref.shape[1]):
        numbers = jnp.where(lane == entry, list_ref[0, entry, 1], numbers)
    pay_zero_ref[80:96] = numbers.astype(F32).astype(BF16)
    right_ref[...] = own_factor(feat)
    left_ref[...] = other_factor(feat)
    vec_ref[...] = rounded


def find_partners(lists_ref, me, slots_ref):
    count, most = lists_ref.shape[0], slots_ref.shape[0] - 2
    for at in range(slots_ref.shape[0]):
        slots_ref[at] = 0
    total = jnp.int32(0)
    for at, place in enumerate(gather_places(count)):
        if at == 0:
            continue
        number = me ^ place
        hit = jnp.bool_(False)
        for entry in range(most):
            hit = hit | (lists_ref[at, entry] == me) | (lists_ref[0, entry] == number)
        slots_ref[1 + total] = jnp.where(hit, at, 0)
        total = total + hit.astype(jnp.int32)
    slots_ref[0] = total


def fetch_from(block_at, block_refs, slots_ref, pay_ref, sem_ref):
    def fetch(which):
        for at, (index, row) in enumerate(block_at):
            @pl.when(slots_ref[1 + which] == at)
            def _():
                pltpu.make_async_copy(
                    block_refs[index].at[pl.ds(row, 80)],
                    pay_ref.at[which % 2],
                    sem_ref.at[which % 2],
                ).start()

    return fetch


def half_tiles(slots_ref, right_ref, fetch, front_ref, back_ref, sum_ref, left_ref, vec_ref, pay_ref, sem_ref):
    slot = pl.program_id(0)
    total = slots_ref[0]

    def arrive(which):
        pltpu.make_async_copy(
            pay_ref.at[(which + 1) % 2], pay_ref.at[which % 2], sem_ref.at[which % 2]
        ).wait()

    def factor(which):
        feat, vec = unpack(pay_ref[which % 2])
        left_ref[which % 2] = other_factor(feat)
        vec_ref[which % 2] = vec

    @pl.when((slot == 0) & (total > 0))
    def _():
        fetch(0)

        @pl.when(total > 1)
        def _():
            fetch(1)

        arrive(0)
        factor(0)

    @pl.when(slot + 1 < total)
    def _():
        arrive(slot + 1)

    left, vec = left_ref.at[slot % 2], vec_ref.at[slot % 2]
    for tile_ref, here in ((front_ref, slot < FRONT), (back_ref, slot >= FRONT)):
        @pl.when((slot < total) & here)
        def _():
            sum_ref[...] += tile_unit(
                left[...], right_ref[...], vec[...], tile_ref.at[0], lambda: factor(slot + 1)
            )

    @pl.when(slot + 2 < total)
    def _():
        fetch(slot + 2)


def pair_zero_kernel(block_at, me_ref, right_ref, *refs):
    first_refs, block_refs = refs[:PARTS], refs[PARTS:-12]
    front_ref, back_ref, sum_ref, slots_ref = refs[-12:-8]
    left_ref, vec_ref, pay_ref, sem_ref, strip_ref, list_ref, lists_ref, strip_sem_ref = refs[-8:]

    @pl.when(pl.program_id(0) == 0)
    def _():
        strips = [
            pltpu.make_async_copy(
                block_refs[index].at[pl.ds(row + 80, 16), pl.ds(0, 128)],
                strip_ref.at[at],
                strip_sem_ref.at[at],
            )
            for at, (index, row) in enumerate(block_at)
        ]
        for strip in strips:
            strip.start()
        sum_ref[...] = functools.reduce(jnp.add, [first_ref[...] for first_ref in first_refs])
        for at, strip in enumerate(strips):
            strip.wait()
            list_ref[at : at + 1, :] = strip_ref[at].astype(F32)[:1].astype(jnp.int32)
        numbers = pltpu.make_async_copy(list_ref, lists_ref, strip_sem_ref.at[0])
        numbers.start()
        numbers.wait()
        find_partners(lists_ref, me_ref[0], slots_ref)

    fetch = fetch_from(block_at, block_refs, slots_ref, pay_ref, sem_ref)
    half_tiles(
        slots_ref, right_ref, fetch, front_ref, back_ref, sum_ref, left_ref, vec_ref, pay_ref, sem_ref
    )


def pair_one_kernel(block_at, slots_ref, right_ref, first_ref, rhs_ref, var_ref, *refs):
    block_refs = refs[:-8]
    front_ref, back_ref, image_ref, send_ref, left_ref, vec_ref, pay_ref, sem_ref = refs[-8:]
    slot = pl.program_id(0)

    @pl.when(slot == 0)
    def _():
        image_ref[...] = first_ref[...]

    fetch = fetch_from(block_at, block_refs, slots_ref, pay_ref, sem_ref)
    half_tiles(
        slots_ref, right_ref, fetch, front_ref, back_ref, image_ref, left_ref, vec_ref, pay_ref, sem_ref
    )

    @pl.when(slot == pl.num_programs(0) - 1)
    def _():
        rhs = rhs_ref[...]
        width = rhs.shape[1]
        image = (var_ref[...] + DIAGONAL) * rhs + SCALE * image_ref[...]
        image_ref[...] = image
        send_ref[:, :width] = image.astype(BF16)
        pieces = split_three(jnp.sum(rhs * rhs, axis=1, keepdims=True))
        pieces += split_three(jnp.sum(rhs * image, axis=1, keepdims=True))
        lane = lax.broadcasted_iota(jnp.int32, (rhs.shape[0], TAIL), 1)
        tail = jnp.zeros((rhs.shape[0], TAIL), F32)
        for place, piece in enumerate(pieces):
            tail = jnp.where(lane == place, piece, tail)
        send_ref[:, width:] = tail.astype(BF16)


def again_kernel(
    slots_ref, front_zero_ref, front_one_ref, back_zero_ref, back_one_ref,
    vec_ref, tails_ref, rhs_ref, var_ref, image_ref, *refs
):
    first_refs = refs[:PARTS]
    rows_ref, dots_ref, step_ref, sum_ref, held_ref, sem_ref = refs[PARTS:]
    slot = pl.program_id(0)
    width = rhs_ref.shape[1]
    steps = width // ROWS
    half = width // 2
    parts = (slots_ref[0] - FRONT) * steps

    def fetch(part, back_ref, first):
        at = pl.ds(pl.multiple_of((part % steps - first) * ROWS, ROWS), ROWS)
        return pltpu.make_async_copy(
            back_ref.at[part // steps, at], held_ref.at[part % HELD], sem_ref.at[part % HELD]
        )

    def start(part):
        @pl.when((part < parts) & (part % steps < steps // 2))
        def _():
            fetch(part, back_zero_ref, 0).start()

        @pl.when((part < parts) & (part % steps >= steps // 2))
        def _():
            fetch(part, back_one_ref, steps // 2).start()

    @pl.when(slot == 0)
    def _():
        sum_ref[...] = functools.reduce(jnp.add, [first_ref[...] for first_ref in first_refs])
        for part in range(HELD):
            start(part)

    @pl.when((slot < slots_ref[0]) & (slot < FRONT))
    def _():
        for index, front_ref in enumerate((front_zero_ref, front_one_ref)):
            sum_ref[...] += jnp.dot(
                vec_ref[0, :, index * half : (index + 1) * half], front_ref[0],
                preferred_element_type=F32,
            )

    @pl.when((slot < slots_ref[0]) & (slot >= FRONT))
    def _():
        for step in range(steps):
            part = (slot - FRONT) * steps + step
            fetch(part % HELD, back_zero_ref, part % HELD // (steps // 2) * (steps // 2)).wait()
            sum_ref[...] += jnp.dot(
                vec_ref[0, :, step * ROWS : (step + 1) * ROWS], held_ref[part % HELD],
                preferred_element_type=F32,
            )
            start(part + HELD)

    @pl.when(slot == pl.num_programs(0) - 1)
    def _():
        rhs = rhs_ref[...]
        image = image_ref[...]
        total = jnp.sum(tails_ref[...].astype(F32), axis=0)
        norm = total[:, 0:1] + total[:, 1:2] + total[:, 2:3]
        curve = total[:, 3:4] + total[:, 4:5] + total[:, 5:6]
        length = norm / curve
        second = (var_ref[...] + DIAGONAL) * image + SCALE * sum_ref[...]
        res = rhs - length * image
        res_image = image - length * second
        rows_ref[0:8] = rhs
        rows_ref[8:16] = res
        rows_ref[16:24] = image
        rows_ref[24:32] = res_image
        lane = lax.broadcasted_iota(jnp.int32, (rhs.shape[0], TAIL), 1)
        dots = jnp.zeros((rhs.shape[0], TAIL), F32)
        for place, product in enumerate((res * res, res * res_image, res * image, rhs * res_image)):
            dots = jnp.where(lane == place, jnp.sum(product, axis=1, keepdims=True), dots)
        dots_ref[...] = dots
        step_ref[...] = jnp.where(lane == 0, norm, jnp.where(lane == 1, curve, 0.0))


def order_kernel(rows_ref, perm_ref, out_ref):
    rows = rows_ref[...]
    count, width = rows.shape
    pieces = jnp.concatenate([piece for piece in split_three(rows)], axis=0).astype(BF16)
    perm = perm_ref[...]
    chunk = 256
    for col in range(0, width, chunk):
        total = jnp.zeros((3 * count, chunk), F32)
        for at in range(0, width, chunk):
            index = lax.broadcasted_iota(jnp.int32, (chunk, chunk), 0) + at
            pick = jnp.where(index == perm[:, col : col + chunk], 1.0, 0.0).astype(BF16)
            total += jnp.dot(pieces[:, at : at + chunk], pick, preferred_element_type=F32)
        out_ref[:, col : col + chunk] = total[:count] + total[count : 2 * count] + total[2 * count :]


def swap(value, mask, count):
    return lax.ppermute(value, "row", [(i, i ^ mask) for i in range(count)])


def levels(count, sizes):
    bits = count.bit_length() - 1
    out = []
    sizes = list(sizes)
    while bits:
        take = min(sizes.pop(0) if sizes else 1, bits)
        bits -= take
        out.append([mask << bits for mask in range(1, 1 << take)])
    return out


def tree_sum(value, count):
    for masks in levels(count, [2, 2, 2]):
        others = [swap(value, mask, count) for mask in masks]
        if len(masks) == 3:
            value = (value + others[0]) + (others[1] + others[2])
        else:
            value = value + others[0]
    return value


def gather_levels(count):
    return levels(count, [2] if count <= 16 else [2, 2])


def gather_places(count):
    places = [0]
    for masks in gather_levels(count):
        places = places + [place ^ mask for mask in masks for place in places]
    return places


def tree_gather(value, count):
    blocks, out = value[None], []
    for masks in gather_levels(count):
        blocks = jnp.concatenate([blocks] + [swap(blocks, mask, count) for mask in masks], axis=0)
        out.append(blocks)
    return out


def gate(block, behind):
    return pl.pallas_call(
        lambda *refs: None,
        in_specs=[pl.BlockSpec(memory_space=pl.ANY)] * 2,
        out_specs=pl.BlockSpec(memory_space=pl.ANY),
        out_shape=jax.ShapeDtypeStruct(block.shape, block.dtype),
        input_output_aliases={0: 0},
        compiler_params=pltpu.CompilerParams(vmem_limit_bytes=1024 * 1024),
        name="gate",
    )(block, behind)


def local(features, right_side, variance, hilbert_order, tile_list):
    width = features.shape[1]
    rhs_count = right_side.shape[0]
    count = lax.axis_size("row")
    most = tile_list.shape[1]
    steps = width // ROWS
    shape = jax.ShapeDtypeStruct
    params = pltpu.CompilerParams(vmem_limit_bytes=10 * 1024 * 1024)
    var_row = variance[None, :]

    whole = lambda *ignored: (0, 0)
    row_spec = pl.BlockSpec(right_side.shape, whole)
    var_spec = pl.BlockSpec(var_row.shape, whole)
    pay_shape = (80, width // 4)
    smem = pl.BlockSpec(memory_space=pltpu.SMEM)
    vmem = pl.BlockSpec(memory_space=pltpu.VMEM)
    in_hbm = lambda array: pltpu.with_memory_space_constraint(array, pltpu.HBM)
    pay_zero, pay_one, right, left, rounded = pl.pallas_call(
        payload_kernel,
        in_specs=[smem, vmem, vmem],
        out_shape=[
            shape((96, width // 4), BF16),
            shape(pay_shape, BF16),
            shape((KDIM, width), BF16),
            shape((width, KDIM), BF16),
            shape(right_side.shape, BF16),
        ],
        compiler_params=params,
        name="payload",
    )(tile_list, in_hbm(features), in_hbm(right_side))
    me = jnp.full((1,), lax.axis_index("row"), jnp.int32)
    any_spec = pl.BlockSpec(memory_space=pl.ANY)

    def own_part(rows, arrived):
        blocks = own_blocks(rows, steps)
        tiles, sums = pl.pallas_call(
            functools.partial(own_kernel, rows),
            in_specs=[vmem, vmem, vmem, any_spec],
            out_specs=[any_spec, vmem],
            out_shape=[pltpu.HBM((len(blocks), ROWS, ROWS), BF16), shape(right_side.shape, F32)],
            scratch_shapes=[
                pltpu.VMEM((len(blocks), ROWS, ROWS), BF16),
                pltpu.SemaphoreType.DMA((len(blocks),)),
            ],
            compiler_params=params,
            cost_estimate=pl.CostEstimate(
                flops=5_000_000_000, bytes_accessed=2 * len(blocks) * ROWS * ROWS, transcendentals=0
            ),
            name=f"own_tile_{rows[0]}",
        )(left, right, rounded, arrived)
        return blocks, tiles, sums

    first_masks, *later = gather_levels(count)
    first_level = lambda pay: jnp.concatenate(
        [pay] + [swap(pay, mask, count) for mask in first_masks], axis=0
    )
    near_zero = first_level(pay_zero)
    own_parts = [own_part(range(1), right)]
    near_zero = gate(near_zero, own_parts[0][2])
    near_one = first_level(gate(pay_one, own_parts[0][2]))
    own_parts.append(own_part(range(1, steps), near_zero))
    near_one = gate(near_one, own_parts[1][2])
    zero, places = [near_zero], [0]
    for level, masks in enumerate(later):
        zero = zero + [swap(array, mask, count) for mask in masks for array in zero]
        places = places + [mask ^ place for mask in masks for place in places]
        if level == 0:
            zero[-1] = gate(zero[-1], own_parts[1][2])
    one = [near_one] + [swap(near_one, place, count) for place in places[1:]]
    each = len(first_masks) + 1
    zero_at = [(at, row * 96) for at in range(len(zero)) for row in range(each)]
    one_at = [(at, row * 80) for at in range(len(one)) for row in range(each)]

    half_block = (1, width // 2, width)
    half_specs = [
        pl.BlockSpec(half_block, lambda k, *ignored: (jnp.minimum(k, FRONT - 1), 0, 0)),
        pl.BlockSpec(half_block, lambda k, *ignored: (jnp.maximum(k - FRONT, 0), 0, 0)),
    ]
    half_params = pltpu.CompilerParams(vmem_limit_bytes=18 * 1024 * 1024)
    half_shapes = [
        pltpu.VMEM((FRONT, width // 2, width), BF16),
        pltpu.HBM((most - FRONT, width // 2, width), BF16),
    ]
    half_scratch = [
        pltpu.VMEM((2, width // 2, KDIM), BF16),
        pltpu.VMEM((2, rhs_count, width // 2), BF16),
        pltpu.VMEM((2,) + pay_shape, BF16),
        pltpu.SemaphoreType.DMA((2,)),
    ]
    right_spec = pl.BlockSpec(right.shape, whole)
    send_shape = (rhs_count, width + TAIL)
    front_zero, back_zero, half_sum, slots = pl.pallas_call(
        functools.partial(pair_zero_kernel, zero_at),
        grid_spec=pltpu.PrefetchScalarGridSpec(
            num_scalar_prefetch=1,
            grid=(most,),
            in_specs=[right_spec] + [row_spec] * PARTS + [any_spec] * len(zero),
            out_specs=half_specs + [row_spec, smem],
            scratch_shapes=half_scratch
            + [
                pltpu.VMEM((count, 16, 128), BF16),
                pltpu.VMEM((count, 128), jnp.int32),
                pltpu.SMEM((count, 128), jnp.int32),
                pltpu.SemaphoreType.DMA((count,)),
            ],
        ),
        out_shape=half_shapes
        + [shape(right_side.shape, F32), shape((most + 2,), jnp.int32)],
        compiler_params=half_params,
        name="pair_zero",
    )(me, right, *[part[2] for part in own_parts], *zero)
    front_one, back_one, image, send = pl.pallas_call(
        functools.partial(pair_one_kernel, one_at),
        grid_spec=pltpu.PrefetchScalarGridSpec(
            num_scalar_prefetch=1,
            grid=(most,),
            in_specs=[right_spec, row_spec, row_spec, var_spec] + [any_spec] * len(one),
            out_specs=half_specs + [row_spec, pl.BlockSpec(send_shape, whole)],
            scratch_shapes=half_scratch,
        ),
        out_shape=half_shapes + [shape(right_side.shape, F32), shape(send_shape, BF16)],
        compiler_params=half_params,
        name="pair_one",
    )(slots, right, half_sum, right_side, var_row, *one)
    fronts = [pltpu.with_memory_space_constraint(part, pltpu.VMEM) for part in (front_zero, front_one)]
    backs = [pltpu.with_memory_space_constraint(part, pltpu.HBM) for part in (back_zero, back_one)]

    every_send = tree_gather(send, count)[-1]
    own_again = [
        pl.pallas_call(
            functools.partial(own_again_kernel, blocks),
            in_specs=[any_spec, pl.BlockSpec(send_shape, whole)],
            out_specs=row_spec,
            out_shape=shape(right_side.shape, F32),
            scratch_shapes=[
                pltpu.VMEM((len(blocks), ROWS, ROWS), BF16),
                pltpu.SemaphoreType.DMA((len(blocks),)),
            ],
            compiler_params=params,
            cost_estimate=pl.CostEstimate(
                flops=5_000_000_000, bytes_accessed=2 * len(blocks) * ROWS * ROWS, transcendentals=0
            ),
            name=f"own_again_{part}",
        )(in_hbm(tiles), send)
        for part, (blocks, tiles, _) in enumerate(own_parts)
    ]
    dots_spec = pl.BlockSpec((rhs_count, TAIL), whole)
    rows, dots, steps_one = pl.pallas_call(
        again_kernel,
        grid_spec=pltpu.PrefetchScalarGridSpec(
            num_scalar_prefetch=1,
            grid=(most,),
            in_specs=[
                pl.BlockSpec((1, width // 2, width), lambda k, s: (jnp.minimum(k, FRONT - 1), 0, 0)),
                pl.BlockSpec((1, width // 2, width), lambda k, s: (jnp.minimum(k, FRONT - 1), 0, 0)),
                any_spec,
                any_spec,
                pl.BlockSpec((1,) + send_shape, lambda k, s: (s[1 + k], 0, 0)),
                pl.BlockSpec((count, rhs_count, TAIL), lambda k, s: (0, 0, width // TAIL)),
                row_spec,
                var_spec,
                row_spec,
            ]
            + [row_spec] * PARTS,
            out_specs=[
                pl.BlockSpec((4 * rhs_count, width), whole),
                dots_spec,
                dots_spec,
            ],
            scratch_shapes=[
                pltpu.VMEM(right_side.shape, F32),
                pltpu.VMEM((HELD, ROWS, width), BF16),
                pltpu.SemaphoreType.DMA((HELD,)),
            ],
        ),
        out_shape=[
            shape((4 * rhs_count, width), F32),
            shape((rhs_count, TAIL), F32),
            shape((rhs_count, TAIL), F32),
        ],
        compiler_params=params,
        name="pair_again",
    )(slots, *fronts, *backs, every_send, every_send, right_side, var_row, image, *own_again)

    dots = tree_sum(dots, count)
    ordered = pl.pallas_call(
        order_kernel,
        out_shape=shape(rows.shape, F32),
        compiler_params=params,
        name="curve_order",
    )(rows, hilbert_order)
    norm, curve = steps_one[:, 0:1], steps_one[:, 1:2]
    length = norm / curve
    norm_next = dots[:, 0:1]
    ratio = norm_next / norm
    curve_next = dots[:, 1:2] + ratio * (dots[:, 2:3] + dots[:, 3:4]) + ratio * ratio * curve
    length_next = norm_next / curve_next
    rhs_o, res_o, image_o, res_image_o = [ordered[at : at + 8] for at in range(0, 32, 8)]
    solved = length * rhs_o + length_next * (res_o + ratio * rhs_o)
    residual = res_o - length_next * (res_image_o + ratio * image_o)
    return (solved, residual)


def solution(mesh):
    in_specs = (
        P(None, ("group", "row")),
        P(None, ("group", "row")),
        P(("group", "row")),
        P(("group", "row"), None),
        P(("group", "row"), None, None),
    )
    out_specs = (P(None, ("group", "row")), P(None, ("group", "row")))
    return jax.shard_map(local, mesh=mesh, in_specs=in_specs, out_specs=out_specs, check_vma=False)
```

```python
import functools

import jax
import jax.numpy as jnp
import numpy as np
from jax import lax
from jax.experimental import pallas as pl
from jax.experimental.pallas import tpu as pltpu
from jax.sharding import PartitionSpec as P

SHRINK = 0.95
GRAM = SHRINK * SHRINK
SCALE = 20.0 * (20.0 / 19.0) ** 19
DIAGONAL = float(1.0 - SCALE * float(np.float32(1.0 / SCALE).astype(jnp.bfloat16)))
KDIM = 128
ROWS = 512
PARTS = 2
PIECE = 256
STRIP = 64
FRONT = 3
HELD = 4
TAIL = 128
BF16 = jnp.bfloat16
F32 = jnp.float32
CONTRACT_LANES = (((1,), (1,)), ((), ()))


def split_three(value):
    high = value.astype(BF16).astype(F32)
    rest = value - high
    middle = rest.astype(BF16).astype(F32)
    return high, middle, rest - middle


def norm_rows(norm, first):
    high, middle, low = split_three(norm)
    row = lax.broadcasted_iota(jnp.int32, (32, norm.shape[1]), 0)
    out = jnp.where(row < 6, 1.0, 0.0)
    out = jnp.where(row == first, high, out)
    out = jnp.where(row == first + 1, middle, out)
    return jnp.where(row == first + 2, low, out).astype(BF16)


def own_factor(feat):
    wide = feat.astype(F32)
    norm = jnp.sum(wide * wide, axis=0, keepdims=True) * GRAM
    pieces = split_three(wide * (-2.0 * GRAM))
    return jnp.concatenate([piece.astype(BF16) for piece in pieces] + [norm_rows(norm, 0)], axis=0)


def other_factor(feat):
    wide = feat.astype(F32)
    norm = jnp.sum(wide * wide, axis=0, keepdims=True) * GRAM
    return jnp.transpose(jnp.concatenate([feat, feat, feat, norm_rows(norm, 3)], axis=0))


def psi_power(dist):
    dist = jnp.maximum(dist, 1e-30)
    radius = dist * lax.rsqrt(dist)
    u = jnp.maximum(SHRINK - radius, 1e-30)
    return (jnp.exp2(19.0 * lax.log2(u)) * (1.0 - u)).astype(BF16)


def psi_natural(dist):
    dist = jnp.maximum(dist, 1e-30)
    radius = dist * lax.rsqrt(dist)
    u = jnp.maximum(SHRINK - radius, 1e-30)
    return (jnp.exp(19.0 * jnp.log(u)) * (1.0 - u)).astype(BF16)


def tile_unit(left, right, vec, tile_ref, aside=None, psi=psi_power):
    pieces = [slice(at, at + PIECE) for at in range(0, right.shape[1], PIECE)]
    gram = lambda piece: jnp.dot(left, right[:, piece], preferred_element_type=F32)
    product = lambda part: jnp.dot(vec, part, preferred_element_type=F32)
    dist, part, terms = gram(pieces[0]), None, []
    for index, piece in enumerate(pieces):
        following = gram(pieces[index + 1]) if index + 1 < len(pieces) else None
        strips = []
        for at in range(0, left.shape[0], STRIP):
            strips.append(psi(dist[at : at + STRIP]))
            tile_ref[at : at + STRIP, piece] = strips[-1]
        if part is not None:
            terms.append(product(part))
        if index == 1 and aside is not None:
            aside()
        dist, part = following, jnp.concatenate(strips, axis=0)
    return jnp.concatenate(terms + [product(part)], axis=1)


def unpack(pay):
    return jnp.concatenate([pay[:32], pay[32:64]], axis=1), jnp.concatenate([pay[64:72], pay[72:80]], axis=1)


def own_blocks(rows, count):
    return [(row, col) for row in rows for col in range(row, count)]


def own_kernel(
    rows, left_ref, right_ref, vec_ref, arrived_ref, out_ref, sum_ref, tile_ref, sem_ref
):
    sum_ref[...] = jnp.zeros_like(sum_ref)
    count = vec_ref.shape[1] // ROWS
    piece = lambda index: pl.ds(pl.multiple_of(index * ROWS, ROWS), ROWS)
    save = lambda at: pltpu.make_async_copy(tile_ref.at[at], out_ref.at[at], sem_ref.at[at])

    def row_step(row, at):
        def col_step(col, at):
            sum_ref[:, piece(col)] += tile_unit(
                left_ref[piece(row), :], right_ref[:, piece(col)], vec_ref[:, piece(row)],
                tile_ref.at[at],
            )
            save(at).start()

            @pl.when(row != col)
            def _():
                sum_ref[:, piece(row)] += lax.dot_general(
                    vec_ref[:, piece(col)], tile_ref[at], CONTRACT_LANES,
                    preferred_element_type=F32,
                )

            return at + 1

        return lax.fori_loop(row, count, col_step, at)

    lax.fori_loop(rows[0], rows[-1] + 1, row_step, 0)
    for at in range(tile_ref.shape[0]):
        save(at).wait()


def own_again_kernel(blocks, in_ref, vec_ref, sum_ref, tile_ref, sem_ref):
    load = lambda index: pltpu.make_async_copy(
        in_ref.at[index], tile_ref.at[index], sem_ref.at[index]
    )
    for index in range(len(blocks)):
        load(index).start()
    sum_ref[...] = jnp.zeros_like(sum_ref)
    piece = lambda index: slice(index * ROWS, (index + 1) * ROWS)
    for index, (row, col) in enumerate(blocks):
        load(index).wait()
        sum_ref[:, piece(col)] += jnp.dot(
            vec_ref[:, piece(row)], tile_ref[index], preferred_element_type=F32
        )
        if row != col:
            sum_ref[:, piece(row)] += lax.dot_general(
                vec_ref[:, piece(col)], tile_ref[index], CONTRACT_LANES, preferred_element_type=F32
            )


def payload_kernel(
    list_ref, feat_ref, rhs_ref, pay_zero_ref, pay_one_ref, right_ref, left_ref, vec_ref
):
    feat = feat_ref[...]
    rounded = rhs_ref[...].astype(BF16)
    quarter = feat.shape[1] // 4
    for half, pay_ref in enumerate((pay_zero_ref, pay_one_ref)):
        first, second = [slice(at * quarter, (at + 1) * quarter) for at in (2 * half, 2 * half + 1)]
        pay_ref[:32] = feat[:, first]
        pay_ref[32:64] = feat[:, second]
        pay_ref[64:80] = jnp.concatenate([rounded[:, first], rounded[:, second]], axis=0)
    lane = lax.broadcasted_iota(jnp.int32, (16, quarter), 1)
    numbers = jnp.full(lane.shape, -1, jnp.int32)
    for entry in range(list_ref.shape[1]):
        numbers = jnp.where(lane == entry, list_ref[0, entry, 1], numbers)
    pay_zero_ref[80:96] = numbers.astype(F32).astype(BF16)
    right_ref[...] = own_factor(feat)
    left_ref[...] = other_factor(feat)
    vec_ref[...] = rounded


def find_partners(lists_ref, me, slots_ref):
    count, most = lists_ref.shape[0], slots_ref.shape[0] - 2
    for at in range(slots_ref.shape[0]):
        slots_ref[at] = 0
    total = jnp.int32(0)
    for at, place in enumerate(gather_places(count)):
        if at == 0:
            continue
        number = me ^ place
        hit = jnp.bool_(False)
        for entry in range(most):
            hit = hit | (lists_ref[at, entry] == me) | (lists_ref[0, entry] == number)
        slots_ref[1 + total] = jnp.where(hit, at, 0)
        total = total + hit.astype(jnp.int32)
    slots_ref[0] = total


def fetch_from(block_at, block_refs, slots_ref, pay_ref, sem_ref):
    def fetch(which):
        for at, (index, row) in enumerate(block_at):
            @pl.when(slots_ref[1 + which] == at)
            def _():
                pltpu.make_async_copy(
                    block_refs[index].at[pl.ds(row, 80)],
                    pay_ref.at[which % 2],
                    sem_ref.at[which % 2],
                ).start()

    return fetch


def half_tiles(early, psi, slots_ref, right_ref, fetch, front_ref, back_ref, sum_ref, left_ref, vec_ref, pay_ref, sem_ref):
    slot, step = pl.program_id(0), pl.program_id(1)
    last = pl.num_programs(1) - 1

    def arrive(which):
        pltpu.make_async_copy(
            pay_ref.at[(which + 1) % 2], pay_ref.at[which % 2], sem_ref.at[which % 2]
        ).wait()

    def factor(which):
        feat, vec = unpack(pay_ref[which % 2])
        left_ref[which % 2] = other_factor(feat)
        vec_ref[which % 2] = vec

    @pl.when((slot == 0) & (step == 0) & (slots_ref[0] > 0))
    def _():
        fetch(0)

    @pl.when(slot < slots_ref[0])
    def _():
        @pl.when((step == 0) & ((slot == 0) | (not early)))
        def _():
            arrive(slot)
            factor(slot)

        @pl.when((step == 0) & (slot + 1 < slots_ref[0]))
        def _():
            fetch(slot + 1)

        if early:
            @pl.when((step == last) & (slot + 1 < slots_ref[0]))
            def _():
                arrive(slot + 1)

        rows = pl.ds(pl.multiple_of(step * ROWS, ROWS), ROWS)
        place = slot % 2
        left, vec = left_ref[place, rows, :], vec_ref[place, :, rows]
        for tile_ref, here in ((front_ref, slot < FRONT), (back_ref, slot >= FRONT)):
            for ends in (False, True) if early else (None,):
                @pl.when(here if ends is None else here & ((step == last) == ends))
                def _():
                    aside = (lambda: factor(slot + 1)) if ends else None
                    sum_ref[...] += tile_unit(left, right_ref[...], vec, tile_ref.at[0], aside, psi)


def pair_zero_kernel(block_at, me_ref, right_ref, *refs):
    first_refs, block_refs = refs[:PARTS], refs[PARTS:-12]
    front_ref, back_ref, sum_ref, slots_ref = refs[-12:-8]
    left_ref, vec_ref, pay_ref, sem_ref, strip_ref, list_ref, lists_ref, strip_sem_ref = refs[-8:]

    @pl.when((pl.program_id(0) == 0) & (pl.program_id(1) == 0))
    def _():
        strips = [
            pltpu.make_async_copy(
                block_refs[index].at[pl.ds(row + 80, 16), pl.ds(0, 128)],
                strip_ref.at[at],
                strip_sem_ref.at[at],
            )
            for at, (index, row) in enumerate(block_at)
        ]
        for strip in strips:
            strip.start()
        sum_ref[...] = functools.reduce(jnp.add, [first_ref[...] for first_ref in first_refs])
        for at, strip in enumerate(strips):
            strip.wait()
            list_ref[at : at + 1, :] = strip_ref[at].astype(F32)[:1].astype(jnp.int32)
        numbers = pltpu.make_async_copy(list_ref, lists_ref, strip_sem_ref.at[0])
        numbers.start()
        numbers.wait()
        find_partners(lists_ref, me_ref[0], slots_ref)

    fetch = fetch_from(block_at, block_refs, slots_ref, pay_ref, sem_ref)
    half_tiles(
        True, psi_natural, slots_ref, right_ref, fetch, front_ref, back_ref, sum_ref, left_ref, vec_ref, pay_ref, sem_ref
    )


def pair_one_kernel(block_at, slots_ref, right_ref, first_ref, rhs_ref, var_ref, *refs):
    block_refs = refs[:-8]
    front_ref, back_ref, image_ref, send_ref, left_ref, vec_ref, pay_ref, sem_ref = refs[-8:]
    slot, step = pl.program_id(0), pl.program_id(1)

    @pl.when((slot == 0) & (step == 0))
    def _():
        image_ref[...] = first_ref[...]

    fetch = fetch_from(block_at, block_refs, slots_ref, pay_ref, sem_ref)
    half_tiles(
        True, psi_power, slots_ref, right_ref, fetch, front_ref, back_ref, image_ref, left_ref, vec_ref, pay_ref, sem_ref
    )

    @pl.when((slot == pl.num_programs(0) - 1) & (step == pl.num_programs(1) - 1))
    def _():
        rhs = rhs_ref[...]
        width = rhs.shape[1]
        image = (var_ref[...] + DIAGONAL) * rhs + SCALE * image_ref[...]
        image_ref[...] = image
        send_ref[:, :width] = image.astype(BF16)
        pieces = split_three(jnp.sum(rhs * rhs, axis=1, keepdims=True))
        pieces += split_three(jnp.sum(rhs * image, axis=1, keepdims=True))
        lane = lax.broadcasted_iota(jnp.int32, (rhs.shape[0], TAIL), 1)
        tail = jnp.zeros((rhs.shape[0], TAIL), F32)
        for place, piece in enumerate(pieces):
            tail = jnp.where(lane == place, piece, tail)
        send_ref[:, width:] = tail.astype(BF16)


def again_kernel(
    slots_ref, front_zero_ref, front_one_ref, back_zero_ref, back_one_ref,
    vec_ref, tails_ref, rhs_ref, var_ref, image_ref, *refs
):
    first_refs = refs[:PARTS]
    rows_ref, dots_ref, step_ref, sum_ref, held_ref, sem_ref = refs[PARTS:]
    slot = pl.program_id(0)
    width = rhs_ref.shape[1]
    steps = width // ROWS
    half = width // 2
    parts = (slots_ref[0] - FRONT) * steps

    def fetch(part, back_ref, first):
        at = pl.ds(pl.multiple_of((part % steps - first) * ROWS, ROWS), ROWS)
        return pltpu.make_async_copy(
            back_ref.at[part // steps, at], held_ref.at[part % HELD], sem_ref.at[part % HELD]
        )

    def start(part):
        @pl.when((part < parts) & (part % steps < steps // 2))
        def _():
            fetch(part, back_zero_ref, 0).start()

        @pl.when((part < parts) & (part % steps >= steps // 2))
        def _():
            fetch(part, back_one_ref, steps // 2).start()

    @pl.when(slot == 0)
    def _():
        sum_ref[...] = functools.reduce(jnp.add, [first_ref[...] for first_ref in first_refs])
        for part in range(HELD):
            start(part)

    @pl.when((slot < slots_ref[0]) & (slot < FRONT))
    def _():
        for index, front_ref in enumerate((front_zero_ref, front_one_ref)):
            sum_ref[...] += jnp.dot(
                vec_ref[0, :, index * half : (index + 1) * half], front_ref[0],
                preferred_element_type=F32,
            )

    @pl.when((slot < slots_ref[0]) & (slot >= FRONT))
    def _():
        for step in range(steps):
            part = (slot - FRONT) * steps + step
            fetch(part % HELD, back_zero_ref, part % HELD // (steps // 2) * (steps // 2)).wait()
            sum_ref[...] += jnp.dot(
                vec_ref[0, :, step * ROWS : (step + 1) * ROWS], held_ref[part % HELD],
                preferred_element_type=F32,
            )
            start(part + HELD)

    @pl.when(slot == pl.num_programs(0) - 1)
    def _():
        rhs = rhs_ref[...]
        image = image_ref[...]
        total = jnp.sum(tails_ref[...].astype(F32), axis=0)
        norm = total[:, 0:1] + total[:, 1:2] + total[:, 2:3]
        curve = total[:, 3:4] + total[:, 4:5] + total[:, 5:6]
        length = norm / curve
        second = (var_ref[...] + DIAGONAL) * image + SCALE * sum_ref[...]
        res = rhs - length * image
        res_image = image - length * second
        rows_ref[0:8] = rhs
        rows_ref[8:16] = res
        rows_ref[16:24] = image
        rows_ref[24:32] = res_image
        lane = lax.broadcasted_iota(jnp.int32, (rhs.shape[0], TAIL), 1)
        dots = jnp.zeros((rhs.shape[0], TAIL), F32)
        for place, product in enumerate((res * res, res * res_image, res * image, rhs * res_image)):
            dots = jnp.where(lane == place, jnp.sum(product, axis=1, keepdims=True), dots)
        dots_ref[...] = dots
        step_ref[...] = jnp.where(lane == 0, norm, jnp.where(lane == 1, curve, 0.0))


def order_kernel(rows_ref, perm_ref, out_ref):
    rows = rows_ref[...]
    count, width = rows.shape
    pieces = jnp.concatenate([piece for piece in split_three(rows)], axis=0).astype(BF16)
    perm = perm_ref[...]
    chunk = 256
    for col in range(0, width, chunk):
        total = jnp.zeros((3 * count, chunk), F32)
        for at in range(0, width, chunk):
            index = lax.broadcasted_iota(jnp.int32, (chunk, chunk), 0) + at
            pick = jnp.where(index == perm[:, col : col + chunk], 1.0, 0.0).astype(BF16)
            total += jnp.dot(pieces[:, at : at + chunk], pick, preferred_element_type=F32)
        out_ref[:, col : col + chunk] = total[:count] + total[count : 2 * count] + total[2 * count :]


def swap(value, mask, count):
    return lax.ppermute(value, "row", [(i, i ^ mask) for i in range(count)])


def levels(count, sizes):
    bits = count.bit_length() - 1
    out = []
    sizes = list(sizes)
    while bits:
        take = min(sizes.pop(0) if sizes else 1, bits)
        bits -= take
        out.append([mask << bits for mask in range(1, 1 << take)])
    return out


def tree_sum(value, count):
    for masks in levels(count, [2, 2, 2]):
        others = [swap(value, mask, count) for mask in masks]
        if len(masks) == 3:
            value = (value + others[0]) + (others[1] + others[2])
        else:
            value = value + others[0]
    return value


def gather_levels(count):
    return levels(count, [2] if count <= 16 else [2, 2])


def gather_places(count):
    places = [0]
    for masks in gather_levels(count):
        places = places + [place ^ mask for mask in masks for place in places]
    return places


def tree_gather(value, count):
    blocks, out = value[None], []
    for masks in gather_levels(count):
        blocks = jnp.concatenate([blocks] + [swap(blocks, mask, count) for mask in masks], axis=0)
        out.append(blocks)
    return out


def gate(block, behind):
    return pl.pallas_call(
        lambda *refs: None,
        in_specs=[pl.BlockSpec(memory_space=pl.ANY)] * 2,
        out_specs=pl.BlockSpec(memory_space=pl.ANY),
        out_shape=jax.ShapeDtypeStruct(block.shape, block.dtype),
        input_output_aliases={0: 0},
        compiler_params=pltpu.CompilerParams(vmem_limit_bytes=1024 * 1024),
        name="gate",
    )(block, behind)


def local(features, right_side, variance, hilbert_order, tile_list):
    width = features.shape[1]
    rhs_count = right_side.shape[0]
    count = lax.axis_size("row")
    most = tile_list.shape[1]
    steps = width // ROWS
    shape = jax.ShapeDtypeStruct
    params = pltpu.CompilerParams(vmem_limit_bytes=10 * 1024 * 1024)
    var_row = variance[None, :]

    whole = lambda *ignored: (0, 0)
    row_spec = pl.BlockSpec(right_side.shape, whole)
    var_spec = pl.BlockSpec(var_row.shape, whole)
    pay_shape = (80, width // 4)
    smem = pl.BlockSpec(memory_space=pltpu.SMEM)
    vmem = pl.BlockSpec(memory_space=pltpu.VMEM)
    in_hbm = lambda array: pltpu.with_memory_space_constraint(array, pltpu.HBM)
    pay_zero, pay_one, right, left, rounded = pl.pallas_call(
        payload_kernel,
        in_specs=[smem, vmem, vmem],
        out_shape=[
            shape((96, width // 4), BF16),
            shape(pay_shape, BF16),
            shape((KDIM, width), BF16),
            shape((width, KDIM), BF16),
            shape(right_side.shape, BF16),
        ],
        compiler_params=params,
        name="payload",
    )(tile_list, in_hbm(features), in_hbm(right_side))
    me = jnp.full((1,), lax.axis_index("row"), jnp.int32)
    any_spec = pl.BlockSpec(memory_space=pl.ANY)

    def own_part(rows, arrived):
        blocks = own_blocks(rows, steps)
        tiles, sums = pl.pallas_call(
            functools.partial(own_kernel, rows),
            in_specs=[vmem, vmem, vmem, any_spec],
            out_specs=[any_spec, vmem],
            out_shape=[pltpu.HBM((len(blocks), ROWS, ROWS), BF16), shape(right_side.shape, F32)],
            scratch_shapes=[
                pltpu.VMEM((len(blocks), ROWS, ROWS), BF16),
                pltpu.SemaphoreType.DMA((len(blocks),)),
            ],
            compiler_params=params,
            cost_estimate=pl.CostEstimate(
                flops=5_000_000_000, bytes_accessed=2 * len(blocks) * ROWS * ROWS, transcendentals=0
            ),
            name=f"own_tile_{rows[0]}",
        )(left, right, rounded, arrived)
        return blocks, tiles, sums

    first_masks, *later = gather_levels(count)
    first_level = lambda pay: jnp.concatenate(
        [pay] + [swap(pay, mask, count) for mask in first_masks], axis=0
    )
    near_zero = first_level(pay_zero)
    own_parts = [own_part(range(1), right)]
    near_zero = gate(near_zero, own_parts[0][2])
    near_one = first_level(gate(pay_one, own_parts[0][2]))
    own_parts.append(own_part(range(1, steps), near_zero))
    near_one = gate(near_one, own_parts[1][2])
    zero, places = [near_zero], [0]
    for level, masks in enumerate(later):
        zero = zero + [swap(array, mask, count) for mask in masks for array in zero]
        places = places + [mask ^ place for mask in masks for place in places]
        if level == 0:
            zero[-1] = gate(zero[-1], own_parts[1][2])
    one = [near_one] + [swap(near_one, place, count) for place in places[1:]]
    each = len(first_masks) + 1
    zero_at = [(at, row * 96) for at in range(len(zero)) for row in range(each)]
    one_at = [(at, row * 80) for at in range(len(one)) for row in range(each)]

    half = steps // 2

    def front_at(k, i, *ignored):
        return (jnp.minimum(k, FRONT - 1), jnp.where(k < FRONT, i, half - 1), 0)

    def back_at(k, i, *ignored):
        return (jnp.maximum(k - FRONT, 0), jnp.where(k < FRONT, 0, i), 0)

    half_specs = [pl.BlockSpec((1, ROWS, width), front_at), pl.BlockSpec((1, ROWS, width), back_at)]
    half_shapes = [
        pltpu.VMEM((FRONT, width // 2, width), BF16),
        pltpu.HBM((most - FRONT, width // 2, width), BF16),
    ]
    half_scratch = [
        pltpu.VMEM((2, width // 2, KDIM), BF16),
        pltpu.VMEM((2, rhs_count, width // 2), BF16),
        pltpu.VMEM((2,) + pay_shape, BF16),
        pltpu.SemaphoreType.DMA((2,)),
    ]
    right_spec = pl.BlockSpec(right.shape, whole)
    send_shape = (rhs_count, width + TAIL)
    front_zero, back_zero, half_sum, slots = pl.pallas_call(
        functools.partial(pair_zero_kernel, zero_at),
        grid_spec=pltpu.PrefetchScalarGridSpec(
            num_scalar_prefetch=1,
            grid=(most, half),
            in_specs=[right_spec] + [row_spec] * PARTS + [any_spec] * len(zero),
            out_specs=half_specs + [row_spec, smem],
            scratch_shapes=half_scratch
            + [
                pltpu.VMEM((count, 16, 128), BF16),
                pltpu.VMEM((count, 128), jnp.int32),
                pltpu.SMEM((count, 128), jnp.int32),
                pltpu.SemaphoreType.DMA((count,)),
            ],
        ),
        out_shape=half_shapes
        + [shape(right_side.shape, F32), shape((most + 2,), jnp.int32)],
        compiler_params=params,
        name="pair_zero",
    )(me, right, *[part[2] for part in own_parts], *zero)
    front_one, back_one, image, send = pl.pallas_call(
        functools.partial(pair_one_kernel, one_at),
        grid_spec=pltpu.PrefetchScalarGridSpec(
            num_scalar_prefetch=1,
            grid=(most, half),
            in_specs=[right_spec, row_spec, row_spec, var_spec] + [any_spec] * len(one),
            out_specs=half_specs + [row_spec, pl.BlockSpec(send_shape, whole)],
            scratch_shapes=half_scratch,
        ),
        out_shape=half_shapes + [shape(right_side.shape, F32), shape(send_shape, BF16)],
        compiler_params=params,
        name="pair_one",
    )(slots, right, half_sum, right_side, var_row, *one)
    fronts = [pltpu.with_memory_space_constraint(part, pltpu.VMEM) for part in (front_zero, front_one)]
    backs = [pltpu.with_memory_space_constraint(part, pltpu.HBM) for part in (back_zero, back_one)]

    every_send = tree_gather(send, count)[-1]
    own_again = [
        pl.pallas_call(
            functools.partial(own_again_kernel, blocks),
            in_specs=[any_spec, pl.BlockSpec(send_shape, whole)],
            out_specs=row_spec,
            out_shape=shape(right_side.shape, F32),
            scratch_shapes=[
                pltpu.VMEM((len(blocks), ROWS, ROWS), BF16),
                pltpu.SemaphoreType.DMA((len(blocks),)),
            ],
            compiler_params=params,
            cost_estimate=pl.CostEstimate(
                flops=5_000_000_000, bytes_accessed=2 * len(blocks) * ROWS * ROWS, transcendentals=0
            ),
            name=f"own_again_{part}",
        )(in_hbm(tiles), send)
        for part, (blocks, tiles, _) in enumerate(own_parts)
    ]
    dots_spec = pl.BlockSpec((rhs_count, TAIL), whole)
    rows, dots, steps_one = pl.pallas_call(
        again_kernel,
        grid_spec=pltpu.PrefetchScalarGridSpec(
            num_scalar_prefetch=1,
            grid=(most,),
            in_specs=[
                pl.BlockSpec((1, width // 2, width), lambda k, s: (jnp.minimum(k, FRONT - 1), 0, 0)),
                pl.BlockSpec((1, width // 2, width), lambda k, s: (jnp.minimum(k, FRONT - 1), 0, 0)),
                any_spec,
                any_spec,
                pl.BlockSpec((1,) + send_shape, lambda k, s: (s[1 + k], 0, 0)),
                pl.BlockSpec((count, rhs_count, TAIL), lambda k, s: (0, 0, width // TAIL)),
                row_spec,
                var_spec,
                row_spec,
            ]
            + [row_spec] * PARTS,
            out_specs=[
                pl.BlockSpec((4 * rhs_count, width), whole),
                dots_spec,
                dots_spec,
            ],
            scratch_shapes=[
                pltpu.VMEM(right_side.shape, F32),
                pltpu.VMEM((HELD, ROWS, width), BF16),
                pltpu.SemaphoreType.DMA((HELD,)),
            ],
        ),
        out_shape=[
            shape((4 * rhs_count, width), F32),
            shape((rhs_count, TAIL), F32),
            shape((rhs_count, TAIL), F32),
        ],
        compiler_params=params,
        name="pair_again",
    )(slots, *fronts, *backs, every_send, every_send, right_side, var_row, image, *own_again)

    dots = tree_sum(dots, count)
    ordered = pl.pallas_call(
        order_kernel,
        out_shape=shape(rows.shape, F32),
        compiler_params=params,
        name="curve_order",
    )(rows, hilbert_order)
    norm, curve = steps_one[:, 0:1], steps_one[:, 1:2]
    length = norm / curve
    norm_next = dots[:, 0:1]
    ratio = norm_next / norm
    curve_next = dots[:, 1:2] + ratio * (dots[:, 2:3] + dots[:, 3:4]) + ratio * ratio * curve
    length_next = norm_next / curve_next
    rhs_o, res_o, image_o, res_image_o = [ordered[at : at + 8] for at in range(0, 32, 8)]
    solved = length * rhs_o + length_next * (res_o + ratio * rhs_o)
    residual = res_o - length_next * (res_image_o + ratio * image_o)
    return (solved, residual)


def solution(mesh):
    in_specs = (
        P(None, ("group", "row")),
        P(None, ("group", "row")),
        P(("group", "row")),
        P(("group", "row"), None),
        P(("group", "row"), None, None),
    )
    out_specs = (P(None, ("group", "row")), P(None, ("group", "row")))
    return jax.shard_map(local, mesh=mesh, in_specs=in_specs, out_specs=out_specs, check_vma=False)
```

```python
import functools

import jax
import jax.numpy as jnp
import numpy as np
from jax import lax
from jax.experimental import pallas as pl
from jax.experimental.pallas import tpu as pltpu
from jax.sharding import PartitionSpec as P

SHRINK = 0.95
GRAM = SHRINK * SHRINK
SCALE = 20.0 * (20.0 / 19.0) ** 19
DIAGONAL = float(1.0 - SCALE * float(np.float32(1.0 / SCALE).astype(jnp.bfloat16)))
KDIM = 128
ROWS = 512
PARTS = 2
PIECE = 256
STRIP = 64
FRONT = 3
HELD = 4
TAIL = 128
BF16 = jnp.bfloat16
F32 = jnp.float32
CONTRACT_LANES = (((1,), (1,)), ((), ()))


def split_three(value):
    high = value.astype(BF16).astype(F32)
    rest = value - high
    middle = rest.astype(BF16).astype(F32)
    return high, middle, rest - middle


def norm_rows(norm, first):
    high, middle, low = split_three(norm)
    row = lax.broadcasted_iota(jnp.int32, (32, norm.shape[1]), 0)
    out = jnp.where(row < 6, 1.0, 0.0)
    out = jnp.where(row == first, high, out)
    out = jnp.where(row == first + 1, middle, out)
    return jnp.where(row == first + 2, low, out).astype(BF16)


def own_factor(feat):
    wide = feat.astype(F32)
    norm = jnp.sum(wide * wide, axis=0, keepdims=True) * GRAM
    pieces = split_three(wide * (-2.0 * GRAM))
    return jnp.concatenate([piece.astype(BF16) for piece in pieces] + [norm_rows(norm, 0)], axis=0)


def other_factor(feat):
    wide = feat.astype(F32)
    norm = jnp.sum(wide * wide, axis=0, keepdims=True) * GRAM
    return jnp.transpose(jnp.concatenate([feat, feat, feat, norm_rows(norm, 3)], axis=0))


def psi_power(dist):
    dist = jnp.maximum(dist, 1e-30)
    radius = dist * lax.rsqrt(dist)
    u = jnp.maximum(SHRINK - radius, 1e-30)
    return (jnp.exp2(19.0 * lax.log2(u)) * (1.0 - u)).astype(BF16)


def psi_root(dist):
    radius = jnp.sqrt(jnp.maximum(dist, 0.0))
    u = jnp.maximum(SHRINK - radius, 1e-30)
    return (jnp.exp2(19.0 * lax.log2(u)) * (1.0 - u)).astype(BF16)


def tile_unit(left, right, vec, tile_ref, aside=None, psi=psi_power):
    pieces = [slice(at, at + PIECE) for at in range(0, right.shape[1], PIECE)]
    gram = lambda piece: jnp.dot(left, right[:, piece], preferred_element_type=F32)
    product = lambda part: jnp.dot(vec, part, preferred_element_type=F32)
    dist, part, terms = gram(pieces[0]), None, []
    for index, piece in enumerate(pieces):
        following = gram(pieces[index + 1]) if index + 1 < len(pieces) else None
        strips = []
        for at in range(0, left.shape[0], STRIP):
            strips.append(psi(dist[at : at + STRIP]))
            tile_ref[at : at + STRIP, piece] = strips[-1]
        if part is not None:
            terms.append(product(part))
        if index == 1 and aside is not None:
            aside()
        dist, part = following, jnp.concatenate(strips, axis=0)
    return jnp.concatenate(terms + [product(part)], axis=1)


def unpack(pay):
    return jnp.concatenate([pay[:32], pay[32:64]], axis=1), jnp.concatenate([pay[64:72], pay[72:80]], axis=1)


def own_blocks(rows, count):
    return [(row, col) for row in rows for col in range(row, count)]


def own_kernel(
    rows, left_ref, right_ref, vec_ref, arrived_ref, out_ref, sum_ref, tile_ref, sem_ref
):
    sum_ref[...] = jnp.zeros_like(sum_ref)
    count = vec_ref.shape[1] // ROWS
    piece = lambda index: pl.ds(pl.multiple_of(index * ROWS, ROWS), ROWS)
    save = lambda at: pltpu.make_async_copy(tile_ref.at[at], out_ref.at[at], sem_ref.at[at])

    def row_step(row, at):
        def col_step(col, at):
            sum_ref[:, piece(col)] += tile_unit(
                left_ref[piece(row), :], right_ref[:, piece(col)], vec_ref[:, piece(row)],
                tile_ref.at[at],
            )
            save(at).start()

            @pl.when(row != col)
            def _():
                sum_ref[:, piece(row)] += lax.dot_general(
                    vec_ref[:, piece(col)], tile_ref[at], CONTRACT_LANES,
                    preferred_element_type=F32,
                )

            return at + 1

        return lax.fori_loop(row, count, col_step, at)

    lax.fori_loop(rows[0], rows[-1] + 1, row_step, 0)
    for at in range(tile_ref.shape[0]):
        save(at).wait()


def own_again_kernel(blocks, in_ref, vec_ref, sum_ref, tile_ref, sem_ref):
    load = lambda index: pltpu.make_async_copy(
        in_ref.at[index], tile_ref.at[index], sem_ref.at[index]
    )
    for index in range(len(blocks)):
        load(index).start()
    sum_ref[...] = jnp.zeros_like(sum_ref)
    piece = lambda index: slice(index * ROWS, (index + 1) * ROWS)
    for index, (row, col) in enumerate(blocks):
        load(index).wait()
        sum_ref[:, piece(col)] += jnp.dot(
            vec_ref[:, piece(row)], tile_ref[index], preferred_element_type=F32
        )
        if row != col:
            sum_ref[:, piece(row)] += lax.dot_general(
                vec_ref[:, piece(col)], tile_ref[index], CONTRACT_LANES, preferred_element_type=F32
            )


def payload_kernel(
    list_ref, feat_ref, rhs_ref, pay_zero_ref, pay_one_ref, right_ref, left_ref, vec_ref
):
    feat = feat_ref[...]
    rounded = rhs_ref[...].astype(BF16)
    quarter = feat.shape[1] // 4
    for half, pay_ref in enumerate((pay_zero_ref, pay_one_ref)):
        first, second = [slice(at * quarter, (at + 1) * quarter) for at in (2 * half, 2 * half + 1)]
        pay_ref[:32] = feat[:, first]
        pay_ref[32:64] = feat[:, second]
        pay_ref[64:80] = jnp.concatenate([rounded[:, first], rounded[:, second]], axis=0)
    lane = lax.broadcasted_iota(jnp.int32, (16, quarter), 1)
    numbers = jnp.full(lane.shape, -1, jnp.int32)
    for entry in range(list_ref.shape[1]):
        numbers = jnp.where(lane == entry, list_ref[0, entry, 1], numbers)
    pay_zero_ref[80:96] = numbers.astype(F32).astype(BF16)
    right_ref[...] = own_factor(feat)
    left_ref[...] = other_factor(feat)
    vec_ref[...] = rounded


def find_partners(lists_ref, me, slots_ref):
    count, most = lists_ref.shape[0], slots_ref.shape[0] - 2
    for at in range(slots_ref.shape[0]):
        slots_ref[at] = 0
    total = jnp.int32(0)
    for at, place in enumerate(gather_places(count)):
        if at == 0:
            continue
        number = me ^ place
        hit = jnp.bool_(False)
        for entry in range(most):
            hit = hit | (lists_ref[at, entry] == me) | (lists_ref[0, entry] == number)
        slots_ref[1 + total] = jnp.where(hit, at, 0)
        total = total + hit.astype(jnp.int32)
    slots_ref[0] = total


def fetch_from(block_at, block_refs, slots_ref, pay_ref, sem_ref):
    def fetch(which):
        for at, (index, row) in enumerate(block_at):
            @pl.when(slots_ref[1 + which] == at)
            def _():
                pltpu.make_async_copy(
                    block_refs[index].at[pl.ds(row, 80)],
                    pay_ref.at[which % 2],
                    sem_ref.at[which % 2],
                ).start()

    return fetch


def half_tiles(early, psi, slots_ref, right_ref, fetch, front_ref, back_ref, sum_ref, left_ref, vec_ref, pay_ref, sem_ref):
    slot, step = pl.program_id(0), pl.program_id(1)
    last = pl.num_programs(1) - 1

    def arrive(which):
        pltpu.make_async_copy(
            pay_ref.at[(which + 1) % 2], pay_ref.at[which % 2], sem_ref.at[which % 2]
        ).wait()

    def factor(which):
        feat, vec = unpack(pay_ref[which % 2])
        left_ref[which % 2] = other_factor(feat)
        vec_ref[which % 2] = vec

    @pl.when((slot == 0) & (step == 0) & (slots_ref[0] > 0))
    def _():
        fetch(0)

    @pl.when(slot < slots_ref[0])
    def _():
        @pl.when((step == 0) & ((slot == 0) | (not early)))
        def _():
            arrive(slot)
            factor(slot)

        @pl.when((step == 0) & (slot + 1 < slots_ref[0]))
        def _():
            fetch(slot + 1)

        if early:
            @pl.when((step == last) & (slot + 1 < slots_ref[0]))
            def _():
                arrive(slot + 1)

        rows = pl.ds(pl.multiple_of(step * ROWS, ROWS), ROWS)
        place = slot % 2
        left, vec = left_ref[place, rows, :], vec_ref[place, :, rows]
        for tile_ref, here in ((front_ref, slot < FRONT), (back_ref, slot >= FRONT)):
            for ends in (False, True) if early else (None,):
                @pl.when(here if ends is None else here & ((step == last) == ends))
                def _():
                    aside = (lambda: factor(slot + 1)) if ends else None
                    sum_ref[...] += tile_unit(left, right_ref[...], vec, tile_ref.at[0], aside, psi)


def pair_zero_kernel(block_at, me_ref, right_ref, *refs):
    first_refs, block_refs = refs[:PARTS], refs[PARTS:-12]
    front_ref, back_ref, sum_ref, slots_ref = refs[-12:-8]
    left_ref, vec_ref, pay_ref, sem_ref, strip_ref, list_ref, lists_ref, strip_sem_ref = refs[-8:]

    @pl.when((pl.program_id(0) == 0) & (pl.program_id(1) == 0))
    def _():
        strips = [
            pltpu.make_async_copy(
                block_refs[index].at[pl.ds(row + 80, 16), pl.ds(0, 128)],
                strip_ref.at[at],
                strip_sem_ref.at[at],
            )
            for at, (index, row) in enumerate(block_at)
        ]
        for strip in strips:
            strip.start()
        sum_ref[...] = functools.reduce(jnp.add, [first_ref[...] for first_ref in first_refs])
        for at, strip in enumerate(strips):
            strip.wait()
            list_ref[at : at + 1, :] = strip_ref[at].astype(F32)[:1].astype(jnp.int32)
        numbers = pltpu.make_async_copy(list_ref, lists_ref, strip_sem_ref.at[0])
        numbers.start()
        numbers.wait()
        find_partners(lists_ref, me_ref[0], slots_ref)

    fetch = fetch_from(block_at, block_refs, slots_ref, pay_ref, sem_ref)
    half_tiles(
        True, psi_root, slots_ref, right_ref, fetch, front_ref, back_ref, sum_ref, left_ref, vec_ref, pay_ref, sem_ref
    )


def pair_one_kernel(block_at, slots_ref, right_ref, first_ref, rhs_ref, var_ref, *refs):
    block_refs = refs[:-8]
    front_ref, back_ref, image_ref, send_ref, left_ref, vec_ref, pay_ref, sem_ref = refs[-8:]
    slot, step = pl.program_id(0), pl.program_id(1)

    @pl.when((slot == 0) & (step == 0))
    def _():
        image_ref[...] = first_ref[...]

    fetch = fetch_from(block_at, block_refs, slots_ref, pay_ref, sem_ref)
    half_tiles(
        True, psi_power, slots_ref, right_ref, fetch, front_ref, back_ref, image_ref, left_ref, vec_ref, pay_ref, sem_ref
    )

    @pl.when((slot == pl.num_programs(0) - 1) & (step == pl.num_programs(1) - 1))
    def _():
        rhs = rhs_ref[...]
        width = rhs.shape[1]
        image = (var_ref[...] + DIAGONAL) * rhs + SCALE * image_ref[...]
        image_ref[...] = image
        send_ref[:, :width] = image.astype(BF16)
        pieces = split_three(jnp.sum(rhs * rhs, axis=1, keepdims=True))
        pieces += split_three(jnp.sum(rhs * image, axis=1, keepdims=True))
        lane = lax.broadcasted_iota(jnp.int32, (rhs.shape[0], TAIL), 1)
        tail = jnp.zeros((rhs.shape[0], TAIL), F32)
        for place, piece in enumerate(pieces):
            tail = jnp.where(lane == place, piece, tail)
        send_ref[:, width:] = tail.astype(BF16)


def again_kernel(
    slots_ref, front_zero_ref, front_one_ref, back_zero_ref, back_one_ref,
    vec_ref, tails_ref, rhs_ref, var_ref, image_ref, *refs
):
    first_refs = refs[:PARTS]
    rows_ref, dots_ref, step_ref, sum_ref, held_ref, sem_ref = refs[PARTS:]
    slot = pl.program_id(0)
    width = rhs_ref.shape[1]
    steps = width // ROWS
    half = width // 2
    parts = (slots_ref[0] - FRONT) * steps

    def fetch(part, back_ref, first):
        at = pl.ds(pl.multiple_of((part % steps - first) * ROWS, ROWS), ROWS)
        return pltpu.make_async_copy(
            back_ref.at[part // steps, at], held_ref.at[part % HELD], sem_ref.at[part % HELD]
        )

    def start(part):
        @pl.when((part < parts) & (part % steps < steps // 2))
        def _():
            fetch(part, back_zero_ref, 0).start()

        @pl.when((part < parts) & (part % steps >= steps // 2))
        def _():
            fetch(part, back_one_ref, steps // 2).start()

    @pl.when(slot == 0)
    def _():
        sum_ref[...] = functools.reduce(jnp.add, [first_ref[...] for first_ref in first_refs])
        for part in range(HELD):
            start(part)

    @pl.when((slot < slots_ref[0]) & (slot < FRONT))
    def _():
        for index, front_ref in enumerate((front_zero_ref, front_one_ref)):
            sum_ref[...] += jnp.dot(
                vec_ref[0, :, index * half : (index + 1) * half], front_ref[0],
                preferred_element_type=F32,
            )

    @pl.when((slot < slots_ref[0]) & (slot >= FRONT))
    def _():
        for step in range(steps):
            part = (slot - FRONT) * steps + step
            fetch(part % HELD, back_zero_ref, part % HELD // (steps // 2) * (steps // 2)).wait()
            sum_ref[...] += jnp.dot(
                vec_ref[0, :, step * ROWS : (step + 1) * ROWS], held_ref[part % HELD],
                preferred_element_type=F32,
            )
            start(part + HELD)

    @pl.when(slot == pl.num_programs(0) - 1)
    def _():
        rhs = rhs_ref[...]
        image = image_ref[...]
        total = jnp.sum(tails_ref[...].astype(F32), axis=0)
        norm = total[:, 0:1] + total[:, 1:2] + total[:, 2:3]
        curve = total[:, 3:4] + total[:, 4:5] + total[:, 5:6]
        length = norm / curve
        second = (var_ref[...] + DIAGONAL) * image + SCALE * sum_ref[...]
        res = rhs - length * image
        res_image = image - length * second
        rows_ref[0:8] = rhs
        rows_ref[8:16] = res
        rows_ref[16:24] = image
        rows_ref[24:32] = res_image
        lane = lax.broadcasted_iota(jnp.int32, (rhs.shape[0], TAIL), 1)
        dots = jnp.zeros((rhs.shape[0], TAIL), F32)
        for place, product in enumerate((res * res, res * res_image, res * image, rhs * res_image)):
            dots = jnp.where(lane == place, jnp.sum(product, axis=1, keepdims=True), dots)
        dots_ref[...] = dots
        step_ref[...] = jnp.where(lane == 0, norm, jnp.where(lane == 1, curve, 0.0))


def order_kernel(rows_ref, perm_ref, out_ref):
    rows = rows_ref[...]
    count, width = rows.shape
    pieces = jnp.concatenate([piece for piece in split_three(rows)], axis=0).astype(BF16)
    perm = perm_ref[...]
    chunk = 256
    for col in range(0, width, chunk):
        total = jnp.zeros((3 * count, chunk), F32)
        for at in range(0, width, chunk):
            index = lax.broadcasted_iota(jnp.int32, (chunk, chunk), 0) + at
            pick = jnp.where(index == perm[:, col : col + chunk], 1.0, 0.0).astype(BF16)
            total += jnp.dot(pieces[:, at : at + chunk], pick, preferred_element_type=F32)
        out_ref[:, col : col + chunk] = total[:count] + total[count : 2 * count] + total[2 * count :]


def swap(value, mask, count):
    return lax.ppermute(value, "row", [(i, i ^ mask) for i in range(count)])


def levels(count, sizes):
    bits = count.bit_length() - 1
    out = []
    sizes = list(sizes)
    while bits:
        take = min(sizes.pop(0) if sizes else 1, bits)
        bits -= take
        out.append([mask << bits for mask in range(1, 1 << take)])
    return out


def tree_sum(value, count):
    for masks in levels(count, [2, 2, 2]):
        others = [swap(value, mask, count) for mask in masks]
        if len(masks) == 3:
            value = (value + others[0]) + (others[1] + others[2])
        else:
            value = value + others[0]
    return value


def gather_levels(count):
    return levels(count, [2] if count <= 16 else [2, 2])


def gather_places(count):
    places = [0]
    for masks in gather_levels(count):
        places = places + [place ^ mask for mask in masks for place in places]
    return places


def tree_gather(value, count):
    blocks, out = value[None], []
    for masks in gather_levels(count):
        blocks = jnp.concatenate([blocks] + [swap(blocks, mask, count) for mask in masks], axis=0)
        out.append(blocks)
    return out


def gate(block, behind):
    return pl.pallas_call(
        lambda *refs: None,
        in_specs=[pl.BlockSpec(memory_space=pl.ANY)] * 2,
        out_specs=pl.BlockSpec(memory_space=pl.ANY),
        out_shape=jax.ShapeDtypeStruct(block.shape, block.dtype),
        input_output_aliases={0: 0},
        compiler_params=pltpu.CompilerParams(vmem_limit_bytes=1024 * 1024),
        name="gate",
    )(block, behind)


def local(features, right_side, variance, hilbert_order, tile_list):
    width = features.shape[1]
    rhs_count = right_side.shape[0]
    count = lax.axis_size("row")
    most = tile_list.shape[1]
    steps = width // ROWS
    shape = jax.ShapeDtypeStruct
    params = pltpu.CompilerParams(vmem_limit_bytes=10 * 1024 * 1024)
    var_row = variance[None, :]

    whole = lambda *ignored: (0, 0)
    row_spec = pl.BlockSpec(right_side.shape, whole)
    var_spec = pl.BlockSpec(var_row.shape, whole)
    pay_shape = (80, width // 4)
    smem = pl.BlockSpec(memory_space=pltpu.SMEM)
    vmem = pl.BlockSpec(memory_space=pltpu.VMEM)
    in_hbm = lambda array: pltpu.with_memory_space_constraint(array, pltpu.HBM)
    pay_zero, pay_one, right, left, rounded = pl.pallas_call(
        payload_kernel,
        in_specs=[smem, vmem, vmem],
        out_shape=[
            shape((96, width // 4), BF16),
            shape(pay_shape, BF16),
            shape((KDIM, width), BF16),
            shape((width, KDIM), BF16),
            shape(right_side.shape, BF16),
        ],
        compiler_params=params,
        name="payload",
    )(tile_list, in_hbm(features), in_hbm(right_side))
    me = jnp.full((1,), lax.axis_index("row"), jnp.int32)
    any_spec = pl.BlockSpec(memory_space=pl.ANY)

    def own_part(rows, arrived):
        blocks = own_blocks(rows, steps)
        tiles, sums = pl.pallas_call(
            functools.partial(own_kernel, rows),
            in_specs=[vmem, vmem, vmem, any_spec],
            out_specs=[any_spec, vmem],
            out_shape=[pltpu.HBM((len(blocks), ROWS, ROWS), BF16), shape(right_side.shape, F32)],
            scratch_shapes=[
                pltpu.VMEM((len(blocks), ROWS, ROWS), BF16),
                pltpu.SemaphoreType.DMA((len(blocks),)),
            ],
            compiler_params=params,
            cost_estimate=pl.CostEstimate(
                flops=5_000_000_000, bytes_accessed=2 * len(blocks) * ROWS * ROWS, transcendentals=0
            ),
            name=f"own_tile_{rows[0]}",
        )(left, right, rounded, arrived)
        return blocks, tiles, sums

    first_masks, *later = gather_levels(count)
    first_level = lambda pay: jnp.concatenate(
        [pay] + [swap(pay, mask, count) for mask in first_masks], axis=0
    )
    near_zero = first_level(pay_zero)
    own_parts = [own_part(range(1), right)]
    near_zero = gate(near_zero, own_parts[0][2])
    near_one = first_level(gate(pay_one, own_parts[0][2]))
    own_parts.append(own_part(range(1, steps), near_zero))
    near_one = gate(near_one, own_parts[1][2])
    zero, places = [near_zero], [0]
    for level, masks in enumerate(later):
        zero = zero + [swap(array, mask, count) for mask in masks for array in zero]
        places = places + [mask ^ place for mask in masks for place in places]
        if level == 0:
            zero[-1] = gate(zero[-1], own_parts[1][2])
    one = [near_one] + [swap(near_one, place, count) for place in places[1:]]
    each = len(first_masks) + 1
    zero_at = [(at, row * 96) for at in range(len(zero)) for row in range(each)]
    one_at = [(at, row * 80) for at in range(len(one)) for row in range(each)]

    half = steps // 2

    def front_at(k, i, *ignored):
        return (jnp.minimum(k, FRONT - 1), jnp.where(k < FRONT, i, half - 1), 0)

    def back_at(k, i, *ignored):
        return (jnp.maximum(k - FRONT, 0), jnp.where(k < FRONT, 0, i), 0)

    half_specs = [pl.BlockSpec((1, ROWS, width), front_at), pl.BlockSpec((1, ROWS, width), back_at)]
    half_shapes = [
        pltpu.VMEM((FRONT, width // 2, width), BF16),
        pltpu.HBM((most - FRONT, width // 2, width), BF16),
    ]
    half_scratch = [
        pltpu.VMEM((2, width // 2, KDIM), BF16),
        pltpu.VMEM((2, rhs_count, width // 2), BF16),
        pltpu.VMEM((2,) + pay_shape, BF16),
        pltpu.SemaphoreType.DMA((2,)),
    ]
    right_spec = pl.BlockSpec(right.shape, whole)
    send_shape = (rhs_count, width + TAIL)
    front_zero, back_zero, half_sum, slots = pl.pallas_call(
        functools.partial(pair_zero_kernel, zero_at),
        grid_spec=pltpu.PrefetchScalarGridSpec(
            num_scalar_prefetch=1,
            grid=(most, half),
            in_specs=[right_spec] + [row_spec] * PARTS + [any_spec] * len(zero),
            out_specs=half_specs + [row_spec, smem],
            scratch_shapes=half_scratch
            + [
                pltpu.VMEM((count, 16, 128), BF16),
                pltpu.VMEM((count, 128), jnp.int32),
                pltpu.SMEM((count, 128), jnp.int32),
                pltpu.SemaphoreType.DMA((count,)),
            ],
        ),
        out_shape=half_shapes
        + [shape(right_side.shape, F32), shape((most + 2,), jnp.int32)],
        compiler_params=params,
        name="pair_zero",
    )(me, right, *[part[2] for part in own_parts], *zero)
    front_one, back_one, image, send = pl.pallas_call(
        functools.partial(pair_one_kernel, one_at),
        grid_spec=pltpu.PrefetchScalarGridSpec(
            num_scalar_prefetch=1,
            grid=(most, half),
            in_specs=[right_spec, row_spec, row_spec, var_spec] + [any_spec] * len(one),
            out_specs=half_specs + [row_spec, pl.BlockSpec(send_shape, whole)],
            scratch_shapes=half_scratch,
        ),
        out_shape=half_shapes + [shape(right_side.shape, F32), shape(send_shape, BF16)],
        compiler_params=params,
        name="pair_one",
    )(slots, right, half_sum, right_side, var_row, *one)
    fronts = [pltpu.with_memory_space_constraint(part, pltpu.VMEM) for part in (front_zero, front_one)]
    backs = [pltpu.with_memory_space_constraint(part, pltpu.HBM) for part in (back_zero, back_one)]

    every_send = tree_gather(send, count)[-1]
    own_again = [
        pl.pallas_call(
            functools.partial(own_again_kernel, blocks),
            in_specs=[any_spec, pl.BlockSpec(send_shape, whole)],
            out_specs=row_spec,
            out_shape=shape(right_side.shape, F32),
            scratch_shapes=[
                pltpu.VMEM((len(blocks), ROWS, ROWS), BF16),
                pltpu.SemaphoreType.DMA((len(blocks),)),
            ],
            compiler_params=params,
            cost_estimate=pl.CostEstimate(
                flops=5_000_000_000, bytes_accessed=2 * len(blocks) * ROWS * ROWS, transcendentals=0
            ),
            name=f"own_again_{part}",
        )(in_hbm(tiles), send)
        for part, (blocks, tiles, _) in enumerate(own_parts)
    ]
    dots_spec = pl.BlockSpec((rhs_count, TAIL), whole)
    rows, dots, steps_one = pl.pallas_call(
        again_kernel,
        grid_spec=pltpu.PrefetchScalarGridSpec(
            num_scalar_prefetch=1,
            grid=(most,),
            in_specs=[
                pl.BlockSpec((1, width // 2, width), lambda k, s: (jnp.minimum(k, FRONT - 1), 0, 0)),
                pl.BlockSpec((1, width // 2, width), lambda k, s: (jnp.minimum(k, FRONT - 1), 0, 0)),
                any_spec,
                any_spec,
                pl.BlockSpec((1,) + send_shape, lambda k, s: (s[1 + k], 0, 0)),
                pl.BlockSpec((count, rhs_count, TAIL), lambda k, s: (0, 0, width // TAIL)),
                row_spec,
                var_spec,
                row_spec,
            ]
            + [row_spec] * PARTS,
            out_specs=[
                pl.BlockSpec((4 * rhs_count, width), whole),
                dots_spec,
                dots_spec,
            ],
            scratch_shapes=[
                pltpu.VMEM(right_side.shape, F32),
                pltpu.VMEM((HELD, ROWS, width), BF16),
                pltpu.SemaphoreType.DMA((HELD,)),
            ],
        ),
        out_shape=[
            shape((4 * rhs_count, width), F32),
            shape((rhs_count, TAIL), F32),
            shape((rhs_count, TAIL), F32),
        ],
        compiler_params=params,
        name="pair_again",
    )(slots, *fronts, *backs, every_send, every_send, right_side, var_row, image, *own_again)

    dots = tree_sum(dots, count)
    ordered = pl.pallas_call(
        order_kernel,
        out_shape=shape(rows.shape, F32),
        compiler_params=params,
        name="curve_order",
    )(rows, hilbert_order)
    norm, curve = steps_one[:, 0:1], steps_one[:, 1:2]
    length = norm / curve
    norm_next = dots[:, 0:1]
    ratio = norm_next / norm
    curve_next = dots[:, 1:2] + ratio * (dots[:, 2:3] + dots[:, 3:4]) + ratio * ratio * curve
    length_next = norm_next / curve_next
    rhs_o, res_o, image_o, res_image_o = [ordered[at : at + 8] for at in range(0, 32, 8)]
    solved = length * rhs_o + length_next * (res_o + ratio * rhs_o)
    residual = res_o - length_next * (res_image_o + ratio * image_o)
    return (solved, residual)


def solution(mesh):
    in_specs = (
        P(None, ("group", "row")),
        P(None, ("group", "row")),
        P(("group", "row")),
        P(("group", "row"), None),
        P(("group", "row"), None, None),
    )
    out_specs = (P(None, ("group", "row")), P(None, ("group", "row")))
    return jax.shard_map(local, mesh=mesh, in_specs=in_specs, out_specs=out_specs, check_vma=False)
```

```python
import functools

import jax
import jax.numpy as jnp
import numpy as np
from jax import lax
from jax.experimental import pallas as pl
from jax.experimental.pallas import tpu as pltpu
from jax.sharding import PartitionSpec as P

SHRINK = 0.95
GRAM = SHRINK * SHRINK
SCALE = 20.0 * (20.0 / 19.0) ** 19
DIAGONAL = float(1.0 - SCALE * float(np.float32(1.0 / SCALE).astype(jnp.bfloat16)))
KDIM = 128
ROWS = 512
PARTS = 2
PIECE = 256
STRIP = 64
FRONT = 3
HELD = 4
TAIL = 128
BF16 = jnp.bfloat16
F32 = jnp.float32
CONTRACT_LANES = (((1,), (1,)), ((), ()))


def split_three(value):
    high = value.astype(BF16).astype(F32)
    rest = value - high
    middle = rest.astype(BF16).astype(F32)
    return high, middle, rest - middle


def norm_rows(norm, first):
    high, middle, low = split_three(norm)
    row = lax.broadcasted_iota(jnp.int32, (32, norm.shape[1]), 0)
    out = jnp.where(row < 6, 1.0, 0.0)
    out = jnp.where(row == first, high, out)
    out = jnp.where(row == first + 1, middle, out)
    return jnp.where(row == first + 2, low, out).astype(BF16)


def own_factor(feat):
    wide = feat.astype(F32)
    norm = jnp.sum(wide * wide, axis=0, keepdims=True) * GRAM
    pieces = split_three(wide * (-2.0 * GRAM))
    return jnp.concatenate([piece.astype(BF16) for piece in pieces] + [norm_rows(norm, 0)], axis=0)


def other_factor(feat):
    wide = feat.astype(F32)
    norm = jnp.sum(wide * wide, axis=0, keepdims=True) * GRAM
    return jnp.transpose(jnp.concatenate([feat, feat, feat, norm_rows(norm, 3)], axis=0))


def psi_power(dist):
    dist = jnp.maximum(dist, 1e-30)
    radius = dist * lax.rsqrt(dist)
    u = jnp.maximum(SHRINK - radius, 1e-30)
    return (jnp.exp2(19.0 * lax.log2(u)) * (1.0 - u)).astype(BF16)


def tile_unit(left, right, vec, tile_ref, aside=None):
    pieces = [slice(at, at + PIECE) for at in range(0, right.shape[1], PIECE)]
    gram = lambda piece: jnp.dot(left, right[:, piece], preferred_element_type=F32)
    product = lambda part: jnp.dot(vec, part, preferred_element_type=F32)
    dist, part, terms = gram(pieces[0]), None, []
    for index, piece in enumerate(pieces):
        following = gram(pieces[index + 1]) if index + 1 < len(pieces) else None
        strips = []
        for at in range(0, left.shape[0], STRIP):
            strips.append(psi_power(dist[at : at + STRIP]))
            tile_ref[at : at + STRIP, piece] = strips[-1]
        if part is not None:
            terms.append(product(part))
        if index == 1 and aside is not None:
            aside()
        dist, part = following, jnp.concatenate(strips, axis=0)
    return jnp.concatenate(terms + [product(part)], axis=1)


def unpack(pay):
    return jnp.concatenate([pay[:32], pay[32:64]], axis=1), jnp.concatenate([pay[64:72], pay[72:80]], axis=1)


def own_blocks(rows, count):
    return [(row, col) for row in rows for col in range(row, count)]


def own_kernel(
    rows, left_ref, right_ref, vec_ref, arrived_ref, out_ref, sum_ref, tile_ref, sem_ref
):
    sum_ref[...] = jnp.zeros_like(sum_ref)
    count = vec_ref.shape[1] // ROWS
    piece = lambda index: pl.ds(pl.multiple_of(index * ROWS, ROWS), ROWS)
    save = lambda at: pltpu.make_async_copy(tile_ref.at[at], out_ref.at[at], sem_ref.at[at])

    def row_step(row, at):
        def col_step(col, at):
            sum_ref[:, piece(col)] += tile_unit(
                left_ref[piece(row), :], right_ref[:, piece(col)], vec_ref[:, piece(row)],
                tile_ref.at[at],
            )
            save(at).start()

            @pl.when(row != col)
            def _():
                sum_ref[:, piece(row)] += lax.dot_general(
                    vec_ref[:, piece(col)], tile_ref[at], CONTRACT_LANES,
                    preferred_element_type=F32,
                )

            return at + 1

        return lax.fori_loop(row, count, col_step, at)

    lax.fori_loop(rows[0], rows[-1] + 1, row_step, 0)
    for at in range(tile_ref.shape[0]):
        save(at).wait()


def own_again_kernel(blocks, in_ref, vec_ref, sum_ref, tile_ref, sem_ref):
    load = lambda index: pltpu.make_async_copy(
        in_ref.at[index], tile_ref.at[index], sem_ref.at[index]
    )
    for index in range(len(blocks)):
        load(index).start()
    sum_ref[...] = jnp.zeros_like(sum_ref)
    piece = lambda index: slice(index * ROWS, (index + 1) * ROWS)
    for index, (row, col) in enumerate(blocks):
        load(index).wait()
        sum_ref[:, piece(col)] += jnp.dot(
            vec_ref[:, piece(row)], tile_ref[index], preferred_element_type=F32
        )
        if row != col:
            sum_ref[:, piece(row)] += lax.dot_general(
                vec_ref[:, piece(col)], tile_ref[index], CONTRACT_LANES, preferred_element_type=F32
            )


def payload_kernel(
    list_ref, feat_ref, rhs_ref, pay_zero_ref, pay_one_ref, right_ref, left_ref, vec_ref
):
    feat = feat_ref[...]
    rounded = rhs_ref[...].astype(BF16)
    quarter = feat.shape[1] // 4
    for half, pay_ref in enumerate((pay_zero_ref, pay_one_ref)):
        first, second = [slice(at * quarter, (at + 1) * quarter) for at in (2 * half, 2 * half + 1)]
        pay_ref[:32] = feat[:, first]
        pay_ref[32:64] = feat[:, second]
        pay_ref[64:80] = jnp.concatenate([rounded[:, first], rounded[:, second]], axis=0)
    lane = lax.broadcasted_iota(jnp.int32, (16, quarter), 1)
    numbers = jnp.full(lane.shape, -1, jnp.int32)
    for entry in range(list_ref.shape[1]):
        numbers = jnp.where(lane == entry, list_ref[0, entry, 1], numbers)
    pay_zero_ref[80:96] = numbers.astype(F32).astype(BF16)
    right_ref[...] = own_factor(feat)
    left_ref[...] = other_factor(feat)
    vec_ref[...] = rounded


def find_partners(lists_ref, me, slots_ref):
    count, most = lists_ref.shape[0], slots_ref.shape[0] - 2
    for at in range(slots_ref.shape[0]):
        slots_ref[at] = 0
    total = jnp.int32(0)
    for at, place in enumerate(gather_places(count)):
        if at == 0:
            continue
        number = me ^ place
        hit = jnp.bool_(False)
        for entry in range(most):
            hit = hit | (lists_ref[at, entry] == me) | (lists_ref[0, entry] == number)
        slots_ref[1 + total] = jnp.where(hit, at, 0)
        total = total + hit.astype(jnp.int32)
    slots_ref[0] = total


def fetch_from(block_at, block_refs, slots_ref, pay_ref, sem_ref):
    def fetch(which):
        for at, (index, row) in enumerate(block_at):
            @pl.when(slots_ref[1 + which] == at)
            def _():
                pltpu.make_async_copy(
                    block_refs[index].at[pl.ds(row, 80)],
                    pay_ref.at[which % 2],
                    sem_ref.at[which % 2],
                ).start()

    return fetch


def half_tiles(early, slots_ref, right_ref, fetch, front_ref, back_ref, sum_ref, left_ref, vec_ref, pay_ref, sem_ref):
    slot, step = pl.program_id(0), pl.program_id(1)
    last = pl.num_programs(1) - 1

    def arrive(which):
        pltpu.make_async_copy(
            pay_ref.at[(which + 1) % 2], pay_ref.at[which % 2], sem_ref.at[which % 2]
        ).wait()

    def factor(which):
        feat, vec = unpack(pay_ref[which % 2])
        left_ref[which % 2] = other_factor(feat)
        vec_ref[which % 2] = vec

    @pl.when((slot == 0) & (step == 0) & (slots_ref[0] > 0))
    def _():
        fetch(0)

    @pl.when(slot < slots_ref[0])
    def _():
        @pl.when((step == 0) & ((slot == 0) | (not early)))
        def _():
            arrive(slot)
            factor(slot)

        @pl.when((step == 0) & (slot + 1 < slots_ref[0]))
        def _():
            fetch(slot + 1)

        if early:
            @pl.when((step == last) & (slot + 1 < slots_ref[0]))
            def _():
                arrive(slot + 1)

        rows = pl.ds(pl.multiple_of(step * ROWS, ROWS), ROWS)
        place = slot % 2
        left, vec = left_ref[place, rows, :], vec_ref[place, :, rows]
        for tile_ref, here in ((front_ref, slot < FRONT), (back_ref, slot >= FRONT)):
            for ends in (False, True) if early else (None,):
                @pl.when(here if ends is None else here & ((step == last) == ends))
                def _():
                    aside = (lambda: factor(slot + 1)) if ends else None
                    sum_ref[...] += tile_unit(left, right_ref[...], vec, tile_ref.at[0], aside)


def pair_zero_kernel(block_at, me_ref, right_ref, *refs):
    first_refs, block_refs = refs[:PARTS], refs[PARTS:-12]
    front_ref, back_ref, sum_ref, slots_ref = refs[-12:-8]
    left_ref, vec_ref, pay_ref, sem_ref, strip_ref, list_ref, lists_ref, strip_sem_ref = refs[-8:]

    @pl.when((pl.program_id(0) == 0) & (pl.program_id(1) == 0))
    def _():
        strips = [
            pltpu.make_async_copy(
                block_refs[index].at[pl.ds(row + 80, 16), pl.ds(0, 128)],
                strip_ref.at[at],
                strip_sem_ref.at[at],
            )
            for at, (index, row) in enumerate(block_at)
        ]
        for strip in strips:
            strip.start()
        sum_ref[...] = functools.reduce(jnp.add, [first_ref[...] for first_ref in first_refs])
        for at, strip in enumerate(strips):
            strip.wait()
            list_ref[at : at + 1, :] = strip_ref[at].astype(F32)[:1].astype(jnp.int32)
        numbers = pltpu.make_async_copy(list_ref, lists_ref, strip_sem_ref.at[0])
        numbers.start()
        numbers.wait()
        find_partners(lists_ref, me_ref[0], slots_ref)

    fetch = fetch_from(block_at, block_refs, slots_ref, pay_ref, sem_ref)
    half_tiles(
        True, slots_ref, right_ref, fetch, front_ref, back_ref, sum_ref, left_ref, vec_ref, pay_ref, sem_ref
    )


def pair_one_kernel(block_at, slots_ref, right_ref, first_ref, rhs_ref, var_ref, *refs):
    block_refs = refs[:-8]
    front_ref, back_ref, image_ref, send_ref, left_ref, vec_ref, pay_ref, sem_ref = refs[-8:]
    slot, step = pl.program_id(0), pl.program_id(1)

    @pl.when((slot == 0) & (step == 0))
    def _():
        image_ref[...] = first_ref[...]

    fetch = fetch_from(block_at, block_refs, slots_ref, pay_ref, sem_ref)
    half_tiles(
        True, slots_ref, right_ref, fetch, front_ref, back_ref, image_ref, left_ref, vec_ref, pay_ref, sem_ref
    )

    @pl.when((slot == pl.num_programs(0) - 1) & (step == pl.num_programs(1) - 1))
    def _():
        rhs = rhs_ref[...]
        width = rhs.shape[1]
        image = (var_ref[...] + DIAGONAL) * rhs + SCALE * image_ref[...]
        image_ref[...] = image
        send_ref[:, :width] = image.astype(BF16)
        pieces = split_three(jnp.sum(rhs * rhs, axis=1, keepdims=True))
        pieces += split_three(jnp.sum(rhs * image, axis=1, keepdims=True))
        lane = lax.broadcasted_iota(jnp.int32, (rhs.shape[0], TAIL), 1)
        tail = jnp.zeros((rhs.shape[0], TAIL), F32)
        for place, piece in enumerate(pieces):
            tail = jnp.where(lane == place, piece, tail)
        send_ref[:, width:] = tail.astype(BF16)


def again_kernel(
    slots_ref, front_zero_ref, front_one_ref, back_zero_ref, back_one_ref,
    vec_ref, tails_ref, rhs_ref, var_ref, image_ref, *refs
):
    first_refs = refs[:PARTS]
    rows_ref, dots_ref, step_ref, sum_ref, held_ref, sem_ref = refs[PARTS:]
    slot = pl.program_id(0)
    width = rhs_ref.shape[1]
    steps = width // ROWS
    half = width // 2
    parts = (slots_ref[0] - FRONT) * steps

    def fetch(part, back_ref, first):
        at = pl.ds(pl.multiple_of((part % steps - first) * ROWS, ROWS), ROWS)
        return pltpu.make_async_copy(
            back_ref.at[part // steps, at], held_ref.at[part % HELD], sem_ref.at[part % HELD]
        )

    def start(part):
        @pl.when((part < parts) & (part % steps < steps // 2))
        def _():
            fetch(part, back_zero_ref, 0).start()

        @pl.when((part < parts) & (part % steps >= steps // 2))
        def _():
            fetch(part, back_one_ref, steps // 2).start()

    @pl.when(slot == 0)
    def _():
        sum_ref[...] = functools.reduce(jnp.add, [first_ref[...] for first_ref in first_refs])
        for part in range(HELD):
            start(part)

    @pl.when((slot < slots_ref[0]) & (slot < FRONT))
    def _():
        for index, front_ref in enumerate((front_zero_ref, front_one_ref)):
            sum_ref[...] += jnp.dot(
                vec_ref[0, :, index * half : (index + 1) * half], front_ref[0],
                preferred_element_type=F32,
            )

    @pl.when((slot < slots_ref[0]) & (slot >= FRONT))
    def _():
        for step in range(steps):
            part = (slot - FRONT) * steps + step
            fetch(part % HELD, back_zero_ref, part % HELD // (steps // 2) * (steps // 2)).wait()
            sum_ref[...] += jnp.dot(
                vec_ref[0, :, step * ROWS : (step + 1) * ROWS], held_ref[part % HELD],
                preferred_element_type=F32,
            )
            start(part + HELD)

    @pl.when(slot == pl.num_programs(0) - 1)
    def _():
        rhs = rhs_ref[...]
        image = image_ref[...]
        total = jnp.sum(tails_ref[...].astype(F32), axis=0)
        norm = total[:, 0:1] + total[:, 1:2] + total[:, 2:3]
        curve = total[:, 3:4] + total[:, 4:5] + total[:, 5:6]
        length = norm / curve
        second = (var_ref[...] + DIAGONAL) * image + SCALE * sum_ref[...]
        res = rhs - length * image
        res_image = image - length * second
        rows_ref[0:8] = rhs
        rows_ref[8:16] = res
        rows_ref[16:24] = image
        rows_ref[24:32] = res_image
        lane = lax.broadcasted_iota(jnp.int32, (rhs.shape[0], TAIL), 1)
        dots = jnp.zeros((rhs.shape[0], TAIL), F32)
        for place, product in enumerate((res * res, res * res_image, res * image, rhs * res_image)):
            dots = jnp.where(lane == place, jnp.sum(product, axis=1, keepdims=True), dots)
        dots_ref[...] = dots
        step_ref[...] = jnp.where(lane == 0, norm, jnp.where(lane == 1, curve, 0.0))


def order_kernel(rows_ref, perm_ref, out_ref):
    rows = rows_ref[...]
    count, width = rows.shape
    pieces = jnp.concatenate([piece for piece in split_three(rows)], axis=0).astype(BF16)
    perm = perm_ref[...]
    chunk = 256
    for col in range(0, width, chunk):
        total = jnp.zeros((3 * count, chunk), F32)
        for at in range(0, width, chunk):
            index = lax.broadcasted_iota(jnp.int32, (chunk, chunk), 0) + at
            pick = jnp.where(index == perm[:, col : col + chunk], 1.0, 0.0).astype(BF16)
            total += jnp.dot(pieces[:, at : at + chunk], pick, preferred_element_type=F32)
        out_ref[:, col : col + chunk] = total[:count] + total[count : 2 * count] + total[2 * count :]


def swap(value, mask, count):
    return lax.ppermute(value, "row", [(i, i ^ mask) for i in range(count)])


def levels(count, sizes):
    bits = count.bit_length() - 1
    out = []
    sizes = list(sizes)
    while bits:
        take = min(sizes.pop(0) if sizes else 1, bits)
        bits -= take
        out.append([mask << bits for mask in range(1, 1 << take)])
    return out


def tree_sum(value, count):
    for masks in levels(count, [2, 2, 2]):
        others = [swap(value, mask, count) for mask in masks]
        if len(masks) == 3:
            value = (value + others[0]) + (others[1] + others[2])
        else:
            value = value + others[0]
    return value


def gather_levels(count):
    return levels(count, [2] if count <= 16 else [2, 2])


def gather_places(count):
    places = [0]
    for masks in gather_levels(count):
        places = places + [place ^ mask for mask in masks for place in places]
    return places


def tree_gather(value, count):
    blocks, out = value[None], []
    for masks in gather_levels(count):
        blocks = jnp.concatenate([blocks] + [swap(blocks, mask, count) for mask in masks], axis=0)
        out.append(blocks)
    return out


def gate(block, behind):
    return pl.pallas_call(
        lambda *refs: None,
        in_specs=[pl.BlockSpec(memory_space=pl.ANY)] * 2,
        out_specs=pl.BlockSpec(memory_space=pl.ANY),
        out_shape=jax.ShapeDtypeStruct(block.shape, block.dtype),
        input_output_aliases={0: 0},
        compiler_params=pltpu.CompilerParams(vmem_limit_bytes=1024 * 1024),
        name="gate",
    )(block, behind)


def local(features, right_side, variance, hilbert_order, tile_list):
    width = features.shape[1]
    rhs_count = right_side.shape[0]
    count = lax.axis_size("row")
    most = tile_list.shape[1]
    steps = width // ROWS
    shape = jax.ShapeDtypeStruct
    params = pltpu.CompilerParams(vmem_limit_bytes=10 * 1024 * 1024)
    var_row = variance[None, :]

    whole = lambda *ignored: (0, 0)
    row_spec = pl.BlockSpec(right_side.shape, whole)
    var_spec = pl.BlockSpec(var_row.shape, whole)
    pay_shape = (80, width // 4)
    smem = pl.BlockSpec(memory_space=pltpu.SMEM)
    vmem = pl.BlockSpec(memory_space=pltpu.VMEM)
    in_hbm = lambda array: pltpu.with_memory_space_constraint(array, pltpu.HBM)
    pay_zero, pay_one, right, left, rounded = pl.pallas_call(
        payload_kernel,
        in_specs=[smem, vmem, vmem],
        out_shape=[
            shape((96, width // 4), BF16),
            shape(pay_shape, BF16),
            shape((KDIM, width), BF16),
            shape((width, KDIM), BF16),
            shape(right_side.shape, BF16),
        ],
        compiler_params=params,
        name="payload",
    )(tile_list, in_hbm(features), in_hbm(right_side))
    me = jnp.full((1,), lax.axis_index("row"), jnp.int32)
    any_spec = pl.BlockSpec(memory_space=pl.ANY)

    def own_part(rows, arrived):
        blocks = own_blocks(rows, steps)
        tiles, sums = pl.pallas_call(
            functools.partial(own_kernel, rows),
            in_specs=[vmem, vmem, vmem, any_spec],
            out_specs=[any_spec, vmem],
            out_shape=[pltpu.HBM((len(blocks), ROWS, ROWS), BF16), shape(right_side.shape, F32)],
            scratch_shapes=[
                pltpu.VMEM((len(blocks), ROWS, ROWS), BF16),
                pltpu.SemaphoreType.DMA((len(blocks),)),
            ],
            compiler_params=params,
            cost_estimate=pl.CostEstimate(
                flops=5_000_000_000, bytes_accessed=2 * len(blocks) * ROWS * ROWS, transcendentals=0
            ),
            name=f"own_tile_{rows[0]}",
        )(left, right, rounded, arrived)
        return blocks, tiles, sums

    first_masks, *later = gather_levels(count)
    first_level = lambda pay: jnp.concatenate(
        [pay] + [swap(pay, mask, count) for mask in first_masks], axis=0
    )
    near_zero = first_level(pay_zero)
    own_parts = [own_part(range(steps - 1, steps), right)]
    near_zero = gate(near_zero, own_parts[0][2])
    near_one = first_level(gate(pay_one, own_parts[0][2]))
    own_parts.append(own_part(range(steps - 1), near_zero))
    near_one = gate(near_one, own_parts[1][2])
    zero, places = [near_zero], [0]
    for level, masks in enumerate(later):
        zero = zero + [swap(array, mask, count) for mask in masks for array in zero]
        places = places + [mask ^ place for mask in masks for place in places]
        if level == 0:
            zero[-1] = gate(zero[-1], own_parts[1][2])
    one = [near_one] + [swap(near_one, place, count) for place in places[1:]]
    each = len(first_masks) + 1
    zero_at = [(at, row * 96) for at in range(len(zero)) for row in range(each)]
    one_at = [(at, row * 80) for at in range(len(one)) for row in range(each)]

    half = steps // 2

    def front_at(k, i, *ignored):
        return (jnp.minimum(k, FRONT - 1), jnp.where(k < FRONT, i, half - 1), 0)

    def back_at(k, i, *ignored):
        return (jnp.maximum(k - FRONT, 0), jnp.where(k < FRONT, 0, i), 0)

    half_specs = [pl.BlockSpec((1, ROWS, width), front_at), pl.BlockSpec((1, ROWS, width), back_at)]
    half_shapes = [
        pltpu.VMEM((FRONT, width // 2, width), BF16),
        pltpu.HBM((most - FRONT, width // 2, width), BF16),
    ]
    half_scratch = [
        pltpu.VMEM((2, width // 2, KDIM), BF16),
        pltpu.VMEM((2, rhs_count, width // 2), BF16),
        pltpu.VMEM((2,) + pay_shape, BF16),
        pltpu.SemaphoreType.DMA((2,)),
    ]
    right_spec = pl.BlockSpec(right.shape, whole)
    send_shape = (rhs_count, width + TAIL)
    front_zero, back_zero, half_sum, slots = pl.pallas_call(
        functools.partial(pair_zero_kernel, zero_at),
        grid_spec=pltpu.PrefetchScalarGridSpec(
            num_scalar_prefetch=1,
            grid=(most, half),
            in_specs=[right_spec] + [row_spec] * PARTS + [any_spec] * len(zero),
            out_specs=half_specs + [row_spec, smem],
            scratch_shapes=half_scratch
            + [
                pltpu.VMEM((count, 16, 128), BF16),
                pltpu.VMEM((count, 128), jnp.int32),
                pltpu.SMEM((count, 128), jnp.int32),
                pltpu.SemaphoreType.DMA((count,)),
            ],
        ),
        out_shape=half_shapes
        + [shape(right_side.shape, F32), shape((most + 2,), jnp.int32)],
        compiler_params=params,
        name="pair_zero",
    )(me, right, *[part[2] for part in own_parts], *zero)
    front_one, back_one, image, send = pl.pallas_call(
        functools.partial(pair_one_kernel, one_at),
        grid_spec=pltpu.PrefetchScalarGridSpec(
            num_scalar_prefetch=1,
            grid=(most, half),
            in_specs=[right_spec, row_spec, row_spec, var_spec] + [any_spec] * len(one),
            out_specs=half_specs + [row_spec, pl.BlockSpec(send_shape, whole)],
            scratch_shapes=half_scratch,
        ),
        out_shape=half_shapes + [shape(right_side.shape, F32), shape(send_shape, BF16)],
        compiler_params=params,
        name="pair_one",
    )(slots, right, half_sum, right_side, var_row, *one)
    fronts = [pltpu.with_memory_space_constraint(part, pltpu.VMEM) for part in (front_zero, front_one)]
    backs = [pltpu.with_memory_space_constraint(part, pltpu.HBM) for part in (back_zero, back_one)]

    every_send = tree_gather(send, count)[-1]
    own_again = [
        pl.pallas_call(
            functools.partial(own_again_kernel, blocks),
            in_specs=[any_spec, pl.BlockSpec(send_shape, whole)],
            out_specs=row_spec,
            out_shape=shape(right_side.shape, F32),
            scratch_shapes=[
                pltpu.VMEM((len(blocks), ROWS, ROWS), BF16),
                pltpu.SemaphoreType.DMA((len(blocks),)),
            ],
            compiler_params=params,
            cost_estimate=pl.CostEstimate(
                flops=5_000_000_000, bytes_accessed=2 * len(blocks) * ROWS * ROWS, transcendentals=0
            ),
            name=f"own_again_{part}",
        )(in_hbm(tiles), send)
        for part, (blocks, tiles, _) in enumerate(own_parts)
    ]
    dots_spec = pl.BlockSpec((rhs_count, TAIL), whole)
    rows, dots, steps_one = pl.pallas_call(
        again_kernel,
        grid_spec=pltpu.PrefetchScalarGridSpec(
            num_scalar_prefetch=1,
            grid=(most,),
            in_specs=[
                pl.BlockSpec((1, width // 2, width), lambda k, s: (jnp.minimum(k, FRONT - 1), 0, 0)),
                pl.BlockSpec((1, width // 2, width), lambda k, s: (jnp.minimum(k, FRONT - 1), 0, 0)),
                any_spec,
                any_spec,
                pl.BlockSpec((1,) + send_shape, lambda k, s: (s[1 + k], 0, 0)),
                pl.BlockSpec((count, rhs_count, TAIL), lambda k, s: (0, 0, width // TAIL)),
                row_spec,
                var_spec,
                row_spec,
            ]
            + [row_spec] * PARTS,
            out_specs=[
                pl.BlockSpec((4 * rhs_count, width), whole),
                dots_spec,
                dots_spec,
            ],
            scratch_shapes=[
                pltpu.VMEM(right_side.shape, F32),
                pltpu.VMEM((HELD, ROWS, width), BF16),
                pltpu.SemaphoreType.DMA((HELD,)),
            ],
        ),
        out_shape=[
            shape((4 * rhs_count, width), F32),
            shape((rhs_count, TAIL), F32),
            shape((rhs_count, TAIL), F32),
        ],
        compiler_params=params,
        name="pair_again",
    )(slots, *fronts, *backs, every_send, every_send, right_side, var_row, image, *own_again)

    dots = tree_sum(dots, count)
    ordered = pl.pallas_call(
        order_kernel,
        out_shape=shape(rows.shape, F32),
        compiler_params=params,
        name="curve_order",
    )(rows, hilbert_order)
    norm, curve = steps_one[:, 0:1], steps_one[:, 1:2]
    length = norm / curve
    norm_next = dots[:, 0:1]
    ratio = norm_next / norm
    curve_next = dots[:, 1:2] + ratio * (dots[:, 2:3] + dots[:, 3:4]) + ratio * ratio * curve
    length_next = norm_next / curve_next
    rhs_o, res_o, image_o, res_image_o = [ordered[at : at + 8] for at in range(0, 32, 8)]
    solved = length * rhs_o + length_next * (res_o + ratio * rhs_o)
    residual = res_o - length_next * (res_image_o + ratio * image_o)
    return (solved, residual)


def solution(mesh):
    in_specs = (
        P(None, ("group", "row")),
        P(None, ("group", "row")),
        P(("group", "row")),
        P(("group", "row"), None),
        P(("group", "row"), None, None),
    )
    out_specs = (P(None, ("group", "row")), P(None, ("group", "row")))
    return jax.shard_map(local, mesh=mesh, in_specs=in_specs, out_specs=out_specs, check_vma=False)
```

```python
import functools

import jax
import jax.numpy as jnp
import numpy as np
from jax import lax
from jax.experimental import pallas as pl
from jax.experimental.pallas import tpu as pltpu
from jax.sharding import PartitionSpec as P

SHRINK = 0.95
GRAM = SHRINK * SHRINK
SCALE = 20.0 * (20.0 / 19.0) ** 19
DIAGONAL = float(1.0 - SCALE * float(np.float32(1.0 / SCALE).astype(jnp.bfloat16)))
KDIM = 128
ROWS = 512
PARTS = 2
PIECE = 256
STRIP = 64
FRONT = 3
HELD = 4
TAIL = 128
BF16 = jnp.bfloat16
F32 = jnp.float32
CONTRACT_LANES = (((1,), (1,)), ((), ()))


def split_three(value):
    high = value.astype(BF16).astype(F32)
    rest = value - high
    middle = rest.astype(BF16).astype(F32)
    return high, middle, rest - middle


def norm_rows(norm, first):
    high, middle, low = split_three(norm)
    row = lax.broadcasted_iota(jnp.int32, (32, norm.shape[1]), 0)
    out = jnp.where(row < 6, 1.0, 0.0)
    out = jnp.where(row == first, high, out)
    out = jnp.where(row == first + 1, middle, out)
    return jnp.where(row == first + 2, low, out).astype(BF16)


def own_factor(feat):
    wide = feat.astype(F32)
    norm = jnp.sum(wide * wide, axis=0, keepdims=True) * GRAM
    pieces = split_three(wide * (-2.0 * GRAM))
    return jnp.concatenate([piece.astype(BF16) for piece in pieces] + [norm_rows(norm, 0)], axis=0)


def other_factor(feat):
    wide = feat.astype(F32)
    norm = jnp.sum(wide * wide, axis=0, keepdims=True) * GRAM
    return jnp.transpose(jnp.concatenate([feat, feat, feat, norm_rows(norm, 3)], axis=0))


def psi_power(dist):
    dist = jnp.maximum(dist, 1e-30)
    radius = dist * lax.rsqrt(dist)
    u = jnp.maximum(SHRINK - radius, 1e-30)
    return (jnp.exp2(19.0 * lax.log2(u)) * (1.0 - u)).astype(BF16)


def tile_unit(left, right, vec, tile_ref, aside=None):
    pieces = [slice(at, at + PIECE) for at in range(0, right.shape[1], PIECE)]
    gram = lambda piece: jnp.dot(left, right[:, piece], preferred_element_type=F32)
    product = lambda part: jnp.dot(vec, part, preferred_element_type=F32)
    dist, part, terms = gram(pieces[0]), None, []
    for index, piece in enumerate(pieces):
        following = gram(pieces[index + 1]) if index + 1 < len(pieces) else None
        strips = []
        for at in range(0, left.shape[0], STRIP):
            strips.append(psi_power(dist[at : at + STRIP]))
            tile_ref[at : at + STRIP, piece] = strips[-1]
        if part is not None:
            terms.append(product(part))
        if index == 1 and aside is not None:
            aside()
        dist, part = following, jnp.concatenate(strips, axis=0)
    return jnp.concatenate(terms + [product(part)], axis=1)


def unpack(pay):
    return jnp.concatenate([pay[:32], pay[32:64]], axis=1), jnp.concatenate([pay[64:72], pay[72:80]], axis=1)


def own_blocks(rows, count):
    return [(row, col) for row in rows for col in range(row, count)]


def own_kernel(
    rows, left_ref, right_ref, vec_ref, arrived_ref, out_ref, sum_ref, tile_ref, sem_ref
):
    sum_ref[...] = jnp.zeros_like(sum_ref)
    count = vec_ref.shape[1] // ROWS
    piece = lambda index: pl.ds(pl.multiple_of(index * ROWS, ROWS), ROWS)
    save = lambda at: pltpu.make_async_copy(tile_ref.at[at], out_ref.at[at], sem_ref.at[at])

    def row_step(row, at):
        def col_step(col, at):
            sum_ref[:, piece(col)] += tile_unit(
                left_ref[piece(row), :], right_ref[:, piece(col)], vec_ref[:, piece(row)],
                tile_ref.at[at],
            )
            save(at).start()

            @pl.when(row != col)
            def _():
                sum_ref[:, piece(row)] += lax.dot_general(
                    vec_ref[:, piece(col)], tile_ref[at], CONTRACT_LANES,
                    preferred_element_type=F32,
                )

            return at + 1

        return lax.fori_loop(row, count, col_step, at)

    lax.fori_loop(rows[0], rows[-1] + 1, row_step, 0)
    for at in range(tile_ref.shape[0]):
        save(at).wait()


def own_again_kernel(blocks, in_ref, vec_ref, sum_ref, tile_ref, sem_ref):
    load = lambda index: pltpu.make_async_copy(
        in_ref.at[index], tile_ref.at[index], sem_ref.at[index]
    )
    for index in range(len(blocks)):
        load(index).start()
    sum_ref[...] = jnp.zeros_like(sum_ref)
    piece = lambda index: slice(index * ROWS, (index + 1) * ROWS)
    for index, (row, col) in enumerate(blocks):
        load(index).wait()
        sum_ref[:, piece(col)] += jnp.dot(
            vec_ref[:, piece(row)], tile_ref[index], preferred_element_type=F32
        )
        if row != col:
            sum_ref[:, piece(row)] += lax.dot_general(
                vec_ref[:, piece(col)], tile_ref[index], CONTRACT_LANES, preferred_element_type=F32
            )


def payload_kernel(
    list_ref, feat_ref, rhs_ref, pay_zero_ref, pay_one_ref, right_ref, left_ref, vec_ref
):
    feat = feat_ref[...]
    rounded = rhs_ref[...].astype(BF16)
    quarter = feat.shape[1] // 4
    for half, pay_ref in enumerate((pay_zero_ref, pay_one_ref)):
        first, second = [slice(at * quarter, (at + 1) * quarter) for at in (2 * half, 2 * half + 1)]
        pay_ref[:32] = feat[:, first]
        pay_ref[32:64] = feat[:, second]
        pay_ref[64:80] = jnp.concatenate([rounded[:, first], rounded[:, second]], axis=0)
    lane = lax.broadcasted_iota(jnp.int32, (16, quarter), 1)
    numbers = jnp.full(lane.shape, -1, jnp.int32)
    for entry in range(list_ref.shape[1]):
        numbers = jnp.where(lane == entry, list_ref[0, entry, 1], numbers)
    pay_zero_ref[80:96] = numbers.astype(F32).astype(BF16)
    right_ref[...] = own_factor(feat)
    left_ref[...] = other_factor(feat)
    vec_ref[...] = rounded


def find_partners(lists_ref, me, slots_ref):
    count, most = lists_ref.shape[0], slots_ref.shape[0] - 2
    for at in range(slots_ref.shape[0]):
        slots_ref[at] = 0
    total = jnp.int32(0)
    for at, place in enumerate(gather_places(count)):
        if at == 0:
            continue
        number = me ^ place
        hit = jnp.bool_(False)
        for entry in range(most):
            hit = hit | (lists_ref[at, entry] == me) | (lists_ref[0, entry] == number)
        slots_ref[1 + total] = jnp.where(hit, at, 0)
        total = total + hit.astype(jnp.int32)
    slots_ref[0] = total


def fetch_from(block_at, block_refs, slots_ref, pay_ref, sem_ref):
    def fetch(which):
        for at, (index, row) in enumerate(block_at):
            @pl.when(slots_ref[1 + which] == at)
            def _():
                pltpu.make_async_copy(
                    block_refs[index].at[pl.ds(row, 80)],
                    pay_ref.at[which % 2],
                    sem_ref.at[which % 2],
                ).start()

    return fetch


def half_tiles(early, slots_ref, right_ref, fetch, front_ref, back_ref, sum_ref, left_ref, vec_ref, pay_ref, sem_ref):
    slot, step = pl.program_id(0), pl.program_id(1)
    last = pl.num_programs(1) - 1

    def arrive(which):
        pltpu.make_async_copy(
            pay_ref.at[(which + 1) % 2], pay_ref.at[which % 2], sem_ref.at[which % 2]
        ).wait()

    def factor(which):
        feat, vec = unpack(pay_ref[which % 2])
        left_ref[which % 2] = other_factor(feat)
        vec_ref[which % 2] = vec

    @pl.when((slot == 0) & (step == 0) & (slots_ref[0] > 0))
    def _():
        fetch(0)

    @pl.when(slot < slots_ref[0])
    def _():
        @pl.when((step == 0) & ((slot == 0) | (not early)))
        def _():
            arrive(slot)
            factor(slot)

        @pl.when((step == 0) & (slot + 1 < slots_ref[0]))
        def _():
            fetch(slot + 1)

        if early:
            @pl.when((step == last) & (slot + 1 < slots_ref[0]))
            def _():
                arrive(slot + 1)

        rows = pl.ds(pl.multiple_of(step * ROWS, ROWS), ROWS)
        place = slot % 2
        left, vec = left_ref[place, rows, :], vec_ref[place, :, rows]
        for tile_ref, here in ((front_ref, slot < FRONT), (back_ref, slot >= FRONT)):
            for ends in (False, True) if early else (None,):
                @pl.when(here if ends is None else here & ((step == last) == ends))
                def _():
                    aside = (lambda: factor(slot + 1)) if ends else None
                    sum_ref[...] += tile_unit(left, right_ref[...], vec, tile_ref.at[0], aside)


def pair_zero_kernel(block_at, me_ref, right_ref, *refs):
    first_refs, block_refs = refs[:PARTS], refs[PARTS:-12]
    front_ref, back_ref, sum_ref, slots_ref = refs[-12:-8]
    left_ref, vec_ref, pay_ref, sem_ref, strip_ref, list_ref, lists_ref, strip_sem_ref = refs[-8:]

    @pl.when((pl.program_id(0) == 0) & (pl.program_id(1) == 0))
    def _():
        strips = [
            pltpu.make_async_copy(
                block_refs[index].at[pl.ds(row + 80, 16), pl.ds(0, 128)],
                strip_ref.at[at],
                strip_sem_ref.at[at],
            )
            for at, (index, row) in enumerate(block_at)
        ]
        for strip in strips:
            strip.start()
        sum_ref[...] = functools.reduce(jnp.add, [first_ref[...] for first_ref in first_refs])
        for at, strip in enumerate(strips):
            strip.wait()
            list_ref[at : at + 1, :] = strip_ref[at].astype(F32)[:1].astype(jnp.int32)
        numbers = pltpu.make_async_copy(list_ref, lists_ref, strip_sem_ref.at[0])
        numbers.start()
        numbers.wait()
        find_partners(lists_ref, me_ref[0], slots_ref)

    fetch = fetch_from(block_at, block_refs, slots_ref, pay_ref, sem_ref)
    half_tiles(
        True, slots_ref, right_ref, fetch, front_ref, back_ref, sum_ref, left_ref, vec_ref, pay_ref, sem_ref
    )


def pair_one_kernel(block_at, slots_ref, right_ref, first_ref, rhs_ref, var_ref, *refs):
    block_refs = refs[:-8]
    front_ref, back_ref, image_ref, send_ref, left_ref, vec_ref, pay_ref, sem_ref = refs[-8:]
    slot, step = pl.program_id(0), pl.program_id(1)

    @pl.when((slot == 0) & (step == 0))
    def _():
        image_ref[...] = first_ref[...]

    fetch = fetch_from(block_at, block_refs, slots_ref, pay_ref, sem_ref)
    half_tiles(
        True, slots_ref, right_ref, fetch, front_ref, back_ref, image_ref, left_ref, vec_ref, pay_ref, sem_ref
    )

    @pl.when((slot == pl.num_programs(0) - 1) & (step == pl.num_programs(1) - 1))
    def _():
        rhs = rhs_ref[...]
        width = rhs.shape[1]
        image = (var_ref[...] + DIAGONAL) * rhs + SCALE * image_ref[...]
        image_ref[...] = image
        send_ref[:, :width] = image.astype(BF16)
        pieces = split_three(jnp.sum(rhs * rhs, axis=1, keepdims=True))
        pieces += split_three(jnp.sum(rhs * image, axis=1, keepdims=True))
        lane = lax.broadcasted_iota(jnp.int32, (rhs.shape[0], TAIL), 1)
        tail = jnp.zeros((rhs.shape[0], TAIL), F32)
        for place, piece in enumerate(pieces):
            tail = jnp.where(lane == place, piece, tail)
        send_ref[:, width:] = tail.astype(BF16)


def again_kernel(
    slots_ref, front_zero_ref, front_one_ref, back_zero_ref, back_one_ref,
    vec_ref, tails_ref, rhs_ref, var_ref, image_ref, *refs
):
    first_refs = refs[:PARTS]
    rows_ref, dots_ref, step_ref, sum_ref, held_ref, sem_ref = refs[PARTS:]
    slot = pl.program_id(0)
    width = rhs_ref.shape[1]
    steps = width // ROWS
    half = width // 2
    parts = (slots_ref[0] - FRONT) * steps

    def fetch(part, back_ref, first):
        at = pl.ds(pl.multiple_of((part % steps - first) * ROWS, ROWS), ROWS)
        return pltpu.make_async_copy(
            back_ref.at[part // steps, at], held_ref.at[part % HELD], sem_ref.at[part % HELD]
        )

    def start(part):
        @pl.when((part < parts) & (part % steps < steps // 2))
        def _():
            fetch(part, back_zero_ref, 0).start()

        @pl.when((part < parts) & (part % steps >= steps // 2))
        def _():
            fetch(part, back_one_ref, steps // 2).start()

    @pl.when(slot == 0)
    def _():
        sum_ref[...] = functools.reduce(jnp.add, [first_ref[...] for first_ref in first_refs])
        for part in range(HELD):
            start(part)

    @pl.when((slot < slots_ref[0]) & (slot < FRONT))
    def _():
        for index, front_ref in enumerate((front_zero_ref, front_one_ref)):
            sum_ref[...] += jnp.dot(
                vec_ref[0, :, index * half : (index + 1) * half], front_ref[0],
                preferred_element_type=F32,
            )

    @pl.when((slot < slots_ref[0]) & (slot >= FRONT))
    def _():
        for step in range(steps):
            part = (slot - FRONT) * steps + step
            fetch(part % HELD, back_zero_ref, part % HELD // (steps // 2) * (steps // 2)).wait()
            sum_ref[...] += jnp.dot(
                vec_ref[0, :, step * ROWS : (step + 1) * ROWS], held_ref[part % HELD],
                preferred_element_type=F32,
            )
            start(part + HELD)

    @pl.when(slot == pl.num_programs(0) - 1)
    def _():
        rhs = rhs_ref[...]
        image = image_ref[...]
        total = jnp.sum(tails_ref[...].astype(F32), axis=0)
        norm = total[:, 0:1] + total[:, 1:2] + total[:, 2:3]
        curve = total[:, 3:4] + total[:, 4:5] + total[:, 5:6]
        length = norm / curve
        second = (var_ref[...] + DIAGONAL) * image + SCALE * sum_ref[...]
        res = rhs - length * image
        res_image = image - length * second
        rows_ref[0:8] = rhs
        rows_ref[8:16] = res
        rows_ref[16:24] = image
        rows_ref[24:32] = res_image
        lane = lax.broadcasted_iota(jnp.int32, (rhs.shape[0], TAIL), 1)
        dots = jnp.zeros((rhs.shape[0], TAIL), F32)
        for place, product in enumerate((res * res, res * res_image, res * image, rhs * res_image)):
            dots = jnp.where(lane == place, jnp.sum(product, axis=1, keepdims=True), dots)
        dots_ref[...] = dots
        step_ref[...] = jnp.where(lane == 0, norm, jnp.where(lane == 1, curve, 0.0))


def order_kernel(rows_ref, perm_ref, out_ref):
    rows = rows_ref[...]
    count, width = rows.shape
    pieces = jnp.concatenate([piece for piece in split_three(rows)], axis=0).astype(BF16)
    perm = perm_ref[...]
    chunk = 256
    for col in range(0, width, chunk):
        total = jnp.zeros((3 * count, chunk), F32)
        for at in range(0, width, chunk):
            index = lax.broadcasted_iota(jnp.int32, (chunk, chunk), 0) + at
            pick = jnp.where(index == perm[:, col : col + chunk], 1.0, 0.0).astype(BF16)
            total += jnp.dot(pieces[:, at : at + chunk], pick, preferred_element_type=F32)
        out_ref[:, col : col + chunk] = total[:count] + total[count : 2 * count] + total[2 * count :]


def swap(value, mask, count):
    return lax.ppermute(value, "row", [(i, i ^ mask) for i in range(count)])


def levels(count, sizes):
    bits = count.bit_length() - 1
    out = []
    sizes = list(sizes)
    while bits:
        take = min(sizes.pop(0) if sizes else 1, bits)
        bits -= take
        out.append([mask << bits for mask in range(1, 1 << take)])
    return out


def tree_sum(value, count):
    for masks in levels(count, [2, 2, 2]):
        others = [swap(value, mask, count) for mask in masks]
        if len(masks) == 3:
            value = (value + others[0]) + (others[1] + others[2])
        else:
            value = value + others[0]
    return value


def gather_levels(count):
    return levels(count, [2] if count <= 16 else [2, 2])


def gather_places(count):
    places = [0]
    for masks in gather_levels(count):
        places = places + [place ^ mask for mask in masks for place in places]
    return places


def tree_gather(value, count):
    blocks, out = value[None], []
    for masks in gather_levels(count):
        blocks = jnp.concatenate([blocks] + [swap(blocks, mask, count) for mask in masks], axis=0)
        out.append(blocks)
    return out


def gate(block, behind):
    return pl.pallas_call(
        lambda *refs: None,
        in_specs=[pl.BlockSpec(memory_space=pl.ANY)] * 2,
        out_specs=pl.BlockSpec(memory_space=pl.ANY),
        out_shape=jax.ShapeDtypeStruct(block.shape, block.dtype),
        input_output_aliases={0: 0},
        compiler_params=pltpu.CompilerParams(vmem_limit_bytes=1024 * 1024),
        name="gate",
    )(block, behind)


def local(features, right_side, variance, hilbert_order, tile_list):
    width = features.shape[1]
    rhs_count = right_side.shape[0]
    count = lax.axis_size("row")
    most = tile_list.shape[1]
    steps = width // ROWS
    shape = jax.ShapeDtypeStruct
    params = pltpu.CompilerParams(vmem_limit_bytes=10 * 1024 * 1024)
    var_row = variance[None, :]

    whole = lambda *ignored: (0, 0)
    row_spec = pl.BlockSpec(right_side.shape, whole)
    var_spec = pl.BlockSpec(var_row.shape, whole)
    pay_shape = (80, width // 4)
    smem = pl.BlockSpec(memory_space=pltpu.SMEM)
    vmem = pl.BlockSpec(memory_space=pltpu.VMEM)
    in_hbm = lambda array: pltpu.with_memory_space_constraint(array, pltpu.HBM)
    pay_zero, pay_one, right, left, rounded = pl.pallas_call(
        payload_kernel,
        in_specs=[smem, vmem, vmem],
        out_shape=[
            shape((96, width // 4), BF16),
            shape(pay_shape, BF16),
            shape((KDIM, width), BF16),
            shape((width, KDIM), BF16),
            shape(right_side.shape, BF16),
        ],
        compiler_params=params,
        name="payload",
    )(tile_list, in_hbm(features), in_hbm(right_side))
    me = jnp.full((1,), lax.axis_index("row"), jnp.int32)
    any_spec = pl.BlockSpec(memory_space=pl.ANY)

    def own_part(rows, arrived):
        blocks = own_blocks(rows, steps)
        tiles, sums = pl.pallas_call(
            functools.partial(own_kernel, rows),
            in_specs=[vmem, vmem, vmem, any_spec],
            out_specs=[any_spec, vmem],
            out_shape=[pltpu.HBM((len(blocks), ROWS, ROWS), BF16), shape(right_side.shape, F32)],
            scratch_shapes=[
                pltpu.VMEM((len(blocks), ROWS, ROWS), BF16),
                pltpu.SemaphoreType.DMA((len(blocks),)),
            ],
            compiler_params=params,
            cost_estimate=pl.CostEstimate(
                flops=5_000_000_000, bytes_accessed=2 * len(blocks) * ROWS * ROWS, transcendentals=0
            ),
            name=f"own_tile_{rows[0]}",
        )(left, right, rounded, arrived)
        return blocks, tiles, sums

    first_masks, *later = gather_levels(count)
    first_level = lambda pay: jnp.concatenate(
        [pay] + [swap(pay, mask, count) for mask in first_masks], axis=0
    )
    near_zero = first_level(pay_zero)
    own_parts = [own_part(range(1), right)]
    near_zero = gate(near_zero, own_parts[0][2])
    near_one = first_level(gate(pay_one, own_parts[0][2]))
    own_parts.append(own_part(range(1, steps), near_zero))
    near_one = gate(near_one, own_parts[1][2])
    zero, places = [near_zero], [0]
    for level, masks in enumerate(later):
        zero = zero + [swap(array, mask, count) for mask in masks for array in zero]
        places = places + [mask ^ place for mask in masks for place in places]
        if level == 0:
            zero[-1] = gate(zero[-1], own_parts[1][2])
    one = [near_one] + [swap(near_one, place, count) for place in places[1:]]
    each = len(first_masks) + 1
    zero_at = [(at, row * 96) for at in range(len(zero)) for row in range(each)]
    one_at = [(at, row * 80) for at in range(len(one)) for row in range(each)]

    half = steps // 2

    def front_at(k, i, *ignored):
        return (jnp.minimum(k, FRONT - 1), jnp.where(k < FRONT, i, half - 1), 0)

    def back_at(k, i, *ignored):
        return (jnp.maximum(k - FRONT, 0), jnp.where(k < FRONT, 0, i), 0)

    half_specs = [pl.BlockSpec((1, ROWS, width), front_at), pl.BlockSpec((1, ROWS, width), back_at)]
    half_shapes = [
        pltpu.VMEM((FRONT, width // 2, width), BF16),
        pltpu.HBM((most - FRONT, width // 2, width), BF16),
    ]
    half_scratch = [
        pltpu.VMEM((2, width // 2, KDIM), BF16),
        pltpu.VMEM((2, rhs_count, width // 2), BF16),
        pltpu.VMEM((2,) + pay_shape, BF16),
        pltpu.SemaphoreType.DMA((2,)),
    ]
    right_spec = pl.BlockSpec(right.shape, whole)
    send_shape = (rhs_count, width + TAIL)
    front_zero, back_zero, half_sum, slots = pl.pallas_call(
        functools.partial(pair_zero_kernel, zero_at),
        grid_spec=pltpu.PrefetchScalarGridSpec(
            num_scalar_prefetch=1,
            grid=(most, half),
            in_specs=[right_spec] + [row_spec] * PARTS + [any_spec] * len(zero),
            out_specs=half_specs + [row_spec, smem],
            scratch_shapes=half_scratch
            + [
                pltpu.VMEM((count, 16, 128), BF16),
                pltpu.VMEM((count, 128), jnp.int32),
                pltpu.SMEM((count, 128), jnp.int32),
                pltpu.SemaphoreType.DMA((count,)),
            ],
        ),
        out_shape=half_shapes
        + [shape(right_side.shape, F32), shape((most + 2,), jnp.int32)],
        compiler_params=params,
        name="pair_zero",
    )(me, right, *[part[2] for part in own_parts], *zero)
    front_one, back_one, image, send = pl.pallas_call(
        functools.partial(pair_one_kernel, one_at),
        grid_spec=pltpu.PrefetchScalarGridSpec(
            num_scalar_prefetch=1,
            grid=(most, half),
            in_specs=[right_spec, row_spec, row_spec, var_spec] + [any_spec] * len(one),
            out_specs=half_specs + [row_spec, pl.BlockSpec(send_shape, whole)],
            scratch_shapes=half_scratch,
        ),
        out_shape=half_shapes + [shape(right_side.shape, F32), shape(send_shape, BF16)],
        compiler_params=params,
        name="pair_one",
    )(slots, right, half_sum, right_side, var_row, *one)
    fronts = [pltpu.with_memory_space_constraint(part, pltpu.VMEM) for part in (front_zero, front_one)]
    backs = [pltpu.with_memory_space_constraint(part, pltpu.HBM) for part in (back_zero, back_one)]

    every_send = tree_gather(send, count)[-1]
    own_again = [
        pl.pallas_call(
            functools.partial(own_again_kernel, blocks),
            in_specs=[any_spec, pl.BlockSpec(send_shape, whole)],
            out_specs=row_spec,
            out_shape=shape(right_side.shape, F32),
            scratch_shapes=[
                pltpu.VMEM((len(blocks), ROWS, ROWS), BF16),
                pltpu.SemaphoreType.DMA((len(blocks),)),
            ],
            compiler_params=params,
            cost_estimate=pl.CostEstimate(
                flops=5_000_000_000, bytes_accessed=2 * len(blocks) * ROWS * ROWS, transcendentals=0
            ),
            name=f"own_again_{part}",
        )(in_hbm(tiles), send)
        for part, (blocks, tiles, _) in enumerate(own_parts)
    ]
    dots_spec = pl.BlockSpec((rhs_count, TAIL), whole)
    rows, dots, steps_one = pl.pallas_call(
        again_kernel,
        grid_spec=pltpu.PrefetchScalarGridSpec(
            num_scalar_prefetch=1,
            grid=(most,),
            in_specs=[
                pl.BlockSpec((1, width // 2, width), lambda k, s: (jnp.minimum(k, FRONT - 1), 0, 0)),
                pl.BlockSpec((1, width // 2, width), lambda k, s: (jnp.minimum(k, FRONT - 1), 0, 0)),
                any_spec,
                any_spec,
                pl.BlockSpec((1,) + send_shape, lambda k, s: (s[1 + k], 0, 0)),
                pl.BlockSpec((count, rhs_count, TAIL), lambda k, s: (0, 0, width // TAIL)),
                row_spec,
                var_spec,
                row_spec,
            ]
            + [row_spec] * PARTS,
            out_specs=[
                pl.BlockSpec((4 * rhs_count, width), whole),
                dots_spec,
                dots_spec,
            ],
            scratch_shapes=[
                pltpu.VMEM(right_side.shape, F32),
                pltpu.VMEM((HELD, ROWS, width), BF16),
                pltpu.SemaphoreType.DMA((HELD,)),
            ],
        ),
        out_shape=[
            shape((4 * rhs_count, width), F32),
            shape((rhs_count, TAIL), F32),
            shape((rhs_count, TAIL), F32),
        ],
        compiler_params=params,
        name="pair_again",
    )(slots, *fronts, *backs, every_send, every_send, right_side, var_row, image, *own_again)

    dots = tree_sum(dots, count)
    ordered = pl.pallas_call(
        order_kernel,
        out_shape=shape(rows.shape, F32),
        compiler_params=params,
        name="curve_order",
    )(rows, hilbert_order)
    norm, curve = steps_one[:, 0:1], steps_one[:, 1:2]
    length = norm / curve
    norm_next = dots[:, 0:1]
    ratio = norm_next / norm
    curve_next = dots[:, 1:2] + ratio * (dots[:, 2:3] + dots[:, 3:4]) + ratio * ratio * curve
    length_next = norm_next / curve_next
    rhs_o, res_o, image_o, res_image_o = [ordered[at : at + 8] for at in range(0, 32, 8)]
    solved = length * rhs_o + length_next * (res_o + ratio * rhs_o)
    residual = res_o - length_next * (res_image_o + ratio * image_o)
    return (solved, residual)


def solution(mesh):
    in_specs = (
        P(None, ("group", "row")),
        P(None, ("group", "row")),
        P(("group", "row")),
        P(("group", "row"), None),
        P(("group", "row"), None, None),
    )
    out_specs = (P(None, ("group", "row")), P(None, ("group", "row")))
    return jax.shard_map(local, mesh=mesh, in_specs=in_specs, out_specs=out_specs, check_vma=False)
```
